32 devices in a mesh: dp: 4 (over y, x), vocab: 8 (over z, core).
Axes of the slice: x: 2, y: 2, z: 4, core: 2. Of those that a mesh axis runs over, the one named last changes fastest.
Arguments:
- src_ids: int32 [4, 1024], P('dp'), may hold values from 0 to 37887
- src_seg: int32 [4, 1024], P('dp'), may hold values from 0 to 30, as said below
- tgt_ids: int32 [4, 1024], P('dp'), may hold values from 0 to 37887
- tgt_seg: int32 [4, 1024], P('dp'), may hold values from 0 to 30, as said below
- pick_pos: int32 [4, 256], P('dp'), may hold values from 0 to 1023
- pick_label: int32 [4, 256], P('dp'), may hold values from 0 to 37887
- attn_w: float32 [12, 512, 512], P(None, 'dp')
- attn_m: float32 [12, 512, 512], P(None, 'dp'), may hold values from -0.00012207031 to 0.00012207031
- attn_v: float32 [12, 512, 512], P(None, 'dp'), may hold values from 1.8694485e-11 to 2.9911176e-10
- ffn_w: float32 [4, 2048, 512], P(None, 'dp'), may hold values from -0.25 to 0.25
- ffn_m: float32 [4, 2048, 512], P(None, 'dp'), may hold values from -0.00012207031 to 0.00012207031
- ffn_v: float32 [4, 2048, 512], P(None, 'dp'), may hold values from 1.8694485e-11 to 2.9911176e-10
- soap_basis: float32 [4, 512, 512], replicated, as said below
- soap_stats: float32 [4, 512, 512], replicated, as said below
- norm_p: float32 [14, 512], P(None, 'dp')
- norm_m: float32 [14, 512], P(None, 'dp'), may hold values from -0.00061035156 to 0.00061035156
- norm_v: float32 [14, 512], P(None, 'dp'), may hold values from 3.738897e-10 to 5.982235e-09
- embedding: float32 [37888, 512], P('vocab', 'dp')
- embed_m: float32 [37888, 512], P('vocab', 'dp'), may hold values from -0.00012207031 to 0.00012207031
- embed_v: float32 [37888, 512], P('vocab', 'dp'), may hold values from 1.8694485e-11 to 2.9911176e-10
Outputs:
- loss_sum: float32 [], replicated
- sentences: float32 [], replicated
- grad_norm: float32 [], replicated
- attn_w_new: float32 [12, 512, 512], P(None, 'dp')
- attn_m_new: float32 [12, 512, 512], P(None, 'dp')
- attn_v_new: float32 [12, 512, 512], P(None, 'dp')
- ffn_w_new: float32 [4, 2048, 512], P(None, 'dp')
- ffn_m_new: float32 [4, 2048, 512], P(None, 'dp')
- ffn_v_new: float32 [4, 2048, 512], P(None, 'dp')
- basis_new: float32 [4, 512, 512], replicated
- stats_new: float32 [4, 512, 512], replicated
- norm_p_new: float32 [14, 512], P(None, 'dp')
- norm_m_new: float32 [14, 512], P(None, 'dp')
- norm_v_new: float32 [14, 512], P(None, 'dp')
- embedding_new: float32 [37888, 512], P('vocab', 'dp')
- embed_m_new: float32 [37888, 512], P('vocab', 'dp')
- embed_v_new: float32 [37888, 512], P('vocab', 'dp')
The draws below stay inside these ranges and needn't reach their ends.
Inputs may be any that keep to these rules, and one draw needn't show every extreme that they name: Sentence numbers of a row start at 0 and rise by one at the first token of each sentence; row r of src_seg and row r of tgt_seg hold the same number of sentences; the last row holds 31 sentences. `tgt_seg`: same law as src_seg, with the same number of sentences in each row. `soap_basis`: orthogonal matrices. `soap_stats`: symmetric positive definite.
All inputs are finite; a program needn't handle non-finite values.
Results may differ from the reference program's by a relative error of at most 0.012.
Values may be sent and summed in bfloat16 or wider, within the bound.
A program may use at most 384 MiB of HBM per device.

```python
import math
import jax
import jax.numpy as jnp
import numpy as np
from jax import lax

D = 512
HEADS = 8
FF = 2048
ROW_LEN = 1024
SENT_LO = 8
STEP = 10
ROWS = 4
VOCAB = 37888
PICKS = 256


def sentence_counts(key):
    row_index = jnp.arange(ROWS)
    least = SENT_LO + 2 * SENT_LO * row_index // max(ROWS - 1, 1)
    counts = least + jax.random.randint(key, (ROWS,), 0, SENT_LO)
    return counts.at[ROWS - 1].set(4 * SENT_LO - 1)


def cuts_to_segments(key, counts):
    row_keys = jax.random.split(key, ROWS)

    def one_row(row_key, count):
        shuffled = jax.random.permutation(row_key, ROW_LEN - 1)[:4 * SENT_LO - 2] + 1
        live_cuts = jnp.arange(4 * SENT_LO - 2) < count - 1
        places = jnp.arange(ROW_LEN)
        return jnp.sum((shuffled[None, :] <= places[:, None]) & live_cuts[None, :], axis=1).astype(jnp.int32)
    return jax.vmap(one_row)(row_keys, counts)


def draw_src_seg(key, part):
    counts = sentence_counts(key)
    key = jax.random.fold_in(key, 11)
    return cuts_to_segments(key, counts)


def draw_tgt_seg(key, part):
    counts = sentence_counts(key)
    key = jax.random.fold_in(key, 13)
    return cuts_to_segments(key, counts)


def draw_attn_w(key, part):
    key = jax.random.fold_in(key, 21)
    entries = jax.random.normal(key, (12, D, D), jnp.float32)
    boost = jnp.where(jnp.arange(12) % 4 == 3, 3.0, 1.0)
    return entries * boost[:, None, None] / math.sqrt(D)


def draw_norm_p(key, part):
    key = jax.random.fold_in(key, 23)
    gain_key, bias_key = jax.random.split(key)
    rising = jnp.arange(D, dtype=jnp.float32) / D
    gain_rows = (0.6 + 1.2 * rising)[None, :] * jax.random.uniform(gain_key, (7, D), jnp.float32, 0.85, 1.15)
    biases = 0.2 * jax.random.normal(bias_key, (7, D), jnp.float32)
    return jnp.concatenate([gain_rows, biases], axis=0)


def draw_embedding(key, part):
    key = jax.random.fold_in(key, 25)
    rows_up = jnp.arange(VOCAB, dtype=jnp.float32) / VOCAB
    entries = jax.random.normal(key, (VOCAB, D), jnp.float32)
    rising = 1.0 + 2.0 * rows_up
    return entries * rising[:, None] / math.sqrt(D)


def draw_soap_basis(key, part):
    key = jax.random.fold_in(key, 27)
    sign_key, order_key = jax.random.split(key)
    index = jnp.arange(D, dtype=jnp.int32)
    phase = (2 * index[:, None] + 1) * index[None, :] % (4 * D)
    cosine = jnp.cos(phase.astype(jnp.float32) * (math.pi / (2 * D))) * math.sqrt(2.0 / D)
    cosine = cosine * jnp.where(index == 0, math.sqrt(0.5), 1.0)[None, :]
    signs = (2 * jax.random.randint(sign_key, (4, D), 0, 2) - 1).astype(jnp.float32)
    orders = jax.vmap(lambda order_seed: jax.random.permutation(order_seed, D))(jax.random.split(order_key, 4))
    columns = jnp.moveaxis(jnp.take(cosine, orders, axis=1), 1, 0)
    return signs[:, :, None] * columns


def draw_soap_stats(key, part):
    key = jax.random.fold_in(key, 29)
    diag_key, noise_key = jax.random.split(key)
    level = 0.053 * FF / (12 * D * D + 4 * FF * D + 14 * D + VOCAB * D)
    diagonal = jax.random.uniform(diag_key, (4, D), jnp.float32, 1.0, 4.0)
    noise = jax.random.normal(noise_key, (4, D, D), jnp.float32) * (0.2 / math.sqrt(D))
    symmetric = noise + jnp.swapaxes(noise, 1, 2)
    identity = jnp.eye(D, dtype=jnp.float32)
    return level * (symmetric * (1.0 - identity) + diagonal[:, :, None] * identity)


def touch_ends(array, key, low, high):
    place = [jax.random.randint(jax.random.fold_in(key, axis), (), 0, length) for axis, length in enumerate(array.shape)]
    main_axis = array.shape.index(max(array.shape))
    neighbour = place[:main_axis] + [(place[main_axis] + 1) % array.shape[main_axis]] + place[main_axis + 1:]
    return array.at[tuple(place)].set(low).at[tuple(neighbour)].set(high)


def block_scale(stream_key, shape, cuts, low, top_value):
    factor_of, own = 1.0, jax.random.fold_in(stream_key, 6)
    for axis_at, blocks in cuts:
        draws = jnp.exp(jax.random.uniform(jax.random.fold_in(own, axis_at), (blocks,), jnp.float32, low / len(cuts), top_value / len(cuts)))
        factor_of = factor_of * jnp.repeat(draws, shape[axis_at] // blocks).reshape([-1 if axis == axis_at else 1 for axis in range(len(shape))])
    return factor_of


def cumulative_ranks(count, skew):
    loads = [(1 << 20) // math.isqrt(grade ** skew) + 1 for grade in range(1, count + 1)]
    scale = 1 + sum(loads) // (1 << 30)
    return np.cumsum(np.array([max(1, weight // scale) for weight in loads]))


def ranked_ids(own_key, dims, number_of, slope):
    table = cumulative_ranks(number_of, slope)
    ticket = jax.random.randint(jax.random.fold_in(own_key, 1), dims, 0, int(table[number_of - 1]))
    grade = jnp.searchsorted(jnp.asarray(table, jnp.int32), ticket, side="right")
    return jax.random.permutation(jax.random.fold_in(own_key, 2), number_of)[grade].astype(jnp.int32)


def centred(own_key, dims, width, limit, cuts=(), kind=jnp.bfloat16):
    result = jax.random.normal(own_key, dims, jnp.float32) * width
    if len(cuts) > 0:
        result = block_scale(own_key, dims, cuts, -0.22, 0.18) * result
    return jnp.clip(result, min=-limit, max=limit).astype(kind)


def setup_inputs(seed: int = 0) -> dict:
    seeds = jax.random.split(jax.random.key(seed), 21)
    src_ids = touch_ends(ranked_ids(seeds[0], (ROWS, ROW_LEN), VOCAB, 2), jax.random.fold_in(seeds[0], 3), 0, VOCAB - 1).astype(jnp.int32)
    src_seg = draw_src_seg(jax.random.fold_in(seeds[20], 71), 0)
    tgt_ids = touch_ends(ranked_ids(seeds[2], (ROWS, ROW_LEN), VOCAB, 2), jax.random.fold_in(seeds[2], 3), 0, VOCAB - 1).astype(jnp.int32)
    tgt_seg = draw_tgt_seg(jax.random.fold_in(seeds[20], 71), 0)
    pick_pos = touch_ends(jax.random.randint(seeds[4], (ROWS, PICKS), 0, ROW_LEN), jax.random.fold_in(seeds[4], 1), 0, ROW_LEN - 1).astype(jnp.int32)
    pick_label = touch_ends(ranked_ids(seeds[5], (ROWS, PICKS), VOCAB, 2), jax.random.fold_in(seeds[5], 3), 0, VOCAB - 1).astype(jnp.int32)
    attn_w = draw_attn_w(jax.random.fold_in(seeds[20], 71), 0)
    attn_m = centred(seeds[7], (12, D, D), (0.11 / (12 * D * D + 4 * FF * D + 14 * D + VOCAB * D) ** 0.5), 0.00012207031, ((1, 4),), jnp.float32)
    attn_v = jnp.clip(jnp.exp(math.log(2.9911176313568433e-10) - 2.7725887 * jax.random.uniform(seeds[8], (12, D, D), jnp.float32) ** block_scale(seeds[8], (12, D, D), ((1, 4),), -0.2, 0.2)), 1.869448519598027e-11, 2.9911176313568433e-10)
    ffn_w = centred(seeds[9], (4, FF, D), D ** -0.5, 0.25, ((1, 4),), jnp.float32)
    ffn_m = centred(seeds[10], (4, FF, D), (0.11 / (12 * D * D + 4 * FF * D + 14 * D + VOCAB * D) ** 0.5), 0.00012207031, ((1, 4),), jnp.float32)
    ffn_v = jnp.clip(jnp.exp(math.log(2.9911176313568433e-10) - 2.7725887 * jax.random.uniform(seeds[11], (4, FF, D), jnp.float32) ** block_scale(seeds[11], (4, FF, D), ((1, 4),), -0.2, 0.2)), 1.869448519598027e-11, 2.9911176313568433e-10)
    soap_basis = draw_soap_basis(jax.random.fold_in(seeds[20], 71), 0)
    soap_stats = draw_soap_stats(jax.random.fold_in(seeds[20], 71), 0)
    norm_p = draw_norm_p(jax.random.fold_in(seeds[20], 71), 0)
    norm_m = centred(seeds[15], (14, D), (0.5 / (12 * D * D + 4 * FF * D + 14 * D + VOCAB * D) ** 0.5), 0.00061035156, ((1, 4),), jnp.float32)
    norm_v = jnp.clip(jnp.exp(math.log(5.982235151691384e-09) - 2.7725887 * jax.random.uniform(seeds[16], (14, D), jnp.float32) ** block_scale(seeds[16], (14, D), ((1, 4),), -0.2, 0.2)), 3.738896969807115e-10, 5.982235151691384e-09)
    embedding = draw_embedding(jax.random.fold_in(seeds[20], 71), 0)
    embed_m = centred(seeds[18], (VOCAB, D), (0.11 / (12 * D * D + 4 * FF * D + 14 * D + VOCAB * D) ** 0.5), 0.00012207031, ((0, 8), (1, 4)), jnp.float32)
    embed_v = jnp.clip(jnp.exp(math.log(2.9911176313568433e-10) - 2.7725887 * jax.random.uniform(seeds[19], (VOCAB, D), jnp.float32) ** block_scale(seeds[19], (VOCAB, D), ((0, 8), (1, 4)), -0.2, 0.2)), 1.869448519598027e-11, 2.9911176313568433e-10)
    return dict(src_ids=src_ids, src_seg=src_seg, tgt_ids=tgt_ids, tgt_seg=tgt_seg, pick_pos=pick_pos, pick_label=pick_label, attn_w=attn_w, attn_m=attn_m, attn_v=attn_v, ffn_w=ffn_w, ffn_m=ffn_m, ffn_v=ffn_v, soap_basis=soap_basis, soap_stats=soap_stats, norm_p=norm_p, norm_m=norm_m, norm_v=norm_v, embedding=embedding, embed_m=embed_m, embed_v=embed_v)


@jax.custom_vjp
def low(v):
    return lax.optimization_barrier(v.astype(jnp.bfloat16)).astype(jnp.float32)

@jax.custom_vjp
def low_back(v):
    return v

def low_keep(v):
    return (low(v), None)

def low_pass(kept, grad):
    return (grad,)

def back_keep(v):
    return (v, None)

def back_low(kept, grad):
    return (low(grad),)
low.defvjp(low_keep, low_pass)
low_back.defvjp(back_keep, back_low)
highest = lax.Precision.HIGHEST
beta_one = 0.9
beta_two = 0.999
adam_eps = 1e-08
decay_rate = 0.01
rate_matrix = 0.03
rate_vector = 0.3
clip_limit = 1.0
stat_decay = 0.95
norm_eps = 1e-06

def rounded(values):
    return low_back(low(values))

def matmul(left, right):
    return jnp.dot(left, right, precision=highest)

def layer_norm(values, gain_row, bias_row):
    centre = values - lax.optimization_barrier(jnp.mean(values, axis=-1, keepdims=True))
    spread = lax.optimization_barrier(jnp.mean(centre * centre, axis=-1, keepdims=True))
    return centre * lax.rsqrt(spread + norm_eps) * gain_row + bias_row

def sinusoid(length, model_width):
    places = jnp.arange(length, dtype=jnp.float32)[:, None]
    halves = jnp.arange(model_width // 2, dtype=jnp.float32)[None, :]
    angles = places * jnp.exp(halves * (-2.0 * math.log(10000.0) / model_width))
    return jnp.stack([jnp.sin(angles), jnp.cos(angles)], axis=-1).reshape(length, model_width)

def allowed_bias(seg_query, seg_keys, place_query, causal):
    allowed = seg_query[:, None] == seg_keys[None, :]
    if causal:
        allowed = allowed & (jnp.arange(seg_keys.shape[0])[None, :] <= place_query[:, None])
    return jnp.where(allowed, 0.0, -1000000000.0).astype(jnp.float32)

def pick_weights(target_seg, pick_rows):
    sentence = jnp.take(target_seg, pick_rows, axis=0)
    return lax.optimization_barrier(jnp.sum((sentence[:, None] == sentence[None, :]).astype(jnp.float32), axis=1))

def attend(query_in, key_in, weights, seg_query, seg_keys, causal):
    length = query_in.shape[0]
    block_rows = min(512, length)
    queries = rounded(matmul(query_in, weights[0])).reshape(length // block_rows, block_rows, HEADS, -1)
    key_heads = rounded(matmul(key_in, weights[1])).reshape(key_in.shape[0], HEADS, -1)
    value_heads = rounded(matmul(key_in, weights[2])).reshape(key_in.shape[0], HEADS, -1)
    score_scale = 1.0 / math.sqrt(key_heads.shape[-1])
    places = jnp.arange(length).reshape(-1, block_rows)

    def one_block(inputs):
        query_part, seg_part, place_part = inputs
        scores = jnp.einsum('qhd,khd->hqk', query_part, key_heads, precision=highest) * score_scale
        scores = low_back(scores + allowed_bias(seg_part, seg_keys, place_part, causal)[None])
        row_top = lax.optimization_barrier(jnp.max(scores, axis=-1, keepdims=True))
        exponent = jnp.exp(scores - row_top)
        softmax_rows = exponent / lax.optimization_barrier(jnp.sum(exponent, axis=-1, keepdims=True))
        return jnp.einsum('hqk,khd->qhd', low(softmax_rows), value_heads, precision=highest)
    mixed = lax.map(jax.checkpoint(one_block), (queries, seg_query.reshape(-1, block_rows), places))
    mixed = rounded(mixed.reshape(length, -1))
    return low_back(matmul(mixed, weights[3]))

def feed_forward(inputs, w_in, w_out):
    hidden = low_back(lax.dot_general(inputs, w_in, (((1,), (1,)), ((), ())), precision=highest))
    active = low(jax.nn.gelu(hidden, approximate=True))
    return low_back(matmul(active, w_out))

def row_loss(params, source, source_seg, target, target_seg, pick_rows, labels):
    attention, ffn_stack, norm_stack, embed_table = params
    w_attn = low(attention)
    w_ffn = low(ffn_stack)
    norm_rows = low(norm_stack)
    table_low = low(embed_table)
    gain_rows, bias_rows = (norm_rows[:7], norm_rows[7:])
    model_width = table_low.shape[1]
    positional = sinusoid(source.shape[0], model_width)
    embed_scale = math.sqrt(model_width)
    residual = low_back(jnp.take(table_low, source, axis=0)) * embed_scale + positional
    normed = low(layer_norm(residual, gain_rows[0], bias_rows[0]))
    residual = residual + attend(normed, normed, w_attn[0:4], source_seg, source_seg, False)
    normed = low(layer_norm(residual, gain_rows[1], bias_rows[1]))
    residual = residual + feed_forward(normed, w_ffn[0], w_ffn[1])
    encoded = low(layer_norm(residual, gain_rows[2], bias_rows[2]))
    residual = low_back(jnp.take(table_low, target, axis=0)) * embed_scale + positional
    normed = low(layer_norm(residual, gain_rows[3], bias_rows[3]))
    residual = residual + attend(normed, normed, w_attn[4:8], target_seg, target_seg, True)
    normed = low(layer_norm(residual, gain_rows[4], bias_rows[4]))
    residual = residual + attend(normed, encoded, w_attn[8:12], target_seg, source_seg, False)
    normed = low(layer_norm(residual, gain_rows[5], bias_rows[5]))
    residual = residual + feed_forward(normed, w_ffn[2], w_ffn[3])
    final_out = layer_norm(residual, gain_rows[6], bias_rows[6])
    picked = low(jnp.take(final_out, pick_rows, axis=0))
    logits = low_back(lax.dot_general(picked, table_low, (((1,), (1,)), ((), ())), precision=highest))
    row_top = lax.optimization_barrier(jnp.max(logits, axis=-1, keepdims=True))
    row_total = row_top[:, 0] + jnp.log(lax.optimization_barrier(jnp.sum(jnp.exp(logits - row_top), axis=-1)))
    chosen = jnp.take_along_axis(logits, labels[:, None], axis=1)[:, 0]
    return jnp.sum((row_total - chosen) / pick_weights(target_seg, pick_rows))

def adam_direction(moment, second):
    return moment / (1.0 - beta_one ** STEP) / (jnp.sqrt(second / (1.0 - beta_two ** STEP)) + adam_eps)

def adam_update(weight, grad_item, moment, second, step_rate, decay_weight):
    moment = beta_one * moment + (1.0 - beta_one) * grad_item
    second = beta_two * second + (1.0 - beta_two) * grad_item * grad_item
    return (weight - step_rate * (adam_direction(moment, second) + decay_weight * weight), moment, second)

def renew_basis(statistic, soap_basis):
    product = jnp.einsum('mde,mef->mdf', statistic, soap_basis, precision=highest)
    gram_matrix = jnp.einsum('mdf,mdg->mfg', product, product, precision=highest)
    factor = jnp.linalg.cholesky(gram_matrix)

    def solve_one(lower_factor, product_one):
        return jax.scipy.linalg.solve_triangular(lower_factor, product_one.T, lower=True)
    return jnp.swapaxes(jax.vmap(solve_one)(factor, product), 1, 2)

def reference(src_ids, src_seg, tgt_ids, tgt_seg, pick_pos, pick_label, attn_w, attn_m, attn_v, ffn_w, ffn_m, ffn_v, soap_basis, soap_stats, norm_p, norm_m, norm_v, embedding, embed_m, embed_v):
    params = (attn_w, ffn_w, norm_p, embedding)

    def one_row(running, row_data):

        def loss_of(values):
            return row_loss(values, *row_data)
        row_value, pullback = jax.vjp(loss_of, params)
        gradients = pullback(jnp.ones((), row_value.dtype))[0]
        return ((running[0] + row_value, jax.tree.map(jnp.add, running[1], gradients)), None)
    initial = (jnp.zeros((), jnp.float32), jax.tree.map(jnp.zeros_like, params))
    (loss_sum, gradients), _ = lax.scan(one_row, initial, (src_ids, src_seg, tgt_ids, tgt_seg, pick_pos, pick_label))
    sentences = jnp.sum(tgt_seg[:, -1] + 1).astype(jnp.float32)
    gradients = [grad_item / sentences for grad_item in gradients]
    squares = jnp.sum(gradients[0] ** 2) + jnp.sum(gradients[1] ** 2) + jnp.sum(gradients[2] ** 2) + jnp.sum(gradients[3] ** 2)
    grad_norm = jnp.sqrt(squares)
    clip_factor = jnp.minimum(1.0, clip_limit / (grad_norm + norm_eps))
    g_attn, g_ffn, g_norm, g_embed = [grad_item * clip_factor for grad_item in gradients]
    new_attn, m_attn, v_attn = adam_update(attn_w, g_attn, attn_m, attn_v, rate_matrix, decay_rate)
    new_norm, m_norm, v_norm = adam_update(norm_p, g_norm, norm_m, norm_v, rate_vector, 0.0)
    new_embed, m_embed, v_embed = adam_update(embedding, g_embed, embed_m, embed_v, rate_matrix, decay_rate)
    rotated = jnp.einsum('mfd,mde->mfe', g_ffn, soap_basis, precision=highest)
    m_ffn = beta_one * ffn_m + (1.0 - beta_one) * rotated
    v_ffn = beta_two * ffn_v + (1.0 - beta_two) * rotated * rotated
    back_rotated = jnp.einsum('mfe,mde->mfd', adam_direction(m_ffn, v_ffn), soap_basis, precision=highest)
    new_ffn = ffn_w - rate_matrix * (back_rotated + decay_rate * ffn_w)
    new_stats = stat_decay * soap_stats + (1.0 - stat_decay) * jnp.einsum('mfd,mfe->mde', g_ffn, g_ffn, precision=highest)
    new_basis = renew_basis(new_stats, soap_basis)
    return (loss_sum, sentences, grad_norm, new_attn, m_attn, v_attn, new_ffn, m_ffn, v_ffn, new_basis, new_stats, new_norm, m_norm, v_norm, new_embed, m_embed, v_embed)
```

```python
from functools import partial
import math

import jax
import jax.numpy as jnp
import numpy as np
from jax import lax
from jax.experimental import pallas as pl
from jax.experimental.pallas import tpu as pltpu
from jax.sharding import PartitionSpec as P

HEADS = 8
STEP = 10
TILE = 128

highest = lax.Precision.HIGHEST
beta_one = 0.9
beta_two = 0.999
adam_eps = 1e-08
decay_rate = 0.01
rate_matrix = 0.03
rate_vector = 0.3
clip_limit = 1.0
stat_decay = 0.95
norm_eps = 1e-06
masked = -1e30
log_two_e = math.log2(math.e)
vmem = pl.BlockSpec(memory_space=pltpu.VMEM)
smem = pl.BlockSpec(memory_space=pltpu.SMEM)


def dot_dims(left, right, left_dim, right_dim):
    return lax.dot_general(
        left, right, (((left_dim,), (right_dim,)), ((), ())), preferred_element_type=jnp.float32
    )


def dot_exact(left, right, left_dim, right_dim):
    return lax.dot_general(
        left,
        right,
        (((left_dim,), (right_dim,)), ((), ())),
        precision=highest,
        preferred_element_type=jnp.float32,
    )


def call(kernel, outs, *args, scratch=(), smem_args=0):
    return pl.pallas_call(
        kernel,
        out_shape=outs,
        in_specs=[vmem] * (len(args) - smem_args) + [smem] * smem_args,
        out_specs=jax.tree.map(lambda _: vmem, outs),
        scratch_shapes=list(scratch),
        compiler_params=pltpu.CompilerParams(vmem_limit_bytes=56 * 2**20),
    )(*args)


def low(*shape):
    return jax.ShapeDtypeStruct(shape, jnp.bfloat16)


def full(*shape):
    return jax.ShapeDtypeStruct(shape, jnp.float32)


def norm_parts(values):
    centre = values - jnp.mean(values, axis=-1, keepdims=True)
    spread = jnp.mean(centre * centre, axis=-1, keepdims=True)
    root = lax.rsqrt(spread + norm_eps)
    return centre * root, root


def norm_forward(values, ln_ref):
    return norm_parts(values)[0] * ln_ref[0:1, :] + ln_ref[1:2, :]


def norm_backward(grad, values, ln_ref, ln_grad_ref):
    normed, root = norm_parts(values)
    ln_grad_ref[0:1, :] = jnp.sum(grad * normed, axis=0, keepdims=True)
    ln_grad_ref[1:2, :] = jnp.sum(grad, axis=0, keepdims=True)
    inner = grad * ln_ref[0:1, :]
    return root * (
        inner
        - jnp.mean(inner, axis=-1, keepdims=True)
        - normed * jnp.mean(inner * normed, axis=-1, keepdims=True)
    )


def at_tile(index):
    return pl.ds(pl.multiple_of(index * TILE, TILE), TILE)


def tile_mask(segq_ref, segk_ref, qi, ki, causal):
    allowed = segk_ref[at_tile(ki), :] == segq_ref[:, at_tile(qi)]
    if causal:
        ahead = lax.broadcasted_iota(jnp.int32, (TILE, TILE), 0) - lax.broadcasted_iota(
            jnp.int32, (TILE, TILE), 1
        )
        allowed = allowed & (ahead <= (qi - ki) * TILE)
    return allowed


def for_tiles(count, edge_ref, causal, step):
    def one(pair, carry):
        qi, ki = pair // count, lax.rem(pair, count)
        live = (edge_ref[0, qi] <= edge_ref[3, ki]) & (edge_ref[2, ki] <= edge_ref[1, qi])
        if causal:
            live = live & (ki <= qi)

        @pl.when(live)
        def _():
            step(qi, ki)

        return carry

    lax.fori_loop(0, count * count, one, 0)


def tile_edges(seg_q, seg_k):
    last = TILE - 1
    return jnp.stack([seg_q[::TILE], seg_q[last::TILE], seg_k[::TILE], seg_k[last::TILE]])


def attn_forward_kernel(causal, cross, *refs):
    refs = list(refs)
    x_ref, ln_ref, w_ref, segq_ref, segk_ref = refs[:5]
    refs = refs[5:]
    key_ref = refs.pop(0) if cross else None
    (edge_ref, out_ref, a_ref, qt_ref, kt_ref, vt_ref, ot_ref, lse_ref, top_ref, sum_ref, acc_ref) = refs
    length, width = x_ref.shape
    head_size = width // HEADS
    a_ref[...] = norm_forward(x_ref[...], ln_ref).astype(jnp.bfloat16)
    key_in = key_ref if cross else a_ref
    qt_ref[...] = dot_dims(a_ref[...], w_ref[0], 1, 0).astype(jnp.bfloat16).T
    kt_ref[...] = dot_dims(key_in[...], w_ref[1], 1, 0).astype(jnp.bfloat16).T
    vt_ref[...] = dot_dims(key_in[...], w_ref[2], 1, 0).astype(jnp.bfloat16).T
    top_ref[...] = jnp.full(top_ref.shape, masked, jnp.float32)
    sum_ref[...] = jnp.zeros(sum_ref.shape, jnp.float32)
    acc_ref[...] = jnp.zeros(acc_ref.shape, jnp.float32)
    scale = log_two_e / math.sqrt(head_size)
    bands = [slice(h * head_size, (h + 1) * head_size) for h in range(HEADS)]

    def step(qi, ki):
        q_at, k_at = at_tile(qi), at_tile(ki)
        allowed = tile_mask(segq_ref, segk_ref, qi, ki, causal)
        scores = [dot_dims(kt_ref[band, k_at], qt_ref[band, q_at], 0, 0) * scale for band in bands]
        scores = [jnp.where(allowed, part, masked) for part in scores]
        top = top_ref[:, q_at]
        new_top = jnp.maximum(
            top,
            jnp.concatenate([jnp.max(part, axis=0, keepdims=True) for part in scores], axis=0),
        )
        fade = jnp.exp2(top - new_top)
        parts = [jnp.exp2(scores[h] - new_top[h : h + 1]) for h in range(HEADS)]
        top_ref[:, q_at] = new_top
        sum_ref[:, q_at] = sum_ref[:, q_at] * fade + jnp.concatenate(
            [jnp.sum(part, axis=0, keepdims=True) for part in parts], axis=0
        )
        mixed = [
            dot_dims(vt_ref[bands[h], k_at], parts[h].astype(jnp.bfloat16), 1, 0)
            for h in range(HEADS)
        ]
        acc = acc_ref[:, q_at]
        acc_ref[:, q_at] = jnp.concatenate(
            [acc[bands[h]] * fade[h : h + 1] + mixed[h] for h in range(HEADS)], axis=0
        )

    for_tiles(length // TILE, edge_ref, causal, step)
    lse_ref[...] = top_ref[...] + jnp.log2(sum_ref[...])
    for h in range(HEADS):
        ot_ref[bands[h], :] = (acc_ref[bands[h], :] / sum_ref[h : h + 1, :]).astype(jnp.bfloat16)
    out_ref[...] = x_ref[...] + dot_dims(ot_ref[...], w_ref[3], 0, 0)


def attn_forward(x, ln, weights, seg_q, seg_k, key_in, causal):
    length, width = x.shape
    cross = key_in is not None
    segs = (seg_q[None, :], jnp.broadcast_to(seg_k[:, None], (length, TILE)))
    edges = tile_edges(seg_q, seg_k)
    args = (x, ln, weights, *segs) + ((key_in,) if cross else ()) + (edges,)
    outs = (full(length, width), low(length, width)) + (low(width, length),) * 4
    out, normed, *stored = call(
        partial(attn_forward_kernel, causal, cross),
        outs + (full(HEADS, length),),
        *args,
        scratch=[
            pltpu.VMEM((HEADS, length), jnp.float32),
            pltpu.VMEM((HEADS, length), jnp.float32),
            pltpu.VMEM((width, length), jnp.float32),
        ],
        smem_args=1,
    )
    return out, (x, ln, weights, segs, edges, causal, cross, normed, stored)


def attn_backward_kernel(causal, cross, *refs):
    (g_ref, x_ref, ln_ref, w_ref, segq_ref, segk_ref, qt_ref, kt_ref, vt_ref, ot_ref, lse_ref) = refs[:11]
    refs = list(refs[11:])
    edge_ref, out_ref, ln_grad_ref, low_ref, gq_ref, gk_ref, gv_ref = refs[:7]
    refs = refs[7:]
    key_grad_ref = refs.pop(0) if cross else None
    got_ref, delta_ref, gqt_ref, gkt_ref, gvt_ref = refs
    length, width = x_ref.shape
    head_size = width // HEADS
    low_ref[...] = g_ref[...].astype(jnp.bfloat16)
    got_ref[...] = dot_dims(low_ref[...], w_ref[3], 1, 1).astype(jnp.bfloat16).T
    bands = [slice(h * head_size, (h + 1) * head_size) for h in range(HEADS)]
    for h in range(HEADS):
        delta_ref[h : h + 1, :] = jnp.sum(
            got_ref[bands[h], :].astype(jnp.float32) * ot_ref[bands[h], :].astype(jnp.float32),
            axis=0,
            keepdims=True,
        )
    for ref in (gqt_ref, gkt_ref, gvt_ref):
        ref[...] = jnp.zeros(ref.shape, jnp.float32)
    scale = log_two_e / math.sqrt(head_size)
    back = 1.0 / math.sqrt(head_size)

    def step(qi, ki):
        q_at, k_at = at_tile(qi), at_tile(ki)
        allowed = tile_mask(segq_ref, segk_ref, qi, ki, causal)
        scores = [dot_dims(kt_ref[band, k_at], qt_ref[band, q_at], 0, 0) for band in bands]
        grads = [dot_dims(vt_ref[band, k_at], got_ref[band, q_at], 0, 0) for band in bands]
        parts = [
            jnp.where(allowed, jnp.exp2(scores[h] * scale - lse_ref[h : h + 1, q_at]), 0.0)
            for h in range(HEADS)
        ]
        grads = [parts[h] * (grads[h] - delta_ref[h : h + 1, q_at]) for h in range(HEADS)]
        parts_t = [part.T.astype(jnp.bfloat16) for part in parts]
        grads_t = [part.T.astype(jnp.bfloat16) for part in grads]
        grads = [part.astype(jnp.bfloat16) for part in grads]
        for ref, place, terms in (
            (gvt_ref, k_at, [dot_dims(got_ref[bands[h], q_at], parts_t[h], 1, 0) for h in range(HEADS)]),
            (gkt_ref, k_at, [dot_dims(qt_ref[bands[h], q_at], grads_t[h], 1, 0) for h in range(HEADS)]),
            (gqt_ref, q_at, [dot_dims(kt_ref[bands[h], k_at], grads[h], 1, 0) for h in range(HEADS)]),
        ):
            ref[:, place] += jnp.concatenate(terms, axis=0)

    for_tiles(length // TILE, edge_ref, causal, step)
    gq_ref[...] = (gqt_ref[...] * back).astype(jnp.bfloat16).T
    gk_ref[...] = (gkt_ref[...] * back).astype(jnp.bfloat16).T
    gv_ref[...] = gvt_ref[...].astype(jnp.bfloat16).T
    from_query = dot_dims(gq_ref[...], w_ref[0], 1, 1)
    from_keys = dot_dims(gk_ref[...], w_ref[1], 1, 1) + dot_dims(gv_ref[...], w_ref[2], 1, 1)
    if cross:
        key_grad_ref[...] = from_keys
    else:
        from_query = from_query + from_keys
    out_ref[...] = g_ref[...] + norm_backward(from_query, x_ref[...], ln_ref, ln_grad_ref)


def attn_backward(grad, stored):
    x, ln, weights, segs, edges, causal, cross, _, kept = stored
    length, width = x.shape
    outs = (full(length, width), full(2, width)) + (low(length, width),) * 4
    if cross:
        outs = outs + (full(length, width),)
    out, ln_grad, *rest = call(
        partial(attn_backward_kernel, causal, cross),
        outs,
        grad,
        x,
        ln,
        weights,
        *segs,
        *kept,
        edges,
        scratch=[pltpu.VMEM((width, length), jnp.bfloat16), pltpu.VMEM((HEADS, length), jnp.float32)]
        + [pltpu.VMEM((width, length), jnp.float32)] * 3,
        smem_args=1,
    )
    return out, ln_grad, rest[:4], rest[4] if cross else None


def gelu_parts(hidden):
    root = math.sqrt(2.0 / math.pi)
    square = hidden * hidden
    bend = jnp.tanh(root * hidden * (1.0 + 0.044715 * square))
    value = 0.5 * hidden * (1.0 + bend)
    slope = 0.5 * (1.0 + bend) + 0.5 * hidden * (1.0 - bend * bend) * root * (
        1.0 + 3.0 * 0.044715 * square
    )
    return value, slope


def ffn_forward_kernel(chunk, x_ref, ln_ref, next_ref, w_in_ref, w_out_ref, out_ref, a_ref, after_ref):
    a_ref[...] = norm_forward(x_ref[...], ln_ref).astype(jnp.bfloat16)
    total = x_ref[...]
    for start in range(0, w_in_ref.shape[0], chunk):
        part = slice(start, start + chunk)
        hidden = dot_dims(a_ref[...], w_in_ref[part, :], 1, 1)
        active = gelu_parts(hidden)[0].astype(jnp.bfloat16)
        total = total + dot_dims(active, w_out_ref[part, :], 1, 0)
    out_ref[...] = total
    after_ref[...] = norm_forward(total, next_ref).astype(after_ref.dtype)


def ffn_forward(x, ln, ln_next, w_in, w_out):
    length, width = x.shape
    out, normed, after = call(
        partial(ffn_forward_kernel, 512),
        (full(length, width), low(length, width), low(length, width)),
        x,
        ln,
        ln_next,
        w_in,
        w_out,
    )
    return out, after, (x, ln, w_in, w_out, normed)


def ffn_backward_kernel(
    chunk, g_ref, x_ref, ln_ref, a_ref, w_in_ref, w_out_ref, out_ref, ln_grad_ref, low_ref, ut_ref, ht_ref
):
    low_ref[...] = g_ref[...].astype(jnp.bfloat16)
    total = jnp.zeros(g_ref.shape, jnp.float32)
    for start in range(0, w_in_ref.shape[0], chunk):
        part = slice(start, start + chunk)
        hidden = dot_dims(a_ref[...], w_in_ref[part, :], 1, 1)
        value, slope = gelu_parts(hidden)
        ut_ref[part, :] = value.astype(jnp.bfloat16).T
        grad = (dot_dims(low_ref[...], w_out_ref[part, :], 1, 1) * slope).astype(jnp.bfloat16)
        ht_ref[part, :] = grad.T
        total = total + dot_dims(grad, w_in_ref[part, :], 1, 0)
    out_ref[...] = g_ref[...] + norm_backward(total, x_ref[...], ln_ref, ln_grad_ref)


def ffn_backward(grad, stored):
    x, ln, w_in, w_out, normed = stored
    length, width = x.shape
    hidden = w_in.shape[0]
    out, ln_grad, *rest = call(
        partial(ffn_backward_kernel, 512),
        (full(length, width), full(2, width), low(length, width), low(hidden, length), low(hidden, length)),
        grad,
        x,
        ln,
        normed,
        w_in,
        w_out,
    )
    return out, ln_grad, rest


def norm_backward_kernel(g_ref, x_ref, ln_ref, out_ref, ln_grad_ref):
    out_ref[...] = norm_backward(g_ref[...], x_ref[...], ln_ref, ln_grad_ref)


def plain_norm_backward(grad, x, ln):
    return call(norm_backward_kernel, (full(*x.shape), full(2, x.shape[1])), grad, x, ln)


def small_factor(block):
    size = block.shape[0]
    eye = (
        lax.broadcasted_iota(jnp.int32, (size, size), 0)
        == lax.broadcasted_iota(jnp.int32, (size, size), 1)
    ).astype(jnp.float32)
    whole = jnp.concatenate([block, eye], axis=1)
    rows = [whole[8 * u : 8 * u + 8] for u in range(size // 8)]
    shape = rows[0].shape
    sub = lax.broadcasted_iota(jnp.int32, shape, 0)

    def lane_splat(value, lane):
        return jnp.broadcast_to(value[:, lane : lane + 1], shape)

    def row_splat(value, row):
        return jnp.broadcast_to(value[row : row + 1, :], shape)

    for g in range(len(rows)):
        first = 8 * g
        lanes = {
            u: [lane_splat(rows[u], first + s) for s in range(8)] for u in range(g, len(rows))
        }
        scale = jnp.zeros(shape, jnp.float32)
        for t in range(8):
            pivot = row_splat(lanes[g][t], t)
            root = lax.rsqrt(pivot)
            inverse = root * root
            scale = jnp.where(sub == t, root, scale)
            row_t = row_splat(rows[g], t) * inverse
            splats = {s: row_splat(lanes[g][s], t) * inverse for s in range(t + 1, 8)}
            for u in range(g, len(rows)):
                factor = lanes[u][t]
                if u == g:
                    factor = jnp.where(sub > t, factor, 0.0)
                rows[u] = rows[u] - factor * row_t
                for s in range(t + 1, 8):
                    lanes[u][s] = lanes[u][s] - factor * splats[s]
        rows[g] = rows[g] * scale
    return jnp.concatenate(rows, axis=0)[:, size:]


def renew_kernel(stat_ref, basis_ref, out_ref, gram_ref, rest_ref):
    size = stat_ref.shape[0]
    product = dot_exact(stat_ref[...], basis_ref[...], 1, 0)
    rest_ref[...] = product
    gram_ref[...] = dot_exact(product, product, 0, 0)
    for low in range(0, size, 128):
        high = low + 128
        block = gram_ref[low:high, low:high]
        corner = small_factor(block[:64, :64])
        across = dot_exact(corner, block[:64, 64:], 1, 0)
        second = small_factor(block[64:, 64:] - dot_exact(across, across, 0, 0))
        below = dot_exact(second, dot_exact(across, corner, 0, 0), 1, 0)
        inverse = jnp.concatenate(
            [
                jnp.concatenate([corner, jnp.zeros_like(corner)], axis=1),
                jnp.concatenate([-below, second], axis=1),
            ],
            axis=0,
        )
        columns = dot_exact(rest_ref[:, low:high], inverse, 1, 1)
        out_ref[:, low:high] = columns
        if high < size:
            panel = dot_exact(inverse, gram_ref[low:high, high:], 1, 0)
            gram_ref[high:, high:] -= dot_exact(panel, panel, 0, 0)
            rest_ref[:, high:] -= dot_exact(columns, panel, 1, 0)


def renew_basis(statistic, basis):
    shape = statistic.shape
    return call(
        renew_kernel,
        full(*shape),
        statistic,
        basis,
        scratch=[pltpu.VMEM(shape, jnp.float32), pltpu.VMEM(shape, jnp.float32)],
    )


def sinusoid(length, model_width):
    places = np.arange(length, dtype=np.float32)[:, None]
    halves = np.arange(model_width // 2, dtype=np.float32)[None, :]
    angles = places * np.exp(halves * np.float32(-2.0 * math.log(10000.0) / model_width))
    angles = angles.astype(np.float64)
    return (
        np.stack([np.sin(angles), np.cos(angles)], axis=-1)
        .reshape(length, model_width)
        .astype(np.float32)
    )


def one_hot(ids, columns):
    return (ids[:, None] == columns[None, :]).astype(jnp.bfloat16)


def pick_weights(target_seg, pick_rows):
    sentence = jnp.take(target_seg, pick_rows, axis=0)
    return jnp.sum((sentence[:, None] == sentence[None, :]).astype(jnp.float32), axis=1)


def combine_stats(tops, totals, chosen):
    top = jnp.max(tops, axis=0)
    return top, jnp.sum(totals * jnp.exp(tops - top), axis=0), jnp.sum(chosen, axis=0)


def adam_direction(moment, second):
    return moment / (1.0 - beta_one**STEP) / (jnp.sqrt(second / (1.0 - beta_two**STEP)) + adam_eps)


def adam_update(weight, grad_item, moment, second, step_rate, decay_weight):
    moment = beta_one * moment + (1.0 - beta_one) * grad_item
    second = beta_two * second + (1.0 - beta_two) * grad_item * grad_item
    return (
        weight - step_rate * (adam_direction(moment, second) + decay_weight * weight),
        moment,
        second,
    )


def share_rows(array, owners, shares, share):
    rows, columns = array.shape
    blocks = array.reshape(owners, shares, rows // (owners * shares), columns)
    return lax.dynamic_index_in_dim(blocks, share, 1, keepdims=False)


def body(
    src_ids,
    src_seg,
    tgt_ids,
    tgt_seg,
    pick_pos,
    pick_label,
    attn_w,
    attn_m,
    attn_v,
    ffn_w,
    ffn_m,
    ffn_v,
    soap_basis,
    soap_stats,
    norm_p,
    norm_m,
    norm_v,
    embedding,
    embed_m,
    embed_v,
):
    owners, replicas = lax.axis_size("dp"), lax.axis_size("vocab")
    replica = lax.axis_index("vocab")
    w_attn, w_ffn, norm_low, table_low = (
        lax.all_gather(attn_w.astype(jnp.bfloat16), "dp", axis=1, tiled=True),
        lax.all_gather(ffn_w.astype(jnp.bfloat16), "dp", axis=1, tiled=True),
        lax.all_gather(norm_p.astype(jnp.bfloat16), "dp", axis=1, tiled=True),
        lax.all_gather(embedding.astype(jnp.bfloat16), "dp", axis=1, tiled=True),
    )
    norm_rows = norm_low.astype(jnp.float32)
    norms = [jnp.stack([norm_rows[k], norm_rows[7 + k]]) for k in range(7)]
    vocab_count, width = table_low.shape
    columns = replica * vocab_count + jnp.arange(vocab_count)
    source, source_seg, target, target_seg = (src_ids[0], src_seg[0], tgt_ids[0], tgt_seg[0])
    pick_rows, labels = (pick_pos[0], pick_label[0])
    length = source.shape[0]
    embed_scale = math.sqrt(width)
    looked_up = [
        lax.psum(
            dot_dims(one_hot(ids, columns), table_low, 1, 0).astype(jnp.bfloat16), "vocab"
        ).astype(jnp.float32)
        for ids in (source, target)
    ]
    positional = sinusoid(length, width)

    enc_in = looked_up[0] * embed_scale + positional
    enc_mid, enc_attn = attn_forward(
        enc_in, norms[0], w_attn[0:4], source_seg, source_seg, None, False
    )
    enc_out, encoded, enc_ffn = ffn_forward(enc_mid, norms[1], norms[2], w_ffn[0], w_ffn[1])
    dec_in = looked_up[1] * embed_scale + positional
    dec_mid, dec_self = attn_forward(
        dec_in, norms[3], w_attn[4:8], target_seg, target_seg, None, True
    )
    dec_late, dec_cross = attn_forward(
        dec_mid, norms[4], w_attn[8:12], target_seg, source_seg, encoded, False
    )
    dec_out, final_low, dec_ffn = ffn_forward(dec_late, norms[5], norms[6], w_ffn[2], w_ffn[3])

    chosen_rows = one_hot(pick_rows, jnp.arange(length))
    picked = dot_dims(chosen_rows, final_low, 1, 0).astype(jnp.bfloat16)
    logits = dot_dims(picked, table_low, 1, 1)
    row_top = jnp.max(logits, axis=-1)
    row_total = jnp.sum(jnp.exp(logits - row_top[:, None]), axis=-1)
    label_hit = labels[:, None] == columns[None, :]
    chosen = jnp.sum(jnp.where(label_hit, logits, 0.0), axis=-1)
    row_top, row_total, chosen = combine_stats(
        *jnp.moveaxis(lax.all_gather(jnp.stack([row_top, row_total, chosen]), "vocab"), 1, 0)
    )
    log_total = row_top + jnp.log(row_total)
    weight = 1.0 / pick_weights(target_seg, pick_rows)
    loss_part = jnp.sum((log_total - chosen) * weight)
    count_part = (target_seg[-1] + 1).astype(jnp.float32)
    grad_logits = (
        weight[:, None] * (jnp.exp(logits - log_total[:, None]) - label_hit.astype(jnp.float32))
    ).astype(jnp.bfloat16)
    grad_picked = lax.psum(dot_dims(grad_logits, table_low, 1, 0), "vocab")
    grad_table = dot_dims(grad_logits, picked, 0, 0)
    picked_high = grad_picked.astype(jnp.bfloat16)
    picked_rest = (grad_picked - picked_high.astype(jnp.float32)).astype(jnp.bfloat16)
    grad_final = dot_dims(chosen_rows, picked_high, 0, 0) + dot_dims(chosen_rows, picked_rest, 0, 0)

    norm_grads = [None] * 7
    grad, norm_grads[6] = plain_norm_backward(grad_final, dec_out, norms[6])
    grad, norm_grads[5], dec_ffn_parts = ffn_backward(grad, dec_ffn)
    grad, norm_grads[4], cross_parts, grad_encoded = attn_backward(grad, dec_cross)
    grad, norm_grads[3], self_parts, _ = attn_backward(grad, dec_self)
    grad_target = (grad * embed_scale).astype(jnp.bfloat16)
    grad, norm_grads[2] = plain_norm_backward(grad_encoded, enc_out, norms[2])
    grad, norm_grads[1], enc_ffn_parts = ffn_backward(grad, enc_ffn)
    grad, norm_grads[0], enc_parts, _ = attn_backward(grad, enc_attn)
    grad_source = (grad * embed_scale).astype(jnp.bfloat16)
    for ids, rows in ((source, grad_source), (target, grad_target)):
        grad_table = grad_table + dot_dims(one_hot(ids, columns), rows, 0, 0)

    chosen_columns = share_rows(jnp.eye(width, dtype=jnp.bfloat16), owners, replicas, replica)
    chosen_columns = chosen_columns.reshape(-1, width)

    def weight_grads(stored, parts):
        normed, kept, cross = stored[7], stored[8], stored[6]
        grad_low, gq, gk, gv = parts
        key_in = encoded if cross else normed
        share = [dot_dims(chosen_columns, rows, 1, 1).astype(jnp.bfloat16) for rows in (normed, key_in)]
        mixed = share_rows(kept[3], owners, replicas, replica).reshape(-1, length)
        return [
            dot_dims(share[0], gq, 1, 0),
            dot_dims(share[1], gk, 1, 0),
            dot_dims(share[1], gv, 1, 0),
            dot_dims(mixed, grad_low, 1, 0),
        ]

    def hidden_grads(stored, parts):
        grad_low, values, grads = parts
        return [
            dot_dims(share_rows(rows, owners, replicas, replica).reshape(-1, length), right, 1, 0)
            for rows, right in ((grads, stored[4]), (values, grad_low))
        ]

    pieces = (
        weight_grads(enc_attn, enc_parts)
        + weight_grads(dec_self, self_parts)
        + weight_grads(dec_cross, cross_parts)
        + hidden_grads(enc_ffn, enc_ffn_parts)
        + hidden_grads(dec_ffn, dec_ffn_parts)
    )
    pieces = [piece.astype(jnp.bfloat16).reshape(owners, -1, width) for piece in pieces]
    summed = lax.psum_scatter(
        jnp.concatenate(pieces, axis=1), "dp", scatter_dimension=0, tiled=False
    )
    shared = lax.all_gather(summed, "vocab")
    attn_rows = 12 * (width // (owners * replicas))
    g_attn = jnp.moveaxis(shared[:, :attn_rows].reshape(replicas, 12, -1, width), 0, 1)
    g_attn = g_attn.reshape(12, -1, width).astype(jnp.float32)
    g_ffn = jnp.moveaxis(shared[:, attn_rows:].reshape(replicas, 4, -1, width), 0, 1)
    g_ffn = g_ffn.reshape(4, -1, width).astype(jnp.float32)
    norm_grad = jnp.stack(norm_grads)
    norm_grad = jnp.concatenate([norm_grad[:, 0], norm_grad[:, 1]], axis=0)
    g_norm = lax.psum_scatter(norm_grad, "dp", scatter_dimension=1, tiled=True)
    g_embed = lax.psum_scatter(
        grad_table.astype(jnp.bfloat16), "dp", scatter_dimension=1, tiled=True
    ).astype(jnp.float32)

    first_copy = (replica == 0).astype(jnp.float32)
    layer_sq = jnp.sum(g_attn * g_attn) + jnp.sum(g_ffn * g_ffn) + jnp.sum(g_norm * g_norm)
    raw_squares = jnp.sum(g_embed * g_embed) + first_copy * layer_sq
    loss_sum, sentences, squares = lax.psum(
        jnp.stack([first_copy * loss_part, first_copy * count_part, raw_squares]), ("dp", "vocab")
    )
    grad_norm = jnp.sqrt(squares) / sentences
    factor = jnp.minimum(1.0, clip_limit / (grad_norm + norm_eps)) / sentences
    g_attn, g_ffn, g_norm, g_embed = (
        g_attn * factor,
        g_ffn * factor,
        g_norm * factor,
        g_embed * factor,
    )
    matrix = replica % 4
    own_grad = lax.dynamic_index_in_dim(g_ffn, matrix, 0, keepdims=False)
    own_stat = stat_decay * lax.dynamic_index_in_dim(soap_stats, matrix, 0, keepdims=False) + (
        1.0 - stat_decay
    ) * lax.psum(dot_exact(own_grad, own_grad, 0, 0), "dp")
    own_basis = renew_basis(own_stat, lax.dynamic_index_in_dim(soap_basis, matrix, 0, keepdims=False))
    renewed = lax.all_gather(jnp.stack([own_stat, own_basis]).astype(jnp.bfloat16), "vocab")[:4]
    new_stats, new_basis = (renewed[:, k].astype(jnp.float32) for k in (0, 1))

    new_attn, m_attn, v_attn = adam_update(attn_w, g_attn, attn_m, attn_v, rate_matrix, decay_rate)
    new_norm, m_norm, v_norm = adam_update(norm_p, g_norm, norm_m, norm_v, rate_vector, 0.0)
    new_embed, m_embed, v_embed = adam_update(
        embedding, g_embed, embed_m, embed_v, rate_matrix, decay_rate
    )
    rotated = jnp.einsum("mfd,mde->mfe", g_ffn, soap_basis, precision=highest)
    m_ffn = beta_one * ffn_m + (1.0 - beta_one) * rotated
    v_ffn = beta_two * ffn_v + (1.0 - beta_two) * rotated * rotated
    back_rotated = jnp.einsum(
        "mfe,mde->mfd", adam_direction(m_ffn, v_ffn), soap_basis, precision=highest
    )
    new_ffn = ffn_w - rate_matrix * (back_rotated + decay_rate * ffn_w)
    return (
        loss_sum,
        sentences,
        grad_norm,
        new_attn,
        m_attn,
        v_attn,
        new_ffn,
        m_ffn,
        v_ffn,
        new_basis,
        new_stats,
        new_norm,
        m_norm,
        v_norm,
        new_embed,
        m_embed,
        v_embed,
    )


def solution(mesh):
    placed = (
        P("dp", None),
        P("dp", None),
        P("dp", None),
        P("dp", None),
        P("dp", None),
        P("dp", None),
        P(None, "dp", None),
        P(None, "dp", None),
        P(None, "dp", None),
        P(None, "dp", None),
        P(None, "dp", None),
        P(None, "dp", None),
        P(),
        P(),
        P(None, "dp"),
        P(None, "dp"),
        P(None, "dp"),
        P("vocab", "dp"),
        P("vocab", "dp"),
        P("vocab", "dp"),
    )
    return jax.shard_map(
        body,
        mesh=mesh,
        in_specs=placed,
        out_specs=(
            P(),
            P(),
            P(),
            P(None, "dp", None),
            P(None, "dp", None),
            P(None, "dp", None),
            P(None, "dp", None),
            P(None, "dp", None),
            P(None, "dp", None),
            P(),
            P(),
            P(None, "dp"),
            P(None, "dp"),
            P(None, "dp"),
            P("vocab", "dp"),
            P("vocab", "dp"),
            P("vocab", "dp"),
        ),
        check_vma=False,
    )
```

```python
from functools import partial
import math

import jax
import jax.numpy as jnp
import numpy as np
from jax import lax
from jax.experimental import pallas as pl
from jax.experimental.pallas import tpu as pltpu
from jax.sharding import PartitionSpec as P

HEADS = 8
STEP = 10
TILE = 128

highest = lax.Precision.HIGHEST
beta_one = 0.9
beta_two = 0.999
adam_eps = 1e-08
decay_rate = 0.01
rate_matrix = 0.03
rate_vector = 0.3
clip_limit = 1.0
stat_decay = 0.95
norm_eps = 1e-06
masked = -1e30
log_two_e = math.log2(math.e)
vmem = pl.BlockSpec(memory_space=pltpu.VMEM)
smem = pl.BlockSpec(memory_space=pltpu.SMEM)
mesh_ids = pl.DeviceIdType.MESH


def dot_dims(left, right, left_dim, right_dim):
    return lax.dot_general(
        left, right, (((left_dim,), (right_dim,)), ((), ())), preferred_element_type=jnp.float32
    )


def dot_exact(left, right, left_dim, right_dim):
    return lax.dot_general(
        left,
        right,
        (((left_dim,), (right_dim,)), ((), ())),
        precision=highest,
        preferred_element_type=jnp.float32,
    )


def call(kernel, outs, *args, scratch=(), smem_args=0):
    return pl.pallas_call(
        kernel,
        out_shape=outs,
        in_specs=[vmem] * (len(args) - smem_args) + [smem] * smem_args,
        out_specs=jax.tree.map(lambda _: vmem, outs),
        scratch_shapes=list(scratch),
        compiler_params=pltpu.CompilerParams(vmem_limit_bytes=56 * 2**20),
    )(*args)


def low(*shape):
    return jax.ShapeDtypeStruct(shape, jnp.bfloat16)


def full(*shape):
    return jax.ShapeDtypeStruct(shape, jnp.float32)


def norm_parts(values):
    centre = values - jnp.mean(values, axis=-1, keepdims=True)
    spread = jnp.mean(centre * centre, axis=-1, keepdims=True)
    root = lax.rsqrt(spread + norm_eps)
    return centre * root, root


def norm_forward(values, ln_ref):
    return norm_parts(values)[0] * ln_ref[0:1, :] + ln_ref[1:2, :]


def norm_backward(grad, values, ln_ref, ln_grad_ref):
    normed, root = norm_parts(values)
    ln_grad_ref[0:1, :] = jnp.sum(grad * normed, axis=0, keepdims=True)
    ln_grad_ref[1:2, :] = jnp.sum(grad, axis=0, keepdims=True)
    inner = grad * ln_ref[0:1, :]
    return root * (
        inner
        - jnp.mean(inner, axis=-1, keepdims=True)
        - normed * jnp.mean(inner * normed, axis=-1, keepdims=True)
    )


def at_tile(index):
    return pl.ds(pl.multiple_of(index * TILE, TILE), TILE)


def tile_mask(segq_ref, segk_ref, qi, ki, causal):
    allowed = segk_ref[at_tile(ki), :] == segq_ref[:, at_tile(qi)]
    if causal:
        ahead = lax.broadcasted_iota(jnp.int32, (TILE, TILE), 0) - lax.broadcasted_iota(
            jnp.int32, (TILE, TILE), 1
        )
        allowed = allowed & (ahead <= (qi - ki) * TILE)
    return allowed


def for_tiles(count, edge_ref, causal, step):
    def one(pair, carry):
        qi, ki = pair // count, lax.rem(pair, count)
        live = (edge_ref[0, qi] <= edge_ref[3, ki]) & (edge_ref[2, ki] <= edge_ref[1, qi])
        if causal:
            live = live & (ki <= qi)

        @pl.when(live)
        def _():
            step(qi, ki)

        return carry

    lax.fori_loop(0, count * count, one, 0)


def tile_edges(seg_q, seg_k):
    last = TILE - 1
    return jnp.stack([seg_q[::TILE], seg_q[last::TILE], seg_k[::TILE], seg_k[last::TILE]])


def attn_forward_kernel(causal, cross, *refs):
    refs = list(refs)
    x_ref, ln_ref, w_ref, segq_ref, segk_ref = refs[:5]
    refs = refs[5:]
    key_ref = refs.pop(0) if cross else None
    (edge_ref, out_ref, a_ref, qt_ref, kt_ref, vt_ref, ot_ref, lse_ref, top_ref, sum_ref, acc_ref) = refs
    length, width = x_ref.shape
    head_size = width // HEADS
    a_ref[...] = norm_forward(x_ref[...], ln_ref).astype(jnp.bfloat16)
    key_in = key_ref if cross else a_ref
    qt_ref[...] = dot_dims(a_ref[...], w_ref[0], 1, 0).astype(jnp.bfloat16).T
    kt_ref[...] = dot_dims(key_in[...], w_ref[1], 1, 0).astype(jnp.bfloat16).T
    vt_ref[...] = dot_dims(key_in[...], w_ref[2], 1, 0).astype(jnp.bfloat16).T
    top_ref[...] = jnp.full(top_ref.shape, masked, jnp.float32)
    sum_ref[...] = jnp.zeros(sum_ref.shape, jnp.float32)
    acc_ref[...] = jnp.zeros(acc_ref.shape, jnp.float32)
    scale = log_two_e / math.sqrt(head_size)
    bands = [slice(h * head_size, (h + 1) * head_size) for h in range(HEADS)]

    def step(qi, ki):
        q_at, k_at = at_tile(qi), at_tile(ki)
        allowed = tile_mask(segq_ref, segk_ref, qi, ki, causal)
        scores = [dot_dims(kt_ref[band, k_at], qt_ref[band, q_at], 0, 0) * scale for band in bands]
        scores = [jnp.where(allowed, part, masked) for part in scores]
        top = top_ref[:, q_at]
        new_top = jnp.maximum(
            top,
            jnp.concatenate([jnp.max(part, axis=0, keepdims=True) for part in scores], axis=0),
        )
        fade = jnp.exp2(top - new_top)
        parts = [jnp.exp2(scores[h] - new_top[h : h + 1]) for h in range(HEADS)]
        top_ref[:, q_at] = new_top
        sum_ref[:, q_at] = sum_ref[:, q_at] * fade + jnp.concatenate(
            [jnp.sum(part, axis=0, keepdims=True) for part in parts], axis=0
        )
        mixed = [
            dot_dims(vt_ref[bands[h], k_at], parts[h].astype(jnp.bfloat16), 1, 0)
            for h in range(HEADS)
        ]
        acc = acc_ref[:, q_at]
        acc_ref[:, q_at] = jnp.concatenate(
            [acc[bands[h]] * fade[h : h + 1] + mixed[h] for h in range(HEADS)], axis=0
        )

    for_tiles(length // TILE, edge_ref, causal, step)
    lse_ref[...] = top_ref[...] + jnp.log2(sum_ref[...])
    for h in range(HEADS):
        ot_ref[bands[h], :] = (acc_ref[bands[h], :] / sum_ref[h : h + 1, :]).astype(jnp.bfloat16)
    out_ref[...] = x_ref[...] + dot_dims(ot_ref[...], w_ref[3], 0, 0)


def attn_forward(x, ln, weights, seg_q, seg_k, key_in, causal):
    length, width = x.shape
    cross = key_in is not None
    segs = (seg_q[None, :], jnp.broadcast_to(seg_k[:, None], (length, TILE)))
    edges = tile_edges(seg_q, seg_k)
    args = (x, ln, weights, *segs) + ((key_in,) if cross else ()) + (edges,)
    outs = (full(length, width), low(length, width)) + (low(width, length),) * 4
    out, normed, *stored = call(
        partial(attn_forward_kernel, causal, cross),
        outs + (full(HEADS, length),),
        *args,
        scratch=[
            pltpu.VMEM((HEADS, length), jnp.float32),
            pltpu.VMEM((HEADS, length), jnp.float32),
            pltpu.VMEM((width, length), jnp.float32),
        ],
        smem_args=1,
    )
    return out, (x, ln, weights, segs, edges, causal, cross, normed, stored)


def attn_backward_kernel(causal, cross, *refs):
    (g_ref, x_ref, ln_ref, w_ref, segq_ref, segk_ref, qt_ref, kt_ref, vt_ref, ot_ref, lse_ref) = refs[:11]
    refs = list(refs[11:])
    edge_ref, out_ref, ln_grad_ref, low_ref, gq_ref, gk_ref, gv_ref = refs[:7]
    refs = refs[7:]
    key_grad_ref = refs.pop(0) if cross else None
    got_ref, delta_ref, gqt_ref, gkt_ref, gvt_ref = refs
    length, width = x_ref.shape
    head_size = width // HEADS
    low_ref[...] = g_ref[...].astype(jnp.bfloat16)
    got_ref[...] = dot_dims(low_ref[...], w_ref[3], 1, 1).astype(jnp.bfloat16).T
    bands = [slice(h * head_size, (h + 1) * head_size) for h in range(HEADS)]
    for h in range(HEADS):
        delta_ref[h : h + 1, :] = jnp.sum(
            got_ref[bands[h], :].astype(jnp.float32) * ot_ref[bands[h], :].astype(jnp.float32),
            axis=0,
            keepdims=True,
        )
    for ref in (gqt_ref, gkt_ref, gvt_ref):
        ref[...] = jnp.zeros(ref.shape, jnp.float32)
    scale = log_two_e / math.sqrt(head_size)
    back = 1.0 / math.sqrt(head_size)

    def step(qi, ki):
        q_at, k_at = at_tile(qi), at_tile(ki)
        allowed = tile_mask(segq_ref, segk_ref, qi, ki, causal)
        scores = [dot_dims(kt_ref[band, k_at], qt_ref[band, q_at], 0, 0) for band in bands]
        grads = [dot_dims(vt_ref[band, k_at], got_ref[band, q_at], 0, 0) for band in bands]
        parts = [
            jnp.where(allowed, jnp.exp2(scores[h] * scale - lse_ref[h : h + 1, q_at]), 0.0)
            for h in range(HEADS)
        ]
        grads = [parts[h] * (grads[h] - delta_ref[h : h + 1, q_at]) for h in range(HEADS)]
        parts_t = [part.T.astype(jnp.bfloat16) for part in parts]
        grads_t = [part.T.astype(jnp.bfloat16) for part in grads]
        grads = [part.astype(jnp.bfloat16) for part in grads]
        for ref, place, terms in (
            (gvt_ref, k_at, [dot_dims(got_ref[bands[h], q_at], parts_t[h], 1, 0) for h in range(HEADS)]),
            (gkt_ref, k_at, [dot_dims(qt_ref[bands[h], q_at], grads_t[h], 1, 0) for h in range(HEADS)]),
            (gqt_ref, q_at, [dot_dims(kt_ref[bands[h], k_at], grads[h], 1, 0) for h in range(HEADS)]),
        ):
            ref[:, place] += jnp.concatenate(terms, axis=0)

    for_tiles(length // TILE, edge_ref, causal, step)
    gq_ref[...] = (gqt_ref[...] * back).astype(jnp.bfloat16).T
    gk_ref[...] = (gkt_ref[...] * back).astype(jnp.bfloat16).T
    gv_ref[...] = gvt_ref[...].astype(jnp.bfloat16).T
    from_query = dot_dims(gq_ref[...], w_ref[0], 1, 1)
    from_keys = dot_dims(gk_ref[...], w_ref[1], 1, 1) + dot_dims(gv_ref[...], w_ref[2], 1, 1)
    if cross:
        key_grad_ref[...] = from_keys
    else:
        from_query = from_query + from_keys
    out_ref[...] = g_ref[...] + norm_backward(from_query, x_ref[...], ln_ref, ln_grad_ref)


def attn_backward(grad, stored):
    x, ln, weights, segs, edges, causal, cross, _, kept = stored
    length, width = x.shape
    outs = (full(length, width), full(2, width)) + (low(length, width),) * 4
    if cross:
        outs = outs + (full(length, width),)
    out, ln_grad, *rest = call(
        partial(attn_backward_kernel, causal, cross),
        outs,
        grad,
        x,
        ln,
        weights,
        *segs,
        *kept,
        edges,
        scratch=[pltpu.VMEM((width, length), jnp.bfloat16), pltpu.VMEM((HEADS, length), jnp.float32)]
        + [pltpu.VMEM((width, length), jnp.float32)] * 3,
        smem_args=1,
    )
    return out, ln_grad, rest[:4], rest[4] if cross else None


def gelu_parts(hidden):
    root = math.sqrt(2.0 / math.pi)
    square = hidden * hidden
    bend = jnp.tanh(root * hidden * (1.0 + 0.044715 * square))
    value = 0.5 * hidden * (1.0 + bend)
    slope = 0.5 * (1.0 + bend) + 0.5 * hidden * (1.0 - bend * bend) * root * (
        1.0 + 3.0 * 0.044715 * square
    )
    return value, slope


def ffn_forward_kernel(chunk, x_ref, ln_ref, next_ref, w_in_ref, w_out_ref, out_ref, a_ref, after_ref):
    a_ref[...] = norm_forward(x_ref[...], ln_ref).astype(jnp.bfloat16)
    total = x_ref[...]
    for start in range(0, w_in_ref.shape[0], chunk):
        part = slice(start, start + chunk)
        hidden = dot_dims(a_ref[...], w_in_ref[part, :], 1, 1)
        active = gelu_parts(hidden)[0].astype(jnp.bfloat16)
        total = total + dot_dims(active, w_out_ref[part, :], 1, 0)
    out_ref[...] = total
    after_ref[...] = norm_forward(total, next_ref).astype(after_ref.dtype)


def ffn_forward(x, ln, ln_next, w_in, w_out):
    length, width = x.shape
    out, normed, after = call(
        partial(ffn_forward_kernel, 512),
        (full(length, width), low(length, width), low(length, width)),
        x,
        ln,
        ln_next,
        w_in,
        w_out,
    )
    return out, after, (x, ln, w_in, w_out, normed)


def ffn_backward_kernel(
    chunk, g_ref, x_ref, ln_ref, a_ref, w_in_ref, w_out_ref, out_ref, ln_grad_ref, low_ref, ut_ref, ht_ref
):
    low_ref[...] = g_ref[...].astype(jnp.bfloat16)
    total = jnp.zeros(g_ref.shape, jnp.float32)
    for start in range(0, w_in_ref.shape[0], chunk):
        part = slice(start, start + chunk)
        hidden = dot_dims(a_ref[...], w_in_ref[part, :], 1, 1)
        value, slope = gelu_parts(hidden)
        ut_ref[part, :] = value.astype(jnp.bfloat16).T
        grad = (dot_dims(low_ref[...], w_out_ref[part, :], 1, 1) * slope).astype(jnp.bfloat16)
        ht_ref[part, :] = grad.T
        total = total + dot_dims(grad, w_in_ref[part, :], 1, 0)
    out_ref[...] = g_ref[...] + norm_backward(total, x_ref[...], ln_ref, ln_grad_ref)


def ffn_backward(grad, stored):
    x, ln, w_in, w_out, normed = stored
    length, width = x.shape
    hidden = w_in.shape[0]
    out, ln_grad, *rest = call(
        partial(ffn_backward_kernel, 512),
        (full(length, width), full(2, width), low(length, width), low(hidden, length), low(hidden, length)),
        grad,
        x,
        ln,
        normed,
        w_in,
        w_out,
    )
    return out, ln_grad, rest


def norm_backward_kernel(g_ref, x_ref, ln_ref, out_ref, ln_grad_ref):
    out_ref[...] = norm_backward(g_ref[...], x_ref[...], ln_ref, ln_grad_ref)


def plain_norm_backward(grad, x, ln):
    return call(norm_backward_kernel, (full(*x.shape), full(2, x.shape[1])), grad, x, ln)


def small_factor(block):
    size = block.shape[0]
    eye = (
        lax.broadcasted_iota(jnp.int32, (size, size), 0)
        == lax.broadcasted_iota(jnp.int32, (size, size), 1)
    ).astype(jnp.float32)
    whole = jnp.concatenate([block, eye], axis=1)
    rows = [whole[8 * u : 8 * u + 8] for u in range(size // 8)]
    shape = rows[0].shape
    sub = lax.broadcasted_iota(jnp.int32, shape, 0)

    def lane_splat(value, lane):
        return jnp.broadcast_to(value[:, lane : lane + 1], shape)

    def row_splat(value, row):
        return jnp.broadcast_to(value[row : row + 1, :], shape)

    for g in range(len(rows)):
        first = 8 * g
        lanes = {
            u: [lane_splat(rows[u], first + s) for s in range(8)] for u in range(g, len(rows))
        }
        scale = jnp.zeros(shape, jnp.float32)
        for t in range(8):
            pivot = row_splat(lanes[g][t], t)
            root = lax.rsqrt(pivot)
            inverse = root * root
            scale = jnp.where(sub == t, root, scale)
            row_t = row_splat(rows[g], t) * inverse
            splats = {s: row_splat(lanes[g][s], t) * inverse for s in range(t + 1, 8)}
            for u in range(g, len(rows)):
                factor = lanes[u][t]
                if u == g:
                    factor = jnp.where(sub > t, factor, 0.0)
                rows[u] = rows[u] - factor * row_t
                for s in range(t + 1, 8):
                    lanes[u][s] = lanes[u][s] - factor * splats[s]
        rows[g] = rows[g] * scale
    return jnp.concatenate(rows, axis=0)[:, size:]


def renew_kernel(stat_ref, basis_ref, out_ref, gram_ref, rest_ref):
    size = stat_ref.shape[0]
    product = dot_exact(stat_ref[...], basis_ref[...], 1, 0)
    rest_ref[...] = product
    gram_ref[...] = dot_exact(product, product, 0, 0)
    for low in range(0, size, 128):
        high = low + 128
        block = gram_ref[low:high, low:high]
        corner = small_factor(block[:64, :64])
        across = dot_exact(corner, block[:64, 64:], 1, 0)
        second = small_factor(block[64:, 64:] - dot_exact(across, across, 0, 0))
        below = dot_exact(second, dot_exact(across, corner, 0, 0), 1, 0)
        inverse = jnp.concatenate(
            [
                jnp.concatenate([corner, jnp.zeros_like(corner)], axis=1),
                jnp.concatenate([-below, second], axis=1),
            ],
            axis=0,
        )
        columns = dot_exact(rest_ref[:, low:high], inverse, 1, 1)
        out_ref[:, low:high] = columns
        if high < size:
            panel = dot_exact(inverse, gram_ref[low:high, high:], 1, 0)
            gram_ref[high:, high:] -= dot_exact(panel, panel, 0, 0)
            rest_ref[:, high:] -= dot_exact(columns, panel, 1, 0)


def renew_basis(statistic, basis):
    shape = statistic.shape
    return call(
        renew_kernel,
        full(*shape),
        statistic,
        basis,
        scratch=[pltpu.VMEM(shape, jnp.float32), pltpu.VMEM(shape, jnp.float32)],
    )


def peers_of(axis):
    size, me = lax.axis_size(axis), lax.axis_index(axis)
    return [
        (step, lax.rem(me + step, size), lax.rem(me + size - step, size)) for step in range(1, size)
    ]


def greet(*places):
    barrier = pltpu.get_barrier_semaphore()
    for axis, index in places:
        pl.semaphore_signal(barrier, inc=1, device_id={axis: index}, device_id_type=mesh_ids)
    pl.semaphore_wait(barrier, len(places))


def push(source, target, sems, slot, axis, index):
    copy = pltpu.make_async_remote_copy(
        src_ref=source,
        dst_ref=target,
        send_sem=sems[0].at[slot],
        recv_sem=sems[1].at[slot],
        device_id={axis: index},
        device_id_type=mesh_ids,
    )
    copy.start()
    return copy


def sem_pair(count):
    return [pltpu.SemaphoreType.DMA((count,)), pltpu.SemaphoreType.DMA((count,))]


def talk(kernel, outs, collective_id, *args, scratch=()):
    return pl.pallas_call(
        kernel,
        out_shape=outs,
        in_specs=[vmem] * len(args),
        out_specs=jax.tree.map(lambda _: vmem, outs),
        scratch_shapes=list(scratch),
        compiler_params=pltpu.CompilerParams(
            collective_id=collective_id, has_side_effects=True, vmem_limit_bytes=56 * 2**20
        ),
    )(*args)


def gather_kernel(axis, x_ref, out_ref, send_sems, recv_sems):
    others = peers_of(axis)
    greet(*[(axis, to) for _, to, _ in others])
    me = lax.axis_index(axis)
    sems = (send_sems, recv_sems)
    copies = [push(x_ref, out_ref.at[me], sems, step - 1, axis, to) for step, to, _ in others]
    out_ref[me] = x_ref[...]
    for copy in copies:
        copy.wait()


def gather_small(x, axis, collective_id):
    size = lax.axis_size(axis)
    out = jax.ShapeDtypeStruct((size, *x.shape), x.dtype)
    return talk(partial(gather_kernel, axis), out, collective_id, x, scratch=sem_pair(size - 1))


def sum_kernel(x_ref, out_ref, parts_ref, mine_ref, s0, r0, s1, r1):
    others = peers_of("vocab")
    greet(*[("vocab", to) for _, to, _ in others])
    size, me = lax.axis_size("vocab"), lax.axis_index("vocab")
    rows = mine_ref.shape[0]

    def rows_of(index):
        return pl.ds(pl.multiple_of(index * rows, rows), rows)

    copies = [
        push(x_ref.at[rows_of(to)], parts_ref.at[me], (s0, r0), step - 1, "vocab", to)
        for step, to, _ in others
    ]
    parts_ref[me] = x_ref[rows_of(me), :]
    for copy in copies:
        copy.wait()
    total = parts_ref[0].astype(jnp.float32)
    for index in range(1, size):
        total = total + parts_ref[index].astype(jnp.float32)
    mine_ref[...] = total.astype(mine_ref.dtype)
    copies = [
        push(mine_ref, out_ref.at[rows_of(me)], (s1, r1), step - 1, "vocab", to)
        for step, to, _ in others
    ]
    out_ref[rows_of(me), :] = mine_ref[...]
    for copy in copies:
        copy.wait()


def sum_vocab(x, collective_id):
    replicas = lax.axis_size("vocab")
    rows, columns = x.shape
    share = rows // replicas
    return talk(
        sum_kernel,
        jax.ShapeDtypeStruct(x.shape, x.dtype),
        collective_id,
        x,
        scratch=[
            pltpu.VMEM((replicas, share, columns), x.dtype),
            pltpu.VMEM((share, columns), x.dtype),
        ]
        + sem_pair(replicas - 1)
        + sem_pair(replicas - 1),
    )


def tail_kernel(
    x_ref, few_ref, out_ref, sum_ref, parts_ref, mine_ref, seen_ref, line_ref, lines_ref,
    s0, r0, s1, r1, s2, r2, s3, r3,
):
    owners, replicas = peers_of("dp"), peers_of("vocab")
    greet(*[("dp", to) for _, to, _ in owners], *[("vocab", to) for _, to, _ in replicas])
    me, here = lax.axis_index("dp"), lax.axis_index("vocab")
    rows = mine_ref.shape[0]

    def rows_of(index):
        return pl.ds(pl.multiple_of(index * rows, rows), rows)

    few = [
        push(few_ref, seen_ref.at[here], (s2, r2), step - 1, "vocab", to) for step, to, _ in replicas
    ]
    wide = [
        push(x_ref.at[rows_of(to)], parts_ref.at[me], (s0, r0), step - 1, "dp", to)
        for step, to, _ in owners
    ]
    seen_ref[here] = few_ref[...]
    parts_ref[me] = x_ref[rows_of(me), :]
    for copy in few:
        copy.wait()
    line_ref[...] = jnp.sum(seen_ref[...], axis=0)
    few = [
        push(line_ref, lines_ref.at[me], (s3, r3), step - 1, "dp", to) for step, to, _ in owners
    ]
    lines_ref[me] = line_ref[...]
    for copy in wide:
        copy.wait()
    mine_ref[...] = jnp.sum(parts_ref[...].astype(jnp.float32), axis=0).astype(mine_ref.dtype)
    wide = [
        push(mine_ref, out_ref.at[rows_of(me)], (s1, r1), step - 1, "dp", to)
        for step, to, _ in owners
    ]
    out_ref[rows_of(me), :] = mine_ref[...]
    for copy in few:
        copy.wait()
    sum_ref[...] = jnp.sum(lines_ref[...], axis=0)
    for copy in wide:
        copy.wait()


def sum_tail(x, few, collective_id):
    owners, replicas = lax.axis_size("dp"), lax.axis_size("vocab")
    rows, columns = x.shape
    share = rows // owners
    return talk(
        tail_kernel,
        (jax.ShapeDtypeStruct(x.shape, x.dtype), full(*few.shape)),
        collective_id,
        x,
        few,
        scratch=[
            pltpu.VMEM((owners, share, columns), x.dtype),
            pltpu.VMEM((share, columns), x.dtype),
            pltpu.VMEM((replicas, *few.shape), jnp.float32),
            pltpu.VMEM(few.shape, jnp.float32),
            pltpu.VMEM((owners, *few.shape), jnp.float32),
        ]
        + sem_pair(owners - 1)
        + sem_pair(owners - 1)
        + sem_pair(replicas - 1)
        + sem_pair(owners - 1),
    )


def flip(index, bit):
    return index + bit - 2 * bit * lax.rem(index // bit, 2)


def quad_kernel(x_ref, out_ref, send_sems, recv_sems):
    here = lax.axis_index("vocab")
    far, near = flip(here, 2), flip(here, 1)
    greet(("vocab", far), ("vocab", near))
    sems = (send_sems, recv_sems)
    mine, theirs = lax.rem(here, 4), lax.rem(far, 4)
    copies = [
        push(x_ref, out_ref.at[mine], sems, 0, "vocab", far),
        push(x_ref, out_ref.at[mine], sems, 1, "vocab", near),
    ]
    out_ref[mine] = x_ref[...]
    copies[0].wait()
    relay = push(out_ref.at[theirs], out_ref.at[theirs], sems, 2, "vocab", near)
    copies[1].wait()
    relay.wait()


def gather_quad(x, collective_id):
    out = jax.ShapeDtypeStruct((4, *x.shape), x.dtype)
    return talk(quad_kernel, out, collective_id, x, scratch=sem_pair(3))


def gradient_kernel(x_ref, out_ref, parts_ref, s0, r0, s1, r1, s2, r2):
    owners = peers_of("dp")
    here, me = lax.axis_index("vocab"), lax.axis_index("dp")
    near = flip(here, 1)
    size = lax.axis_size("vocab")
    steps = range(2, size, 2)
    chunks = x_ref.shape[1]
    greet(
        *[("dp", to) for _, to, _ in owners],
        *[("vocab", lax.rem(here + step, size)) for step in steps],
        ("vocab", near),
    )

    def spread(c, origin, sems, slot, to):
        place = out_ref.at[origin, c]
        return push(place, place, sems, slot, "vocab", to)

    arriving = [
        [
            push(x_ref.at[to, c], parts_ref.at[me, c], (s0, r0), (step - 1) * chunks + c, "dp", to)
            for step, to, _ in owners
        ]
        for c in range(chunks)
    ]
    far, close = [], []
    for c in range(chunks):
        parts_ref[me, c] = x_ref[me, c]
        for copy in arriving[c]:
            copy.wait()
        total = jnp.sum(parts_ref[:, c].astype(jnp.float32), axis=0)
        out_ref[here, c] = total.astype(out_ref.dtype)
        far.append(
            [
                spread(c, here, (s1, r1), k * chunks + c, lax.rem(here + step, size))
                for k, step in enumerate(steps)
            ]
        )
        close.append(spread(c, here, (s2, r2), c, near))
    for c in range(chunks):
        for k, step in enumerate(steps):
            far[c][k].wait()
            origin = lax.rem(here + size - step, size)
            close.append(spread(c, origin, (s2, r2), (k + 1) * chunks + c, near))
    for copy in close:
        copy.wait()


def share_gradients(x, collective_id):
    owners, replicas = lax.axis_size("dp"), lax.axis_size("vocab")
    chunks = x.shape[1]
    others = (replicas // 2 - 1) * chunks
    return talk(
        gradient_kernel,
        jax.ShapeDtypeStruct((replicas, *x.shape[1:]), x.dtype),
        collective_id,
        x,
        scratch=[pltpu.VMEM(x.shape, x.dtype)]
        + sem_pair((owners - 1) * chunks)
        + sem_pair(others)
        + sem_pair(others + chunks),
    )


def swap_kernel(x_ref, out_ref, send_sems, recv_sems):
    others = peers_of("dp")
    greet(*[("dp", to) for _, to, _ in others])
    me = lax.axis_index("dp")
    copies = [
        push(x_ref.at[to], out_ref.at[me], (send_sems, recv_sems), step - 1, "dp", to)
        for step, to, _ in others
    ]
    out_ref[me] = x_ref[me]
    for copy in copies:
        copy.wait()


def swap_owners(x, collective_id):
    owners = lax.axis_size("dp")
    return talk(
        swap_kernel,
        jax.ShapeDtypeStruct(x.shape, x.dtype),
        collective_id,
        x,
        scratch=sem_pair(owners - 1),
    )


def sinusoid(length, model_width):
    places = np.arange(length, dtype=np.float32)[:, None]
    halves = np.arange(model_width // 2, dtype=np.float32)[None, :]
    angles = places * np.exp(halves * np.float32(-2.0 * math.log(10000.0) / model_width))
    angles = angles.astype(np.float64)
    return (
        np.stack([np.sin(angles), np.cos(angles)], axis=-1)
        .reshape(length, model_width)
        .astype(np.float32)
    )


def one_hot(ids, columns):
    return (ids[:, None] == columns[None, :]).astype(jnp.bfloat16)


def pick_weights(target_seg, pick_rows):
    sentence = jnp.take(target_seg, pick_rows, axis=0)
    return jnp.sum((sentence[:, None] == sentence[None, :]).astype(jnp.float32), axis=1)


def combine_stats(tops, totals, chosen):
    top = jnp.max(tops, axis=0)
    return top, jnp.sum(totals * jnp.exp(tops - top), axis=0), jnp.sum(chosen, axis=0)


def adam_direction(moment, second):
    return moment / (1.0 - beta_one**STEP) / (jnp.sqrt(second / (1.0 - beta_two**STEP)) + adam_eps)


def adam_update(weight, grad_item, moment, second, step_rate, decay_weight):
    moment = beta_one * moment + (1.0 - beta_one) * grad_item
    second = beta_two * second + (1.0 - beta_two) * grad_item * grad_item
    return (
        weight - step_rate * (adam_direction(moment, second) + decay_weight * weight),
        moment,
        second,
    )


def share_rows(array, owners, shares, share):
    rows, columns = array.shape
    blocks = array.reshape(owners, shares, rows // (owners * shares), columns)
    return lax.dynamic_index_in_dim(blocks, share, 1, keepdims=False)


def body(
    src_ids,
    src_seg,
    tgt_ids,
    tgt_seg,
    pick_pos,
    pick_label,
    attn_w,
    attn_m,
    attn_v,
    ffn_w,
    ffn_m,
    ffn_v,
    soap_basis,
    soap_stats,
    norm_p,
    norm_m,
    norm_v,
    embedding,
    embed_m,
    embed_v,
):
    owners, replicas = lax.axis_size("dp"), lax.axis_size("vocab")
    replica = lax.axis_index("vocab")
    own_table = embedding.astype(jnp.bfloat16)
    w_attn, w_ffn, norm_low, table_low = (
        lax.all_gather(attn_w.astype(jnp.bfloat16), "dp", axis=1, tiled=True),
        lax.all_gather(ffn_w.astype(jnp.bfloat16), "dp", axis=1, tiled=True),
        lax.all_gather(norm_p.astype(jnp.bfloat16), "dp", axis=1, tiled=True),
        lax.all_gather(own_table, "dp", axis=1, tiled=True),
    )
    norm_rows = norm_low.astype(jnp.float32)
    norms = [jnp.stack([norm_rows[k], norm_rows[7 + k]]) for k in range(7)]
    vocab_count, width = table_low.shape
    columns = replica * vocab_count + jnp.arange(vocab_count)
    source, source_seg, target, target_seg = (src_ids[0], src_seg[0], tgt_ids[0], tgt_seg[0])
    pick_rows, labels = (pick_pos[0], pick_label[0])
    length = source.shape[0]
    embed_scale = math.sqrt(width)
    all_ids = gather_small(jnp.concatenate([src_ids, tgt_ids]), "dp", 1)
    halves = replica * (vocab_count // 2) + jnp.arange(vocab_count // 2)
    paired = own_table.reshape(vocab_count // 2, -1)

    def look_up(ids):
        wide = lax.dot_general(one_hot(ids // 2, halves), paired, (((1,), (0,)), ((), ())))
        left, right = jnp.split(wide, 2, axis=1)
        return jnp.where((ids % 2 == 0)[:, None], left, right)

    source_part, target_part = (look_up(all_ids[:, k].reshape(-1)) for k in (0, 1))
    source_sum = lax.psum(source_part, "vocab")
    source_sum, target_part = lax.optimization_barrier((source_sum, target_part))
    target_sum = lax.psum(target_part, "vocab")

    def own_row(summed, collective_id):
        blocks = swap_owners(summed.reshape(owners, length, -1), collective_id)
        return jnp.swapaxes(blocks, 0, 1).reshape(length, -1).astype(jnp.float32)

    looked_up = [own_row(source_sum, 2), own_row(target_sum, 3)]
    positional = sinusoid(length, width)

    enc_in = looked_up[0] * embed_scale + positional
    enc_mid, enc_attn = attn_forward(
        enc_in, norms[0], w_attn[0:4], source_seg, source_seg, None, False
    )
    enc_out, encoded, enc_ffn = ffn_forward(enc_mid, norms[1], norms[2], w_ffn[0], w_ffn[1])
    dec_in = looked_up[1] * embed_scale + positional
    dec_mid, dec_self = attn_forward(
        dec_in, norms[3], w_attn[4:8], target_seg, target_seg, None, True
    )
    dec_late, dec_cross = attn_forward(
        dec_mid, norms[4], w_attn[8:12], target_seg, source_seg, encoded, False
    )
    dec_out, final_low, dec_ffn = ffn_forward(dec_late, norms[5], norms[6], w_ffn[2], w_ffn[3])

    chosen_rows = one_hot(pick_rows, jnp.arange(length))
    picked = dot_dims(chosen_rows, final_low, 1, 0).astype(jnp.bfloat16)
    logits = dot_dims(picked, table_low, 1, 1)
    row_top = jnp.max(logits, axis=-1)
    row_total = jnp.sum(jnp.exp(logits - row_top[:, None]), axis=-1)
    label_hit = labels[:, None] == columns[None, :]
    chosen = jnp.sum(jnp.where(label_hit, logits, 0.0), axis=-1)
    seen = gather_small(
        jnp.pad(jnp.stack([row_top, row_total, chosen]), ((0, 5), (0, 0))), "vocab", 4
    )
    row_top, row_total, chosen = combine_stats(seen[:, 0], seen[:, 1], seen[:, 2])
    log_total = row_top + jnp.log(row_total)
    weight = 1.0 / pick_weights(target_seg, pick_rows)
    loss_part = jnp.sum((log_total - chosen) * weight)
    count_part = (target_seg[-1] + 1).astype(jnp.float32)
    grad_logits = (
        weight[:, None] * (jnp.exp(logits - log_total[:, None]) - label_hit.astype(jnp.float32))
    ).astype(jnp.bfloat16)
    grad_picked = sum_vocab(dot_dims(grad_logits, table_low, 1, 0).astype(jnp.bfloat16), 5)
    grad_table = lax.psum_scatter(
        dot_dims(grad_logits, picked, 0, 0).astype(jnp.bfloat16),
        "dp",
        scatter_dimension=1,
        tiled=True,
    )
    grad_final = dot_dims(chosen_rows, grad_picked, 0, 0)

    norm_grads = [None] * 7
    grad, norm_grads[6] = plain_norm_backward(grad_final, dec_out, norms[6])
    grad, norm_grads[5], dec_ffn_parts = ffn_backward(grad, dec_ffn)
    grad, norm_grads[4], cross_parts, grad_encoded = attn_backward(grad, dec_cross)
    grad, norm_grads[3], self_parts, _ = attn_backward(grad, dec_self)
    grad_target = (grad * embed_scale).astype(jnp.bfloat16)
    grad, norm_grads[2] = plain_norm_backward(grad_encoded, enc_out, norms[2])
    grad, norm_grads[1], enc_ffn_parts = ffn_backward(grad, enc_ffn)
    grad, norm_grads[0], enc_parts, _ = attn_backward(grad, enc_attn)
    grad_source = (grad * embed_scale).astype(jnp.bfloat16)
    token_grads = jnp.concatenate([grad_source, grad_target]).reshape(2 * length, owners, -1)
    token_grads = swap_owners(jnp.swapaxes(token_grads, 0, 1), 6).reshape(owners * 2 * length, -1)
    flat_ids = all_ids.reshape(-1)
    even = (flat_ids % 2 == 0)[:, None]
    token_grads = jnp.concatenate(
        [jnp.where(even, token_grads, 0), jnp.where(even, 0, token_grads)], axis=1
    )
    g_embed = grad_table.astype(jnp.float32) + dot_dims(
        one_hot(flat_ids // 2, halves), token_grads, 0, 0
    ).reshape(vocab_count, -1)

    chosen_columns = share_rows(jnp.eye(width, dtype=jnp.bfloat16), owners, replicas, replica)
    chosen_columns = chosen_columns.reshape(-1, width)

    def weight_grads(stored, parts):
        normed, kept, cross = stored[7], stored[8], stored[6]
        grad_low, gq, gk, gv = parts
        key_in = encoded if cross else normed
        share = [dot_dims(chosen_columns, rows, 1, 1).astype(jnp.bfloat16) for rows in (normed, key_in)]
        mixed = share_rows(kept[3], owners, replicas, replica).reshape(-1, length)
        return [
            dot_dims(share[0], gq, 1, 0),
            dot_dims(share[1], gk, 1, 0),
            dot_dims(share[1], gv, 1, 0),
            dot_dims(mixed, grad_low, 1, 0),
        ]

    def hidden_grads(stored, parts):
        grad_low, values, grads = parts
        return [
            dot_dims(share_rows(rows, owners, replicas, replica).reshape(-1, length), right, 1, 0)
            for rows, right in ((grads, stored[4]), (values, grad_low))
        ]

    pieces = (
        weight_grads(enc_attn, enc_parts)
        + weight_grads(dec_self, self_parts)
        + weight_grads(dec_cross, cross_parts)
        + hidden_grads(enc_ffn, enc_ffn_parts)
        + hidden_grads(dec_ffn, dec_ffn_parts)
    )
    blocks = [piece.astype(jnp.bfloat16).reshape(owners, -1, width) for piece in pieces]
    blocks = [jnp.concatenate(blocks[k : k + 4], axis=1) for k in (0, 4, 8)] + blocks[12:]
    shared = share_gradients(jnp.stack(blocks, axis=1), 7)
    g_attn = shared[:, :3].reshape(replicas, 12, -1, width)
    g_attn = jnp.swapaxes(g_attn, 0, 1).reshape(12, -1, width).astype(jnp.float32)
    g_ffn = jnp.swapaxes(shared[:, 3:], 0, 1).reshape(4, -1, width)
    norm_grad = jnp.stack(norm_grads)
    norm_grad = jnp.concatenate([norm_grad[:, 0], norm_grad[:, 1]], axis=0)
    g_norm = lax.psum_scatter(norm_grad, "dp", scatter_dimension=1, tiled=True)

    matrix = replica % 4
    own_grad = lax.dynamic_index_in_dim(g_ffn, matrix, 0, keepdims=False)
    own_products = dot_dims(own_grad, own_grad, 0, 0)
    g_ffn = g_ffn.astype(jnp.float32)
    first_copy = (replica == 0).astype(jnp.float32)
    layer_sq = jnp.sum(g_attn * g_attn) + jnp.sum(g_ffn * g_ffn) + jnp.sum(g_norm * g_norm)
    raw_squares = jnp.sum(g_embed * g_embed) + first_copy * layer_sq
    few = jnp.stack([first_copy * loss_part, first_copy * count_part, raw_squares])
    few = jnp.broadcast_to(jnp.pad(few, (0, 5))[:, None], (8, 128))
    own_products, few = sum_tail(own_products, few, 8)
    loss_sum, sentences, squares = few[0, 0], few[1, 0], few[2, 0]
    grad_norm = jnp.sqrt(squares) / sentences
    factor = jnp.minimum(1.0, clip_limit / (grad_norm + norm_eps)) / sentences
    g_attn, g_ffn, g_norm, g_embed = (
        g_attn * factor,
        g_ffn * factor,
        g_norm * factor,
        g_embed * factor,
    )
    all_products = lax.all_gather(own_products.astype(jnp.bfloat16), "vocab")[:4]
    new_stats = stat_decay * soap_stats + (1.0 - stat_decay) * (factor * factor) * (
        all_products.astype(jnp.float32)
    )
    own_stat = stat_decay * lax.dynamic_index_in_dim(soap_stats, matrix, 0, keepdims=False) + (
        1.0 - stat_decay
    ) * (factor * factor) * own_products
    own_basis = renew_basis(own_stat, lax.dynamic_index_in_dim(soap_basis, matrix, 0, keepdims=False))
    new_basis = gather_quad(own_basis.astype(jnp.bfloat16), 9).astype(jnp.float32)

    new_attn, m_attn, v_attn = adam_update(attn_w, g_attn, attn_m, attn_v, rate_matrix, decay_rate)
    new_norm, m_norm, v_norm = adam_update(norm_p, g_norm, norm_m, norm_v, rate_vector, 0.0)
    new_embed, m_embed, v_embed = adam_update(
        embedding, g_embed, embed_m, embed_v, rate_matrix, decay_rate
    )
    rotated = jnp.einsum("mfd,mde->mfe", g_ffn, soap_basis, precision=highest)
    m_ffn = beta_one * ffn_m + (1.0 - beta_one) * rotated
    v_ffn = beta_two * ffn_v + (1.0 - beta_two) * rotated * rotated
    back_rotated = jnp.einsum(
        "mfe,mde->mfd", adam_direction(m_ffn, v_ffn), soap_basis, precision=highest
    )
    new_ffn = ffn_w - rate_matrix * (back_rotated + decay_rate * ffn_w)
    return (
        loss_sum,
        sentences,
        grad_norm,
        new_attn,
        m_attn,
        v_attn,
        new_ffn,
        m_ffn,
        v_ffn,
        new_basis,
        new_stats,
        new_norm,
        m_norm,
        v_norm,
        new_embed,
        m_embed,
        v_embed,
    )


def solution(mesh):
    placed = (
        P("dp", None),
        P("dp", None),
        P("dp", None),
        P("dp", None),
        P("dp", None),
        P("dp", None),
        P(None, "dp", None),
        P(None, "dp", None),
        P(None, "dp", None),
        P(None, "dp", None),
        P(None, "dp", None),
        P(None, "dp", None),
        P(),
        P(),
        P(None, "dp"),
        P(None, "dp"),
        P(None, "dp"),
        P("vocab", "dp"),
        P("vocab", "dp"),
        P("vocab", "dp"),
    )
    return jax.shard_map(
        body,
        mesh=mesh,
        in_specs=placed,
        out_specs=(
            P(),
            P(),
            P(),
            P(None, "dp", None),
            P(None, "dp", None),
            P(None, "dp", None),
            P(None, "dp", None),
            P(None, "dp", None),
            P(None, "dp", None),
            P(),
            P(),
            P(None, "dp"),
            P(None, "dp"),
            P(None, "dp"),
            P("vocab", "dp"),
            P("vocab", "dp"),
            P("vocab", "dp"),
        ),
        check_vma=False,
    )
```

```python
from functools import partial
import math

import jax
import jax.numpy as jnp
import numpy as np
from jax import lax
from jax.experimental import pallas as pl
from jax.experimental.pallas import tpu as pltpu
from jax.sharding import PartitionSpec as P

HEADS = 8
STEP = 10
TILE = 128

highest = lax.Precision.HIGHEST
beta_one = 0.9
beta_two = 0.999
adam_eps = 1e-08
decay_rate = 0.01
rate_matrix = 0.03
rate_vector = 0.3
clip_limit = 1.0
stat_decay = 0.95
norm_eps = 1e-06
masked = -1e30
log_two_e = math.log2(math.e)
vmem = pl.BlockSpec(memory_space=pltpu.VMEM)
smem = pl.BlockSpec(memory_space=pltpu.SMEM)
mesh_ids = pl.DeviceIdType.MESH


def dot_dims(left, right, left_dim, right_dim):
    return lax.dot_general(
        left, right, (((left_dim,), (right_dim,)), ((), ())), preferred_element_type=jnp.float32
    )


def dot_exact(left, right, left_dim, right_dim):
    return lax.dot_general(
        left,
        right,
        (((left_dim,), (right_dim,)), ((), ())),
        precision=highest,
        preferred_element_type=jnp.float32,
    )


def call(kernel, outs, *args, scratch=(), smem_args=0):
    return pl.pallas_call(
        kernel,
        out_shape=outs,
        in_specs=[vmem] * (len(args) - smem_args) + [smem] * smem_args,
        out_specs=jax.tree.map(lambda _: vmem, outs),
        scratch_shapes=list(scratch),
        compiler_params=pltpu.CompilerParams(vmem_limit_bytes=56 * 2**20),
    )(*args)


def low(*shape):
    return jax.ShapeDtypeStruct(shape, jnp.bfloat16)


def full(*shape):
    return jax.ShapeDtypeStruct(shape, jnp.float32)


def norm_parts(values):
    centre = values - jnp.mean(values, axis=-1, keepdims=True)
    spread = jnp.mean(centre * centre, axis=-1, keepdims=True)
    root = lax.rsqrt(spread + norm_eps)
    return centre * root, root


def norm_forward(values, ln_ref):
    return norm_parts(values)[0] * ln_ref[0:1, :] + ln_ref[1:2, :]


def norm_backward(grad, values, ln_ref, ln_grad_ref):
    normed, root = norm_parts(values)
    ln_grad_ref[0:1, :] = jnp.sum(grad * normed, axis=0, keepdims=True)
    ln_grad_ref[1:2, :] = jnp.sum(grad, axis=0, keepdims=True)
    inner = grad * ln_ref[0:1, :]
    return root * (
        inner
        - jnp.mean(inner, axis=-1, keepdims=True)
        - normed * jnp.mean(inner * normed, axis=-1, keepdims=True)
    )


def at_tile(index):
    return pl.ds(pl.multiple_of(index * TILE, TILE), TILE)


def tile_mask(segq_ref, segk_ref, qi, ki, causal):
    allowed = segk_ref[at_tile(ki), :] == segq_ref[:, at_tile(qi)]
    if causal:
        ahead = lax.broadcasted_iota(jnp.int32, (TILE, TILE), 0) - lax.broadcasted_iota(
            jnp.int32, (TILE, TILE), 1
        )
        allowed = allowed & (ahead <= (qi - ki) * TILE)
    return allowed


def for_tiles(count, edge_ref, causal, step):
    def one(pair, carry):
        qi, ki = pair // count, lax.rem(pair, count)
        live = (edge_ref[0, qi] <= edge_ref[3, ki]) & (edge_ref[2, ki] <= edge_ref[1, qi])
        if causal:
            live = live & (ki <= qi)

        @pl.when(live)
        def _():
            step(qi, ki)

        return carry

    lax.fori_loop(0, count * count, one, 0)


def tile_edges(seg_q, seg_k):
    last = TILE - 1
    return jnp.stack([seg_q[::TILE], seg_q[last::TILE], seg_k[::TILE], seg_k[last::TILE]])


def lay_weights(w_ref, piece_refs):
    own = piece_refs[0]
    w_ref_rows = own.shape[1]
    me, side = lax.axis_index("dp"), lax.rem(lax.axis_index("vocab"), 2)
    half = own.shape[0] // 2

    def rows_of(index):
        return pl.ds(pl.multiple_of(index * w_ref_rows, w_ref_rows), w_ref_rows)

    w_ref[:, rows_of(me), :] = own[...]
    for k in range(1, 4):
        rows = rows_of(me ^ k)
        w_ref[pl.ds(side * half, half), rows, :] = piece_refs[k][...]
        w_ref[pl.ds((1 - side) * half, half), rows, :] = piece_refs[k + 3][...]


def gather_weights(own, after):
    if after is not None:
        own, _ = lax.optimization_barrier((own, after))
    owners, replicas = lax.axis_size("dp"), lax.axis_size("vocab")
    if owners != 4:
        whole = lax.all_gather(own, "dp", axis=1, tiled=True)
        return (whole,), whole[0, 0]
    half = own.shape[0] // 2
    mine = lax.dynamic_slice_in_dim(own, lax.axis_index("vocab") % 2 * half, half, 0)
    got = [lax.ppermute(mine, "dp", [(s, s ^ k) for s in range(owners)]) for k in range(1, 4)]
    swapped = [lax.ppermute(part, "vocab", [(s, s ^ 1) for s in range(replicas)]) for part in got]
    return (own, *got, *swapped), swapped[-1][0, 0]


def attn_forward_kernel(causal, cross, pieces, *refs):
    refs = list(refs)
    x_ref, ln_ref, segq_ref, segk_ref = refs[:4]
    refs = refs[4:]
    key_ref = refs.pop(0) if cross else None
    piece_refs, refs = refs[:pieces], refs[pieces:]
    edge_ref, out_ref, a_ref, qt_ref, kt_ref, vt_ref, ot_ref, lse_ref = refs[:8]
    refs = refs[8:]
    w_ref = piece_refs[0]
    if pieces > 1:
        w_ref = refs.pop(0)
        lay_weights(w_ref, piece_refs)
    top_ref, sum_ref, acc_ref = refs
    length, width = x_ref.shape
    head_size = width // HEADS
    a_ref[...] = norm_forward(x_ref[...], ln_ref).astype(jnp.bfloat16)
    key_in = key_ref if cross else a_ref
    qt_ref[...] = dot_dims(a_ref[...], w_ref[0], 1, 0).astype(jnp.bfloat16).T
    kt_ref[...] = dot_dims(key_in[...], w_ref[1], 1, 0).astype(jnp.bfloat16).T
    vt_ref[...] = dot_dims(key_in[...], w_ref[2], 1, 0).astype(jnp.bfloat16).T
    top_ref[...] = jnp.full(top_ref.shape, masked, jnp.float32)
    sum_ref[...] = jnp.zeros(sum_ref.shape, jnp.float32)
    acc_ref[...] = jnp.zeros(acc_ref.shape, jnp.float32)
    scale = log_two_e / math.sqrt(head_size)
    bands = [slice(h * head_size, (h + 1) * head_size) for h in range(HEADS)]

    def step(qi, ki):
        q_at, k_at = at_tile(qi), at_tile(ki)
        allowed = tile_mask(segq_ref, segk_ref, qi, ki, causal)
        scores = [dot_dims(kt_ref[band, k_at], qt_ref[band, q_at], 0, 0) * scale for band in bands]
        scores = [jnp.where(allowed, part, masked) for part in scores]
        top = top_ref[:, q_at]
        new_top = jnp.maximum(
            top,
            jnp.concatenate([jnp.max(part, axis=0, keepdims=True) for part in scores], axis=0),
        )
        fade = jnp.exp2(top - new_top)
        parts = [jnp.exp2(scores[h] - new_top[h : h + 1]) for h in range(HEADS)]
        top_ref[:, q_at] = new_top
        sum_ref[:, q_at] = sum_ref[:, q_at] * fade + jnp.concatenate(
            [jnp.sum(part, axis=0, keepdims=True) for part in parts], axis=0
        )
        mixed = [
            dot_dims(vt_ref[bands[h], k_at], parts[h].astype(jnp.bfloat16), 1, 0)
            for h in range(HEADS)
        ]
        acc = acc_ref[:, q_at]
        acc_ref[:, q_at] = jnp.concatenate(
            [acc[bands[h]] * fade[h : h + 1] + mixed[h] for h in range(HEADS)], axis=0
        )

    for_tiles(length // TILE, edge_ref, causal, step)
    lse_ref[...] = top_ref[...] + jnp.log2(sum_ref[...])
    for h in range(HEADS):
        ot_ref[bands[h], :] = (acc_ref[bands[h], :] / sum_ref[h : h + 1, :]).astype(jnp.bfloat16)
    out_ref[...] = x_ref[...] + dot_dims(ot_ref[...], w_ref[3], 0, 0)


def attn_forward(x, ln, weights, seg_q, seg_k, key_in, causal):
    length, width = x.shape
    cross = key_in is not None
    segs = (seg_q[None, :], jnp.broadcast_to(seg_k[:, None], (length, TILE)))
    edges = tile_edges(seg_q, seg_k)
    args = (x, ln, *segs) + ((key_in,) if cross else ()) + (*weights, edges)
    outs = (full(length, width), low(length, width)) + (low(width, length),) * 4
    outs = outs + (full(HEADS, length),)
    if len(weights) > 1:
        outs = outs + (low(4, width, width),)
    out, normed, *stored = call(
        partial(attn_forward_kernel, causal, cross, len(weights)),
        outs,
        *args,
        scratch=[
            pltpu.VMEM((HEADS, length), jnp.float32),
            pltpu.VMEM((HEADS, length), jnp.float32),
            pltpu.VMEM((width, length), jnp.float32),
        ],
        smem_args=1,
    )
    whole = stored.pop() if len(weights) > 1 else weights[0]
    return out, (x, ln, whole, segs, edges, causal, cross, normed, stored)


def attn_backward_kernel(causal, cross, *refs):
    (g_ref, x_ref, ln_ref, w_ref, segq_ref, segk_ref, qt_ref, kt_ref, vt_ref, ot_ref, lse_ref) = refs[:11]
    refs = list(refs[11:])
    edge_ref, out_ref, ln_grad_ref, low_ref, gq_ref, gk_ref, gv_ref = refs[:7]
    refs = refs[7:]
    key_grad_ref = refs.pop(0) if cross else None
    got_ref, delta_ref, gqt_ref, gkt_ref, gvt_ref = refs
    length, width = x_ref.shape
    head_size = width // HEADS
    low_ref[...] = g_ref[...].astype(jnp.bfloat16)
    got_ref[...] = dot_dims(low_ref[...], w_ref[3], 1, 1).astype(jnp.bfloat16).T
    bands = [slice(h * head_size, (h + 1) * head_size) for h in range(HEADS)]
    for h in range(HEADS):
        delta_ref[h : h + 1, :] = jnp.sum(
            got_ref[bands[h], :].astype(jnp.float32) * ot_ref[bands[h], :].astype(jnp.float32),
            axis=0,
            keepdims=True,
        )
    for ref in (gqt_ref, gkt_ref, gvt_ref):
        ref[...] = jnp.zeros(ref.shape, jnp.float32)
    scale = log_two_e / math.sqrt(head_size)
    back = 1.0 / math.sqrt(head_size)

    def step(qi, ki):
        q_at, k_at = at_tile(qi), at_tile(ki)
        allowed = tile_mask(segq_ref, segk_ref, qi, ki, causal)
        scores = [dot_dims(kt_ref[band, k_at], qt_ref[band, q_at], 0, 0) for band in bands]
        grads = [dot_dims(vt_ref[band, k_at], got_ref[band, q_at], 0, 0) for band in bands]
        parts = [
            jnp.where(allowed, jnp.exp2(scores[h] * scale - lse_ref[h : h + 1, q_at]), 0.0)
            for h in range(HEADS)
        ]
        grads = [parts[h] * (grads[h] - delta_ref[h : h + 1, q_at]) for h in range(HEADS)]
        parts_t = [part.T.astype(jnp.bfloat16) for part in parts]
        grads_t = [part.T.astype(jnp.bfloat16) for part in grads]
        grads = [part.astype(jnp.bfloat16) for part in grads]
        for ref, place, terms in (
            (gvt_ref, k_at, [dot_dims(got_ref[bands[h], q_at], parts_t[h], 1, 0) for h in range(HEADS)]),
            (gkt_ref, k_at, [dot_dims(qt_ref[bands[h], q_at], grads_t[h], 1, 0) for h in range(HEADS)]),
            (gqt_ref, q_at, [dot_dims(kt_ref[bands[h], k_at], grads[h], 1, 0) for h in range(HEADS)]),
        ):
            ref[:, place] += jnp.concatenate(terms, axis=0)

    for_tiles(length // TILE, edge_ref, causal, step)
    gq_ref[...] = (gqt_ref[...] * back).astype(jnp.bfloat16).T
    gk_ref[...] = (gkt_ref[...] * back).astype(jnp.bfloat16).T
    gv_ref[...] = gvt_ref[...].astype(jnp.bfloat16).T
    from_query = dot_dims(gq_ref[...], w_ref[0], 1, 1)
    from_keys = dot_dims(gk_ref[...], w_ref[1], 1, 1) + dot_dims(gv_ref[...], w_ref[2], 1, 1)
    if cross:
        key_grad_ref[...] = from_keys
    else:
        from_query = from_query + from_keys
    out_ref[...] = g_ref[...] + norm_backward(from_query, x_ref[...], ln_ref, ln_grad_ref)


def attn_backward(grad, stored):
    x, ln, weights, segs, edges, causal, cross, _, kept = stored
    length, width = x.shape
    outs = (full(length, width), full(2, width)) + (low(length, width),) * 4
    if cross:
        outs = outs + (full(length, width),)
    out, ln_grad, *rest = call(
        partial(attn_backward_kernel, causal, cross),
        outs,
        grad,
        x,
        ln,
        weights,
        *segs,
        *kept,
        edges,
        scratch=[pltpu.VMEM((width, length), jnp.bfloat16), pltpu.VMEM((HEADS, length), jnp.float32)]
        + [pltpu.VMEM((width, length), jnp.float32)] * 3,
        smem_args=1,
    )
    return out, ln_grad, rest[:4], rest[4] if cross else None


def gelu_parts(hidden):
    root = math.sqrt(2.0 / math.pi)
    square = hidden * hidden
    bend = jnp.tanh(root * hidden * (1.0 + 0.044715 * square))
    value = 0.5 * hidden * (1.0 + bend)
    slope = 0.5 * (1.0 + bend) + 0.5 * hidden * (1.0 - bend * bend) * root * (
        1.0 + 3.0 * 0.044715 * square
    )
    return value, slope


def ffn_forward_kernel(chunk, pieces, x_ref, ln_ref, next_ref, *refs):
    piece_refs, (out_ref, a_ref, after_ref, *refs) = refs[:pieces], refs[pieces:]
    w_ref = piece_refs[0]
    if pieces > 1:
        (w_ref,) = refs
        lay_weights(w_ref, piece_refs)
    w_in_ref, w_out_ref = w_ref.at[0], w_ref.at[1]
    a_ref[...] = norm_forward(x_ref[...], ln_ref).astype(jnp.bfloat16)
    total = x_ref[...]
    for start in range(0, w_in_ref.shape[0], chunk):
        part = slice(start, start + chunk)
        hidden = dot_dims(a_ref[...], w_in_ref[part, :], 1, 1)
        active = gelu_parts(hidden)[0].astype(jnp.bfloat16)
        total = total + dot_dims(active, w_out_ref[part, :], 1, 0)
    out_ref[...] = total
    after_ref[...] = norm_forward(total, next_ref).astype(after_ref.dtype)


def ffn_forward(x, ln, ln_next, weights):
    length, width = x.shape
    outs = (full(length, width), low(length, width), low(length, width))
    if len(weights) > 1:
        outs = outs + (low(2, 4 * weights[0].shape[1], width),)
    out, normed, after, *whole = call(
        partial(ffn_forward_kernel, 512, len(weights)), outs, x, ln, ln_next, *weights
    )
    return out, after, (x, ln, whole[0] if whole else weights[0], normed)


def ffn_backward_kernel(
    chunk, g_ref, x_ref, ln_ref, a_ref, w_ref, out_ref, ln_grad_ref, low_ref, ut_ref, ht_ref
):
    w_in_ref, w_out_ref = w_ref.at[0], w_ref.at[1]
    low_ref[...] = g_ref[...].astype(jnp.bfloat16)
    total = jnp.zeros(g_ref.shape, jnp.float32)
    for start in range(0, w_in_ref.shape[0], chunk):
        part = slice(start, start + chunk)
        hidden = dot_dims(a_ref[...], w_in_ref[part, :], 1, 1)
        value, slope = gelu_parts(hidden)
        ut_ref[part, :] = value.astype(jnp.bfloat16).T
        grad = (dot_dims(low_ref[...], w_out_ref[part, :], 1, 1) * slope).astype(jnp.bfloat16)
        ht_ref[part, :] = grad.T
        total = total + dot_dims(grad, w_in_ref[part, :], 1, 0)
    out_ref[...] = g_ref[...] + norm_backward(total, x_ref[...], ln_ref, ln_grad_ref)


def ffn_backward(grad, stored):
    x, ln, weights, normed = stored
    length, width = x.shape
    hidden = weights.shape[1]
    out, ln_grad, *rest = call(
        partial(ffn_backward_kernel, 512),
        (full(length, width), full(2, width), low(length, width), low(hidden, length), low(hidden, length)),
        grad,
        x,
        ln,
        normed,
        weights,
    )
    return out, ln_grad, rest


def norm_backward_kernel(g_ref, x_ref, ln_ref, out_ref, ln_grad_ref):
    out_ref[...] = norm_backward(g_ref[...], x_ref[...], ln_ref, ln_grad_ref)


def plain_norm_backward(grad, x, ln):
    return call(norm_backward_kernel, (full(*x.shape), full(2, x.shape[1])), grad, x, ln)


def small_factor(block):
    size = block.shape[0]
    eye = (
        lax.broadcasted_iota(jnp.int32, (size, size), 0)
        == lax.broadcasted_iota(jnp.int32, (size, size), 1)
    ).astype(jnp.float32)
    whole = jnp.concatenate([block, eye], axis=1)
    rows = [whole[8 * u : 8 * u + 8] for u in range(size // 8)]
    shape = rows[0].shape
    sub = lax.broadcasted_iota(jnp.int32, shape, 0)

    def lane_splat(value, lane):
        return jnp.broadcast_to(value[:, lane : lane + 1], shape)

    def row_splat(value, row):
        return jnp.broadcast_to(value[row : row + 1, :], shape)

    for g in range(len(rows)):
        first = 8 * g
        lanes = {
            u: [lane_splat(rows[u], first + s) for s in range(8)] for u in range(g, len(rows))
        }
        scale = jnp.zeros(shape, jnp.float32)
        for t in range(8):
            pivot = row_splat(lanes[g][t], t)
            root = lax.rsqrt(pivot)
            inverse = root * root
            scale = jnp.where(sub == t, root, scale)
            row_t = row_splat(rows[g], t) * inverse
            splats = {s: row_splat(lanes[g][s], t) * inverse for s in range(t + 1, 8)}
            for u in range(g, len(rows)):
                factor = lanes[u][t]
                if u == g:
                    factor = jnp.where(sub > t, factor, 0.0)
                rows[u] = rows[u] - factor * row_t
                for s in range(t + 1, 8):
                    lanes[u][s] = lanes[u][s] - factor * splats[s]
        rows[g] = rows[g] * scale
    return jnp.concatenate(rows, axis=0)[:, size:]


def renew_kernel(stat_ref, basis_ref, out_ref, gram_ref, rest_ref):
    size = stat_ref.shape[0]
    product = dot_exact(stat_ref[...], basis_ref[...], 1, 0)
    rest_ref[...] = product
    gram_ref[...] = dot_exact(product, product, 0, 0)
    for low in range(0, size, 128):
        high = low + 128
        block = gram_ref[low:high, low:high]
        corner = small_factor(block[:64, :64])
        across = dot_exact(corner, block[:64, 64:], 1, 0)
        second = small_factor(block[64:, 64:] - dot_exact(across, across, 0, 0))
        below = dot_exact(second, dot_exact(across, corner, 0, 0), 1, 0)
        inverse = jnp.concatenate(
            [
                jnp.concatenate([corner, jnp.zeros_like(corner)], axis=1),
                jnp.concatenate([-below, second], axis=1),
            ],
            axis=0,
        )
        columns = dot_exact(rest_ref[:, low:high], inverse, 1, 1)
        out_ref[:, low:high] = columns
        if high < size:
            panel = dot_exact(inverse, gram_ref[low:high, high:], 1, 0)
            gram_ref[high:, high:] -= dot_exact(panel, panel, 0, 0)
            rest_ref[:, high:] -= dot_exact(columns, panel, 1, 0)


def renew_basis(statistic, basis):
    shape = statistic.shape
    return call(
        renew_kernel,
        full(*shape),
        statistic,
        basis,
        scratch=[pltpu.VMEM(shape, jnp.float32), pltpu.VMEM(shape, jnp.float32)],
    )


def peers_of(axis):
    size, me = lax.axis_size(axis), lax.axis_index(axis)
    return [
        (step, lax.rem(me + step, size), lax.rem(me + size - step, size)) for step in range(1, size)
    ]


def greet(*places):
    barrier = pltpu.get_barrier_semaphore()
    for axis, index in places:
        pl.semaphore_signal(barrier, inc=1, device_id={axis: index}, device_id_type=mesh_ids)
    pl.semaphore_wait(barrier, len(places))


def push(source, target, sems, slot, axis, index):
    copy = pltpu.make_async_remote_copy(
        src_ref=source,
        dst_ref=target,
        send_sem=sems[0].at[slot],
        recv_sem=sems[1].at[slot],
        device_id={axis: index},
        device_id_type=mesh_ids,
    )
    copy.start()
    return copy


def sem_pair(count):
    return [pltpu.SemaphoreType.DMA((count,)), pltpu.SemaphoreType.DMA((count,))]


def talk(kernel, outs, collective_id, *args, scratch=()):
    return pl.pallas_call(
        kernel,
        out_shape=outs,
        in_specs=[vmem] * len(args),
        out_specs=jax.tree.map(lambda _: vmem, outs),
        scratch_shapes=list(scratch),
        compiler_params=pltpu.CompilerParams(
            collective_id=collective_id, has_side_effects=True, vmem_limit_bytes=56 * 2**20
        ),
    )(*args)


def gather_kernel(axis, *refs):
    count = (len(refs) - 2) // 2
    others = peers_of(axis)
    greet(*[(axis, to) for _, to, _ in others])
    me = lax.axis_index(axis)
    copies = [
        push(refs[k], refs[count + k].at[me], refs[-2:], k * len(others) + step - 1, axis, to)
        for k in range(count)
        for step, to, _ in others
    ]
    for k in range(count):
        refs[count + k][me] = refs[k][...]
    for copy in copies:
        copy.wait()


def gather_small(axis, collective_id, *arrays):
    size = lax.axis_size(axis)
    outs = tuple(jax.ShapeDtypeStruct((size, *x.shape), x.dtype) for x in arrays)
    sems = sem_pair((size - 1) * len(arrays))
    return talk(partial(gather_kernel, axis), outs, collective_id, *arrays, scratch=sems)


def sum_kernel(x_ref, out_ref, parts_ref, mine_ref, s0, r0, s1, r1):
    others = peers_of("vocab")
    greet(*[("vocab", to) for _, to, _ in others])
    size, me = lax.axis_size("vocab"), lax.axis_index("vocab")
    rows = mine_ref.shape[0]

    def rows_of(index):
        return pl.ds(pl.multiple_of(index * rows, rows), rows)

    copies = [
        push(x_ref.at[rows_of(to)], parts_ref.at[me], (s0, r0), step - 1, "vocab", to)
        for step, to, _ in others
    ]
    parts_ref[me] = x_ref[rows_of(me), :]
    for copy in copies:
        copy.wait()
    total = parts_ref[0].astype(jnp.float32)
    for index in range(1, size):
        total = total + parts_ref[index].astype(jnp.float32)
    mine_ref[...] = total.astype(mine_ref.dtype)
    copies = [
        push(mine_ref, out_ref.at[rows_of(me)], (s1, r1), step - 1, "vocab", to)
        for step, to, _ in others
    ]
    out_ref[rows_of(me), :] = mine_ref[...]
    for copy in copies:
        copy.wait()


def sum_vocab(x, collective_id):
    replicas = lax.axis_size("vocab")
    rows, columns = x.shape
    share = rows // replicas
    return talk(
        sum_kernel,
        jax.ShapeDtypeStruct(x.shape, x.dtype),
        collective_id,
        x,
        scratch=[
            pltpu.VMEM((replicas, share, columns), x.dtype),
            pltpu.VMEM((share, columns), x.dtype),
        ]
        + sem_pair(replicas - 1)
        + sem_pair(replicas - 1),
    )


def flip(index, bit):
    return index + bit - 2 * bit * lax.rem(index // bit, 2)


def tail_kernel(
    x_ref, few_ref, out_ref, sum_ref, parts_ref, seen_ref, line_ref, lines_ref,
    s0, r0, s1, r1, s2, r2, s3, r3, s4, r4,
):
    owners, replicas = peers_of("dp"), peers_of("vocab")
    greet(*[("dp", to) for _, to, _ in owners], *[("vocab", to) for _, to, _ in replicas])
    size, me, here = lax.axis_size("dp"), lax.axis_index("dp"), lax.axis_index("vocab")
    near, side = flip(here, 1), lax.rem(here, 2)
    rows = parts_ref.shape[1]

    def rows_of(index):
        return pl.ds(pl.multiple_of((side * size + index) * rows, rows), rows)

    few = [
        push(few_ref, seen_ref.at[here], (s2, r2), step - 1, "vocab", to) for step, to, _ in replicas
    ]
    wide = [
        push(x_ref.at[rows_of(to)], parts_ref.at[me], (s0, r0), step - 1, "dp", to)
        for step, to, _ in owners
    ]
    seen_ref[here] = few_ref[...]
    parts_ref[me] = x_ref[rows_of(me), :]
    for copy in few:
        copy.wait()
    line_ref[...] = jnp.sum(seen_ref[...], axis=0)
    few = [
        push(line_ref, lines_ref.at[me], (s3, r3), step - 1, "dp", to) for step, to, _ in owners
    ]
    lines_ref[me] = line_ref[...]
    for copy in wide:
        copy.wait()
    out_ref[rows_of(me), :] = jnp.sum(parts_ref[...], axis=0)
    mine = out_ref.at[rows_of(me)]
    wide = [push(mine, mine, (s1, r1), step - 1, "dp", to) for step, to, _ in owners]
    close = [push(mine, mine, (s4, r4), 0, "vocab", near)]
    for copy in few:
        copy.wait()
    sum_ref[...] = jnp.sum(lines_ref[...], axis=0)
    for copy, (step, _, origin) in zip(wide, owners):
        copy.wait()
        theirs = out_ref.at[rows_of(origin)]
        close.append(push(theirs, theirs, (s4, r4), step, "vocab", near))
    for copy in close:
        copy.wait()


def sum_tail(x, few, collective_id):
    owners, replicas = lax.axis_size("dp"), lax.axis_size("vocab")
    rows, columns = x.shape
    share = rows // (2 * owners)
    return talk(
        tail_kernel,
        (full(*x.shape), full(*few.shape)),
        collective_id,
        x,
        few,
        scratch=[
            pltpu.VMEM((owners, share, columns), jnp.float32),
            pltpu.VMEM((replicas, *few.shape), jnp.float32),
            pltpu.VMEM(few.shape, jnp.float32),
            pltpu.VMEM((owners, *few.shape), jnp.float32),
        ]
        + sem_pair(owners - 1)
        + sem_pair(owners - 1)
        + sem_pair(replicas - 1)
        + sem_pair(owners - 1)
        + sem_pair(owners),
    )


def far_replicas():
    here, size = lax.axis_index("vocab"), lax.axis_size("vocab")
    return [
        (step // 2 - 1, lax.rem(here + step, size), lax.rem(here + size - step, size))
        for step in range(2, size, 2)
    ]


def basis_kernel(x_ref, out_ref, s0, r0, s1, r1):
    here = lax.axis_index("vocab")
    near, side = flip(here, 1), lax.rem(here, 2)
    others = far_replicas()
    greet(*[("vocab", to) for _, to, _ in others], ("vocab", near))
    rows = x_ref.shape[0] // 2
    half = pl.ds(pl.multiple_of(side * rows, rows), rows)
    copies = [
        push(x_ref.at[half], out_ref.at[here // 2, half], (s0, r0), slot, "vocab", to)
        for slot, to, _ in others
    ]
    out_ref[here // 2] = x_ref[...]
    close = []
    for copy, (slot, _, origin) in zip(copies, others):
        copy.wait()
        place = out_ref.at[origin // 2, half]
        close.append(push(place, place, (s1, r1), slot, "vocab", near))
    for copy in close:
        copy.wait()


def gather_basis(x, collective_id):
    pairs = lax.axis_size("vocab") // 2
    out = jax.ShapeDtypeStruct((pairs, *x.shape), x.dtype)
    sems = sem_pair(pairs - 1) + sem_pair(pairs - 1)
    return talk(basis_kernel, out, collective_id, x, scratch=sems)


def gradient_kernel(x_ref, out_ref, parts_ref, s0, r0, s1, r1, s2, r2):
    owners = peers_of("dp")
    here, me = lax.axis_index("vocab"), lax.axis_index("dp")
    near = flip(here, 1)
    size = lax.axis_size("vocab")
    steps = range(2, size, 2)
    chunks = x_ref.shape[1]
    greet(
        *[("dp", to) for _, to, _ in owners],
        *[("vocab", lax.rem(here + step, size)) for step in steps],
        ("vocab", near),
    )

    def spread(c, origin, sems, slot, to):
        place = out_ref.at[origin, c]
        return push(place, place, sems, slot, "vocab", to)

    arriving = [
        [
            push(x_ref.at[to, c], parts_ref.at[me, c], (s0, r0), (step - 1) * chunks + c, "dp", to)
            for step, to, _ in owners
        ]
        for c in range(chunks)
    ]
    far, close = [], []
    for c in range(chunks):
        parts_ref[me, c] = x_ref[me, c]
        for copy in arriving[c]:
            copy.wait()
        total = jnp.sum(parts_ref[:, c].astype(jnp.float32), axis=0)
        out_ref[here, c] = total.astype(out_ref.dtype)
        far.append(
            [
                spread(c, here, (s1, r1), k * chunks + c, lax.rem(here + step, size))
                for k, step in enumerate(steps)
            ]
        )
        close.append(spread(c, here, (s2, r2), c, near))
    for c in range(chunks):
        for k, step in enumerate(steps):
            far[c][k].wait()
            origin = lax.rem(here + size - step, size)
            close.append(spread(c, origin, (s2, r2), (k + 1) * chunks + c, near))
    for copy in close:
        copy.wait()


def share_gradients(x, collective_id):
    owners, replicas = lax.axis_size("dp"), lax.axis_size("vocab")
    chunks = x.shape[1]
    others = (replicas // 2 - 1) * chunks
    return talk(
        gradient_kernel,
        jax.ShapeDtypeStruct((replicas, *x.shape[1:]), x.dtype),
        collective_id,
        x,
        scratch=[pltpu.VMEM(x.shape, x.dtype)]
        + sem_pair((owners - 1) * chunks)
        + sem_pair(others)
        + sem_pair(others + chunks),
    )


def swap_kernel(x_ref, out_ref, s0, r0, s1, r1):
    others = peers_of("dp")
    me, here = lax.axis_index("dp"), lax.axis_index("vocab")
    near, side = flip(here, 1), lax.rem(here, 2)
    greet(*[("dp", to) for _, to, _ in others], ("vocab", near))
    rows = x_ref.shape[1] // 2
    half = pl.ds(pl.multiple_of(side * rows, rows), rows)
    copies = [
        push(x_ref.at[to, half], out_ref.at[me, half], (s0, r0), step - 1, "dp", to)
        for step, to, _ in others
    ]
    out_ref[me] = x_ref[me]
    close = []
    for copy, (step, _, origin) in zip(copies, others):
        copy.wait()
        place = out_ref.at[origin, half]
        close.append(push(place, place, (s1, r1), step - 1, "vocab", near))
    for copy in close:
        copy.wait()


def swap_owners(x, collective_id):
    owners = lax.axis_size("dp")
    return talk(
        swap_kernel,
        jax.ShapeDtypeStruct(x.shape, x.dtype),
        collective_id,
        x,
        scratch=sem_pair(owners - 1) + sem_pair(owners - 1),
    )


def token_kernel(
    scale, x_ref, place_ref, out_ref, near_ref, parts_ref, blocks_ref, row_ref,
    s0, r0, s1, r1, s2, r2, s3, r3, s4, r4,
):
    owners, others = peers_of("dp"), far_replicas()
    me, here = lax.axis_index("dp"), lax.axis_index("vocab")
    near, side = flip(here, 1), lax.rem(here, 2)
    greet(
        *[("dp", to) for _, to, _ in owners], *[("vocab", to) for _, to, _ in others], ("vocab", near)
    )
    count, length, columns = x_ref.shape
    half, pairs = length // 2, lax.axis_size("vocab") // 2
    share = half // pairs

    def half_of(which):
        return pl.ds(pl.multiple_of(which * half, half), half)

    def share_of(index):
        return pl.ds(pl.multiple_of(index // 2 * share, share), share)

    def place_of(index):
        return pl.ds(pl.multiple_of(side * half + index // 2 * share, share), share)

    first = push(x_ref.at[:, half_of(1 - side)], near_ref, (s0, r0), 0, "vocab", near)
    first.wait()
    near_ref[...] += x_ref[:, half_of(side)]
    copies = [
        push(near_ref.at[:, share_of(to)], parts_ref.at[slot], (s1, r1), slot, "vocab", to)
        for slot, to, _ in others
    ]
    for copy in copies:
        copy.wait()
    total = near_ref[:, share_of(here)]
    for slot, _, _ in others:
        total = total + parts_ref[slot]
    blocks_ref[...] = total
    copies = [
        push(
            blocks_ref.at[to],
            row_ref.at[me, place_of(here)],
            (s2, r2),
            step - 1,
            "dp",
            to,
        )
        for step, to, _ in owners
    ]
    row_ref[me, place_of(here)] = blocks_ref[me]
    for copy in copies:
        copy.wait()
    mine = row_ref.at[:, place_of(here)]
    copies = [push(mine, mine, (s3, r3), slot, "vocab", to) for slot, to, _ in others]
    close = [push(mine, mine, (s4, r4), 0, "vocab", near)]
    for copy, (slot, _, origin) in zip(copies, others):
        copy.wait()
        theirs = row_ref.at[:, place_of(origin)]
        close.append(push(theirs, theirs, (s4, r4), slot + 1, "vocab", near))
    for copy in close:
        copy.wait()
    for owner in range(count):
        band = slice(owner * columns, (owner + 1) * columns)
        out_ref[:, band] = row_ref[owner].astype(jnp.float32) * scale + place_ref[:, band]


def gather_tokens(x, places, scale, collective_id):
    owners, pairs = lax.axis_size("dp"), lax.axis_size("vocab") // 2
    _, length, columns = x.shape
    half = length // 2
    return talk(
        partial(token_kernel, scale),
        full(length, owners * columns),
        collective_id,
        x,
        places,
        scratch=[
            pltpu.VMEM((owners, half, columns), x.dtype),
            pltpu.VMEM((pairs - 1, owners, half // pairs, columns), x.dtype),
            pltpu.VMEM((owners, half // pairs, columns), x.dtype),
            pltpu.VMEM((owners, length, columns), x.dtype),
        ]
        + sem_pair(1)
        + sem_pair(pairs - 1)
        + sem_pair(owners - 1)
        + sem_pair(pairs - 1)
        + sem_pair(pairs),
    )


def sinusoid(length, model_width):
    places = np.arange(length, dtype=np.float32)[:, None]
    halves = np.arange(model_width // 2, dtype=np.float32)[None, :]
    angles = places * np.exp(halves * np.float32(-2.0 * math.log(10000.0) / model_width))
    angles = angles.astype(np.float64)
    return (
        np.stack([np.sin(angles), np.cos(angles)], axis=-1)
        .reshape(length, model_width)
        .astype(np.float32)
    )


def one_hot(ids, columns):
    return (ids[:, None] == columns[None, :]).astype(jnp.bfloat16)


def pick_weights(target_seg, pick_rows):
    sentence = jnp.take(target_seg, pick_rows, axis=0)
    return jnp.sum((sentence[:, None] == sentence[None, :]).astype(jnp.float32), axis=1)


def combine_stats(tops, totals, chosen):
    top = jnp.max(tops, axis=0)
    return top, jnp.sum(totals * jnp.exp(tops - top), axis=0), jnp.sum(chosen, axis=0)


def adam_direction(moment, second):
    return moment / (1.0 - beta_one**STEP) / (jnp.sqrt(second / (1.0 - beta_two**STEP)) + adam_eps)


def adam_update(weight, grad_item, moment, second, step_rate, decay_weight):
    moment = beta_one * moment + (1.0 - beta_one) * grad_item
    second = beta_two * second + (1.0 - beta_two) * grad_item * grad_item
    return (
        weight - step_rate * (adam_direction(moment, second) + decay_weight * weight),
        moment,
        second,
    )


def rotate(values, basis):
    high = basis.astype(jnp.bfloat16)
    rest = (basis - high.astype(jnp.float32)).astype(jnp.bfloat16)

    def product(part):
        return jnp.einsum("mfd,mde->mfe", values, part, preferred_element_type=jnp.float32)

    return product(high) + product(rest)


def share_rows(array, owners, shares, share):
    rows, columns = array.shape
    blocks = array.reshape(owners, shares, rows // (owners * shares), columns)
    return lax.dynamic_index_in_dim(blocks, share, 1, keepdims=False)


def body(
    src_ids,
    src_seg,
    tgt_ids,
    tgt_seg,
    pick_pos,
    pick_label,
    attn_w,
    attn_m,
    attn_v,
    ffn_w,
    ffn_m,
    ffn_v,
    soap_basis,
    soap_stats,
    norm_p,
    norm_m,
    norm_v,
    embedding,
    embed_m,
    embed_v,
):
    owners, replicas = lax.axis_size("dp"), lax.axis_size("vocab")
    replica = lax.axis_index("vocab")
    own_table = embedding.astype(jnp.bfloat16)
    own_norms = jnp.pad(norm_p.astype(jnp.bfloat16).astype(jnp.float32), ((0, 2), (0, 0)))
    all_ids, norm_rows = gather_small("dp", 1, jnp.concatenate([src_ids, tgt_ids]), own_norms)
    norm_rows = jnp.swapaxes(norm_rows, 0, 1).reshape(16, -1)
    w_attn = [None] * 3
    w_ffn = [None] * 2
    w_attn[0], ready = gather_weights(attn_w[0:4].astype(jnp.bfloat16), None)
    w_ffn[0], ready = gather_weights(ffn_w[0:2].astype(jnp.bfloat16), ready)
    w_attn[1], ready = gather_weights(attn_w[4:8].astype(jnp.bfloat16), ready)
    w_attn[2], ready = gather_weights(attn_w[8:12].astype(jnp.bfloat16), ready)
    w_ffn[1], ready = gather_weights(ffn_w[2:4].astype(jnp.bfloat16), ready)
    late_table, _ = lax.optimization_barrier((own_table, ready))
    table_low = lax.all_gather(late_table, "dp", axis=1, tiled=True)
    norms = [jnp.stack([norm_rows[k], norm_rows[7 + k]]) for k in range(7)]
    vocab_count, width = table_low.shape
    columns = replica * vocab_count + jnp.arange(vocab_count)
    source, source_seg, target, target_seg = (src_ids[0], src_seg[0], tgt_ids[0], tgt_seg[0])
    pick_rows, labels = (pick_pos[0], pick_label[0])
    length = source.shape[0]
    embed_scale = math.sqrt(width)
    halves = replica * (vocab_count // 2) + jnp.arange(vocab_count // 2)
    paired = own_table.reshape(vocab_count // 2, -1)

    def look_up(ids):
        wide = lax.dot_general(one_hot(ids // 2, halves), paired, (((1,), (0,)), ((), ())))
        left, right = jnp.split(wide, 2, axis=1)
        return jnp.where((ids % 2 == 0)[:, None], left, right)

    source_part, target_part = (look_up(all_ids[:, k].reshape(-1)) for k in (0, 1))
    target_sum = lax.psum(target_part, "vocab")
    positional = sinusoid(length, width)
    source_part = source_part.reshape(owners, length, -1)
    enc_in = gather_tokens(source_part, positional, embed_scale, 2)
    enc_mid, enc_attn = attn_forward(
        enc_in, norms[0], w_attn[0], source_seg, source_seg, None, False
    )
    enc_out, encoded, enc_ffn = ffn_forward(enc_mid, norms[1], norms[2], w_ffn[0])
    target_rows = swap_owners(target_sum.reshape(owners, length, -1), 3)
    target_rows = jnp.swapaxes(target_rows, 0, 1).reshape(length, -1).astype(jnp.float32)
    dec_in = target_rows * embed_scale + positional
    dec_mid, dec_self = attn_forward(
        dec_in, norms[3], w_attn[1], target_seg, target_seg, None, True
    )
    dec_late, dec_cross = attn_forward(
        dec_mid, norms[4], w_attn[2], target_seg, source_seg, encoded, False
    )
    dec_out, final_low, dec_ffn = ffn_forward(dec_late, norms[5], norms[6], w_ffn[1])

    chosen_rows = one_hot(pick_rows, jnp.arange(length))
    picked = dot_dims(chosen_rows, final_low, 1, 0).astype(jnp.bfloat16)
    logits = dot_dims(picked, table_low, 1, 1)
    row_top = jnp.max(logits, axis=-1)
    row_total = jnp.sum(jnp.exp(logits - row_top[:, None]), axis=-1)
    label_hit = labels[:, None] == columns[None, :]
    chosen = jnp.sum(jnp.where(label_hit, logits, 0.0), axis=-1)
    seen = jnp.pad(jnp.stack([row_top, row_total, chosen]), ((0, 5), (0, 0)))
    (seen,) = gather_small("vocab", 4, seen)
    row_top, row_total, chosen = combine_stats(seen[:, 0], seen[:, 1], seen[:, 2])
    log_total = row_top + jnp.log(row_total)
    weight = 1.0 / pick_weights(target_seg, pick_rows)
    loss_part = jnp.sum((log_total - chosen) * weight)
    count_part = (target_seg[-1] + 1).astype(jnp.float32)
    grad_logits = (
        weight[:, None] * (jnp.exp(logits - log_total[:, None]) - label_hit.astype(jnp.float32))
    ).astype(jnp.bfloat16)
    grad_picked = sum_vocab(dot_dims(grad_logits, table_low, 1, 0).astype(jnp.bfloat16), 5)
    grad_table = lax.psum_scatter(
        dot_dims(grad_logits, picked, 0, 0).astype(jnp.bfloat16),
        "dp",
        scatter_dimension=1,
        tiled=True,
    )
    grad_final = dot_dims(chosen_rows, grad_picked, 0, 0)

    norm_grads = [None] * 7
    grad, norm_grads[6] = plain_norm_backward(grad_final, dec_out, norms[6])
    grad, norm_grads[5], dec_ffn_parts = ffn_backward(grad, dec_ffn)
    grad, norm_grads[4], cross_parts, grad_encoded = attn_backward(grad, dec_cross)
    grad, norm_grads[3], self_parts, _ = attn_backward(grad, dec_self)
    grad_target = (grad * embed_scale).astype(jnp.bfloat16)
    grad, norm_grads[2] = plain_norm_backward(grad_encoded, enc_out, norms[2])
    grad, norm_grads[1], enc_ffn_parts = ffn_backward(grad, enc_ffn)
    grad, norm_grads[0], enc_parts, _ = attn_backward(grad, enc_attn)
    grad_source = (grad * embed_scale).astype(jnp.bfloat16)
    token_grads = jnp.concatenate([grad_source, grad_target]).reshape(2 * length, owners, -1)
    token_grads = swap_owners(jnp.swapaxes(token_grads, 0, 1), 6).reshape(owners * 2 * length, -1)
    flat_ids = all_ids.reshape(-1)
    even = (flat_ids % 2 == 0)[:, None]
    token_grads = jnp.concatenate(
        [jnp.where(even, token_grads, 0), jnp.where(even, 0, token_grads)], axis=1
    )
    g_embed = grad_table.astype(jnp.float32) + dot_dims(
        one_hot(flat_ids // 2, halves), token_grads, 0, 0
    ).reshape(vocab_count, -1)

    chosen_columns = share_rows(jnp.eye(width, dtype=jnp.bfloat16), owners, replicas, replica)
    chosen_columns = chosen_columns.reshape(-1, width)

    def weight_grads(stored, parts):
        normed, kept, cross = stored[7], stored[8], stored[6]
        grad_low, gq, gk, gv = parts
        key_in = encoded if cross else normed
        share = [dot_dims(chosen_columns, rows, 1, 1).astype(jnp.bfloat16) for rows in (normed, key_in)]
        mixed = share_rows(kept[3], owners, replicas, replica).reshape(-1, length)
        return [
            dot_dims(share[0], gq, 1, 0),
            dot_dims(share[1], gk, 1, 0),
            dot_dims(share[1], gv, 1, 0),
            dot_dims(mixed, grad_low, 1, 0),
        ]

    def hidden_grads(stored, parts):
        grad_low, values, grads = parts
        return [
            dot_dims(share_rows(rows, owners, replicas, replica).reshape(-1, length), right, 1, 0)
            for rows, right in ((grads, stored[3]), (values, grad_low))
        ]

    pieces = (
        weight_grads(enc_attn, enc_parts)
        + weight_grads(dec_self, self_parts)
        + weight_grads(dec_cross, cross_parts)
        + hidden_grads(enc_ffn, enc_ffn_parts)
        + hidden_grads(dec_ffn, dec_ffn_parts)
    )
    blocks = [piece.astype(jnp.bfloat16).reshape(owners, -1, width) for piece in pieces]
    blocks = [jnp.concatenate(blocks[k : k + 4], axis=1) for k in (0, 4, 8)] + blocks[12:]
    shared = share_gradients(jnp.stack(blocks, axis=1), 7)
    g_attn = shared[:, :3].reshape(replicas, 12, -1, width)
    g_attn = jnp.swapaxes(g_attn, 0, 1).reshape(12, -1, width).astype(jnp.float32)
    g_ffn = jnp.swapaxes(shared[:, 3:], 0, 1).reshape(4, -1, width)
    norm_grad = jnp.stack(norm_grads)
    norm_grad = jnp.concatenate([norm_grad[:, 0], norm_grad[:, 1]], axis=0)
    g_norm = lax.psum_scatter(norm_grad, "dp", scatter_dimension=1, tiled=True)

    matrix = replica // 2
    own_grad = lax.dynamic_index_in_dim(g_ffn, matrix, 0, keepdims=False)
    own_products = dot_dims(own_grad, own_grad, 0, 0)
    g_ffn_low, g_ffn = g_ffn, g_ffn.astype(jnp.float32)
    first_copy = (replica == 0).astype(jnp.float32)
    layer_sq = jnp.sum(g_attn * g_attn) + jnp.sum(g_ffn * g_ffn) + jnp.sum(g_norm * g_norm)
    raw_squares = jnp.sum(g_embed * g_embed) + first_copy * layer_sq
    few = jnp.stack([first_copy * loss_part, first_copy * count_part, raw_squares])
    few = jnp.broadcast_to(jnp.pad(few, (0, 5))[:, None], (8, 128))
    own_products, few = sum_tail(own_products, few, 8)
    loss_sum, sentences, squares = few[0, 0], few[1, 0], few[2, 0]
    grad_norm = jnp.sqrt(squares) / sentences
    factor = jnp.minimum(1.0, clip_limit / (grad_norm + norm_eps)) / sentences
    g_attn, g_norm, g_embed = (
        g_attn * factor,
        g_norm * factor,
        g_embed * factor,
    )
    all_products = lax.all_gather(own_products.astype(jnp.bfloat16), "vocab")[::2]
    new_stats = stat_decay * soap_stats + (1.0 - stat_decay) * (factor * factor) * (
        all_products.astype(jnp.float32)
    )
    own_stat = stat_decay * lax.dynamic_index_in_dim(soap_stats, matrix, 0, keepdims=False) + (
        1.0 - stat_decay
    ) * (factor * factor) * own_products
    own_basis = renew_basis(own_stat, lax.dynamic_index_in_dim(soap_basis, matrix, 0, keepdims=False))
    new_basis = gather_basis(own_basis.astype(jnp.bfloat16), 9).astype(jnp.float32)

    new_attn, m_attn, v_attn = adam_update(attn_w, g_attn, attn_m, attn_v, rate_matrix, decay_rate)
    new_norm, m_norm, v_norm = adam_update(norm_p, g_norm, norm_m, norm_v, rate_vector, 0.0)
    new_embed, m_embed, v_embed = adam_update(
        embedding, g_embed, embed_m, embed_v, rate_matrix, decay_rate
    )
    rotated = factor * rotate(g_ffn_low, soap_basis)
    m_ffn = beta_one * ffn_m + (1.0 - beta_one) * rotated
    v_ffn = beta_two * ffn_v + (1.0 - beta_two) * rotated * rotated
    back_rotated = jnp.einsum(
        "mfe,mde->mfd", adam_direction(m_ffn, v_ffn), soap_basis, precision=lax.Precision.HIGH
    )
    new_ffn = ffn_w - rate_matrix * (back_rotated + decay_rate * ffn_w)
    return (
        loss_sum,
        sentences,
        grad_norm,
        new_attn,
        m_attn,
        v_attn,
        new_ffn,
        m_ffn,
        v_ffn,
        new_basis,
        new_stats,
        new_norm,
        m_norm,
        v_norm,
        new_embed,
        m_embed,
        v_embed,
    )


def solution(mesh):
    placed = (
        P("dp", None),
        P("dp", None),
        P("dp", None),
        P("dp", None),
        P("dp", None),
        P("dp", None),
        P(None, "dp", None),
        P(None, "dp", None),
        P(None, "dp", None),
        P(None, "dp", None),
        P(None, "dp", None),
        P(None, "dp", None),
        P(),
        P(),
        P(None, "dp"),
        P(None, "dp"),
        P(None, "dp"),
        P("vocab", "dp"),
        P("vocab", "dp"),
        P("vocab", "dp"),
    )
    return jax.shard_map(
        body,
        mesh=mesh,
        in_specs=placed,
        out_specs=(
            P(),
            P(),
            P(),
            P(None, "dp", None),
            P(None, "dp", None),
            P(None, "dp", None),
            P(None, "dp", None),
            P(None, "dp", None),
            P(None, "dp", None),
            P(),
            P(),
            P(None, "dp"),
            P(None, "dp"),
            P(None, "dp"),
            P("vocab", "dp"),
            P("vocab", "dp"),
            P("vocab", "dp"),
        ),
        check_vma=False,
    )
```

```python
from functools import partial
import math

import jax
import jax.numpy as jnp
import numpy as np
from jax import lax
from jax.experimental import pallas as pl
from jax.experimental.pallas import tpu as pltpu
from jax.sharding import PartitionSpec as P

HEADS = 8
STEP = 10
TILE = 128

highest = lax.Precision.HIGHEST
beta_one = 0.9
beta_two = 0.999
adam_eps = 1e-08
decay_rate = 0.01
rate_matrix = 0.03
rate_vector = 0.3
clip_limit = 1.0
stat_decay = 0.95
norm_eps = 1e-06
masked = -1e30
log_two_e = math.log2(math.e)
vmem = pl.BlockSpec(memory_space=pltpu.VMEM)
smem = pl.BlockSpec(memory_space=pltpu.SMEM)
mesh_ids = pl.DeviceIdType.MESH


def dot_dims(left, right, left_dim, right_dim):
    return lax.dot_general(
        left, right, (((left_dim,), (right_dim,)), ((), ())), preferred_element_type=jnp.float32
    )


def dot_exact(left, right, left_dim, right_dim):
    return lax.dot_general(
        left,
        right,
        (((left_dim,), (right_dim,)), ((), ())),
        precision=highest,
        preferred_element_type=jnp.float32,
    )


def call(kernel, outs, *args, scratch=(), smem_args=0):
    return pl.pallas_call(
        kernel,
        out_shape=outs,
        in_specs=[vmem] * (len(args) - smem_args) + [smem] * smem_args,
        out_specs=jax.tree.map(lambda _: vmem, outs),
        scratch_shapes=list(scratch),
        compiler_params=pltpu.CompilerParams(vmem_limit_bytes=56 * 2**20),
    )(*args)


def low(*shape):
    return jax.ShapeDtypeStruct(shape, jnp.bfloat16)


def full(*shape):
    return jax.ShapeDtypeStruct(shape, jnp.float32)


def norm_parts(values):
    centre = values - jnp.mean(values, axis=-1, keepdims=True)
    spread = jnp.mean(centre * centre, axis=-1, keepdims=True)
    root = lax.rsqrt(spread + norm_eps)
    return centre * root, root


def norm_forward(values, ln_ref):
    return norm_parts(values)[0] * ln_ref[0:1, :] + ln_ref[1:2, :]


def norm_backward(grad, values, ln_ref, ln_grad_ref):
    normed, root = norm_parts(values)
    ln_grad_ref[0:1, :] = jnp.sum(grad * normed, axis=0, keepdims=True)
    ln_grad_ref[1:2, :] = jnp.sum(grad, axis=0, keepdims=True)
    inner = grad * ln_ref[0:1, :]
    return root * (
        inner
        - jnp.mean(inner, axis=-1, keepdims=True)
        - normed * jnp.mean(inner * normed, axis=-1, keepdims=True)
    )


def at_tile(index):
    return pl.ds(pl.multiple_of(index * TILE, TILE), TILE)


def tile_mask(segq_ref, segk_ref, qi, ki, causal):
    allowed = segk_ref[at_tile(ki), :] == segq_ref[:, at_tile(qi)]
    if causal:
        ahead = lax.broadcasted_iota(jnp.int32, (TILE, TILE), 0) - lax.broadcasted_iota(
            jnp.int32, (TILE, TILE), 1
        )
        allowed = allowed & (ahead <= (qi - ki) * TILE)
    return allowed


def for_tiles(count, edge_ref, causal, step):
    def one(pair, carry):
        qi, ki = pair // count, lax.rem(pair, count)
        live = (edge_ref[0, qi] <= edge_ref[3, ki]) & (edge_ref[2, ki] <= edge_ref[1, qi])
        if causal:
            live = live & (ki <= qi)

        @pl.when(live)
        def _():
            step(qi, ki)

        return carry

    lax.fori_loop(0, count * count, one, 0)


def tile_edges(seg_q, seg_k):
    last = TILE - 1
    return jnp.stack([seg_q[::TILE], seg_q[last::TILE], seg_k[::TILE], seg_k[last::TILE]])


def lay_weights(w_ref, piece_refs, part, first):
    own = piece_refs[0]
    matrices, rows = w_ref.shape[0], w_ref.shape[1] // 4
    half = own.shape[0] // 2
    me, side = lax.axis_index("dp"), lax.rem(lax.axis_index("vocab"), 2)
    for m in range(matrices):
        span = slice(first + m * rows, first + (m + 1) * rows)
        w_ref[m, pl.ds(pl.multiple_of(me * rows, rows), rows), :] = own[
            part * half + span.start : part * half + span.stop, :
        ]
        for k in range(1, 4):
            place = pl.ds(pl.multiple_of((me ^ k) * rows, rows), rows)

            @pl.when(side == part)
            def _():
                w_ref[m, place, :] = piece_refs[k][span, :]

            @pl.when(side != part)
            def _():
                w_ref[m, place, :] = piece_refs[k + 3][span, :]


def flip_sites(part, axis, bit):
    return lax.ppermute(part, axis, [(s, s ^ bit) for s in range(lax.axis_size(axis))])


def late_weights(attn, ffn, after, later):
    owners = lax.axis_size("dp")
    width = attn.shape[-1]
    attn, ffn = attn.astype(jnp.bfloat16), ffn.astype(jnp.bfloat16)
    if owners != 4:
        attn, ffn = (lax.all_gather(part, "dp", axis=1, tiled=True) for part in (attn, ffn))
        return ((attn[:4],), 0, 0), ((attn[4:],), 0, 0), ((ffn,), 0, 0), ffn[0, 0]
    halves = [
        jnp.concatenate([attn[4 * k : 4 * k + 4].reshape(-1, width), ffn[k]]) for k in range(2)
    ]
    own = jnp.concatenate(halves)
    side = lax.axis_index("vocab") % 2
    mine = jnp.where(side == 0, halves[0], halves[1])
    mine, _ = lax.optimization_barrier((mine, after))
    got = [flip_sites(mine, "dp", k) for k in range(1, 4)]
    *got, _ = lax.optimization_barrier((*got, later))
    swapped = [flip_sites(part, "vocab", 1) for part in got]
    pieces = (own, *got, *swapped)
    rows = 4 * attn.shape[1]
    return (pieces, 0, 0), (pieces, 1, 0), (pieces, None, rows), swapped[-1][0]


def attn_forward_kernel(causal, cross, pieces, part, first, *refs):
    refs = list(refs)
    x_ref, ln_ref, segq_ref, segk_ref = refs[:4]
    refs = refs[4:]
    key_ref = refs.pop(0) if cross else None
    piece_refs, refs = refs[:pieces], refs[pieces:]
    edge_ref, out_ref, a_ref, qt_ref, kt_ref, vt_ref, ot_ref, lse_ref = refs[:8]
    refs = refs[8:]
    w_ref = piece_refs[0]
    if pieces > 1:
        w_ref = refs.pop(0)
        lay_weights(w_ref, piece_refs, part, first)
    top_ref, sum_ref, acc_ref = refs
    length, width = x_ref.shape
    head_size = width // HEADS
    a_ref[...] = norm_forward(x_ref[...], ln_ref).astype(jnp.bfloat16)
    key_in = key_ref if cross else a_ref
    qt_ref[...] = dot_dims(a_ref[...], w_ref[0], 1, 0).astype(jnp.bfloat16).T
    kt_ref[...] = dot_dims(key_in[...], w_ref[1], 1, 0).astype(jnp.bfloat16).T
    vt_ref[...] = dot_dims(key_in[...], w_ref[2], 1, 0).astype(jnp.bfloat16).T
    top_ref[...] = jnp.full(top_ref.shape, masked, jnp.float32)
    sum_ref[...] = jnp.zeros(sum_ref.shape, jnp.float32)
    acc_ref[...] = jnp.zeros(acc_ref.shape, jnp.float32)
    scale = log_two_e / math.sqrt(head_size)
    bands = [slice(h * head_size, (h + 1) * head_size) for h in range(HEADS)]

    def step(qi, ki):
        q_at, k_at = at_tile(qi), at_tile(ki)
        allowed = tile_mask(segq_ref, segk_ref, qi, ki, causal)
        scores = [dot_dims(kt_ref[band, k_at], qt_ref[band, q_at], 0, 0) * scale for band in bands]
        scores = [jnp.where(allowed, part, masked) for part in scores]
        top = top_ref[:, q_at]
        new_top = jnp.maximum(
            top,
            jnp.concatenate([jnp.max(part, axis=0, keepdims=True) for part in scores], axis=0),
        )
        fade = jnp.exp2(top - new_top)
        parts = [jnp.exp2(scores[h] - new_top[h : h + 1]) for h in range(HEADS)]
        top_ref[:, q_at] = new_top
        sum_ref[:, q_at] = sum_ref[:, q_at] * fade + jnp.concatenate(
            [jnp.sum(part, axis=0, keepdims=True) for part in parts], axis=0
        )
        mixed = [
            dot_dims(vt_ref[bands[h], k_at], parts[h].astype(jnp.bfloat16), 1, 0)
            for h in range(HEADS)
        ]
        acc = acc_ref[:, q_at]
        acc_ref[:, q_at] = jnp.concatenate(
            [acc[bands[h]] * fade[h : h + 1] + mixed[h] for h in range(HEADS)], axis=0
        )

    for_tiles(length // TILE, edge_ref, causal, step)
    lse_ref[...] = top_ref[...] + jnp.log2(sum_ref[...])
    for h in range(HEADS):
        ot_ref[bands[h], :] = (acc_ref[bands[h], :] / sum_ref[h : h + 1, :]).astype(jnp.bfloat16)
    out_ref[...] = x_ref[...] + dot_dims(ot_ref[...], w_ref[3], 0, 0)


def attn_forward(x, ln, weights, seg_q, seg_k, key_in, causal):
    length, width = x.shape
    weights, part, first = weights
    cross = key_in is not None
    segs = (seg_q[None, :], jnp.broadcast_to(seg_k[:, None], (length, TILE)))
    edges = tile_edges(seg_q, seg_k)
    args = (x, ln, *segs) + ((key_in,) if cross else ()) + (*weights, edges)
    outs = (full(length, width), low(length, width)) + (low(width, length),) * 4
    outs = outs + (full(HEADS, length),)
    if len(weights) > 1:
        outs = outs + (low(4, width, width),)
    out, normed, *stored = call(
        partial(attn_forward_kernel, causal, cross, len(weights), part, first),
        outs,
        *args,
        scratch=[
            pltpu.VMEM((HEADS, length), jnp.float32),
            pltpu.VMEM((HEADS, length), jnp.float32),
            pltpu.VMEM((width, length), jnp.float32),
        ],
        smem_args=1,
    )
    whole = stored.pop() if len(weights) > 1 else weights[0]
    return out, (x, ln, whole, segs, edges, causal, cross, normed, stored)


def attn_backward_kernel(causal, cross, *refs):
    (g_ref, x_ref, ln_ref, w_ref, segq_ref, segk_ref, qt_ref, kt_ref, vt_ref, ot_ref, lse_ref) = refs[:11]
    refs = list(refs[11:])
    edge_ref, out_ref, ln_grad_ref, low_ref, gq_ref, gk_ref, gv_ref = refs[:7]
    refs = refs[7:]
    key_grad_ref = refs.pop(0) if cross else None
    got_ref, delta_ref, gqt_ref, gkt_ref, gvt_ref = refs
    length, width = x_ref.shape
    head_size = width // HEADS
    low_ref[...] = g_ref[...].astype(jnp.bfloat16)
    got_ref[...] = dot_dims(low_ref[...], w_ref[3], 1, 1).astype(jnp.bfloat16).T
    bands = [slice(h * head_size, (h + 1) * head_size) for h in range(HEADS)]
    for h in range(HEADS):
        delta_ref[h : h + 1, :] = jnp.sum(
            got_ref[bands[h], :].astype(jnp.float32) * ot_ref[bands[h], :].astype(jnp.float32),
            axis=0,
            keepdims=True,
        )
    for ref in (gqt_ref, gkt_ref, gvt_ref):
        ref[...] = jnp.zeros(ref.shape, jnp.float32)
    scale = log_two_e / math.sqrt(head_size)
    back = 1.0 / math.sqrt(head_size)

    def step(qi, ki):
        q_at, k_at = at_tile(qi), at_tile(ki)
        allowed = tile_mask(segq_ref, segk_ref, qi, ki, causal)
        scores = [dot_dims(kt_ref[band, k_at], qt_ref[band, q_at], 0, 0) for band in bands]
        grads = [dot_dims(vt_ref[band, k_at], got_ref[band, q_at], 0, 0) for band in bands]
        parts = [
            jnp.where(allowed, jnp.exp2(scores[h] * scale - lse_ref[h : h + 1, q_at]), 0.0)
            for h in range(HEADS)
        ]
        grads = [parts[h] * (grads[h] - delta_ref[h : h + 1, q_at]) for h in range(HEADS)]
        parts_t = [part.T.astype(jnp.bfloat16) for part in parts]
        grads_t = [part.T.astype(jnp.bfloat16) for part in grads]
        grads = [part.astype(jnp.bfloat16) for part in grads]
        for ref, place, terms in (
            (gvt_ref, k_at, [dot_dims(got_ref[bands[h], q_at], parts_t[h], 1, 0) for h in range(HEADS)]),
            (gkt_ref, k_at, [dot_dims(qt_ref[bands[h], q_at], grads_t[h], 1, 0) for h in range(HEADS)]),
            (gqt_ref, q_at, [dot_dims(kt_ref[bands[h], k_at], grads[h], 1, 0) for h in range(HEADS)]),
        ):
            ref[:, place] += jnp.concatenate(terms, axis=0)

    for_tiles(length // TILE, edge_ref, causal, step)
    gq_ref[...] = (gqt_ref[...] * back).astype(jnp.bfloat16).T
    gk_ref[...] = (gkt_ref[...] * back).astype(jnp.bfloat16).T
    gv_ref[...] = gvt_ref[...].astype(jnp.bfloat16).T
    from_query = dot_dims(gq_ref[...], w_ref[0], 1, 1)
    from_keys = dot_dims(gk_ref[...], w_ref[1], 1, 1) + dot_dims(gv_ref[...], w_ref[2], 1, 1)
    if cross:
        key_grad_ref[...] = from_keys
    else:
        from_query = from_query + from_keys
    out_ref[...] = g_ref[...] + norm_backward(from_query, x_ref[...], ln_ref, ln_grad_ref)


def attn_backward(grad, stored):
    x, ln, weights, segs, edges, causal, cross, _, kept = stored
    length, width = x.shape
    outs = (full(length, width), full(2, width)) + (low(length, width),) * 4
    if cross:
        outs = outs + (full(length, width),)
    out, ln_grad, *rest = call(
        partial(attn_backward_kernel, causal, cross),
        outs,
        grad,
        x,
        ln,
        weights,
        *segs,
        *kept,
        edges,
        scratch=[pltpu.VMEM((width, length), jnp.bfloat16), pltpu.VMEM((HEADS, length), jnp.float32)]
        + [pltpu.VMEM((width, length), jnp.float32)] * 3,
        smem_args=1,
    )
    return out, ln_grad, rest[:4], rest[4] if cross else None


def gelu_parts(hidden):
    root = math.sqrt(2.0 / math.pi)
    square = hidden * hidden
    bend = jnp.tanh(root * hidden * (1.0 + 0.044715 * square))
    value = 0.5 * hidden * (1.0 + bend)
    slope = 0.5 * (1.0 + bend) + 0.5 * hidden * (1.0 - bend * bend) * root * (
        1.0 + 3.0 * 0.044715 * square
    )
    return value, slope


def ffn_forward_kernel(chunk, pieces, first, x_ref, ln_ref, next_ref, *refs):
    piece_refs, (out_ref, a_ref, after_ref, *refs) = refs[:pieces], refs[pieces:]
    w_ref = piece_refs[0]
    if pieces > 1:
        (w_ref,) = refs
        for part in range(2):
            lay_weights(w_ref.at[part : part + 1], piece_refs, part, first)
    w_in_ref, w_out_ref = w_ref.at[0], w_ref.at[1]
    a_ref[...] = norm_forward(x_ref[...], ln_ref).astype(jnp.bfloat16)
    total = x_ref[...]
    for start in range(0, w_in_ref.shape[0], chunk):
        part = slice(start, start + chunk)
        hidden = dot_dims(a_ref[...], w_in_ref[part, :], 1, 1)
        active = gelu_parts(hidden)[0].astype(jnp.bfloat16)
        total = total + dot_dims(active, w_out_ref[part, :], 1, 0)
    out_ref[...] = total
    after_ref[...] = norm_forward(total, next_ref).astype(after_ref.dtype)


def ffn_forward(x, ln, ln_next, weights):
    length, width = x.shape
    weights, _, first = weights
    outs = (full(length, width), low(length, width), low(length, width))
    if len(weights) > 1:
        outs = outs + (low(2, 4 * (weights[0].shape[0] // 2 - first), width),)
    out, normed, after, *whole = call(
        partial(ffn_forward_kernel, 512, len(weights), first), outs, x, ln, ln_next, *weights
    )
    return out, after, (x, ln, whole[0] if whole else weights[0], normed, out, ln_next)


def ffn_backward_kernel(
    chunk, after_ref, y_ref, next_ref, x_ref, ln_ref, a_ref, w_ref,
    out_ref, next_grad_ref, ln_grad_ref, low_ref, ut_ref, ht_ref, g_ref,
):
    w_in_ref, w_out_ref = w_ref.at[0], w_ref.at[1]
    g_ref[...] = norm_backward(after_ref[...], y_ref[...], next_ref, next_grad_ref)
    low_ref[...] = g_ref[...].astype(jnp.bfloat16)
    total = jnp.zeros(g_ref.shape, jnp.float32)
    for start in range(0, w_in_ref.shape[0], chunk):
        part = slice(start, start + chunk)
        hidden = dot_dims(a_ref[...], w_in_ref[part, :], 1, 1)
        value, slope = gelu_parts(hidden)
        ut_ref[part, :] = value.astype(jnp.bfloat16).T
        grad = (dot_dims(low_ref[...], w_out_ref[part, :], 1, 1) * slope).astype(jnp.bfloat16)
        ht_ref[part, :] = grad.T
        total = total + dot_dims(grad, w_in_ref[part, :], 1, 0)
    out_ref[...] = g_ref[...] + norm_backward(total, x_ref[...], ln_ref, ln_grad_ref)


def ffn_backward(grad_after, stored):
    x, ln, weights, normed, out, ln_next = stored
    length, width = x.shape
    hidden = weights.shape[1]
    outs = (full(length, width), full(2, width), full(2, width))
    outs = outs + (low(length, width), low(hidden, length), low(hidden, length))
    out, next_grad, ln_grad, *rest = call(
        partial(ffn_backward_kernel, 512),
        outs,
        grad_after,
        out,
        ln_next,
        x,
        ln,
        normed,
        weights,
        scratch=[pltpu.VMEM((length, width), jnp.float32)],
    )
    return out, next_grad, ln_grad, rest


def small_factor(block):
    size = block.shape[0]
    eye = (
        lax.broadcasted_iota(jnp.int32, (size, size), 0)
        == lax.broadcasted_iota(jnp.int32, (size, size), 1)
    ).astype(jnp.float32)
    whole = jnp.concatenate([block, eye], axis=1)
    rows = [whole[8 * u : 8 * u + 8] for u in range(size // 8)]
    shape = rows[0].shape
    sub = lax.broadcasted_iota(jnp.int32, shape, 0)

    def lane_splat(value, lane):
        return jnp.broadcast_to(value[:, lane : lane + 1], shape)

    def row_splat(value, row):
        return jnp.broadcast_to(value[row : row + 1, :], shape)

    for g in range(len(rows)):
        first = 8 * g
        lanes = {
            u: [lane_splat(rows[u], first + s) for s in range(8)] for u in range(g, len(rows))
        }
        scale = jnp.zeros(shape, jnp.float32)
        for t in range(8):
            pivot = row_splat(lanes[g][t], t)
            root = lax.rsqrt(pivot)
            inverse = root * root
            scale = jnp.where(sub == t, root, scale)
            row_t = row_splat(rows[g], t) * inverse
            splats = {s: row_splat(lanes[g][s], t) * inverse for s in range(t + 1, 8)}
            for u in range(g, len(rows)):
                factor = lanes[u][t]
                if u == g:
                    factor = jnp.where(sub > t, factor, 0.0)
                rows[u] = rows[u] - factor * row_t
                for s in range(t + 1, 8):
                    lanes[u][s] = lanes[u][s] - factor * splats[s]
        rows[g] = rows[g] * scale
    return jnp.concatenate(rows, axis=0)[:, size:]


def renew_kernel(stat_ref, basis_ref, out_ref, gram_ref, rest_ref):
    size = stat_ref.shape[0]
    product = dot_exact(stat_ref[...], basis_ref[...], 1, 0)
    rest_ref[...] = product
    gram_ref[...] = dot_exact(product, product, 0, 0)
    for low in range(0, size, 128):
        high = low + 128
        block = gram_ref[low:high, low:high]
        corner = small_factor(block[:64, :64])
        across = dot_exact(corner, block[:64, 64:], 1, 0)
        second = small_factor(block[64:, 64:] - dot_exact(across, across, 0, 0))
        below = dot_exact(second, dot_exact(across, corner, 0, 0), 1, 0)
        inverse = jnp.concatenate(
            [
                jnp.concatenate([corner, jnp.zeros_like(corner)], axis=1),
                jnp.concatenate([-below, second], axis=1),
            ],
            axis=0,
        )
        columns = dot_exact(rest_ref[:, low:high], inverse, 1, 1)
        out_ref[:, low:high] = columns
        if high < size:
            panel = dot_exact(inverse, gram_ref[low:high, high:], 1, 0)
            gram_ref[high:, high:] -= dot_exact(panel, panel, 0, 0)
            rest_ref[:, high:] -= dot_exact(columns, panel, 1, 0)


def renew_basis(statistic, basis):
    shape = statistic.shape
    return call(
        renew_kernel,
        full(*shape),
        statistic,
        basis,
        scratch=[pltpu.VMEM(shape, jnp.float32), pltpu.VMEM(shape, jnp.float32)],
    )


def peers_of(axis):
    size, me = lax.axis_size(axis), lax.axis_index(axis)
    return [
        (step, lax.rem(me + step, size), lax.rem(me + size - step, size)) for step in range(1, size)
    ]


def greet(*places):
    barrier = pltpu.get_barrier_semaphore()
    for axis, index in places:
        pl.semaphore_signal(barrier, inc=1, device_id={axis: index}, device_id_type=mesh_ids)
    pl.semaphore_wait(barrier, len(places))


def push(source, target, sems, slot, axis, index):
    copy = pltpu.make_async_remote_copy(
        src_ref=source,
        dst_ref=target,
        send_sem=sems[0].at[slot],
        recv_sem=sems[1].at[slot],
        device_id={axis: index},
        device_id_type=mesh_ids,
    )
    copy.start()
    return copy


def sem_pair(count):
    return [pltpu.SemaphoreType.DMA((count,)), pltpu.SemaphoreType.DMA((count,))]


def talk(kernel, outs, collective_id, *args, scratch=()):
    return pl.pallas_call(
        kernel,
        out_shape=outs,
        in_specs=[vmem] * len(args),
        out_specs=jax.tree.map(lambda _: vmem, outs),
        scratch_shapes=list(scratch),
        compiler_params=pltpu.CompilerParams(
            collective_id=collective_id, has_side_effects=True, vmem_limit_bytes=56 * 2**20
        ),
    )(*args)


def gather_kernel(axis, *refs):
    count = (len(refs) - 2) // 2
    others = peers_of(axis)
    greet(*[(axis, to) for _, to, _ in others])
    me = lax.axis_index(axis)
    copies = [
        push(refs[k], refs[count + k].at[me], refs[-2:], k * len(others) + step - 1, axis, to)
        for k in range(count)
        for step, to, _ in others
    ]
    for k in range(count):
        refs[count + k][me] = refs[k][...]
    for copy in copies:
        copy.wait()


def gather_small(axis, collective_id, *arrays):
    size = lax.axis_size(axis)
    outs = tuple(jax.ShapeDtypeStruct((size, *x.shape), x.dtype) for x in arrays)
    sems = sem_pair((size - 1) * len(arrays))
    return talk(partial(gather_kernel, axis), outs, collective_id, *arrays, scratch=sems)


def sum_kernel(x_ref, out_ref, parts_ref, mine_ref, s0, r0, s1, r1):
    others = peers_of("vocab")
    greet(*[("vocab", to) for _, to, _ in others])
    size, me = lax.axis_size("vocab"), lax.axis_index("vocab")
    rows = mine_ref.shape[0]

    def rows_of(index):
        return pl.ds(pl.multiple_of(index * rows, rows), rows)

    copies = [
        push(x_ref.at[rows_of(to)], parts_ref.at[me], (s0, r0), step - 1, "vocab", to)
        for step, to, _ in others
    ]
    parts_ref[me] = x_ref[rows_of(me), :]
    for copy in copies:
        copy.wait()
    total = parts_ref[0].astype(jnp.float32)
    for index in range(1, size):
        total = total + parts_ref[index].astype(jnp.float32)
    mine_ref[...] = total.astype(mine_ref.dtype)
    copies = [
        push(mine_ref, out_ref.at[rows_of(me)], (s1, r1), step - 1, "vocab", to)
        for step, to, _ in others
    ]
    out_ref[rows_of(me), :] = mine_ref[...]
    for copy in copies:
        copy.wait()


def sum_vocab(x, collective_id):
    replicas = lax.axis_size("vocab")
    rows, columns = x.shape
    share = rows // replicas
    return talk(
        sum_kernel,
        jax.ShapeDtypeStruct(x.shape, x.dtype),
        collective_id,
        x,
        scratch=[
            pltpu.VMEM((replicas, share, columns), x.dtype),
            pltpu.VMEM((share, columns), x.dtype),
        ]
        + sem_pair(replicas - 1)
        + sem_pair(replicas - 1),
    )


def flip(index, bit):
    return index + bit - 2 * bit * lax.rem(index // bit, 2)


def tail_kernel(
    x_ref, few_ref, out_ref, sum_ref, parts_ref, seen_ref, line_ref, lines_ref,
    s0, r0, s1, r1, s2, r2, s3, r3, s4, r4,
):
    owners, replicas = peers_of("dp"), peers_of("vocab")
    greet(*[("dp", to) for _, to, _ in owners], *[("vocab", to) for _, to, _ in replicas])
    size, me, here = lax.axis_size("dp"), lax.axis_index("dp"), lax.axis_index("vocab")
    near, side = flip(here, 1), lax.rem(here, 2)
    rows = parts_ref.shape[1]

    def rows_of(index):
        return pl.ds(pl.multiple_of((side * size + index) * rows, rows), rows)

    few = [
        push(few_ref, seen_ref.at[here], (s2, r2), step - 1, "vocab", to) for step, to, _ in replicas
    ]
    wide = [
        push(x_ref.at[rows_of(to)], parts_ref.at[me], (s0, r0), step - 1, "dp", to)
        for step, to, _ in owners
    ]
    seen_ref[here] = few_ref[...]
    parts_ref[me] = x_ref[rows_of(me), :]
    for copy in few:
        copy.wait()
    line_ref[...] = jnp.sum(seen_ref[...], axis=0)
    few = [
        push(line_ref, lines_ref.at[me], (s3, r3), step - 1, "dp", to) for step, to, _ in owners
    ]
    lines_ref[me] = line_ref[...]
    for copy in wide:
        copy.wait()
    out_ref[rows_of(me), :] = jnp.sum(parts_ref[...], axis=0)
    mine = out_ref.at[rows_of(me)]
    wide = [push(mine, mine, (s1, r1), step - 1, "dp", to) for step, to, _ in owners]
    close = [push(mine, mine, (s4, r4), 0, "vocab", near)]
    for copy in few:
        copy.wait()
    sum_ref[...] = jnp.sum(lines_ref[...], axis=0)
    for copy, (step, _, origin) in zip(wide, owners):
        copy.wait()
        theirs = out_ref.at[rows_of(origin)]
        close.append(push(theirs, theirs, (s4, r4), step, "vocab", near))
    for copy in close:
        copy.wait()


def sum_tail(x, few, collective_id):
    owners, replicas = lax.axis_size("dp"), lax.axis_size("vocab")
    rows, columns = x.shape
    share = rows // (2 * owners)
    return talk(
        tail_kernel,
        (full(*x.shape), full(*few.shape)),
        collective_id,
        x,
        few,
        scratch=[
            pltpu.VMEM((owners, share, columns), jnp.float32),
            pltpu.VMEM((replicas, *few.shape), jnp.float32),
            pltpu.VMEM(few.shape, jnp.float32),
            pltpu.VMEM((owners, *few.shape), jnp.float32),
        ]
        + sem_pair(owners - 1)
        + sem_pair(owners - 1)
        + sem_pair(replicas - 1)
        + sem_pair(owners - 1)
        + sem_pair(owners),
    )


def far_replicas():
    here, size = lax.axis_index("vocab"), lax.axis_size("vocab")
    return [
        (step // 2 - 1, lax.rem(here + step, size), lax.rem(here + size - step, size))
        for step in range(2, size, 2)
    ]


def gradient_kernel(
    x_ref, rows_ref, out_ref, swapped_ref, parts_ref, s0, r0, s1, r1, s2, r2, s3, r3, s4, r4
):
    owners = peers_of("dp")
    here, me = lax.axis_index("vocab"), lax.axis_index("dp")
    near = flip(here, 1)
    size = lax.axis_size("vocab")
    steps = range(2, size, 2)
    chunks = x_ref.shape[1]
    greet(
        *[("dp", to) for _, to, _ in owners],
        *[("vocab", lax.rem(here + step, size)) for step in steps],
        ("vocab", near),
    )

    def spread(c, origin, sems, slot, to):
        place = out_ref.at[origin, c]
        return push(place, place, sems, slot, "vocab", to)

    arriving = [
        [
            push(x_ref.at[to, c], parts_ref.at[me, c], (s0, r0), (step - 1) * chunks + c, "dp", to)
            for step, to, _ in owners
        ]
        for c in range(chunks)
    ]
    half_rows = rows_ref.shape[1] // 2
    half = pl.ds(pl.multiple_of(lax.rem(here, 2) * half_rows, half_rows), half_rows)
    swaps = [
        push(rows_ref.at[to, half], swapped_ref.at[me, half], (s3, r3), step - 1, "dp", to)
        for step, to, _ in owners
    ]
    swapped_ref[me] = rows_ref[me]
    far, close = [], []
    for c in range(chunks):
        parts_ref[me, c] = x_ref[me, c]
        for copy in arriving[c]:
            copy.wait()
        total = jnp.sum(parts_ref[:, c].astype(jnp.float32), axis=0)
        out_ref[here, c] = total.astype(out_ref.dtype)
        far.append(
            [
                spread(c, here, (s1, r1), k * chunks + c, lax.rem(here + step, size))
                for k, step in enumerate(steps)
            ]
        )
        close.append(spread(c, here, (s2, r2), c, near))
    for c in range(chunks):
        for k, step in enumerate(steps):
            far[c][k].wait()
            origin = lax.rem(here + size - step, size)
            close.append(spread(c, origin, (s2, r2), (k + 1) * chunks + c, near))
    for copy, (step, _, origin) in zip(swaps, owners):
        copy.wait()
        place = swapped_ref.at[origin, half]
        close.append(push(place, place, (s4, r4), step - 1, "vocab", near))
    for copy in close:
        copy.wait()


def share_gradients(x, rows, collective_id):
    owners, replicas = lax.axis_size("dp"), lax.axis_size("vocab")
    chunks = x.shape[1]
    others = (replicas // 2 - 1) * chunks
    return talk(
        gradient_kernel,
        (
            jax.ShapeDtypeStruct((replicas, *x.shape[1:]), x.dtype),
            jax.ShapeDtypeStruct(rows.shape, rows.dtype),
        ),
        collective_id,
        x,
        rows,
        scratch=[pltpu.VMEM(x.shape, x.dtype)]
        + sem_pair((owners - 1) * chunks)
        + sem_pair(others)
        + sem_pair(others + chunks)
        + sem_pair(owners - 1)
        + sem_pair(owners - 1),
    )


def swap_kernel(x_ref, out_ref, s0, r0, s1, r1):
    others = peers_of("dp")
    me, here = lax.axis_index("dp"), lax.axis_index("vocab")
    near, side = flip(here, 1), lax.rem(here, 2)
    greet(*[("dp", to) for _, to, _ in others], ("vocab", near))
    rows = x_ref.shape[1] // 2
    half = pl.ds(pl.multiple_of(side * rows, rows), rows)
    copies = [
        push(x_ref.at[to, half], out_ref.at[me, half], (s0, r0), step - 1, "dp", to)
        for step, to, _ in others
    ]
    out_ref[me] = x_ref[me]
    close = []
    for copy, (step, _, origin) in zip(copies, others):
        copy.wait()
        place = out_ref.at[origin, half]
        close.append(push(place, place, (s1, r1), step - 1, "vocab", near))
    for copy in close:
        copy.wait()


def swap_owners(x, collective_id):
    owners = lax.axis_size("dp")
    return talk(
        swap_kernel,
        jax.ShapeDtypeStruct(x.shape, x.dtype),
        collective_id,
        x,
        scratch=sem_pair(owners - 1) + sem_pair(owners - 1),
    )


def token_kernel(
    scale, x_ref, place_ref, attn_ref, ffn_ref, out_ref, attn_out_ref, ffn_out_ref,
    near_ref, parts_ref, blocks_ref, row_ref,
    s0, r0, s1, r1, s2, r2, s3, r3, s4, r4, s5, r5, s6, r6,
):
    owners, others = peers_of("dp"), far_replicas()
    me, here = lax.axis_index("dp"), lax.axis_index("vocab")
    near, side = flip(here, 1), lax.rem(here, 2)
    greet(
        *[("dp", to) for _, to, _ in owners], *[("vocab", to) for _, to, _ in others], ("vocab", near)
    )
    count, length, columns = x_ref.shape
    half, pairs = length // 2, lax.axis_size("vocab") // 2
    share = half // pairs

    def half_of(which):
        return pl.ds(pl.multiple_of(which * half, half), half)

    def share_of(index):
        return pl.ds(pl.multiple_of(index // 2 * share, share), share)

    def place_of(index):
        return pl.ds(pl.multiple_of(side * half + index // 2 * share, share), share)

    def weight_place(ref, own_ref, origin):
        count, rows = own_ref.shape[0] // 2, own_ref.shape[1]
        return ref.at[pl.ds(side * count, count), pl.ds(pl.multiple_of(origin * rows, rows), rows)]

    def send_weights(ref, own_ref, slot):
        mine = own_ref.at[pl.ds(side * (own_ref.shape[0] // 2), own_ref.shape[0] // 2)]
        return [
            push(mine, weight_place(ref, own_ref, me), (s5, r5), slot + step - 1, "dp", to)
            for step, to, _ in owners
        ]

    def relay_weights(ref, own_ref, copies, slot):
        relays = []
        for copy, (step, _, origin) in zip(copies, owners):
            copy.wait()
            place = weight_place(ref, own_ref, origin)
            relays.append(push(place, place, (s6, r6), slot + step - 1, "vocab", near))
        return relays

    first = push(x_ref.at[:, half_of(1 - side)], near_ref, (s0, r0), 0, "vocab", near)
    attn_copies = send_weights(attn_out_ref, attn_ref, 0)
    for ref, own_ref in ((attn_out_ref, attn_ref), (ffn_out_ref, ffn_ref)):
        rows = own_ref.shape[1]
        ref[:, pl.ds(pl.multiple_of(me * rows, rows), rows), :] = own_ref[...]
    first.wait()
    near_ref[...] += x_ref[:, half_of(side)]
    copies = [
        push(near_ref.at[:, share_of(to)], parts_ref.at[slot], (s1, r1), slot, "vocab", to)
        for slot, to, _ in others
    ]
    for copy in copies:
        copy.wait()
    total = near_ref[:, share_of(here)]
    for slot, _, _ in others:
        total = total + parts_ref[slot]
    blocks_ref[...] = total
    copies = [
        push(
            blocks_ref.at[to],
            row_ref.at[me, place_of(here)],
            (s2, r2),
            step - 1,
            "dp",
            to,
        )
        for step, to, _ in owners
    ]
    row_ref[me, place_of(here)] = blocks_ref[me]
    for copy in copies:
        copy.wait()
    ffn_copies = send_weights(ffn_out_ref, ffn_ref, len(owners))
    mine = row_ref.at[:, place_of(here)]
    copies = [push(mine, mine, (s3, r3), slot, "vocab", to) for slot, to, _ in others]
    close = [push(mine, mine, (s4, r4), 0, "vocab", near)]
    for copy, (slot, _, origin) in zip(copies, others):
        copy.wait()
        theirs = row_ref.at[:, place_of(origin)]
        close.append(push(theirs, theirs, (s4, r4), slot + 1, "vocab", near))
    close += relay_weights(attn_out_ref, attn_ref, attn_copies, 0)
    for copy in close[: pairs]:
        copy.wait()
    for owner in range(count):
        band = slice(owner * columns, (owner + 1) * columns)
        out_ref[:, band] = row_ref[owner].astype(jnp.float32) * scale + place_ref[:, band]
    close += relay_weights(ffn_out_ref, ffn_ref, ffn_copies, len(owners))
    for copy in close[pairs:]:
        copy.wait()


def gather_tokens(x, places, attn, ffn, scale, collective_id):
    owners, pairs = lax.axis_size("dp"), lax.axis_size("vocab") // 2
    _, length, columns = x.shape
    half = length // 2
    width = owners * columns
    whole = [low(w.shape[0], owners * w.shape[1], width) for w in (attn, ffn)]
    return talk(
        partial(token_kernel, scale),
        (full(length, width), *whole),
        collective_id,
        x,
        places,
        attn,
        ffn,
        scratch=[
            pltpu.VMEM((owners, half, columns), x.dtype),
            pltpu.VMEM((pairs - 1, owners, half // pairs, columns), x.dtype),
            pltpu.VMEM((owners, half // pairs, columns), x.dtype),
            pltpu.VMEM((owners, length, columns), x.dtype),
        ]
        + sem_pair(1)
        + sem_pair(pairs - 1)
        + sem_pair(owners - 1)
        + sem_pair(pairs - 1)
        + sem_pair(pairs)
        + sem_pair(2 * owners - 2)
        + sem_pair(2 * owners - 2),
    )


def sinusoid(length, model_width):
    places = np.arange(length, dtype=np.float32)[:, None]
    halves = np.arange(model_width // 2, dtype=np.float32)[None, :]
    angles = places * np.exp(halves * np.float32(-2.0 * math.log(10000.0) / model_width))
    angles = angles.astype(np.float64)
    return (
        np.stack([np.sin(angles), np.cos(angles)], axis=-1)
        .reshape(length, model_width)
        .astype(np.float32)
    )


def one_hot(ids, columns):
    return (ids[:, None] == columns[None, :]).astype(jnp.bfloat16)


def pick_weights(target_seg, pick_rows):
    sentence = jnp.take(target_seg, pick_rows, axis=0)
    return jnp.sum((sentence[:, None] == sentence[None, :]).astype(jnp.float32), axis=1)


def combine_stats(tops, totals, chosen):
    top = jnp.max(tops, axis=0)
    return top, jnp.sum(totals * jnp.exp(tops - top), axis=0), jnp.sum(chosen, axis=0)


def adam_direction(moment, second):
    return moment / (1.0 - beta_one**STEP) / (jnp.sqrt(second / (1.0 - beta_two**STEP)) + adam_eps)


def adam_update(weight, grad_item, moment, second, step_rate, decay_weight):
    moment = beta_one * moment + (1.0 - beta_one) * grad_item
    second = beta_two * second + (1.0 - beta_two) * grad_item * grad_item
    return (
        weight - step_rate * (adam_direction(moment, second) + decay_weight * weight),
        moment,
        second,
    )


def rotate(values, basis):
    high = basis.astype(jnp.bfloat16)
    rest = (basis - high.astype(jnp.float32)).astype(jnp.bfloat16)

    def product(part):
        return jnp.einsum("mfd,mde->mfe", values, part, preferred_element_type=jnp.float32)

    return product(high) + product(rest)


def share_rows(array, owners, shares, share):
    rows, columns = array.shape
    blocks = array.reshape(owners, shares, rows // (owners * shares), columns)
    return lax.dynamic_index_in_dim(blocks, share, 1, keepdims=False)


def body(
    src_ids,
    src_seg,
    tgt_ids,
    tgt_seg,
    pick_pos,
    pick_label,
    attn_w,
    attn_m,
    attn_v,
    ffn_w,
    ffn_m,
    ffn_v,
    soap_basis,
    soap_stats,
    norm_p,
    norm_m,
    norm_v,
    embedding,
    embed_m,
    embed_v,
):
    owners, replicas = lax.axis_size("dp"), lax.axis_size("vocab")
    replica = lax.axis_index("vocab")
    own_table = embedding.astype(jnp.bfloat16)
    own_norms = jnp.pad(norm_p.astype(jnp.bfloat16).astype(jnp.float32), ((0, 2), (0, 0)))
    all_ids, norm_rows = gather_small("dp", 1, jnp.concatenate([src_ids, tgt_ids]), own_norms)
    norm_rows = jnp.swapaxes(norm_rows, 0, 1).reshape(16, -1)
    norms = [jnp.stack([norm_rows[k], norm_rows[7 + k]]) for k in range(7)]
    vocab_count, width = embedding.shape[0], attn_w.shape[2]
    columns = replica * vocab_count + jnp.arange(vocab_count)
    source, source_seg, target, target_seg = (src_ids[0], src_seg[0], tgt_ids[0], tgt_seg[0])
    pick_rows, labels = (pick_pos[0], pick_label[0])
    length = source.shape[0]
    embed_scale = math.sqrt(width)
    halves = replica * (vocab_count // 2) + jnp.arange(vocab_count // 2)
    paired = own_table.reshape(vocab_count // 2, -1)

    def look_up(ids):
        wide = lax.dot_general(one_hot(ids // 2, halves), paired, (((1,), (0,)), ((), ())))
        left, right = jnp.split(wide, 2, axis=1)
        return jnp.where((ids % 2 == 0)[:, None], left, right)

    source_part, target_part = (look_up(all_ids[:, k].reshape(-1)) for k in (0, 1))
    positional = sinusoid(length, width)
    enc_in, enc_attn_w, enc_ffn_w = gather_tokens(
        source_part.reshape(owners, length, -1),
        positional,
        attn_w[0:4].astype(jnp.bfloat16),
        ffn_w[0:2].astype(jnp.bfloat16),
        embed_scale,
        2,
    )
    target_part, _ = lax.optimization_barrier((target_part, enc_in))
    target_sum = lax.psum(target_part, "vocab")
    enc_mid, enc_attn = attn_forward(
        enc_in, norms[0], ((enc_attn_w,), 0, 0), source_seg, source_seg, None, False
    )
    self_w, cross_w, dec_ffn_w, ready = late_weights(attn_w[4:], ffn_w[2:], enc_in, enc_mid)
    late_table, _ = lax.optimization_barrier((own_table, ready))
    table_low = lax.all_gather(late_table, "dp", axis=1, tiled=True)
    enc_out, encoded, enc_ffn = ffn_forward(enc_mid, norms[1], norms[2], ((enc_ffn_w,), 0, 0))
    target_rows = swap_owners(target_sum.reshape(owners, length, -1), 3)
    target_rows = jnp.swapaxes(target_rows, 0, 1).reshape(length, -1).astype(jnp.float32)
    dec_in = target_rows * embed_scale + positional
    dec_mid, dec_self = attn_forward(
        dec_in, norms[3], self_w, target_seg, target_seg, None, True
    )
    dec_late, dec_cross = attn_forward(
        dec_mid, norms[4], cross_w, target_seg, source_seg, encoded, False
    )
    dec_out, final_low, dec_ffn = ffn_forward(dec_late, norms[5], norms[6], dec_ffn_w)

    chosen_rows = one_hot(pick_rows, jnp.arange(length))
    picked = dot_dims(chosen_rows, final_low, 1, 0).astype(jnp.bfloat16)
    logits = dot_dims(picked, table_low, 1, 1)
    row_top = jnp.max(logits, axis=-1)
    row_total = jnp.sum(jnp.exp(logits - row_top[:, None]), axis=-1)
    label_hit = labels[:, None] == columns[None, :]
    chosen = jnp.sum(jnp.where(label_hit, logits, 0.0), axis=-1)
    seen = jnp.pad(jnp.stack([row_top, row_total, chosen]), ((0, 5), (0, 0)))
    (seen,) = gather_small("vocab", 4, seen)
    row_top, row_total, chosen = combine_stats(seen[:, 0], seen[:, 1], seen[:, 2])
    log_total = row_top + jnp.log(row_total)
    weight = 1.0 / pick_weights(target_seg, pick_rows)
    loss_part = jnp.sum((log_total - chosen) * weight)
    count_part = (target_seg[-1] + 1).astype(jnp.float32)
    grad_logits = (
        weight[:, None] * (jnp.exp(logits - log_total[:, None]) - label_hit.astype(jnp.float32))
    ).astype(jnp.bfloat16)
    grad_picked = sum_vocab(dot_dims(grad_logits, table_low, 1, 0).astype(jnp.bfloat16), 5)
    grad_table = lax.psum_scatter(
        dot_dims(grad_logits, picked, 0, 0).astype(jnp.bfloat16),
        "dp",
        scatter_dimension=1,
        tiled=True,
    )
    grad_final = dot_dims(chosen_rows, grad_picked, 0, 0)

    chosen_columns = share_rows(jnp.eye(width, dtype=jnp.bfloat16), owners, replicas, replica)
    chosen_columns = chosen_columns.reshape(-1, width)

    def weight_grads(stored, parts):
        normed, kept, cross = stored[7], stored[8], stored[6]
        grad_low, gq, gk, gv = parts
        key_in = encoded if cross else normed
        share = [dot_dims(chosen_columns, rows, 1, 1).astype(jnp.bfloat16) for rows in (normed, key_in)]
        mixed = share_rows(kept[3], owners, replicas, replica).reshape(-1, length)
        return [
            dot_dims(share[0], gq, 1, 0),
            dot_dims(share[1], gk, 1, 0),
            dot_dims(share[1], gv, 1, 0),
            dot_dims(mixed, grad_low, 1, 0),
        ]

    def hidden_grads(stored, parts):
        grad_low, values, grads = parts
        return [
            dot_dims(share_rows(rows, owners, replicas, replica).reshape(-1, length), right, 1, 0)
            for rows, right in ((grads, stored[3]), (values, grad_low))
        ]

    def gradient_blocks(pieces):
        blocks = [piece.astype(jnp.bfloat16).reshape(owners, -1, width) for piece in pieces]
        return blocks if len(blocks) == 2 else [jnp.concatenate(blocks, axis=1)]

    norm_grads = [None] * 7
    grad, norm_grads[6], norm_grads[5], dec_ffn_parts = ffn_backward(grad_final, dec_ffn)
    grad, norm_grads[4], cross_parts, grad_encoded = attn_backward(grad, dec_cross)
    grad, norm_grads[3], self_parts, _ = attn_backward(grad, dec_self)
    grad_target = (grad * embed_scale).astype(jnp.bfloat16)
    early = (
        gradient_blocks(weight_grads(dec_self, self_parts))
        + gradient_blocks(weight_grads(dec_cross, cross_parts))
        + gradient_blocks(hidden_grads(dec_ffn, dec_ffn_parts))
    )
    early = jnp.concatenate(early, axis=1)
    early, grad_encoded = lax.optimization_barrier((early, grad_encoded))
    early = lax.psum_scatter(early, "dp", scatter_dimension=0, tiled=False)
    early = lax.all_gather(early, "vocab")
    grad, norm_grads[2], norm_grads[1], enc_ffn_parts = ffn_backward(grad_encoded, enc_ffn)
    grad, norm_grads[0], enc_parts, _ = attn_backward(grad, enc_attn)
    grad_source = (grad * embed_scale).astype(jnp.bfloat16)
    token_grads = jnp.concatenate([grad_source, grad_target]).reshape(2 * length, owners, -1)
    late = gradient_blocks(weight_grads(enc_attn, enc_parts)) + gradient_blocks(
        hidden_grads(enc_ffn, enc_ffn_parts)
    )
    late, token_grads = share_gradients(
        jnp.stack(late, axis=1), jnp.swapaxes(token_grads, 0, 1), 7
    )
    token_grads = token_grads.reshape(owners * 2 * length, -1)
    flat_ids = all_ids.reshape(-1)
    even = (flat_ids % 2 == 0)[:, None]
    token_grads = jnp.concatenate(
        [jnp.where(even, token_grads, 0), jnp.where(even, 0, token_grads)], axis=1
    )
    g_embed = grad_table.astype(jnp.float32) + dot_dims(
        one_hot(flat_ids // 2, halves), token_grads, 0, 0
    ).reshape(vocab_count, -1)

    def by_matrix(shared, count):
        blocks = jnp.swapaxes(shared.reshape(replicas, count, -1, width), 0, 1)
        return blocks.reshape(count, -1, width)

    early, late = by_matrix(early, 4), by_matrix(late, 3)
    g_attn = [by_matrix(part, 4) for part in (late[0], early[0], early[1])]
    g_attn = jnp.concatenate(g_attn).astype(jnp.float32)
    g_ffn = jnp.concatenate([late[1:], early[2:]])
    norm_grad = jnp.stack(norm_grads)
    norm_grad = jnp.concatenate([norm_grad[:, 0], norm_grad[:, 1]], axis=0)
    g_norm = lax.psum_scatter(norm_grad, "dp", scatter_dimension=1, tiled=True)

    matrix = replica // 2
    own_grad = lax.dynamic_index_in_dim(g_ffn, matrix, 0, keepdims=False)
    own_products = dot_dims(own_grad, own_grad, 0, 0)
    g_ffn_low, g_ffn = g_ffn, g_ffn.astype(jnp.float32)
    first_copy = (replica == 0).astype(jnp.float32)
    layer_sq = jnp.sum(g_attn * g_attn) + jnp.sum(g_ffn * g_ffn) + jnp.sum(g_norm * g_norm)
    raw_squares = jnp.sum(g_embed * g_embed) + first_copy * layer_sq
    few = jnp.stack([first_copy * loss_part, first_copy * count_part, raw_squares])
    few = jnp.broadcast_to(jnp.pad(few, (0, 5))[:, None], (8, 128))
    own_products, few = sum_tail(own_products, few, 8)
    loss_sum, sentences, squares = few[0, 0], few[1, 0], few[2, 0]
    grad_norm = jnp.sqrt(squares) / sentences
    factor = jnp.minimum(1.0, clip_limit / (grad_norm + norm_eps)) / sentences
    g_attn, g_norm, g_embed = (
        g_attn * factor,
        g_norm * factor,
        g_embed * factor,
    )

    def all_matrices(own):
        rows = own.shape[0] // 2
        half = lax.dynamic_slice_in_dim(own.astype(jnp.bfloat16), replica % 2 * rows, rows, 0)
        return lax.all_gather(half, "vocab").reshape(4, 2 * rows, -1).astype(jnp.float32)

    all_products = all_matrices(own_products)
    new_stats = stat_decay * soap_stats + (1.0 - stat_decay) * (factor * factor) * (
        all_products
    )
    own_stat = stat_decay * lax.dynamic_index_in_dim(soap_stats, matrix, 0, keepdims=False) + (
        1.0 - stat_decay
    ) * (factor * factor) * own_products
    own_basis = renew_basis(own_stat, lax.dynamic_index_in_dim(soap_basis, matrix, 0, keepdims=False))
    new_basis = all_matrices(own_basis)

    new_attn, m_attn, v_attn = adam_update(attn_w, g_attn, attn_m, attn_v, rate_matrix, decay_rate)
    new_norm, m_norm, v_norm = adam_update(norm_p, g_norm, norm_m, norm_v, rate_vector, 0.0)
    new_embed, m_embed, v_embed = adam_update(
        embedding, g_embed, embed_m, embed_v, rate_matrix, decay_rate
    )
    rotated = factor * rotate(g_ffn_low, soap_basis)
    m_ffn = beta_one * ffn_m + (1.0 - beta_one) * rotated
    v_ffn = beta_two * ffn_v + (1.0 - beta_two) * rotated * rotated
    back_rotated = jnp.einsum(
        "mfe,mde->mfd", adam_direction(m_ffn, v_ffn), soap_basis, precision=lax.Precision.HIGH
    )
    new_ffn = ffn_w - rate_matrix * (back_rotated + decay_rate * ffn_w)
    return (
        loss_sum,
        sentences,
        grad_norm,
        new_attn,
        m_attn,
        v_attn,
        new_ffn,
        m_ffn,
        v_ffn,
        new_basis,
        new_stats,
        new_norm,
        m_norm,
        v_norm,
        new_embed,
        m_embed,
        v_embed,
    )


def solution(mesh):
    placed = (
        P("dp", None),
        P("dp", None),
        P("dp", None),
        P("dp", None),
        P("dp", None),
        P("dp", None),
        P(None, "dp", None),
        P(None, "dp", None),
        P(None, "dp", None),
        P(None, "dp", None),
        P(None, "dp", None),
        P(None, "dp", None),
        P(),
        P(),
        P(None, "dp"),
        P(None, "dp"),
        P(None, "dp"),
        P("vocab", "dp"),
        P("vocab", "dp"),
        P("vocab", "dp"),
    )
    return jax.shard_map(
        body,
        mesh=mesh,
        in_specs=placed,
        out_specs=(
            P(),
            P(),
            P(),
            P(None, "dp", None),
            P(None, "dp", None),
            P(None, "dp", None),
            P(None, "dp", None),
            P(None, "dp", None),
            P(None, "dp", None),
            P(),
            P(),
            P(None, "dp"),
            P(None, "dp"),
            P(None, "dp"),
            P("vocab", "dp"),
            P("vocab", "dp"),
            P("vocab", "dp"),
        ),
        check_vma=False,
    )
```

```python
from functools import partial
import math

import jax
import jax.numpy as jnp
import numpy as np
from jax import lax
from jax.experimental import pallas as pl
from jax.experimental.pallas import tpu as pltpu
from jax.sharding import PartitionSpec as P

HEADS = 8
STEP = 10
TILE = 128

highest = lax.Precision.HIGHEST
beta_one = 0.9
beta_two = 0.999
adam_eps = 1e-08
decay_rate = 0.01
rate_matrix = 0.03
rate_vector = 0.3
clip_limit = 1.0
stat_decay = 0.95
norm_eps = 1e-06
masked = -1e30
log_two_e = math.log2(math.e)
vmem = pl.BlockSpec(memory_space=pltpu.VMEM)
smem = pl.BlockSpec(memory_space=pltpu.SMEM)
mesh_ids = pl.DeviceIdType.MESH


def dot_dims(left, right, left_dim, right_dim):
    return lax.dot_general(
        left, right, (((left_dim,), (right_dim,)), ((), ())), preferred_element_type=jnp.float32
    )


def dot_exact(left, right, left_dim, right_dim):
    return lax.dot_general(
        left,
        right,
        (((left_dim,), (right_dim,)), ((), ())),
        precision=highest,
        preferred_element_type=jnp.float32,
    )


def cost_of(microseconds):
    return pl.CostEstimate(flops=microseconds * 10**9, bytes_accessed=0, transcendentals=0)


def call(kernel, outs, *args, scratch=(), smem_args=0, microseconds=5, before=()):
    def body(*refs):
        kernel(*refs[: len(args)], *refs[len(args) + len(before) :])

    return pl.pallas_call(
        body,
        out_shape=outs,
        in_specs=[vmem] * (len(args) - smem_args)
        + [smem] * smem_args
        + [pl.BlockSpec(memory_space=pl.ANY)] * len(before),
        out_specs=jax.tree.map(lambda _: vmem, outs),
        scratch_shapes=list(scratch),
        compiler_params=pltpu.CompilerParams(vmem_limit_bytes=56 * 2**20),
        cost_estimate=cost_of(microseconds),
    )(*args, *before)


def low(*shape):
    return jax.ShapeDtypeStruct(shape, jnp.bfloat16)


def full(*shape):
    return jax.ShapeDtypeStruct(shape, jnp.float32)


def norm_parts(values):
    centre = values - jnp.mean(values, axis=-1, keepdims=True)
    spread = jnp.mean(centre * centre, axis=-1, keepdims=True)
    root = lax.rsqrt(spread + norm_eps)
    return centre * root, root


def norm_forward(values, ln_ref):
    return norm_parts(values)[0] * ln_ref[0:1, :] + ln_ref[1:2, :]


def norm_backward(grad, values, ln_ref, ln_grad_ref):
    normed, root = norm_parts(values)
    ln_grad_ref[0:1, :] = jnp.sum(grad * normed, axis=0, keepdims=True)
    ln_grad_ref[1:2, :] = jnp.sum(grad, axis=0, keepdims=True)
    inner = grad * ln_ref[0:1, :]
    return root * (
        inner
        - jnp.mean(inner, axis=-1, keepdims=True)
        - normed * jnp.mean(inner * normed, axis=-1, keepdims=True)
    )


def at_tile(index, size):
    return pl.ds(pl.multiple_of(index * size, size), size)


def tile_mask(segq_ref, segk_ref, qi, ki, tile_q, tile_k, causal):
    seg_k = segk_ref[at_tile(ki, tile_k), :]
    seg_k = jnp.concatenate([seg_k] * (tile_q // TILE), axis=1)
    allowed = seg_k == segq_ref[:, at_tile(qi, tile_q)]
    if causal:
        shape = (tile_k, tile_q)
        ahead = lax.broadcasted_iota(jnp.int32, shape, 0) - lax.broadcasted_iota(
            jnp.int32, shape, 1
        )
        allowed = allowed & (ahead <= qi * tile_q - ki * tile_k)
    return allowed


def for_tiles(length, tile_q, tile_k, edge_ref, causal, step):
    count_q, count_k = length // tile_q, length // tile_k
    per_q, per_k = tile_q // TILE, tile_k // TILE

    def one(pair, carry):
        qi, ki = pair // count_k, lax.rem(pair, count_k)
        live = (edge_ref[0, qi * per_q] <= edge_ref[3, (ki + 1) * per_k - 1]) & (
            edge_ref[2, ki * per_k] <= edge_ref[1, (qi + 1) * per_q - 1]
        )
        if causal:
            live = live & (ki * tile_k < (qi + 1) * tile_q)

        @pl.when(live)
        def _():
            step(qi, ki)

        return carry

    lax.fori_loop(0, count_q * count_k, one, 0)


def tile_edges(seg_q, seg_k):
    last = TILE - 1
    return jnp.stack([seg_q[::TILE], seg_q[last::TILE], seg_k[::TILE], seg_k[last::TILE]])


def share_selector(rows, owners, shares, share, count):
    size = rows // (owners * shares)
    index = jnp.arange(count // shares)
    picked = index // size * (rows // owners) + share * size + index % size
    return (picked[:, None] == jnp.arange(count)[None, :]).astype(jnp.bfloat16)


def lay_weights(w_ref, piece_refs, part, first):
    own = piece_refs[0]
    matrices, rows = w_ref.shape[0], w_ref.shape[1] // 4
    half = own.shape[0] // 2
    me, side = lax.axis_index("dp"), lax.rem(lax.axis_index("vocab"), 2)
    for m in range(matrices):
        span = slice(first + m * rows, first + (m + 1) * rows)
        w_ref[m, pl.ds(pl.multiple_of(me * rows, rows), rows), :] = own[
            part * half + span.start : part * half + span.stop, :
        ]
        for k in range(1, 4):
            place = pl.ds(pl.multiple_of((me ^ k) * rows, rows), rows)

            @pl.when(side == part)
            def _():
                w_ref[m, place, :] = piece_refs[k][span, :]

            @pl.when(side != part)
            def _():
                w_ref[m, place, :] = piece_refs[k + 3][span, :]


def flip_sites(part, axis, bit):
    return lax.ppermute(part, axis, [(s, s ^ bit) for s in range(lax.axis_size(axis))])


def late_weights(attn, ffn, after, later):
    owners = lax.axis_size("dp")
    width = attn.shape[-1]
    attn, ffn = attn.astype(jnp.bfloat16), ffn.astype(jnp.bfloat16)
    if owners != 4:
        attn, ffn = (lax.all_gather(part, "dp", axis=1, tiled=True) for part in (attn, ffn))
        return ((attn[:4],), 0, 0), ((attn[4:],), 0, 0), ((ffn,), 0, 0), ffn[0, 0, 0]
    halves = [
        jnp.concatenate([attn[4 * k : 4 * k + 4].reshape(-1, width), ffn[k]]) for k in range(2)
    ]
    own = jnp.concatenate(halves)
    side = lax.axis_index("vocab") % 2
    mine = jnp.where(side == 0, halves[0], halves[1])
    mine, _ = lax.optimization_barrier((mine, after))
    got = [flip_sites(mine, "dp", k) for k in range(1, 4)]
    *got, _ = lax.optimization_barrier((*got, later))
    swapped = [flip_sites(part, "vocab", 1) for part in got]
    pieces = (own, *got, *swapped)
    rows = 4 * attn.shape[1]
    return (pieces, 0, 0), (pieces, 1, 0), (pieces, None, rows), swapped[-1][0, 0]


def attn_forward_kernel(causal, cross, pieces, part, first, *refs):
    refs = list(refs)
    x_ref, ln_ref, segq_ref, segk_ref = refs[:4]
    refs = refs[4:]
    key_ref = refs.pop(0) if cross else None
    piece_refs, refs = refs[:pieces], refs[pieces:]
    edge_ref, out_ref, a_ref, qt_ref, kt_ref, vt_ref, ot_ref, lse_ref = refs[:8]
    refs = refs[8:]
    w_ref = piece_refs[0]
    if pieces > 1:
        w_ref = refs.pop(0)
        lay_weights(w_ref, piece_refs, part, first)
    top_ref, sum_ref, acc_ref = refs
    length, width = x_ref.shape
    head_size = width // HEADS
    a_ref[...] = norm_forward(x_ref[...], ln_ref).astype(jnp.bfloat16)
    key_in = key_ref if cross else a_ref
    qt_ref[...] = dot_dims(a_ref[...], w_ref[0], 1, 0).astype(jnp.bfloat16).T
    kt_ref[...] = dot_dims(key_in[...], w_ref[1], 1, 0).astype(jnp.bfloat16).T
    vt_ref[...] = dot_dims(key_in[...], w_ref[2], 1, 0).astype(jnp.bfloat16).T
    top_ref[...] = jnp.full(top_ref.shape, masked, jnp.float32)
    sum_ref[...] = jnp.zeros(sum_ref.shape, jnp.float32)
    acc_ref[...] = jnp.zeros(acc_ref.shape, jnp.float32)
    scale = log_two_e / math.sqrt(head_size)
    bands = [slice(h * head_size, (h + 1) * head_size) for h in range(HEADS)]

    def step(qi, ki):
        q_at, k_at = at_tile(qi, 256), at_tile(ki, 256)
        allowed = tile_mask(segq_ref, segk_ref, qi, ki, 256, 256, causal)
        scores = [dot_dims(kt_ref[band, k_at], qt_ref[band, q_at], 0, 0) * scale for band in bands]
        scores = [jnp.where(allowed, part, masked) for part in scores]
        top = top_ref[:, q_at]
        new_top = jnp.maximum(
            top,
            jnp.concatenate([jnp.max(part, axis=0, keepdims=True) for part in scores], axis=0),
        )
        fade = jnp.exp2(top - new_top)
        parts = [jnp.exp2(scores[h] - new_top[h : h + 1]) for h in range(HEADS)]
        top_ref[:, q_at] = new_top
        sum_ref[:, q_at] = sum_ref[:, q_at] * fade + jnp.concatenate(
            [jnp.sum(part, axis=0, keepdims=True) for part in parts], axis=0
        )
        mixed = [
            dot_dims(vt_ref[bands[h], k_at], parts[h].astype(jnp.bfloat16), 1, 0)
            for h in range(HEADS)
        ]
        acc = acc_ref[:, q_at]
        acc_ref[:, q_at] = jnp.concatenate(
            [acc[bands[h]] * fade[h : h + 1] + mixed[h] for h in range(HEADS)], axis=0
        )

    for_tiles(length, 256, 256, edge_ref, causal, step)
    lse_ref[...] = top_ref[...] + jnp.log2(sum_ref[...])
    for h in range(HEADS):
        ot_ref[bands[h], :] = (acc_ref[bands[h], :] / sum_ref[h : h + 1, :]).astype(jnp.bfloat16)
    out_ref[...] = x_ref[...] + dot_dims(ot_ref[...], w_ref[3], 0, 0)


def attn_forward(x, ln, weights, seg_q, seg_k, key_in, causal):
    length, width = x.shape
    weights, part, first = weights
    cross = key_in is not None
    segs = (seg_q[None, :], jnp.broadcast_to(seg_k[:, None], (length, TILE)))
    edges = tile_edges(seg_q, seg_k)
    args = (x, ln, *segs) + ((key_in,) if cross else ()) + (*weights, edges)
    outs = (full(length, width), low(length, width)) + (low(width, length),) * 4
    outs = outs + (full(HEADS, length),)
    if len(weights) > 1:
        outs = outs + (low(4, width, width),)
    out, normed, *stored = call(
        partial(attn_forward_kernel, causal, cross, len(weights), part, first),
        outs,
        *args,
        scratch=[
            pltpu.VMEM((HEADS, length), jnp.float32),
            pltpu.VMEM((HEADS, length), jnp.float32),
            pltpu.VMEM((width, length), jnp.float32),
        ],
        smem_args=1,
        microseconds=20,
    )
    whole = stored.pop() if len(weights) > 1 else weights[0]
    return out, (x, ln, whole, segs, edges, causal, key_in, normed, stored)


def attn_backward_kernel(causal, cross, row_scale, *refs):
    g_ref, x_ref, ln_ref, w_ref, pick_ref, segq_ref, segk_ref, a_ref = refs[:8]
    refs = list(refs[8:])
    key_ref = refs.pop(0) if cross else a_ref
    qt_ref, kt_ref, vt_ref, ot_ref, lse_ref, edge_ref, out_ref, ln_grad_ref, block_ref, extra_ref = refs[:10]
    low_ref, gq_ref, gk_ref, gv_ref, got_ref, delta_ref, gqt_ref, gkt_ref, gvt_ref = refs[10:]
    length, width = x_ref.shape
    head_size = width // HEADS
    low_ref[...] = g_ref[...].astype(jnp.bfloat16)
    got_ref[...] = dot_dims(low_ref[...], w_ref[3], 1, 1).astype(jnp.bfloat16).T
    bands = [slice(h * head_size, (h + 1) * head_size) for h in range(HEADS)]
    for h in range(HEADS):
        delta_ref[h : h + 1, :] = jnp.sum(
            got_ref[bands[h], :].astype(jnp.float32) * ot_ref[bands[h], :].astype(jnp.float32),
            axis=0,
            keepdims=True,
        )
    for ref in (gqt_ref, gkt_ref, gvt_ref):
        ref[...] = jnp.zeros(ref.shape, jnp.float32)
    scale = log_two_e / math.sqrt(head_size)
    back = 1.0 / math.sqrt(head_size)

    def step(qi, ki):
        q_at, k_at = at_tile(qi, 256), at_tile(ki, TILE)
        allowed = tile_mask(segq_ref, segk_ref, qi, ki, 256, TILE, causal)
        scores = [dot_dims(kt_ref[band, k_at], qt_ref[band, q_at], 0, 0) for band in bands]
        grads = [dot_dims(vt_ref[band, k_at], got_ref[band, q_at], 0, 0) for band in bands]
        parts = [
            jnp.where(allowed, jnp.exp2(scores[h] * scale - lse_ref[h : h + 1, q_at]), 0.0)
            for h in range(HEADS)
        ]
        grads = [parts[h] * (grads[h] - delta_ref[h : h + 1, q_at]) for h in range(HEADS)]
        parts_t = [part.T.astype(jnp.bfloat16) for part in parts]
        grads_t = [part.T.astype(jnp.bfloat16) for part in grads]
        grads = [part.astype(jnp.bfloat16) for part in grads]
        for ref, place, terms in (
            (gvt_ref, k_at, [dot_dims(got_ref[bands[h], q_at], parts_t[h], 1, 0) for h in range(HEADS)]),
            (gkt_ref, k_at, [dot_dims(qt_ref[bands[h], q_at], grads_t[h], 1, 0) for h in range(HEADS)]),
            (gqt_ref, q_at, [dot_dims(kt_ref[bands[h], k_at], grads[h], 1, 0) for h in range(HEADS)]),
        ):
            ref[:, place] += jnp.concatenate(terms, axis=0)

    for_tiles(length, 256, TILE, edge_ref, causal, step)
    gq_ref[...] = (gqt_ref[...] * back).astype(jnp.bfloat16).T
    gk_ref[...] = (gkt_ref[...] * back).astype(jnp.bfloat16).T
    gv_ref[...] = gvt_ref[...].astype(jnp.bfloat16).T
    from_query = dot_dims(gq_ref[...], w_ref[0], 1, 1)
    from_keys = dot_dims(gk_ref[...], w_ref[1], 1, 1) + dot_dims(gv_ref[...], w_ref[2], 1, 1)
    if cross:
        extra_ref[...] = from_keys
    else:
        from_query = from_query + from_keys
    total = g_ref[...] + norm_backward(from_query, x_ref[...], ln_ref, ln_grad_ref)
    out_ref[...] = total
    owners = block_ref.shape[0]
    if not cross:
        columns = width // owners
        for owner in range(owners):
            band = slice(owner * columns, (owner + 1) * columns)
            extra_ref[owner] = (total[:, band] * row_scale).astype(jnp.bfloat16)
    own_a = dot_dims(pick_ref[...], a_ref[...], 1, 1).astype(jnp.bfloat16)
    own_key = dot_dims(pick_ref[...], key_ref[...], 1, 1).astype(jnp.bfloat16) if cross else own_a
    own_o = dot_dims(pick_ref[...], ot_ref[...], 1, 0).astype(jnp.bfloat16)
    size = own_a.shape[0] // owners
    products = ((own_a, gq_ref), (own_key, gk_ref), (own_key, gv_ref), (own_o, low_ref))
    for m, (rows, right_ref) in enumerate(products):
        product = dot_dims(rows, right_ref[...], 1, 0).astype(jnp.bfloat16)
        for owner in range(owners):
            block_ref[owner, m * size : (m + 1) * size, :] = product[owner * size : (owner + 1) * size]


def attn_backward(grad, stored, picks, owners, row_scale, before=()):
    x, ln, weights, segs, edges, causal, key_in, normed, kept = stored
    length, width = x.shape
    cross = key_in is not None
    extra = full(length, width) if cross else low(owners, length, width // owners)
    outs = (full(length, width), full(2, width), low(owners, 4 * picks.shape[0] // owners, width), extra)
    keys = (key_in,) if cross else ()
    return call(
        partial(attn_backward_kernel, causal, cross, row_scale),
        outs,
        grad,
        x,
        ln,
        weights,
        picks,
        *segs,
        normed,
        *keys,
        *kept,
        edges,
        scratch=[pltpu.VMEM((length, width), jnp.bfloat16)] * 4
        + [pltpu.VMEM((width, length), jnp.bfloat16), pltpu.VMEM((HEADS, length), jnp.float32)]
        + [pltpu.VMEM((width, length), jnp.float32)] * 3,
        smem_args=1,
        microseconds=25,
        before=before,
    )


def gelu_parts(hidden):
    root = math.sqrt(2.0 / math.pi)
    square = hidden * hidden
    bend = jnp.tanh(root * hidden * (1.0 + 0.044715 * square))
    value = 0.5 * hidden * (1.0 + bend)
    slope = 0.5 * (1.0 + bend) + 0.5 * hidden * (1.0 - bend * bend) * root * (
        1.0 + 3.0 * 0.044715 * square
    )
    return value, slope


def ffn_forward_kernel(chunk, pieces, first, x_ref, ln_ref, next_ref, *refs):
    piece_refs, (out_ref, a_ref, after_ref, *refs) = refs[:pieces], refs[pieces:]
    w_ref = piece_refs[0]
    if pieces > 1:
        (w_ref,) = refs
        for part in range(2):
            lay_weights(w_ref.at[part : part + 1], piece_refs, part, first)
    w_in_ref, w_out_ref = w_ref.at[0], w_ref.at[1]
    a_ref[...] = norm_forward(x_ref[...], ln_ref).astype(jnp.bfloat16)
    total = x_ref[...]
    for start in range(0, w_in_ref.shape[0], chunk):
        part = slice(start, start + chunk)
        hidden = dot_dims(a_ref[...], w_in_ref[part, :], 1, 1)
        active = gelu_parts(hidden)[0].astype(jnp.bfloat16)
        total = total + dot_dims(active, w_out_ref[part, :], 1, 0)
    out_ref[...] = total
    after_ref[...] = norm_forward(total, next_ref).astype(after_ref.dtype)


def ffn_forward(x, ln, ln_next, weights):
    length, width = x.shape
    weights, _, first = weights
    outs = (full(length, width), low(length, width), low(length, width))
    if len(weights) > 1:
        outs = outs + (low(2, 4 * (weights[0].shape[0] // 2 - first), width),)
    out, normed, after, *whole = call(
        partial(ffn_forward_kernel, 512, len(weights), first),
        outs,
        x,
        ln,
        ln_next,
        *weights,
        microseconds=12,
    )
    return out, after, (x, ln, whole[0] if whole else weights[0], normed, out, ln_next)


def ffn_backward_kernel(
    chunk, after_ref, y_ref, next_ref, x_ref, ln_ref, a_ref, w_ref, pick_ref,
    out_ref, next_grad_ref, ln_grad_ref, in_ref, back_ref, low_ref, g_ref,
):
    w_in_ref, w_out_ref = w_ref.at[0], w_ref.at[1]
    g_ref[...] = norm_backward(after_ref[...], y_ref[...], next_ref, next_grad_ref)
    low_ref[...] = g_ref[...].astype(jnp.bfloat16)
    total = jnp.zeros(g_ref.shape, jnp.float32)
    owners, size = in_ref.shape[:2]
    blocks = pick_ref.shape[0] // size
    for index in range(w_in_ref.shape[0] // chunk):
        part = slice(index * chunk, (index + 1) * chunk)
        hidden = dot_dims(a_ref[...], w_in_ref[part, :], 1, 1)
        value, slope = gelu_parts(hidden)
        grad = (dot_dims(low_ref[...], w_out_ref[part, :], 1, 1) * slope).astype(jnp.bfloat16)
        total = total + dot_dims(grad, w_in_ref[part, :], 1, 0)
        pairs = ((in_ref, grad, a_ref), (back_ref, value.astype(jnp.bfloat16), low_ref))
        for ref, left, right_ref in pairs:
            rows = dot_dims(pick_ref[...], left, 1, 1).astype(jnp.bfloat16)
            product = dot_dims(rows, right_ref[...], 1, 0).astype(jnp.bfloat16)
            for block in range(blocks):
                ref[index * blocks + block] = product[block * size : (block + 1) * size]
    out_ref[...] = g_ref[...] + norm_backward(total, x_ref[...], ln_ref, ln_grad_ref)


def ffn_backward(grad_after, stored, picks, owners, before=()):
    x, ln, weights, normed, out, ln_next = stored
    length, width = x.shape
    chunk = picks.shape[1]
    size = picks.shape[0] * weights.shape[1] // chunk // owners
    block = low(owners, size, width)
    return call(
        partial(ffn_backward_kernel, chunk),
        (full(length, width), full(2, width), full(2, width), block, block),
        grad_after,
        out,
        ln_next,
        x,
        ln,
        normed,
        weights,
        picks,
        scratch=[
            pltpu.VMEM((length, width), jnp.bfloat16),
            pltpu.VMEM((length, width), jnp.float32),
        ],
        microseconds=17,
        before=before,
    )


def update_kernel(factor_ref, g_ref, basis_ref, w_ref, m_ref, v_ref, new_w_ref, new_m_ref, new_v_ref):
    high = basis_ref[0].astype(jnp.bfloat16)
    rest = (basis_ref[0] - high.astype(jnp.float32)).astype(jnp.bfloat16)
    grad = g_ref[0]
    rotated = (dot_dims(grad, high, 1, 0) + dot_dims(grad, rest, 1, 0)) * factor_ref[0]
    moment = beta_one * m_ref[0] + (1.0 - beta_one) * rotated
    second = beta_two * v_ref[0] + (1.0 - beta_two) * rotated * rotated
    new_m_ref[0] = moment
    new_v_ref[0] = second
    step = adam_direction(moment, second)
    step_high = step.astype(jnp.bfloat16)
    step_rest = (step - step_high.astype(jnp.float32)).astype(jnp.bfloat16)
    back = (
        dot_dims(step_high, high, 1, 1)
        + dot_dims(step_high, rest, 1, 1)
        + dot_dims(step_rest, high, 1, 1)
    )
    new_w_ref[0] = w_ref[0] - rate_matrix * (back + decay_rate * w_ref[0])


def update_rotated(factor, grads, bases, weights, moments, seconds):
    count, rows, width = weights.shape
    block = pl.BlockSpec((1, rows, width), lambda k: (k, 0, 0))
    square = pl.BlockSpec((1, width, width), lambda k: (k, 0, 0))
    return pl.pallas_call(
        update_kernel,
        grid=(count,),
        out_shape=(full(count, rows, width),) * 3,
        in_specs=[smem, block, square, block, block, block],
        out_specs=(block,) * 3,
        compiler_params=pltpu.CompilerParams(vmem_limit_bytes=56 * 2**20),
        cost_estimate=cost_of(10),
    )(factor.reshape(1), grads, bases, weights, moments, seconds)


def small_factor(block):
    size = block.shape[0]
    eye = (
        lax.broadcasted_iota(jnp.int32, (size, size), 0)
        == lax.broadcasted_iota(jnp.int32, (size, size), 1)
    ).astype(jnp.float32)
    whole = jnp.concatenate([block, eye], axis=1)
    rows = [whole[8 * u : 8 * u + 8] for u in range(size // 8)]
    shape = rows[0].shape
    sub = lax.broadcasted_iota(jnp.int32, shape, 0)

    def lane_splat(value, lane):
        return jnp.broadcast_to(value[:, lane : lane + 1], shape)

    def row_splat(value, row):
        return jnp.broadcast_to(value[row : row + 1, :], shape)

    for g in range(len(rows)):
        first = 8 * g
        lanes = {
            u: [lane_splat(rows[u], first + s) for s in range(8)] for u in range(g, len(rows))
        }
        scale = jnp.zeros(shape, jnp.float32)
        for t in range(8):
            pivot = row_splat(lanes[g][t], t)
            root = lax.rsqrt(pivot)
            inverse = root * root
            scale = jnp.where(sub == t, root, scale)
            row_t = row_splat(rows[g], t) * inverse
            splats = {s: row_splat(lanes[g][s], t) * inverse for s in range(t + 1, 8)}
            for u in range(g, len(rows)):
                factor = lanes[u][t]
                if u == g:
                    factor = jnp.where(sub > t, factor, 0.0)
                rows[u] = rows[u] - factor * row_t
                for s in range(t + 1, 8):
                    lanes[u][s] = lanes[u][s] - factor * splats[s]
        rows[g] = rows[g] * scale
    return jnp.concatenate(rows, axis=0)[:, size:]


def renew_kernel(stat_ref, basis_ref, out_ref, gram_ref, rest_ref):
    size = stat_ref.shape[0]
    product = dot_exact(stat_ref[...], basis_ref[...], 1, 0)
    rest_ref[...] = product
    gram_ref[...] = dot_exact(product, product, 0, 0)
    for low in range(0, size, 128):
        high = low + 128
        block = gram_ref[low:high, low:high]
        corner = small_factor(block[:64, :64])
        across = dot_exact(corner, block[:64, 64:], 1, 0)
        second = small_factor(block[64:, 64:] - dot_exact(across, across, 0, 0))
        below = dot_exact(second, dot_exact(across, corner, 0, 0), 1, 0)
        inverse = jnp.concatenate(
            [
                jnp.concatenate([corner, jnp.zeros_like(corner)], axis=1),
                jnp.concatenate([-below, second], axis=1),
            ],
            axis=0,
        )
        columns = dot_exact(rest_ref[:, low:high], inverse, 1, 1)
        out_ref[:, low:high] = columns
        if high < size:
            panel = dot_exact(inverse, gram_ref[low:high, high:], 1, 0)
            gram_ref[high:, high:] -= dot_exact(panel, panel, 0, 0)
            rest_ref[:, high:] -= dot_exact(columns, panel, 1, 0)


def renew_basis(statistic, basis):
    shape = statistic.shape
    return call(
        renew_kernel,
        full(*shape),
        statistic,
        basis,
        scratch=[pltpu.VMEM(shape, jnp.float32), pltpu.VMEM(shape, jnp.float32)],
        microseconds=29,
    )


def peers_of(axis):
    size, me = lax.axis_size(axis), lax.axis_index(axis)
    return [
        (step, lax.rem(me + step, size), lax.rem(me + size - step, size)) for step in range(1, size)
    ]


def greet(*places):
    barrier = pltpu.get_barrier_semaphore()
    for axis, index in places:
        pl.semaphore_signal(barrier, inc=1, device_id={axis: index}, device_id_type=mesh_ids)
    pl.semaphore_wait(barrier, len(places))


def push(source, target, sems, slot, axis, index):
    copy = pltpu.make_async_remote_copy(
        src_ref=source,
        dst_ref=target,
        send_sem=sems[0].at[slot],
        recv_sem=sems[1].at[slot],
        device_id={axis: index},
        device_id_type=mesh_ids,
    )
    copy.start()
    return copy


def sem_pair(count):
    return [pltpu.SemaphoreType.DMA((count,)), pltpu.SemaphoreType.DMA((count,))]


def talk(kernel, outs, collective_id, *args, scratch=(), microseconds=15, before=()):
    def body(*refs):
        kernel(*refs[: len(args)], *refs[len(args) + len(before) :])

    return pl.pallas_call(
        body,
        out_shape=outs,
        in_specs=[vmem] * len(args) + [pl.BlockSpec(memory_space=pl.ANY)] * len(before),
        out_specs=jax.tree.map(lambda _: vmem, outs),
        scratch_shapes=list(scratch),
        compiler_params=pltpu.CompilerParams(
            collective_id=collective_id, has_side_effects=True, vmem_limit_bytes=56 * 2**20
        ),
        cost_estimate=cost_of(microseconds),
    )(*args, *before)


def gather_kernel(axis, *refs):
    count = (len(refs) - 2) // 2
    others = peers_of(axis)
    greet(*[(axis, to) for _, to, _ in others])
    me = lax.axis_index(axis)
    copies = [
        push(refs[k], refs[count + k].at[me], refs[-2:], k * len(others) + step - 1, axis, to)
        for k in range(count)
        for step, to, _ in others
    ]
    for k in range(count):
        refs[count + k][me] = refs[k][...]
    for copy in copies:
        copy.wait()


def gather_small(axis, collective_id, *arrays):
    size = lax.axis_size(axis)
    outs = tuple(jax.ShapeDtypeStruct((size, *x.shape), x.dtype) for x in arrays)
    sems = sem_pair((size - 1) * len(arrays))
    return talk(partial(gather_kernel, axis), outs, collective_id, *arrays, scratch=sems)


def sum_kernel(x_ref, out_ref, parts_ref, mine_ref, s0, r0, s1, r1):
    others = peers_of("vocab")
    greet(*[("vocab", to) for _, to, _ in others])
    size, me = lax.axis_size("vocab"), lax.axis_index("vocab")
    rows = mine_ref.shape[0]

    def rows_of(index):
        return pl.ds(pl.multiple_of(index * rows, rows), rows)

    copies = [
        push(x_ref.at[rows_of(to)], parts_ref.at[me], (s0, r0), step - 1, "vocab", to)
        for step, to, _ in others
    ]
    parts_ref[me] = x_ref[rows_of(me), :]
    for copy in copies:
        copy.wait()
    total = parts_ref[0].astype(jnp.float32)
    for index in range(1, size):
        total = total + parts_ref[index].astype(jnp.float32)
    mine_ref[...] = total.astype(mine_ref.dtype)
    copies = [
        push(mine_ref, out_ref.at[rows_of(me)], (s1, r1), step - 1, "vocab", to)
        for step, to, _ in others
    ]
    out_ref[rows_of(me), :] = mine_ref[...]
    for copy in copies:
        copy.wait()


def sum_vocab(x, collective_id):
    replicas = lax.axis_size("vocab")
    rows, columns = x.shape
    share = rows // replicas
    return talk(
        sum_kernel,
        jax.ShapeDtypeStruct(x.shape, x.dtype),
        collective_id,
        x,
        scratch=[
            pltpu.VMEM((replicas, share, columns), x.dtype),
            pltpu.VMEM((share, columns), x.dtype),
        ]
        + sem_pair(replicas - 1)
        + sem_pair(replicas - 1),
    )


def flip(index, bit):
    return index + bit - 2 * bit * lax.rem(index // bit, 2)


def tail_kernel(
    x_ref, few_ref, out_ref, sum_ref, parts_ref, seen_ref, line_ref, lines_ref,
    s0, r0, s1, r1, s2, r2, s3, r3, s4, r4,
):
    owners, replicas = peers_of("dp"), peers_of("vocab")
    greet(*[("dp", to) for _, to, _ in owners], *[("vocab", to) for _, to, _ in replicas])
    size, me, here = lax.axis_size("dp"), lax.axis_index("dp"), lax.axis_index("vocab")
    near, side = flip(here, 1), lax.rem(here, 2)
    rows = parts_ref.shape[1]

    def rows_of(index):
        return pl.ds(pl.multiple_of((side * size + index) * rows, rows), rows)

    few = [
        push(few_ref, seen_ref.at[here], (s2, r2), step - 1, "vocab", to) for step, to, _ in replicas
    ]
    wide = [
        push(x_ref.at[rows_of(to)], parts_ref.at[me], (s0, r0), step - 1, "dp", to)
        for step, to, _ in owners
    ]
    seen_ref[here] = few_ref[...]
    parts_ref[me] = x_ref[rows_of(me), :]
    for copy in few:
        copy.wait()
    line_ref[...] = jnp.sum(seen_ref[...], axis=0)
    few = [
        push(line_ref, lines_ref.at[me], (s3, r3), step - 1, "dp", to) for step, to, _ in owners
    ]
    lines_ref[me] = line_ref[...]
    for copy in wide:
        copy.wait()
    out_ref[rows_of(me), :] = jnp.sum(parts_ref[...], axis=0)
    mine = out_ref.at[rows_of(me)]
    wide = [push(mine, mine, (s1, r1), step - 1, "dp", to) for step, to, _ in owners]
    close = [push(mine, mine, (s4, r4), 0, "vocab", near)]
    for copy in few:
        copy.wait()
    sum_ref[...] = jnp.sum(lines_ref[...], axis=0)
    for copy, (step, _, origin) in zip(wide, owners):
        copy.wait()
        theirs = out_ref.at[rows_of(origin)]
        close.append(push(theirs, theirs, (s4, r4), step, "vocab", near))
    for copy in close:
        copy.wait()


def sum_tail(x, few, collective_id):
    owners, replicas = lax.axis_size("dp"), lax.axis_size("vocab")
    rows, columns = x.shape
    share = rows // (2 * owners)
    return talk(
        tail_kernel,
        (full(*x.shape), full(*few.shape)),
        collective_id,
        x,
        few,
        scratch=[
            pltpu.VMEM((owners, share, columns), jnp.float32),
            pltpu.VMEM((replicas, *few.shape), jnp.float32),
            pltpu.VMEM(few.shape, jnp.float32),
            pltpu.VMEM((owners, *few.shape), jnp.float32),
        ]
        + sem_pair(owners - 1)
        + sem_pair(owners - 1)
        + sem_pair(replicas - 1)
        + sem_pair(owners - 1)
        + sem_pair(owners),
    )


def far_replicas():
    here, size = lax.axis_index("vocab"), lax.axis_size("vocab")
    return [
        (step // 2 - 1, lax.rem(here + step, size), lax.rem(here + size - step, size))
        for step in range(2, size, 2)
    ]


def gradient_kernel(chunks, count, *refs):
    x_refs, refs = refs[:chunks], refs[chunks:]
    rows_refs, (out_ref, *refs) = refs[:count], refs[count:]
    swapped_refs, (parts_ref, s0, r0, s1, r1, s2, r2, s3, r3, s4, r4) = refs[:count], refs[count:]
    owners = peers_of("dp")
    here, me = lax.axis_index("vocab"), lax.axis_index("dp")
    near = flip(here, 1)
    size = lax.axis_size("vocab")
    steps = range(2, size, 2)
    greet(
        *[("dp", to) for _, to, _ in owners],
        *[("vocab", lax.rem(here + step, size)) for step in steps],
        ("vocab", near),
    )

    def spread(c, origin, sems, slot, to):
        place = out_ref.at[c, origin]
        return push(place, place, sems, slot, "vocab", to)

    arriving = [
        [
            push(x_refs[c].at[to], parts_ref.at[c, me], (s0, r0), (step - 1) * chunks + c, "dp", to)
            for step, to, _ in owners
        ]
        for c in range(chunks)
    ]

    def half_of(ref):
        rows = ref.shape[1] // 2
        return pl.ds(pl.multiple_of(lax.rem(here, 2) * rows, rows), rows)

    swaps = [
        [
            push(
                rows_ref.at[to, half_of(rows_ref)],
                swapped_ref.at[me, half_of(rows_ref)],
                (s3, r3),
                k * len(owners) + step - 1,
                "dp",
                to,
            )
            for step, to, _ in owners
        ]
        for k, (rows_ref, swapped_ref) in enumerate(zip(rows_refs, swapped_refs))
    ]
    for rows_ref, swapped_ref in zip(rows_refs, swapped_refs):
        swapped_ref[me] = rows_ref[me]
    far, close = [], []
    for c in range(chunks):
        parts_ref[c, me] = x_refs[c][me]
        for copy in arriving[c]:
            copy.wait()
        total = jnp.sum(parts_ref[c].astype(jnp.float32), axis=0)
        out_ref[c, here] = total.astype(out_ref.dtype)
        far.append(
            [
                spread(c, here, (s1, r1), k * chunks + c, lax.rem(here + step, size))
                for k, step in enumerate(steps)
            ]
        )
        close.append(spread(c, here, (s2, r2), c, near))
    for c in range(chunks):
        for k, step in enumerate(steps):
            far[c][k].wait()
            origin = lax.rem(here + size - step, size)
            close.append(spread(c, origin, (s2, r2), (k + 1) * chunks + c, near))
    for k, swapped_ref in enumerate(swapped_refs):
        for copy, (step, _, origin) in zip(swaps[k], owners):
            copy.wait()
            place = swapped_ref.at[origin, half_of(swapped_ref)]
            close.append(push(place, place, (s4, r4), k * len(owners) + step - 1, "vocab", near))
    for copy in close:
        copy.wait()


def share_gradients(blocks, rows, collective_id, before):
    owners, replicas = lax.axis_size("dp"), lax.axis_size("vocab")
    chunks = len(blocks)
    others = (replicas // 2 - 1) * chunks
    shape, kind = blocks[0].shape, blocks[0].dtype
    return talk(
        partial(gradient_kernel, chunks, len(rows)),
        (
            jax.ShapeDtypeStruct((chunks, replicas, *shape[1:]), kind),
            *[jax.ShapeDtypeStruct(part.shape, part.dtype) for part in rows],
        ),
        collective_id,
        *blocks,
        *rows,
        scratch=[pltpu.VMEM((chunks, *shape), kind)]
        + sem_pair((owners - 1) * chunks)
        + sem_pair(others)
        + sem_pair(others + chunks)
        + sem_pair(len(rows) * (owners - 1))
        + sem_pair(len(rows) * (owners - 1)),
        microseconds=40,
        before=before,
    )


def swap_kernel(x_ref, out_ref, s0, r0, s1, r1):
    others = peers_of("dp")
    me, here = lax.axis_index("dp"), lax.axis_index("vocab")
    near, side = flip(here, 1), lax.rem(here, 2)
    greet(*[("dp", to) for _, to, _ in others], ("vocab", near))
    rows = x_ref.shape[1] // 2
    half = pl.ds(pl.multiple_of(side * rows, rows), rows)
    copies = [
        push(x_ref.at[to, half], out_ref.at[me, half], (s0, r0), step - 1, "dp", to)
        for step, to, _ in others
    ]
    out_ref[me] = x_ref[me]
    close = []
    for copy, (step, _, origin) in zip(copies, others):
        copy.wait()
        place = out_ref.at[origin, half]
        close.append(push(place, place, (s1, r1), step - 1, "vocab", near))
    for copy in close:
        copy.wait()


def swap_owners(x, collective_id):
    owners = lax.axis_size("dp")
    return talk(
        swap_kernel,
        jax.ShapeDtypeStruct(x.shape, x.dtype),
        collective_id,
        x,
        scratch=sem_pair(owners - 1) + sem_pair(owners - 1),
    )


def token_kernel(
    scale, x_ref, place_ref, attn_ref, ffn_ref, out_ref, attn_out_ref, ffn_out_ref,
    near_ref, parts_ref, blocks_ref, row_ref,
    s0, r0, s1, r1, s2, r2, s3, r3, s4, r4, s5, r5, s6, r6,
):
    owners, others = peers_of("dp"), far_replicas()
    me, here = lax.axis_index("dp"), lax.axis_index("vocab")
    near, side = flip(here, 1), lax.rem(here, 2)
    greet(
        *[("dp", to) for _, to, _ in owners], *[("vocab", to) for _, to, _ in others], ("vocab", near)
    )
    count, length, columns = x_ref.shape
    half, pairs = length // 2, lax.axis_size("vocab") // 2
    share = half // pairs

    def half_of(which):
        return pl.ds(pl.multiple_of(which * half, half), half)

    def share_of(index):
        return pl.ds(pl.multiple_of(index // 2 * share, share), share)

    def place_of(index):
        return pl.ds(pl.multiple_of(side * half + index // 2 * share, share), share)

    def weight_place(ref, own_ref, origin):
        count, rows = own_ref.shape[0] // 2, own_ref.shape[1]
        return ref.at[pl.ds(side * count, count), pl.ds(pl.multiple_of(origin * rows, rows), rows)]

    def send_weights(ref, own_ref, slot):
        mine = own_ref.at[pl.ds(side * (own_ref.shape[0] // 2), own_ref.shape[0] // 2)]
        return [
            push(mine, weight_place(ref, own_ref, me), (s5, r5), slot + step - 1, "dp", to)
            for step, to, _ in owners
        ]

    def relay_weights(ref, own_ref, copies, slot):
        relays = []
        for copy, (step, _, origin) in zip(copies, owners):
            copy.wait()
            place = weight_place(ref, own_ref, origin)
            relays.append(push(place, place, (s6, r6), slot + step - 1, "vocab", near))
        return relays

    first = push(x_ref.at[:, half_of(1 - side)], near_ref, (s0, r0), 0, "vocab", near)
    attn_copies = send_weights(attn_out_ref, attn_ref, 0)
    for ref, own_ref in ((attn_out_ref, attn_ref), (ffn_out_ref, ffn_ref)):
        rows = own_ref.shape[1]
        ref[:, pl.ds(pl.multiple_of(me * rows, rows), rows), :] = own_ref[...]
    first.wait()
    near_ref[...] += x_ref[:, half_of(side)]
    copies = [
        push(near_ref.at[:, share_of(to)], parts_ref.at[slot], (s1, r1), slot, "vocab", to)
        for slot, to, _ in others
    ]
    for copy in copies:
        copy.wait()
    total = near_ref[:, share_of(here)]
    for slot, _, _ in others:
        total = total + parts_ref[slot]
    blocks_ref[...] = total
    copies = [
        push(
            blocks_ref.at[to],
            row_ref.at[me, place_of(here)],
            (s2, r2),
            step - 1,
            "dp",
            to,
        )
        for step, to, _ in owners
    ]
    row_ref[me, place_of(here)] = blocks_ref[me]
    for copy in copies:
        copy.wait()
    ffn_copies = send_weights(ffn_out_ref, ffn_ref, len(owners))
    mine = row_ref.at[:, place_of(here)]
    copies = [push(mine, mine, (s3, r3), slot, "vocab", to) for slot, to, _ in others]
    close = [push(mine, mine, (s4, r4), 0, "vocab", near)]
    for copy, (slot, _, origin) in zip(copies, others):
        copy.wait()
        theirs = row_ref.at[:, place_of(origin)]
        close.append(push(theirs, theirs, (s4, r4), slot + 1, "vocab", near))
    close += relay_weights(attn_out_ref, attn_ref, attn_copies, 0)
    for copy in close[: pairs]:
        copy.wait()
    for owner in range(count):
        band = slice(owner * columns, (owner + 1) * columns)
        out_ref[:, band] = row_ref[owner].astype(jnp.float32) * scale + place_ref[:, band]
    close += relay_weights(ffn_out_ref, ffn_ref, ffn_copies, len(owners))
    for copy in close[pairs:]:
        copy.wait()


def gather_tokens(x, places, attn, ffn, scale, collective_id):
    owners, pairs = lax.axis_size("dp"), lax.axis_size("vocab") // 2
    _, length, columns = x.shape
    half = length // 2
    width = owners * columns
    whole = [low(w.shape[0], owners * w.shape[1], width) for w in (attn, ffn)]
    return talk(
        partial(token_kernel, scale),
        (full(length, width), *whole),
        collective_id,
        x,
        places,
        attn,
        ffn,
        scratch=[
            pltpu.VMEM((owners, half, columns), x.dtype),
            pltpu.VMEM((pairs - 1, owners, half // pairs, columns), x.dtype),
            pltpu.VMEM((owners, half // pairs, columns), x.dtype),
            pltpu.VMEM((owners, length, columns), x.dtype),
        ]
        + sem_pair(1)
        + sem_pair(pairs - 1)
        + sem_pair(owners - 1)
        + sem_pair(pairs - 1)
        + sem_pair(pairs)
        + sem_pair(2 * owners - 2)
        + sem_pair(2 * owners - 2),
        microseconds=50,
    )


def sinusoid(length, model_width):
    places = np.arange(length, dtype=np.float32)[:, None]
    halves = np.arange(model_width // 2, dtype=np.float32)[None, :]
    angles = places * np.exp(halves * np.float32(-2.0 * math.log(10000.0) / model_width))
    angles = angles.astype(np.float64)
    return (
        np.stack([np.sin(angles), np.cos(angles)], axis=-1)
        .reshape(length, model_width)
        .astype(np.float32)
    )


def one_hot(ids, columns):
    return (ids[:, None] == columns[None, :]).astype(jnp.bfloat16)


def pick_weights(target_seg, pick_rows):
    sentence = jnp.take(target_seg, pick_rows, axis=0)
    return jnp.sum((sentence[:, None] == sentence[None, :]).astype(jnp.float32), axis=1)


def combine_stats(tops, totals, chosen):
    top = jnp.max(tops, axis=0)
    return top, jnp.sum(totals * jnp.exp(tops - top), axis=0), jnp.sum(chosen, axis=0)


def adam_direction(moment, second):
    return moment / (1.0 - beta_one**STEP) / (jnp.sqrt(second / (1.0 - beta_two**STEP)) + adam_eps)


def adam_update(weight, grad_item, moment, second, step_rate, decay_weight):
    moment = beta_one * moment + (1.0 - beta_one) * grad_item
    second = beta_two * second + (1.0 - beta_two) * grad_item * grad_item
    return (
        weight - step_rate * (adam_direction(moment, second) + decay_weight * weight),
        moment,
        second,
    )


def after(array, number):
    return array + jnp.where(jnp.isnan(number), 1, 0).astype(array.dtype)


def body(
    src_ids,
    src_seg,
    tgt_ids,
    tgt_seg,
    pick_pos,
    pick_label,
    attn_w,
    attn_m,
    attn_v,
    ffn_w,
    ffn_m,
    ffn_v,
    soap_basis,
    soap_stats,
    norm_p,
    norm_m,
    norm_v,
    embedding,
    embed_m,
    embed_v,
):
    owners, replicas = lax.axis_size("dp"), lax.axis_size("vocab")
    replica = lax.axis_index("vocab")
    own_table = embedding.astype(jnp.bfloat16)
    own_norms = jnp.pad(norm_p.astype(jnp.bfloat16).astype(jnp.float32), ((0, 2), (0, 0)))
    all_ids, norm_rows = gather_small("dp", 1, jnp.concatenate([src_ids, tgt_ids]), own_norms)
    norm_rows = jnp.swapaxes(norm_rows, 0, 1).reshape(16, -1)
    norms = [jnp.stack([norm_rows[k], norm_rows[7 + k]]) for k in range(7)]
    vocab_count, width = embedding.shape[0], attn_w.shape[2]
    columns = replica * vocab_count + jnp.arange(vocab_count)
    source, source_seg, target, target_seg = (src_ids[0], src_seg[0], tgt_ids[0], tgt_seg[0])
    pick_rows, labels = (pick_pos[0], pick_label[0])
    length = source.shape[0]
    embed_scale = math.sqrt(width)
    half = vocab_count // 2
    halves = jnp.arange(half)
    paired = jnp.concatenate([own_table[:half], own_table[half:]], axis=1)

    def paired_places(ids):
        place = ids - replica * vocab_count
        inside = (place >= 0) & (place < vocab_count)
        return jnp.where(inside, place % half, -1), place < half

    def look_up(ids):
        place, left = paired_places(ids)
        wide = lax.dot_general(one_hot(place, halves), paired, (((1,), (0,)), ((), ())))
        return jnp.where(left[:, None], wide[:, :paired.shape[1] // 2], wide[:, paired.shape[1] // 2 :])

    source_part, target_part = (look_up(all_ids[:, k].reshape(-1)) for k in (0, 1))
    positional = sinusoid(length, width)
    enc_in, enc_attn_w, enc_ffn_w = gather_tokens(
        source_part.reshape(owners, length, -1),
        positional,
        attn_w[0:4].astype(jnp.bfloat16),
        ffn_w[0:2].astype(jnp.bfloat16),
        embed_scale,
        2,
    )
    target_part, _ = lax.optimization_barrier((target_part, enc_in))
    target_sum = lax.psum(target_part, "vocab")
    enc_mid, enc_attn = attn_forward(
        enc_in, norms[0], ((enc_attn_w,), 0, 0), source_seg, source_seg, None, False
    )
    self_w, cross_w, dec_ffn_w, ready = late_weights(attn_w[4:], ffn_w[2:], enc_in, enc_mid)
    table_low = lax.all_gather(after(own_table, ready), "dp", axis=1, tiled=True)
    enc_out, encoded, enc_ffn = ffn_forward(enc_mid, norms[1], norms[2], ((enc_ffn_w,), 0, 0))
    target_rows = swap_owners(target_sum.reshape(owners, length, -1), 3)
    target_rows = jnp.swapaxes(target_rows, 0, 1).reshape(length, -1).astype(jnp.float32)
    dec_in = target_rows * embed_scale + positional
    dec_mid, dec_self = attn_forward(
        dec_in, norms[3], self_w, target_seg, target_seg, None, True
    )
    dec_late, dec_cross = attn_forward(
        dec_mid, norms[4], cross_w, target_seg, source_seg, encoded, False
    )
    dec_out, final_low, dec_ffn = ffn_forward(dec_late, norms[5], norms[6], dec_ffn_w)

    chosen_rows = one_hot(pick_rows, jnp.arange(length))
    picked = dot_dims(chosen_rows, final_low, 1, 0).astype(jnp.bfloat16)
    logits = dot_dims(picked, table_low, 1, 1)
    row_top = jnp.max(logits, axis=-1)
    row_total = jnp.sum(jnp.exp(logits - row_top[:, None]), axis=-1)
    label_hit = labels[:, None] == columns[None, :]
    chosen = jnp.sum(jnp.where(label_hit, logits, 0.0), axis=-1)
    seen = jnp.pad(jnp.stack([row_top, row_total, chosen]), ((0, 5), (0, 0)))
    (seen,) = gather_small("vocab", 4, seen)
    row_top, row_total, chosen = combine_stats(seen[:, 0], seen[:, 1], seen[:, 2])
    log_total = row_top + jnp.log(row_total)
    weight = 1.0 / pick_weights(target_seg, pick_rows)
    loss_part = jnp.sum((log_total - chosen) * weight)
    count_part = (target_seg[-1] + 1).astype(jnp.float32)
    grad_logits = (
        weight[:, None] * (jnp.exp(logits - log_total[:, None]) - label_hit.astype(jnp.float32))
    ).astype(jnp.bfloat16)
    grad_picked = sum_vocab(dot_dims(grad_logits, table_low, 1, 0).astype(jnp.bfloat16), 5)
    grad_table = [
        dot_dims(grad_logits, part, 0, 0).astype(jnp.bfloat16)
        for part in jnp.split(picked, owners, axis=1)
    ]
    table_parts = jnp.stack(grad_table)
    grad_table = lax.psum_scatter(table_parts, "dp", scatter_dimension=0, tiled=False)
    grad_final = dot_dims(chosen_rows, grad_picked, 0, 0)

    picks = share_selector(width, owners, replicas, replica, width)
    hidden = ffn_w.shape[1] * owners
    hidden_picks = share_selector(hidden, owners, replicas, replica, 512)
    norm_grads = [None] * 7
    grad, norm_grads[6], norm_grads[5], *ffn_blocks = ffn_backward(
        grad_final, dec_ffn, hidden_picks, owners, before=(table_parts,)
    )
    grad, norm_grads[4], block, grad_encoded = attn_backward(grad, dec_cross, picks, owners, None)
    early = lax.psum_scatter(
        jnp.concatenate([block, *ffn_blocks], axis=1), "dp", scatter_dimension=0, tiled=False
    )
    grad, norm_grads[3], self_block, target_rows = attn_backward(
        grad, dec_self, picks, owners, embed_scale
    )
    grad, norm_grads[2], norm_grads[1], *ffn_blocks = ffn_backward(
        grad_encoded, enc_ffn, hidden_picks, owners, before=(grad_table, grad)
    )
    early_sum = after(early, grad[0, 0])
    early = lax.all_gather(early_sum, "vocab")
    grad, norm_grads[0], block, source_rows = attn_backward(
        grad, enc_attn, picks, owners, embed_scale, before=(early_sum,)
    )
    norm_grad = jnp.stack([after(part, early[0, 0, 0]) for part in norm_grads])
    norm_grad = jnp.concatenate([norm_grad[:, 0], norm_grad[:, 1], jnp.zeros((2, width))], axis=0)
    norm_grad = jnp.swapaxes(norm_grad.reshape(16, owners, -1), 0, 1)
    late, source_rows, target_rows, norm_grad = share_gradients(
        [block, self_block, *ffn_blocks], [source_rows, target_rows, norm_grad], 7, (early,)
    )
    g_norm = jnp.sum(norm_grad, axis=0)[:14]
    token_grads = jnp.concatenate([source_rows, target_rows], axis=1).reshape(
        owners * 2 * length, -1
    )
    place, left = paired_places(all_ids.reshape(-1))
    left = left[:, None]
    token_grads = jnp.concatenate(
        [jnp.where(left, token_grads, 0), jnp.where(left, 0, token_grads)], axis=1
    )
    g_paired = dot_dims(one_hot(place, halves), token_grads, 0, 0)
    g_embed = grad_table.astype(jnp.float32) + jnp.concatenate(
        jnp.split(g_paired, 2, axis=1), axis=0
    )

    def by_matrix(shared, count):
        blocks = jnp.swapaxes(shared.reshape(replicas, count, -1, width), 0, 1)
        return blocks.reshape(count, -1, width)

    early = by_matrix(early, 3)
    g_attn = [by_matrix(part, 4) for part in (late[0], late[1], early[0])]
    g_attn = jnp.concatenate(g_attn).astype(jnp.float32)
    g_ffn = jnp.concatenate([late[2:].reshape(2, -1, width), early[1:]])

    matrix = replica // 2
    own_grad = lax.dynamic_index_in_dim(g_ffn, matrix, 0, keepdims=False)
    own_products = dot_dims(own_grad, own_grad, 0, 0)
    g_ffn_low, g_ffn = g_ffn, g_ffn.astype(jnp.float32)
    first_copy = (replica == 0).astype(jnp.float32)
    layer_sq = jnp.sum(g_attn * g_attn) + jnp.sum(g_ffn * g_ffn) + jnp.sum(g_norm * g_norm)
    raw_squares = jnp.sum(g_embed * g_embed) + first_copy * layer_sq
    few = jnp.stack([first_copy * loss_part, first_copy * count_part, raw_squares])
    few = jnp.broadcast_to(jnp.pad(few, (0, 5))[:, None], (8, 128))
    own_products, few = sum_tail(own_products, few, 8)
    loss_sum, sentences, squares = few[0, 0], few[1, 0], few[2, 0]
    grad_norm = jnp.sqrt(squares) / sentences
    factor = jnp.minimum(1.0, clip_limit / (grad_norm + norm_eps)) / sentences
    g_attn, g_norm, g_embed = (
        g_attn * factor,
        g_norm * factor,
        g_embed * factor,
    )

    def all_matrices(own):
        rows = own.shape[0] // 2
        half = lax.dynamic_slice_in_dim(own.astype(jnp.bfloat16), replica % 2 * rows, rows, 0)
        return lax.all_gather(half, "vocab").reshape(4, 2 * rows, -1).astype(jnp.float32)

    all_products = all_matrices(own_products)
    new_stats = stat_decay * soap_stats + (1.0 - stat_decay) * (factor * factor) * (
        all_products
    )
    own_stat = stat_decay * lax.dynamic_index_in_dim(soap_stats, matrix, 0, keepdims=False) + (
        1.0 - stat_decay
    ) * (factor * factor) * own_products
    own_basis = renew_basis(own_stat, lax.dynamic_index_in_dim(soap_basis, matrix, 0, keepdims=False))
    new_basis = all_matrices(own_basis)

    new_attn, m_attn, v_attn = adam_update(attn_w, g_attn, attn_m, attn_v, rate_matrix, decay_rate)
    new_norm, m_norm, v_norm = adam_update(norm_p, g_norm, norm_m, norm_v, rate_vector, 0.0)
    new_embed, m_embed, v_embed = adam_update(
        embedding, g_embed, embed_m, embed_v, rate_matrix, decay_rate
    )
    new_ffn, m_ffn, v_ffn = update_rotated(factor, g_ffn_low, soap_basis, ffn_w, ffn_m, ffn_v)
    return (
        loss_sum,
        sentences,
        grad_norm,
        new_attn,
        m_attn,
        v_attn,
        new_ffn,
        m_ffn,
        v_ffn,
        new_basis,
        new_stats,
        new_norm,
        m_norm,
        v_norm,
        new_embed,
        m_embed,
        v_embed,
    )


def solution(mesh):
    placed = (
        P("dp", None),
        P("dp", None),
        P("dp", None),
        P("dp", None),
        P("dp", None),
        P("dp", None),
        P(None, "dp", None),
        P(None, "dp", None),
        P(None, "dp", None),
        P(None, "dp", None),
        P(None, "dp", None),
        P(None, "dp", None),
        P(),
        P(),
        P(None, "dp"),
        P(None, "dp"),
        P(None, "dp"),
        P("vocab", "dp"),
        P("vocab", "dp"),
        P("vocab", "dp"),
    )
    return jax.shard_map(
        body,
        mesh=mesh,
        in_specs=placed,
        out_specs=(
            P(),
            P(),
            P(),
            P(None, "dp", None),
            P(None, "dp", None),
            P(None, "dp", None),
            P(None, "dp", None),
            P(None, "dp", None),
            P(None, "dp", None),
            P(),
            P(),
            P(None, "dp"),
            P(None, "dp"),
            P(None, "dp"),
            P("vocab", "dp"),
            P("vocab", "dp"),
            P("vocab", "dp"),
        ),
        check_vma=False,
    )
```

```python
from functools import partial
import math

import jax
import jax.numpy as jnp
import numpy as np
from jax import lax
from jax.experimental import pallas as pl
from jax.experimental.pallas import tpu as pltpu
from jax.sharding import PartitionSpec as P

HEADS = 8
STEP = 10
TILE = 128

highest = lax.Precision.HIGHEST
beta_one = 0.9
beta_two = 0.999
adam_eps = 1e-08
decay_rate = 0.01
rate_matrix = 0.03
rate_vector = 0.3
clip_limit = 1.0
stat_decay = 0.95
norm_eps = 1e-06
masked = -1e30
log_two_e = math.log2(math.e)
vmem = pl.BlockSpec(memory_space=pltpu.VMEM)
smem = pl.BlockSpec(memory_space=pltpu.SMEM)
mesh_ids = pl.DeviceIdType.MESH


def dot_dims(left, right, left_dim, right_dim):
    return lax.dot_general(
        left, right, (((left_dim,), (right_dim,)), ((), ())), preferred_element_type=jnp.float32
    )


def dot_exact(left, right, left_dim, right_dim):
    return lax.dot_general(
        left,
        right,
        (((left_dim,), (right_dim,)), ((), ())),
        precision=highest,
        preferred_element_type=jnp.float32,
    )


def cost_of(microseconds):
    return pl.CostEstimate(flops=microseconds * 10**9, bytes_accessed=0, transcendentals=0)


def call(kernel, outs, *args, scratch=(), smem_args=0, microseconds=5, before=()):
    def body(*refs):
        kernel(*refs[: len(args)], *refs[len(args) + len(before) :])

    return pl.pallas_call(
        body,
        out_shape=outs,
        in_specs=[vmem] * (len(args) - smem_args)
        + [smem] * smem_args
        + [pl.BlockSpec(memory_space=pl.ANY)] * len(before),
        out_specs=jax.tree.map(lambda _: vmem, outs),
        scratch_shapes=list(scratch),
        compiler_params=pltpu.CompilerParams(vmem_limit_bytes=56 * 2**20),
        cost_estimate=cost_of(microseconds),
    )(*args, *before)


def low(*shape):
    return jax.ShapeDtypeStruct(shape, jnp.bfloat16)


def full(*shape):
    return jax.ShapeDtypeStruct(shape, jnp.float32)


def norm_parts(values):
    centre = values - jnp.mean(values, axis=-1, keepdims=True)
    spread = jnp.mean(centre * centre, axis=-1, keepdims=True)
    root = lax.rsqrt(spread + norm_eps)
    return centre * root, root


def norm_forward(values, ln_ref):
    return norm_parts(values)[0] * ln_ref[0:1, :] + ln_ref[1:2, :]


def norm_backward(grad, values, ln_ref, ln_grad_ref):
    normed, root = norm_parts(values)
    ln_grad_ref[0:1, :] = jnp.sum(grad * normed, axis=0, keepdims=True)
    ln_grad_ref[1:2, :] = jnp.sum(grad, axis=0, keepdims=True)
    inner = grad * ln_ref[0:1, :]
    return root * (
        inner
        - jnp.mean(inner, axis=-1, keepdims=True)
        - normed * jnp.mean(inner * normed, axis=-1, keepdims=True)
    )


def at_tile(index, size):
    return pl.ds(pl.multiple_of(index * size, size), size)


def tile_mask(segq_ref, segk_ref, qi, ki, tile_q, tile_k, causal):
    seg_k = segk_ref[at_tile(ki, tile_k), :]
    seg_k = jnp.concatenate([seg_k] * (tile_q // TILE), axis=1)
    allowed = seg_k == segq_ref[:, at_tile(qi, tile_q)]
    if causal:
        shape = (tile_k, tile_q)
        ahead = lax.broadcasted_iota(jnp.int32, shape, 0) - lax.broadcasted_iota(
            jnp.int32, shape, 1
        )
        allowed = allowed & (ahead <= qi * tile_q - ki * tile_k)
    return allowed


def for_tiles(length, tile_q, tile_k, edge_ref, causal, step):
    count_q, count_k = length // tile_q, length // tile_k
    per_q, per_k = tile_q // TILE, tile_k // TILE

    def one(pair, carry):
        qi, ki = pair // count_k, lax.rem(pair, count_k)
        live = (edge_ref[0, qi * per_q] <= edge_ref[3, (ki + 1) * per_k - 1]) & (
            edge_ref[2, ki * per_k] <= edge_ref[1, (qi + 1) * per_q - 1]
        )
        if causal:
            live = live & (ki * tile_k < (qi + 1) * tile_q)

        @pl.when(live)
        def _():
            step(qi, ki)

        return carry

    lax.fori_loop(0, count_q * count_k, one, 0)


def tile_edges(seg_q, seg_k):
    last = TILE - 1
    return jnp.stack([seg_q[::TILE], seg_q[last::TILE], seg_k[::TILE], seg_k[last::TILE]])


def share_selector(rows, owners, shares, share, count):
    size = rows // (owners * shares)
    index = jnp.arange(count // shares)
    picked = index // size * (rows // owners) + share * size + index % size
    return (picked[:, None] == jnp.arange(count)[None, :]).astype(jnp.bfloat16)


def lay_weights(w_ref, piece_refs, part, first):
    own = piece_refs[0]
    matrices, rows = w_ref.shape[0], w_ref.shape[1] // 4
    half = own.shape[0] // 2
    me, side = lax.axis_index("dp"), lax.rem(lax.axis_index("vocab"), 2)
    for m in range(matrices):
        span = slice(first + m * rows, first + (m + 1) * rows)
        w_ref[m, pl.ds(pl.multiple_of(me * rows, rows), rows), :] = own[
            part * half + span.start : part * half + span.stop, :
        ]
        for k in range(1, 4):
            place = pl.ds(pl.multiple_of((me ^ k) * rows, rows), rows)

            @pl.when(side == part)
            def _():
                w_ref[m, place, :] = piece_refs[k][span, :]

            @pl.when(side != part)
            def _():
                w_ref[m, place, :] = piece_refs[k + 3][span, :]


def flip_sites(part, axis, bit):
    return lax.ppermute(part, axis, [(s, s ^ bit) for s in range(lax.axis_size(axis))])


def late_weights(attn, ffn, after, later):
    owners = lax.axis_size("dp")
    width = attn.shape[-1]
    attn, ffn = attn.astype(jnp.bfloat16), ffn.astype(jnp.bfloat16)
    if owners != 4:
        attn, ffn = (lax.all_gather(part, "dp", axis=1, tiled=True) for part in (attn, ffn))
        return ((attn[:4],), 0, 0), ((attn[4:],), 0, 0), ((ffn,), 0, 0), ffn[0, 0, 0]
    halves = [
        jnp.concatenate([attn[4 * k : 4 * k + 4].reshape(-1, width), ffn[k]]) for k in range(2)
    ]
    own = jnp.concatenate(halves)
    side = lax.axis_index("vocab") % 2
    mine = jnp.where(side == 0, halves[0], halves[1])
    mine, _ = lax.optimization_barrier((mine, after))
    got = [flip_sites(mine, "dp", k) for k in range(1, 4)]
    *got, _ = lax.optimization_barrier((*got, later))
    swapped = [flip_sites(part, "vocab", 1) for part in got]
    pieces = (own, *got, *swapped)
    rows = 4 * attn.shape[1]
    return (pieces, 0, 0), (pieces, 1, 0), (pieces, None, rows), swapped[-1][0, 0]


def attn_forward_kernel(causal, cross, pieces, part, first, *refs):
    refs = list(refs)
    x_ref, ln_ref, segq_ref, segk_ref = refs[:4]
    refs = refs[4:]
    key_ref = refs.pop(0) if cross else None
    piece_refs, refs = refs[:pieces], refs[pieces:]
    edge_ref, out_ref, a_ref, qt_ref, kt_ref, vt_ref, ot_ref, lse_ref = refs[:8]
    refs = refs[8:]
    w_ref = piece_refs[0]
    if pieces > 1:
        w_ref = refs.pop(0)
        lay_weights(w_ref, piece_refs, part, first)
    top_ref, sum_ref, acc_ref = refs
    length, width = x_ref.shape
    head_size = width // HEADS
    a_ref[...] = norm_forward(x_ref[...], ln_ref).astype(jnp.bfloat16)
    key_in = key_ref if cross else a_ref
    qt_ref[...] = dot_dims(a_ref[...], w_ref[0], 1, 0).astype(jnp.bfloat16).T
    kt_ref[...] = dot_dims(key_in[...], w_ref[1], 1, 0).astype(jnp.bfloat16).T
    vt_ref[...] = dot_dims(key_in[...], w_ref[2], 1, 0).astype(jnp.bfloat16).T
    top_ref[...] = jnp.full(top_ref.shape, masked, jnp.float32)
    sum_ref[...] = jnp.zeros(sum_ref.shape, jnp.float32)
    acc_ref[...] = jnp.zeros(acc_ref.shape, jnp.float32)
    scale = log_two_e / math.sqrt(head_size)
    bands = [slice(h * head_size, (h + 1) * head_size) for h in range(HEADS)]

    def step(qi, ki):
        q_at, k_at = at_tile(qi, 256), at_tile(ki, 256)
        allowed = tile_mask(segq_ref, segk_ref, qi, ki, 256, 256, causal)
        scores = [dot_dims(kt_ref[band, k_at], qt_ref[band, q_at], 0, 0) * scale for band in bands]
        scores = [jnp.where(allowed, part, masked) for part in scores]
        top = top_ref[:, q_at]
        new_top = jnp.maximum(
            top,
            jnp.concatenate([jnp.max(part, axis=0, keepdims=True) for part in scores], axis=0),
        )
        fade = jnp.exp2(top - new_top)
        parts = [jnp.exp2(scores[h] - new_top[h : h + 1]) for h in range(HEADS)]
        top_ref[:, q_at] = new_top
        sum_ref[:, q_at] = sum_ref[:, q_at] * fade + jnp.concatenate(
            [jnp.sum(part, axis=0, keepdims=True) for part in parts], axis=0
        )
        mixed = [
            dot_dims(vt_ref[bands[h], k_at], parts[h].astype(jnp.bfloat16), 1, 0)
            for h in range(HEADS)
        ]
        acc = acc_ref[:, q_at]
        acc_ref[:, q_at] = jnp.concatenate(
            [acc[bands[h]] * fade[h : h + 1] + mixed[h] for h in range(HEADS)], axis=0
        )

    for_tiles(length, 256, 256, edge_ref, causal, step)
    lse_ref[...] = top_ref[...] + jnp.log2(sum_ref[...])
    for h in range(HEADS):
        ot_ref[bands[h], :] = (acc_ref[bands[h], :] / sum_ref[h : h + 1, :]).astype(jnp.bfloat16)
    out_ref[...] = x_ref[...] + dot_dims(ot_ref[...], w_ref[3], 0, 0)


def attn_forward(x, ln, weights, seg_q, seg_k, key_in, causal):
    length, width = x.shape
    weights, part, first = weights
    cross = key_in is not None
    segs = (seg_q[None, :], jnp.broadcast_to(seg_k[:, None], (length, TILE)))
    edges = tile_edges(seg_q, seg_k)
    args = (x, ln, *segs) + ((key_in,) if cross else ()) + (*weights, edges)
    outs = (full(length, width), low(length, width)) + (low(width, length),) * 4
    outs = outs + (full(HEADS, length),)
    if len(weights) > 1:
        outs = outs + (low(4, width, width),)
    out, normed, *stored = call(
        partial(attn_forward_kernel, causal, cross, len(weights), part, first),
        outs,
        *args,
        scratch=[
            pltpu.VMEM((HEADS, length), jnp.float32),
            pltpu.VMEM((HEADS, length), jnp.float32),
            pltpu.VMEM((width, length), jnp.float32),
        ],
        smem_args=1,
        microseconds=20,
    )
    whole = stored.pop() if len(weights) > 1 else weights[0]
    return out, (x, ln, whole, segs, edges, causal, key_in, normed, stored)


def attn_backward_kernel(causal, cross, row_scale, *refs):
    g_ref, x_ref, ln_ref, w_ref, pick_ref, segq_ref, segk_ref, a_ref = refs[:8]
    refs = list(refs[8:])
    key_ref = refs.pop(0) if cross else a_ref
    qt_ref, kt_ref, vt_ref, ot_ref, lse_ref, edge_ref, out_ref, ln_grad_ref, block_ref, extra_ref = refs[:10]
    low_ref, gq_ref, gk_ref, gv_ref, got_ref, delta_ref, gqt_ref, gkt_ref, gvt_ref = refs[10:]
    length, width = x_ref.shape
    head_size = width // HEADS
    low_ref[...] = g_ref[...].astype(jnp.bfloat16)
    got_ref[...] = dot_dims(low_ref[...], w_ref[3], 1, 1).astype(jnp.bfloat16).T
    bands = [slice(h * head_size, (h + 1) * head_size) for h in range(HEADS)]
    for h in range(HEADS):
        delta_ref[h : h + 1, :] = jnp.sum(
            got_ref[bands[h], :].astype(jnp.float32) * ot_ref[bands[h], :].astype(jnp.float32),
            axis=0,
            keepdims=True,
        )
    for ref in (gqt_ref, gkt_ref, gvt_ref):
        ref[...] = jnp.zeros(ref.shape, jnp.float32)
    scale = log_two_e / math.sqrt(head_size)
    back = 1.0 / math.sqrt(head_size)

    def step(qi, ki):
        q_at, k_at = at_tile(qi, 256), at_tile(ki, TILE)
        allowed = tile_mask(segq_ref, segk_ref, qi, ki, 256, TILE, causal)
        scores = [dot_dims(kt_ref[band, k_at], qt_ref[band, q_at], 0, 0) for band in bands]
        grads = [dot_dims(vt_ref[band, k_at], got_ref[band, q_at], 0, 0) for band in bands]
        parts = [
            jnp.where(allowed, jnp.exp2(scores[h] * scale - lse_ref[h : h + 1, q_at]), 0.0)
            for h in range(HEADS)
        ]
        grads = [parts[h] * (grads[h] - delta_ref[h : h + 1, q_at]) for h in range(HEADS)]
        parts_t = [part.T.astype(jnp.bfloat16) for part in parts]
        grads_t = [part.T.astype(jnp.bfloat16) for part in grads]
        grads = [part.astype(jnp.bfloat16) for part in grads]
        for ref, place, terms in (
            (gvt_ref, k_at, [dot_dims(got_ref[bands[h], q_at], parts_t[h], 1, 0) for h in range(HEADS)]),
            (gkt_ref, k_at, [dot_dims(qt_ref[bands[h], q_at], grads_t[h], 1, 0) for h in range(HEADS)]),
            (gqt_ref, q_at, [dot_dims(kt_ref[bands[h], k_at], grads[h], 1, 0) for h in range(HEADS)]),
        ):
            ref[:, place] += jnp.concatenate(terms, axis=0)

    for_tiles(length, 256, TILE, edge_ref, causal, step)
    gq_ref[...] = (gqt_ref[...] * back).astype(jnp.bfloat16).T
    gk_ref[...] = (gkt_ref[...] * back).astype(jnp.bfloat16).T
    gv_ref[...] = gvt_ref[...].astype(jnp.bfloat16).T
    from_query = dot_dims(gq_ref[...], w_ref[0], 1, 1)
    from_keys = dot_dims(gk_ref[...], w_ref[1], 1, 1) + dot_dims(gv_ref[...], w_ref[2], 1, 1)
    if cross:
        extra_ref[...] = from_keys
    else:
        from_query = from_query + from_keys
    total = g_ref[...] + norm_backward(from_query, x_ref[...], ln_ref, ln_grad_ref)
    out_ref[...] = total
    owners = block_ref.shape[0]
    if not cross:
        columns = width // owners
        for owner in range(owners):
            band = slice(owner * columns, (owner + 1) * columns)
            extra_ref[owner] = (total[:, band] * row_scale).astype(jnp.bfloat16)
    own_a = dot_dims(pick_ref[...], a_ref[...], 1, 1).astype(jnp.bfloat16)
    own_key = dot_dims(pick_ref[...], key_ref[...], 1, 1).astype(jnp.bfloat16) if cross else own_a
    own_o = dot_dims(pick_ref[...], ot_ref[...], 1, 0).astype(jnp.bfloat16)
    size = own_a.shape[0] // owners
    products = ((own_a, gq_ref), (own_key, gk_ref), (own_key, gv_ref), (own_o, low_ref))
    for m, (rows, right_ref) in enumerate(products):
        product = dot_dims(rows, right_ref[...], 1, 0).astype(jnp.bfloat16)
        for owner in range(owners):
            block_ref[owner, m * size : (m + 1) * size, :] = product[owner * size : (owner + 1) * size]


def attn_backward(grad, stored, picks, owners, row_scale, before=()):
    x, ln, weights, segs, edges, causal, key_in, normed, kept = stored
    length, width = x.shape
    cross = key_in is not None
    extra = full(length, width) if cross else low(owners, length, width // owners)
    outs = (full(length, width), full(2, width), low(owners, 4 * picks.shape[0] // owners, width), extra)
    keys = (key_in,) if cross else ()
    return call(
        partial(attn_backward_kernel, causal, cross, row_scale),
        outs,
        grad,
        x,
        ln,
        weights,
        picks,
        *segs,
        normed,
        *keys,
        *kept,
        edges,
        scratch=[pltpu.VMEM((length, width), jnp.bfloat16)] * 4
        + [pltpu.VMEM((width, length), jnp.bfloat16), pltpu.VMEM((HEADS, length), jnp.float32)]
        + [pltpu.VMEM((width, length), jnp.float32)] * 3,
        smem_args=1,
        microseconds=25,
        before=before,
    )


def gelu_parts(hidden):
    root = math.sqrt(2.0 / math.pi)
    square = hidden * hidden
    bend = jnp.tanh(root * hidden * (1.0 + 0.044715 * square))
    value = 0.5 * hidden * (1.0 + bend)
    slope = 0.5 * (1.0 + bend) + 0.5 * hidden * (1.0 - bend * bend) * root * (
        1.0 + 3.0 * 0.044715 * square
    )
    return value, slope


def ffn_forward_kernel(chunk, pieces, first, x_ref, ln_ref, next_ref, *refs):
    piece_refs, (out_ref, a_ref, after_ref, *refs) = refs[:pieces], refs[pieces:]
    w_ref = piece_refs[0]
    if pieces > 1:
        (w_ref,) = refs
        for part in range(2):
            lay_weights(w_ref.at[part : part + 1], piece_refs, part, first)
    w_in_ref, w_out_ref = w_ref.at[0], w_ref.at[1]
    a_ref[...] = norm_forward(x_ref[...], ln_ref).astype(jnp.bfloat16)
    total = x_ref[...]
    for start in range(0, w_in_ref.shape[0], chunk):
        part = slice(start, start + chunk)
        hidden = dot_dims(a_ref[...], w_in_ref[part, :], 1, 1)
        active = gelu_parts(hidden)[0].astype(jnp.bfloat16)
        total = total + dot_dims(active, w_out_ref[part, :], 1, 0)
    out_ref[...] = total
    after_ref[...] = norm_forward(total, next_ref).astype(after_ref.dtype)


def ffn_forward(x, ln, ln_next, weights):
    length, width = x.shape
    weights, _, first = weights
    outs = (full(length, width), low(length, width), low(length, width))
    if len(weights) > 1:
        outs = outs + (low(2, 4 * (weights[0].shape[0] // 2 - first), width),)
    out, normed, after, *whole = call(
        partial(ffn_forward_kernel, 512, len(weights), first),
        outs,
        x,
        ln,
        ln_next,
        *weights,
        microseconds=12,
    )
    return out, after, (x, ln, whole[0] if whole else weights[0], normed, out, ln_next)


def ffn_backward_kernel(
    chunk, picked, after_ref, *refs
):
    if picked:
        place_ref, *refs = refs
        shape = (refs[0].shape[0], place_ref.shape[1])
        chosen = lax.broadcasted_iota(jnp.int32, shape, 0) == place_ref[...]
        after = dot_dims(chosen.astype(jnp.bfloat16), after_ref[...], 1, 0)
    else:
        after = after_ref[...]
    ffn_backward_rest(chunk, after, *refs)


def ffn_backward_rest(
    chunk, after, y_ref, next_ref, x_ref, ln_ref, a_ref, w_ref, pick_ref,
    out_ref, next_grad_ref, ln_grad_ref, in_ref, back_ref, low_ref, g_ref,
):
    w_in_ref, w_out_ref = w_ref.at[0], w_ref.at[1]
    g_ref[...] = norm_backward(after, y_ref[...], next_ref, next_grad_ref)
    low_ref[...] = g_ref[...].astype(jnp.bfloat16)
    total = jnp.zeros(g_ref.shape, jnp.float32)
    owners, size = in_ref.shape[:2]
    blocks = pick_ref.shape[0] // size
    for index in range(w_in_ref.shape[0] // chunk):
        part = slice(index * chunk, (index + 1) * chunk)
        hidden = dot_dims(a_ref[...], w_in_ref[part, :], 1, 1)
        value, slope = gelu_parts(hidden)
        grad = (dot_dims(low_ref[...], w_out_ref[part, :], 1, 1) * slope).astype(jnp.bfloat16)
        total = total + dot_dims(grad, w_in_ref[part, :], 1, 0)
        pairs = ((in_ref, grad, a_ref), (back_ref, value.astype(jnp.bfloat16), low_ref))
        for ref, left, right_ref in pairs:
            rows = dot_dims(pick_ref[...], left, 1, 1).astype(jnp.bfloat16)
            product = dot_dims(rows, right_ref[...], 1, 0).astype(jnp.bfloat16)
            for block in range(blocks):
                ref[index * blocks + block] = product[block * size : (block + 1) * size]
    out_ref[...] = g_ref[...] + norm_backward(total, x_ref[...], ln_ref, ln_grad_ref)


def ffn_backward(grad_after, stored, picks, owners, before=(), places=None):
    x, ln, weights, normed, out, ln_next = stored
    length, width = x.shape
    chunk = picks.shape[1]
    size = picks.shape[0] * weights.shape[1] // chunk // owners
    block = low(owners, size, width)
    return call(
        partial(ffn_backward_kernel, chunk, places is not None),
        (full(length, width), full(2, width), full(2, width), block, block),
        grad_after,
        *(() if places is None else (places[None, :],)),
        out,
        ln_next,
        x,
        ln,
        normed,
        weights,
        picks,
        scratch=[
            pltpu.VMEM((length, width), jnp.bfloat16),
            pltpu.VMEM((length, width), jnp.float32),
        ],
        microseconds=17,
        before=before,
    )


def loss_forward_kernel(chunks, final_ref, pick_ref, label_ref, table_ref, picked_ref, stat_ref, logit_ref):
    count, length = pick_ref.shape[0], final_ref.shape[0]
    places = lax.broadcasted_iota(jnp.int32, (count, length), 1)
    chosen = (places == pick_ref[...]).astype(jnp.bfloat16)
    picked_ref[...] = dot_dims(chosen, final_ref[...], 1, 0).astype(jnp.bfloat16)
    rows = table_ref.shape[0] // chunks
    top = jnp.full((1, count), masked, jnp.float32)
    label = jnp.zeros((1, count), jnp.float32)
    for index in range(chunks):
        span = slice(index * rows, (index + 1) * rows)
        logits = dot_dims(table_ref[span, :], picked_ref[...], 1, 1)
        logit_ref[span, :] = logits
        top = jnp.maximum(top, jnp.max(logits, axis=0, keepdims=True))
        hit = lax.broadcasted_iota(jnp.int32, logits.shape, 0) + index * rows == label_ref[...]
        label = label + jnp.sum(jnp.where(hit, logits, 0.0), axis=0, keepdims=True)
    total = jnp.zeros((1, count), jnp.float32)
    for index in range(chunks):
        span = slice(index * rows, (index + 1) * rows)
        total = total + jnp.sum(jnp.exp(logit_ref[span, :] - top), axis=0, keepdims=True)
    stat_ref[...] = jnp.concatenate([top, total, label, jnp.zeros((5, count), jnp.float32)], axis=0)


def loss_forward(final, pick_rows, labels, table):
    count, width = pick_rows.shape[0], final.shape[1]
    return call(
        partial(loss_forward_kernel, 8),
        (low(count, width), full(8, count)),
        final,
        pick_rows[:, None],
        labels[None, :],
        table,
        scratch=[pltpu.VMEM((table.shape[0], count), jnp.float32)],
        microseconds=6,
    )


def loss_backward_kernel(
    chunks, picked_ref, seen_ref, weight_ref, label_ref, table_ref, grad_ref, parts_ref, loss_ref
):
    tops, totals, labels = (
        jnp.concatenate([seen_ref[k, m : m + 1, :] for k in range(seen_ref.shape[0])], axis=0)
        for m in range(3)
    )
    top = jnp.max(tops, axis=0, keepdims=True)
    total = top + jnp.log(jnp.sum(totals * jnp.exp(tops - top), axis=0, keepdims=True))
    loss_ref[...] = (total - jnp.sum(labels, axis=0, keepdims=True)) * weight_ref[...]
    rows = table_ref.shape[0] // chunks
    columns = parts_ref.shape[2]
    grad = jnp.zeros(grad_ref.shape, jnp.float32)
    for index in range(chunks):
        span = slice(index * rows, (index + 1) * rows)
        logits = dot_dims(table_ref[span, :], picked_ref[...], 1, 1)
        hit = lax.broadcasted_iota(jnp.int32, logits.shape, 0) + index * rows == label_ref[...]
        slopes = weight_ref[...] * (jnp.exp(logits - total) - jnp.where(hit, 1.0, 0.0))
        slopes = slopes.astype(jnp.bfloat16)
        product = dot_dims(slopes, picked_ref[...], 1, 0).astype(jnp.bfloat16)
        for owner in range(parts_ref.shape[0]):
            parts_ref[owner, span, :] = product[:, owner * columns : (owner + 1) * columns]
        grad = grad + dot_dims(slopes, table_ref[span, :], 0, 0)
    grad_ref[...] = grad.astype(jnp.bfloat16)


def loss_backward(picked, seen, weight, labels, table, owners):
    count, width = picked.shape
    return call(
        partial(loss_backward_kernel, 8),
        (low(count, width), low(owners, table.shape[0], width // owners), full(1, count)),
        picked,
        seen,
        weight[None, :],
        labels[None, :],
        table,
        microseconds=8,
    )


def adam_parts(weight, grad, moment, second):
    moment = beta_one * moment + (1.0 - beta_one) * grad
    second = beta_two * second + (1.0 - beta_two) * grad * grad
    step = adam_direction(moment, second) + decay_rate * weight
    return weight - rate_matrix * step, moment, second


def update_kernel(*refs):
    factor_ref, basis_ref, *ins = refs[:14]
    outs = refs[14:]
    factor = factor_ref[0]
    for k in (0, 1):
        grad_ref, weight_ref, moment_ref, second_ref = ins[4 * k : 4 * k + 4]
        grad = grad_ref[...].astype(jnp.float32) * factor
        results = adam_parts(weight_ref[...], grad, moment_ref[...], second_ref[...])
        for ref, result in zip(outs[3 * k : 3 * k + 3], results):
            ref[...] = result
    g_ref, w_ref, m_ref, v_ref = ins[8:]
    new_w_ref, new_m_ref, new_v_ref = outs[6:]
    high = basis_ref[0].astype(jnp.bfloat16)
    rest = (basis_ref[0] - high.astype(jnp.float32)).astype(jnp.bfloat16)
    grad = g_ref[0]
    rotated = (dot_dims(grad, high, 1, 0) + dot_dims(grad, rest, 1, 0)) * factor
    moment = beta_one * m_ref[0] + (1.0 - beta_one) * rotated
    second = beta_two * v_ref[0] + (1.0 - beta_two) * rotated * rotated
    new_m_ref[0] = moment
    new_v_ref[0] = second
    step = adam_direction(moment, second)
    step_high = step.astype(jnp.bfloat16)
    step_rest = (step - step_high.astype(jnp.float32)).astype(jnp.bfloat16)
    back = (
        dot_dims(step_high, high, 1, 1)
        + dot_dims(step_high, rest, 1, 1)
        + dot_dims(step_rest, high, 1, 1)
    )
    new_w_ref[0] = w_ref[0] - rate_matrix * (back + decay_rate * w_ref[0])


def update_matrices(factor, bases, attn, table, ffn):
    def blocks(array):
        shape = (array.shape[0] // 4, *array.shape[1:])
        return pl.BlockSpec(shape, lambda k: (k,) + (0,) * (len(shape) - 1))

    arrays = (*attn, *table, *ffn)
    results = [part for group in (attn, table, ffn) for part in group[1:]]
    return pl.pallas_call(
        update_kernel,
        grid=(4,),
        out_shape=tuple(full(*part.shape) for part in results),
        in_specs=[smem, blocks(bases)] + [blocks(part) for part in arrays],
        out_specs=tuple(blocks(part) for part in results),
        compiler_params=pltpu.CompilerParams(vmem_limit_bytes=56 * 2**20),
        cost_estimate=cost_of(20),
    )(factor.reshape(1), bases, *arrays)


def small_factor(block):
    size = block.shape[0]
    eye = (
        lax.broadcasted_iota(jnp.int32, (size, size), 0)
        == lax.broadcasted_iota(jnp.int32, (size, size), 1)
    ).astype(jnp.float32)
    whole = jnp.concatenate([block, eye], axis=1)
    rows = [whole[8 * u : 8 * u + 8] for u in range(size // 8)]
    shape = rows[0].shape
    sub = lax.broadcasted_iota(jnp.int32, shape, 0)

    def lane_splat(value, lane):
        return jnp.broadcast_to(value[:, lane : lane + 1], shape)

    def row_splat(value, row):
        return jnp.broadcast_to(value[row : row + 1, :], shape)

    for g in range(len(rows)):
        first = 8 * g
        lanes = {
            u: [lane_splat(rows[u], first + s) for s in range(8)] for u in range(g, len(rows))
        }
        scale = jnp.zeros(shape, jnp.float32)
        for t in range(8):
            pivot = row_splat(lanes[g][t], t)
            root = lax.rsqrt(pivot)
            inverse = root * root
            scale = jnp.where(sub == t, root, scale)
            row_t = row_splat(rows[g], t) * inverse
            splats = {s: row_splat(lanes[g][s], t) * inverse for s in range(t + 1, 8)}
            for u in range(g, len(rows)):
                factor = lanes[u][t]
                if u == g:
                    factor = jnp.where(sub > t, factor, 0.0)
                rows[u] = rows[u] - factor * row_t
                for s in range(t + 1, 8):
                    lanes[u][s] = lanes[u][s] - factor * splats[s]
        rows[g] = rows[g] * scale
    return jnp.concatenate(rows, axis=0)[:, size:]


def renew_kernel(stat_ref, basis_ref, out_ref, gram_ref, rest_ref):
    size = stat_ref.shape[0]
    product = dot_exact(stat_ref[...], basis_ref[...], 1, 0)
    rest_ref[...] = product
    gram_ref[...] = dot_exact(product, product, 0, 0)
    for low in range(0, size, 128):
        high = low + 128
        block = gram_ref[low:high, low:high]
        corner = small_factor(block[:64, :64])
        across = dot_exact(corner, block[:64, 64:], 1, 0)
        second = small_factor(block[64:, 64:] - dot_exact(across, across, 0, 0))
        below = dot_exact(second, dot_exact(across, corner, 0, 0), 1, 0)
        inverse = jnp.concatenate(
            [
                jnp.concatenate([corner, jnp.zeros_like(corner)], axis=1),
                jnp.concatenate([-below, second], axis=1),
            ],
            axis=0,
        )
        columns = dot_exact(rest_ref[:, low:high], inverse, 1, 1)
        out_ref[:, low:high] = columns
        if high < size:
            panel = dot_exact(inverse, gram_ref[low:high, high:], 1, 0)
            gram_ref[high:, high:] -= dot_exact(panel, panel, 0, 0)
            rest_ref[:, high:] -= dot_exact(columns, panel, 1, 0)


def renew_basis(statistic, basis):
    shape = statistic.shape
    return call(
        renew_kernel,
        full(*shape),
        statistic,
        basis,
        scratch=[pltpu.VMEM(shape, jnp.float32), pltpu.VMEM(shape, jnp.float32)],
        microseconds=29,
    )


def peers_of(axis):
    size, me = lax.axis_size(axis), lax.axis_index(axis)
    return [
        (step, lax.rem(me + step, size), lax.rem(me + size - step, size)) for step in range(1, size)
    ]


def greet(*places):
    barrier = pltpu.get_barrier_semaphore()
    for axis, index in places:
        pl.semaphore_signal(barrier, inc=1, device_id={axis: index}, device_id_type=mesh_ids)
    pl.semaphore_wait(barrier, len(places))


def push(source, target, sems, slot, axis, index):
    copy = pltpu.make_async_remote_copy(
        src_ref=source,
        dst_ref=target,
        send_sem=sems[0].at[slot],
        recv_sem=sems[1].at[slot],
        device_id={axis: index},
        device_id_type=mesh_ids,
    )
    copy.start()
    return copy


def sem_pair(count):
    return [pltpu.SemaphoreType.DMA((count,)), pltpu.SemaphoreType.DMA((count,))]


def talk(kernel, outs, collective_id, *args, scratch=(), microseconds=15, before=()):
    def body(*refs):
        kernel(*refs[: len(args)], *refs[len(args) + len(before) :])

    return pl.pallas_call(
        body,
        out_shape=outs,
        in_specs=[vmem] * len(args) + [pl.BlockSpec(memory_space=pl.ANY)] * len(before),
        out_specs=jax.tree.map(lambda _: vmem, outs),
        scratch_shapes=list(scratch),
        compiler_params=pltpu.CompilerParams(
            collective_id=collective_id, has_side_effects=True, vmem_limit_bytes=56 * 2**20
        ),
        cost_estimate=cost_of(microseconds),
    )(*args, *before)


def gather_kernel(axis, *refs):
    count = (len(refs) - 2) // 2
    others = peers_of(axis)
    greet(*[(axis, to) for _, to, _ in others])
    me = lax.axis_index(axis)
    copies = [
        push(refs[k], refs[count + k].at[me], refs[-2:], k * len(others) + step - 1, axis, to)
        for k in range(count)
        for step, to, _ in others
    ]
    for k in range(count):
        refs[count + k][me] = refs[k][...]
    for copy in copies:
        copy.wait()


def gather_small(axis, collective_id, *arrays):
    size = lax.axis_size(axis)
    outs = tuple(jax.ShapeDtypeStruct((size, *x.shape), x.dtype) for x in arrays)
    sems = sem_pair((size - 1) * len(arrays))
    return talk(partial(gather_kernel, axis), outs, collective_id, *arrays, scratch=sems)


def sum_kernel(x_ref, out_ref, parts_ref, mine_ref, s0, r0, s1, r1):
    others = peers_of("vocab")
    greet(*[("vocab", to) for _, to, _ in others])
    size, me = lax.axis_size("vocab"), lax.axis_index("vocab")
    rows = mine_ref.shape[0]

    def rows_of(index):
        return pl.ds(pl.multiple_of(index * rows, rows), rows)

    copies = [
        push(x_ref.at[rows_of(to)], parts_ref.at[me], (s0, r0), step - 1, "vocab", to)
        for step, to, _ in others
    ]
    parts_ref[me] = x_ref[rows_of(me), :]
    for copy in copies:
        copy.wait()
    total = parts_ref[0].astype(jnp.float32)
    for index in range(1, size):
        total = total + parts_ref[index].astype(jnp.float32)
    mine_ref[...] = total.astype(mine_ref.dtype)
    copies = [
        push(mine_ref, out_ref.at[rows_of(me)], (s1, r1), step - 1, "vocab", to)
        for step, to, _ in others
    ]
    out_ref[rows_of(me), :] = mine_ref[...]
    for copy in copies:
        copy.wait()


def sum_vocab(x, collective_id):
    replicas = lax.axis_size("vocab")
    rows, columns = x.shape
    share = rows // replicas
    return talk(
        sum_kernel,
        jax.ShapeDtypeStruct(x.shape, x.dtype),
        collective_id,
        x,
        scratch=[
            pltpu.VMEM((replicas, share, columns), x.dtype),
            pltpu.VMEM((share, columns), x.dtype),
        ]
        + sem_pair(replicas - 1)
        + sem_pair(replicas - 1),
    )


def flip(index, bit):
    return index + bit - 2 * bit * lax.rem(index // bit, 2)


def tail_kernel(
    x_ref, few_ref, out_ref, sum_ref, parts_ref, seen_ref, line_ref, lines_ref,
    s0, r0, s1, r1, s2, r2, s3, r3, s4, r4,
):
    owners, replicas = peers_of("dp"), peers_of("vocab")
    greet(*[("dp", to) for _, to, _ in owners], *[("vocab", to) for _, to, _ in replicas])
    size, me, here = lax.axis_size("dp"), lax.axis_index("dp"), lax.axis_index("vocab")
    near, side = flip(here, 1), lax.rem(here, 2)
    rows = parts_ref.shape[1]

    def rows_of(index):
        return pl.ds(pl.multiple_of((side * size + index) * rows, rows), rows)

    few = [
        push(few_ref, seen_ref.at[here], (s2, r2), step - 1, "vocab", to) for step, to, _ in replicas
    ]
    wide = [
        push(x_ref.at[rows_of(to)], parts_ref.at[me], (s0, r0), step - 1, "dp", to)
        for step, to, _ in owners
    ]
    seen_ref[here] = few_ref[...]
    parts_ref[me] = x_ref[rows_of(me), :]
    for copy in few:
        copy.wait()
    line_ref[...] = jnp.sum(seen_ref[...], axis=0)
    few = [
        push(line_ref, lines_ref.at[me], (s3, r3), step - 1, "dp", to) for step, to, _ in owners
    ]
    lines_ref[me] = line_ref[...]
    for copy in wide:
        copy.wait()
    out_ref[rows_of(me), :] = jnp.sum(parts_ref[...], axis=0)
    mine = out_ref.at[rows_of(me)]
    wide = [push(mine, mine, (s1, r1), step - 1, "dp", to) for step, to, _ in owners]
    close = [push(mine, mine, (s4, r4), 0, "vocab", near)]
    for copy in few:
        copy.wait()
    sum_ref[...] = jnp.sum(lines_ref[...], axis=0)
    for copy, (step, _, origin) in zip(wide, owners):
        copy.wait()
        theirs = out_ref.at[rows_of(origin)]
        close.append(push(theirs, theirs, (s4, r4), step, "vocab", near))
    for copy in close:
        copy.wait()


def sum_tail(x, few, collective_id):
    owners, replicas = lax.axis_size("dp"), lax.axis_size("vocab")
    rows, columns = x.shape
    share = rows // (2 * owners)
    return talk(
        tail_kernel,
        (full(*x.shape), full(*few.shape)),
        collective_id,
        x,
        few,
        scratch=[
            pltpu.VMEM((owners, share, columns), jnp.float32),
            pltpu.VMEM((replicas, *few.shape), jnp.float32),
            pltpu.VMEM(few.shape, jnp.float32),
            pltpu.VMEM((owners, *few.shape), jnp.float32),
        ]
        + sem_pair(owners - 1)
        + sem_pair(owners - 1)
        + sem_pair(replicas - 1)
        + sem_pair(owners - 1)
        + sem_pair(owners),
    )


def far_replicas():
    here, size = lax.axis_index("vocab"), lax.axis_size("vocab")
    return [
        (step // 2 - 1, lax.rem(here + step, size), lax.rem(here + size - step, size))
        for step in range(2, size, 2)
    ]


def gradient_kernel(chunks, count, *refs):
    x_refs, refs = refs[:chunks], refs[chunks:]
    rows_refs, (out_ref, *refs) = refs[:count], refs[count:]
    swapped_refs, (parts_ref, s0, r0, s1, r1, s2, r2, s3, r3, s4, r4) = refs[:count], refs[count:]
    owners = peers_of("dp")
    here, me = lax.axis_index("vocab"), lax.axis_index("dp")
    near = flip(here, 1)
    size = lax.axis_size("vocab")
    steps = range(2, size, 2)
    greet(
        *[("dp", to) for _, to, _ in owners],
        *[("vocab", lax.rem(here + step, size)) for step in steps],
        ("vocab", near),
    )

    def spread(c, origin, sems, slot, to):
        place = out_ref.at[c, origin]
        return push(place, place, sems, slot, "vocab", to)

    arriving = [
        [
            push(x_refs[c].at[to], parts_ref.at[c, me], (s0, r0), (step - 1) * chunks + c, "dp", to)
            for step, to, _ in owners
        ]
        for c in range(chunks)
    ]

    def half_of(ref):
        rows = ref.shape[1] // 2
        return pl.ds(pl.multiple_of(lax.rem(here, 2) * rows, rows), rows)

    swaps = [
        [
            push(
                rows_ref.at[to, half_of(rows_ref)],
                swapped_ref.at[me, half_of(rows_ref)],
                (s3, r3),
                k * len(owners) + step - 1,
                "dp",
                to,
            )
            for step, to, _ in owners
        ]
        for k, (rows_ref, swapped_ref) in enumerate(zip(rows_refs, swapped_refs))
    ]
    for rows_ref, swapped_ref in zip(rows_refs, swapped_refs):
        swapped_ref[me] = rows_ref[me]
    far, close = [], []
    for c in range(chunks):
        parts_ref[c, me] = x_refs[c][me]
        for copy in arriving[c]:
            copy.wait()
        total = jnp.sum(parts_ref[c].astype(jnp.float32), axis=0)
        out_ref[c, here] = total.astype(out_ref.dtype)
        far.append(
            [
                spread(c, here, (s1, r1), k * chunks + c, lax.rem(here + step, size))
                for k, step in enumerate(steps)
            ]
        )
        close.append(spread(c, here, (s2, r2), c, near))
    for c in range(chunks):
        for k, step in enumerate(steps):
            far[c][k].wait()
            origin = lax.rem(here + size - step, size)
            close.append(spread(c, origin, (s2, r2), (k + 1) * chunks + c, near))
    for k, swapped_ref in enumerate(swapped_refs):
        for copy, (step, _, origin) in zip(swaps[k], owners):
            copy.wait()
            place = swapped_ref.at[origin, half_of(swapped_ref)]
            close.append(push(place, place, (s4, r4), k * len(owners) + step - 1, "vocab", near))
    for copy in close:
        copy.wait()


def share_gradients(blocks, rows, collective_id, before):
    owners, replicas = lax.axis_size("dp"), lax.axis_size("vocab")
    chunks = len(blocks)
    others = (replicas // 2 - 1) * chunks
    shape, kind = blocks[0].shape, blocks[0].dtype
    return talk(
        partial(gradient_kernel, chunks, len(rows)),
        (
            jax.ShapeDtypeStruct((chunks, replicas, *shape[1:]), kind),
            *[jax.ShapeDtypeStruct(part.shape, part.dtype) for part in rows],
        ),
        collective_id,
        *blocks,
        *rows,
        scratch=[pltpu.VMEM((chunks, *shape), kind)]
        + sem_pair((owners - 1) * chunks)
        + sem_pair(others)
        + sem_pair(others + chunks)
        + sem_pair(len(rows) * (owners - 1))
        + sem_pair(len(rows) * (owners - 1)),
        microseconds=40,
        before=before,
    )


def swap_kernel(x_ref, out_ref, s0, r0, s1, r1):
    others = peers_of("dp")
    me, here = lax.axis_index("dp"), lax.axis_index("vocab")
    near, side = flip(here, 1), lax.rem(here, 2)
    greet(*[("dp", to) for _, to, _ in others], ("vocab", near))
    rows = x_ref.shape[1] // 2
    half = pl.ds(pl.multiple_of(side * rows, rows), rows)
    copies = [
        push(x_ref.at[to, half], out_ref.at[me, half], (s0, r0), step - 1, "dp", to)
        for step, to, _ in others
    ]
    out_ref[me] = x_ref[me]
    close = []
    for copy, (step, _, origin) in zip(copies, others):
        copy.wait()
        place = out_ref.at[origin, half]
        close.append(push(place, place, (s1, r1), step - 1, "vocab", near))
    for copy in close:
        copy.wait()


def swap_owners(x, collective_id):
    owners = lax.axis_size("dp")
    return talk(
        swap_kernel,
        jax.ShapeDtypeStruct(x.shape, x.dtype),
        collective_id,
        x,
        scratch=sem_pair(owners - 1) + sem_pair(owners - 1),
    )


def token_kernel(
    scale, x_ref, place_ref, attn_ref, ffn_ref, out_ref, attn_out_ref, ffn_out_ref,
    near_ref, parts_ref, blocks_ref, row_ref,
    s0, r0, s1, r1, s2, r2, s3, r3, s4, r4, s5, r5, s6, r6,
):
    owners, others = peers_of("dp"), far_replicas()
    me, here = lax.axis_index("dp"), lax.axis_index("vocab")
    near, side = flip(here, 1), lax.rem(here, 2)
    greet(
        *[("dp", to) for _, to, _ in owners], *[("vocab", to) for _, to, _ in others], ("vocab", near)
    )
    count, length, columns = x_ref.shape
    half, pairs = length // 2, lax.axis_size("vocab") // 2
    share = half // pairs

    def half_of(which):
        return pl.ds(pl.multiple_of(which * half, half), half)

    def share_of(index):
        return pl.ds(pl.multiple_of(index // 2 * share, share), share)

    def place_of(index):
        return pl.ds(pl.multiple_of(side * half + index // 2 * share, share), share)

    def send_weights(ref, own_ref, slot, span):
        count, rows = own_ref.shape[0] // 2, own_ref.shape[1]
        mine = pl.ds(side * count, count)

        def place(origin):
            return ref.at[mine, pl.ds(pl.multiple_of(origin * rows + span[0], span[1]), span[1])]

        copies = [
            push(own_ref.at[mine, pl.ds(*span)], place(me), (s5, r5), slot + step - 1, "dp", to)
            for step, to, _ in owners
        ]
        return [(copy, place(origin), slot + step - 1) for copy, (step, _, origin) in zip(copies, owners)]

    def relay_weights(sent):
        relays = []
        for copy, place, slot in sent:
            copy.wait()
            relays.append(push(place, place, (s6, r6), slot, "vocab", near))
        return relays

    first = push(x_ref.at[:, half_of(1 - side)], near_ref, (s0, r0), 0, "vocab", near)
    some = ffn_ref.shape[1] // 2
    early = send_weights(attn_out_ref, attn_ref, 0, (0, attn_ref.shape[1]))
    early += send_weights(ffn_out_ref, ffn_ref, len(owners), (0, some))
    for ref, own_ref in ((attn_out_ref, attn_ref), (ffn_out_ref, ffn_ref)):
        rows = own_ref.shape[1]
        ref[:, pl.ds(pl.multiple_of(me * rows, rows), rows), :] = own_ref[...]
    first.wait()
    near_ref[...] += x_ref[:, half_of(side)]
    copies = [
        push(near_ref.at[:, share_of(to)], parts_ref.at[slot], (s1, r1), slot, "vocab", to)
        for slot, to, _ in others
    ]
    for copy in copies:
        copy.wait()
    total = near_ref[:, share_of(here)]
    for slot, _, _ in others:
        total = total + parts_ref[slot]
    blocks_ref[...] = total
    copies = [
        push(
            blocks_ref.at[to],
            row_ref.at[me, place_of(here)],
            (s2, r2),
            step - 1,
            "dp",
            to,
        )
        for step, to, _ in owners
    ]
    row_ref[me, place_of(here)] = blocks_ref[me]
    for copy in copies:
        copy.wait()
    late = send_weights(ffn_out_ref, ffn_ref, 2 * len(owners), (some, some))
    mine = row_ref.at[:, place_of(here)]
    copies = [push(mine, mine, (s3, r3), slot, "vocab", to) for slot, to, _ in others]
    close = [push(mine, mine, (s4, r4), 0, "vocab", near)]
    for copy, (slot, _, origin) in zip(copies, others):
        copy.wait()
        theirs = row_ref.at[:, place_of(origin)]
        close.append(push(theirs, theirs, (s4, r4), slot + 1, "vocab", near))
    close += relay_weights(early)
    for copy in close[: pairs]:
        copy.wait()
    for owner in range(count):
        band = slice(owner * columns, (owner + 1) * columns)
        out_ref[:, band] = row_ref[owner].astype(jnp.float32) * scale + place_ref[:, band]
    close += relay_weights(late)
    for copy in close[pairs:]:
        copy.wait()


def gather_tokens(x, places, attn, ffn, scale, collective_id):
    owners, pairs = lax.axis_size("dp"), lax.axis_size("vocab") // 2
    _, length, columns = x.shape
    half = length // 2
    width = owners * columns
    whole = [low(w.shape[0], owners * w.shape[1], width) for w in (attn, ffn)]
    return talk(
        partial(token_kernel, scale),
        (full(length, width), *whole),
        collective_id,
        x,
        places,
        attn,
        ffn,
        scratch=[
            pltpu.VMEM((owners, half, columns), x.dtype),
            pltpu.VMEM((pairs - 1, owners, half // pairs, columns), x.dtype),
            pltpu.VMEM((owners, half // pairs, columns), x.dtype),
            pltpu.VMEM((owners, length, columns), x.dtype),
        ]
        + sem_pair(1)
        + sem_pair(pairs - 1)
        + sem_pair(owners - 1)
        + sem_pair(pairs - 1)
        + sem_pair(pairs)
        + sem_pair(3 * owners - 3)
        + sem_pair(3 * owners - 3),
        microseconds=50,
    )


def sinusoid(length, model_width):
    places = np.arange(length, dtype=np.float32)[:, None]
    halves = np.arange(model_width // 2, dtype=np.float32)[None, :]
    angles = places * np.exp(halves * np.float32(-2.0 * math.log(10000.0) / model_width))
    angles = angles.astype(np.float64)
    return (
        np.stack([np.sin(angles), np.cos(angles)], axis=-1)
        .reshape(length, model_width)
        .astype(np.float32)
    )


def one_hot(ids, columns):
    return (ids[:, None] == columns[None, :]).astype(jnp.bfloat16)


def pick_weights(target_seg, pick_rows):
    sentence = jnp.take(target_seg, pick_rows, axis=0)
    return jnp.sum((sentence[:, None] == sentence[None, :]).astype(jnp.float32), axis=1)


def adam_direction(moment, second):
    return moment / (1.0 - beta_one**STEP) / (jnp.sqrt(second / (1.0 - beta_two**STEP)) + adam_eps)


def adam_update(weight, grad_item, moment, second, step_rate, decay_weight):
    moment = beta_one * moment + (1.0 - beta_one) * grad_item
    second = beta_two * second + (1.0 - beta_two) * grad_item * grad_item
    return (
        weight - step_rate * (adam_direction(moment, second) + decay_weight * weight),
        moment,
        second,
    )


def after(array, number):
    return array + jnp.where(jnp.isnan(number), 1, 0).astype(array.dtype)


def body(
    src_ids,
    src_seg,
    tgt_ids,
    tgt_seg,
    pick_pos,
    pick_label,
    attn_w,
    attn_m,
    attn_v,
    ffn_w,
    ffn_m,
    ffn_v,
    soap_basis,
    soap_stats,
    norm_p,
    norm_m,
    norm_v,
    embedding,
    embed_m,
    embed_v,
):
    owners, replicas = lax.axis_size("dp"), lax.axis_size("vocab")
    replica = lax.axis_index("vocab")
    own_table = embedding.astype(jnp.bfloat16)
    own_norms = jnp.pad(norm_p.astype(jnp.bfloat16).astype(jnp.float32), ((0, 2), (0, 0)))
    all_ids, norm_rows = gather_small("dp", 1, jnp.concatenate([src_ids, tgt_ids]), own_norms)
    norm_rows = jnp.swapaxes(norm_rows, 0, 1).reshape(16, -1)
    norms = [jnp.stack([norm_rows[k], norm_rows[7 + k]]) for k in range(7)]
    vocab_count, width = embedding.shape[0], attn_w.shape[2]
    source, source_seg, target, target_seg = (src_ids[0], src_seg[0], tgt_ids[0], tgt_seg[0])
    pick_rows, labels = (pick_pos[0], pick_label[0])
    length = source.shape[0]
    embed_scale = math.sqrt(width)
    half = vocab_count // 2
    halves = jnp.arange(half)
    paired = jnp.concatenate([own_table[:half], own_table[half:]], axis=1)

    def paired_places(ids):
        place = ids - replica * vocab_count
        inside = (place >= 0) & (place < vocab_count)
        return jnp.where(inside, place % half, -1), place < half

    def look_up(ids):
        place, left = paired_places(ids)
        wide = lax.dot_general(one_hot(place, halves), paired, (((1,), (0,)), ((), ())))
        return jnp.where(left[:, None], wide[:, :paired.shape[1] // 2], wide[:, paired.shape[1] // 2 :])

    source_part, target_part = (look_up(all_ids[:, k].reshape(-1)) for k in (0, 1))
    positional = sinusoid(length, width)
    enc_in, enc_attn_w, enc_ffn_w = gather_tokens(
        source_part.reshape(owners, length, -1),
        positional,
        attn_w[0:4].astype(jnp.bfloat16),
        ffn_w[0:2].astype(jnp.bfloat16),
        embed_scale,
        2,
    )
    target_part, _ = lax.optimization_barrier((target_part, enc_in))
    target_sum = lax.psum(target_part, "vocab")
    enc_mid, enc_attn = attn_forward(
        enc_in, norms[0], ((enc_attn_w,), 0, 0), source_seg, source_seg, None, False
    )
    self_w, cross_w, dec_ffn_w, ready = late_weights(attn_w[4:], ffn_w[2:], enc_in, enc_mid)
    enc_out, encoded, enc_ffn = ffn_forward(enc_mid, norms[1], norms[2], ((enc_ffn_w,), 0, 0))
    target_rows = swap_owners(target_sum.reshape(owners, length, -1), 3)
    table_low = after(own_table, ready)
    table_low = lax.all_gather(after(table_low, target_rows[0, 0, 0]), "dp", axis=1, tiled=True)
    target_rows = jnp.swapaxes(target_rows, 0, 1).reshape(length, -1).astype(jnp.float32)
    dec_in = target_rows * embed_scale + positional
    dec_mid, dec_self = attn_forward(
        dec_in, norms[3], self_w, target_seg, target_seg, None, True
    )
    dec_late, dec_cross = attn_forward(
        dec_mid, norms[4], cross_w, target_seg, source_seg, encoded, False
    )
    dec_out, final_low, dec_ffn = ffn_forward(dec_late, norms[5], norms[6], dec_ffn_w)

    own_labels = labels - replica * vocab_count
    picked, own_stats = loss_forward(final_low, pick_rows, own_labels, table_low)
    (seen,) = gather_small("vocab", 4, own_stats)
    weight = 1.0 / pick_weights(target_seg, pick_rows)
    grad_picked, table_parts, losses = loss_backward(
        picked, seen, weight, own_labels, table_low, owners
    )
    grad_table = lax.psum_scatter(table_parts, "dp", scatter_dimension=0, tiled=False)
    grad_picked = sum_vocab(grad_picked, 5)
    loss_part = jnp.sum(losses)
    count_part = (target_seg[-1] + 1).astype(jnp.float32)

    picks = share_selector(width, owners, replicas, replica, width)
    hidden = ffn_w.shape[1] * owners
    hidden_picks = share_selector(hidden, owners, replicas, replica, 512)
    norm_grads = [None] * 7
    grad, norm_grads[6], norm_grads[5], *ffn_blocks = ffn_backward(
        grad_picked, dec_ffn, hidden_picks, owners, places=pick_rows
    )
    grad, norm_grads[4], block, grad_encoded = attn_backward(grad, dec_cross, picks, owners, None)
    early = lax.psum_scatter(
        jnp.concatenate([block, *ffn_blocks], axis=1), "dp", scatter_dimension=0, tiled=False
    )
    grad, norm_grads[3], self_block, target_rows = attn_backward(
        grad, dec_self, picks, owners, embed_scale
    )
    grad, norm_grads[2], norm_grads[1], *ffn_blocks = ffn_backward(
        grad_encoded, enc_ffn, hidden_picks, owners, before=(grad_table, grad)
    )
    early_sum = after(early, grad[0, 0])
    early = lax.all_gather(early_sum, "vocab")
    grad, norm_grads[0], block, source_rows = attn_backward(
        grad, enc_attn, picks, owners, embed_scale, before=(early_sum,)
    )
    norm_grad = jnp.stack([after(part, early[0, 0, 0]) for part in norm_grads])
    norm_grad = jnp.concatenate([norm_grad[:, 0], norm_grad[:, 1], jnp.zeros((2, width))], axis=0)
    norm_grad = jnp.swapaxes(norm_grad.reshape(16, owners, -1), 0, 1)
    late, source_rows, target_rows, norm_grad = share_gradients(
        [block, self_block, *ffn_blocks], [source_rows, target_rows, norm_grad], 7, (early,)
    )
    g_norm = jnp.sum(norm_grad, axis=0)[:14]
    token_grads = jnp.concatenate([source_rows, target_rows], axis=1).reshape(
        owners * 2 * length, -1
    )
    place, left = paired_places(all_ids.reshape(-1))
    left = left[:, None]
    token_grads = jnp.concatenate(
        [jnp.where(left, token_grads, 0), jnp.where(left, 0, token_grads)], axis=1
    )
    g_paired = dot_dims(one_hot(place, halves), token_grads, 0, 0)
    g_embed = grad_table.astype(jnp.float32) + jnp.concatenate(
        jnp.split(g_paired, 2, axis=1), axis=0
    )

    def by_matrix(shared, count):
        blocks = jnp.swapaxes(shared.reshape(replicas, count, -1, width), 0, 1)
        return blocks.reshape(count, -1, width)

    early = by_matrix(early, 3)
    g_attn = [by_matrix(part, 4) for part in (late[0], late[1], early[0])]
    g_attn = jnp.concatenate(g_attn)
    g_ffn = jnp.concatenate([late[2:].reshape(2, -1, width), early[1:]])

    matrix = replica // 2
    own_grad = lax.dynamic_index_in_dim(g_ffn, matrix, 0, keepdims=False)
    own_products = dot_dims(own_grad, own_grad, 0, 0)
    g_ffn_low, g_ffn = g_ffn, g_ffn.astype(jnp.float32)
    first_copy = (replica == 0).astype(jnp.float32)
    layer_sq = jnp.sum(jnp.square(g_attn.astype(jnp.float32))) + jnp.sum(g_ffn * g_ffn) + jnp.sum(g_norm * g_norm)
    raw_squares = jnp.sum(g_embed * g_embed) + first_copy * layer_sq
    few = jnp.stack([first_copy * loss_part, first_copy * count_part, raw_squares])
    few = jnp.broadcast_to(jnp.pad(few, (0, 5))[:, None], (8, 128))
    own_products, few = sum_tail(own_products, few, 8)
    loss_sum, sentences, squares = few[0, 0], few[1, 0], few[2, 0]
    grad_norm = jnp.sqrt(squares) / sentences
    factor = jnp.minimum(1.0, clip_limit / (grad_norm + norm_eps)) / sentences
    g_norm = g_norm * factor

    def all_matrices(own):
        rows = own.shape[0] // 2
        half = lax.dynamic_slice_in_dim(own.astype(jnp.bfloat16), replica % 2 * rows, rows, 0)
        return lax.all_gather(half, "vocab").reshape(4, 2 * rows, -1)

    all_products = all_matrices(own_products)
    new_stats = stat_decay * soap_stats + (1.0 - stat_decay) * (factor * factor) * (
        all_products.astype(jnp.float32)
    )
    own_stat = stat_decay * lax.dynamic_index_in_dim(soap_stats, matrix, 0, keepdims=False) + (
        1.0 - stat_decay
    ) * (factor * factor) * own_products
    own_basis = renew_basis(own_stat, lax.dynamic_index_in_dim(soap_basis, matrix, 0, keepdims=False))
    new_basis = all_matrices(after(own_basis, new_stats[0, 0, 0])).astype(jnp.float32)

    new_norm, m_norm, v_norm = adam_update(norm_p, g_norm, norm_m, norm_v, rate_vector, 0.0)
    updated = update_matrices(
        factor,
        soap_basis,
        (g_attn, attn_w, attn_m, attn_v),
        (g_embed, embedding, embed_m, embed_v),
        (g_ffn_low, ffn_w, ffn_m, ffn_v),
    )
    new_attn, m_attn, v_attn, new_embed, m_embed, v_embed, new_ffn, m_ffn, v_ffn = updated
    return (
        loss_sum,
        sentences,
        grad_norm,
        new_attn,
        m_attn,
        v_attn,
        new_ffn,
        m_ffn,
        v_ffn,
        new_basis,
        new_stats,
        new_norm,
        m_norm,
        v_norm,
        new_embed,
        m_embed,
        v_embed,
    )


def solution(mesh):
    placed = (
        P("dp", None),
        P("dp", None),
        P("dp", None),
        P("dp", None),
        P("dp", None),
        P("dp", None),
        P(None, "dp", None),
        P(None, "dp", None),
        P(None, "dp", None),
        P(None, "dp", None),
        P(None, "dp", None),
        P(None, "dp", None),
        P(),
        P(),
        P(None, "dp"),
        P(None, "dp"),
        P(None, "dp"),
        P("vocab", "dp"),
        P("vocab", "dp"),
        P("vocab", "dp"),
    )
    return jax.shard_map(
        body,
        mesh=mesh,
        in_specs=placed,
        out_specs=(
            P(),
            P(),
            P(),
            P(None, "dp", None),
            P(None, "dp", None),
            P(None, "dp", None),
            P(None, "dp", None),
            P(None, "dp", None),
            P(None, "dp", None),
            P(),
            P(),
            P(None, "dp"),
            P(None, "dp"),
            P(None, "dp"),
            P("vocab", "dp"),
            P("vocab", "dp"),
            P("vocab", "dp"),
        ),
        check_vma=False,
    )
```

```python
from functools import partial
import math

import jax
import jax.numpy as jnp
import numpy as np
from jax import lax
from jax.experimental import pallas as pl
from jax.experimental.pallas import tpu as pltpu
from jax.sharding import PartitionSpec as P

HEADS = 8
STEP = 10
TILE = 128

highest = lax.Precision.HIGHEST
beta_one = 0.9
beta_two = 0.999
adam_eps = 1e-08
decay_rate = 0.01
rate_matrix = 0.03
rate_vector = 0.3
clip_limit = 1.0
stat_decay = 0.95
norm_eps = 1e-06
masked = -1e30
log_two_e = math.log2(math.e)
vmem = pl.BlockSpec(memory_space=pltpu.VMEM)
smem = pl.BlockSpec(memory_space=pltpu.SMEM)
mesh_ids = pl.DeviceIdType.MESH


def dot_dims(left, right, left_dim, right_dim):
    return lax.dot_general(
        left, right, (((left_dim,), (right_dim,)), ((), ())), preferred_element_type=jnp.float32
    )


def dot_exact(left, right, left_dim, right_dim):
    return lax.dot_general(
        left,
        right,
        (((left_dim,), (right_dim,)), ((), ())),
        precision=highest,
        preferred_element_type=jnp.float32,
    )


def cost_of(microseconds):
    return pl.CostEstimate(flops=microseconds * 10**9, bytes_accessed=0, transcendentals=0)


def call(kernel, outs, *args, scratch=(), smem_args=0, microseconds=5, before=()):
    def body(*refs):
        kernel(*refs[: len(args)], *refs[len(args) + len(before) :])

    return pl.pallas_call(
        body,
        out_shape=outs,
        in_specs=[vmem] * (len(args) - smem_args)
        + [smem] * smem_args
        + [pl.BlockSpec(memory_space=pl.ANY)] * len(before),
        out_specs=jax.tree.map(lambda _: vmem, outs),
        scratch_shapes=list(scratch),
        compiler_params=pltpu.CompilerParams(vmem_limit_bytes=56 * 2**20),
        cost_estimate=cost_of(microseconds),
    )(*args, *before)


def low(*shape):
    return jax.ShapeDtypeStruct(shape, jnp.bfloat16)


def full(*shape):
    return jax.ShapeDtypeStruct(shape, jnp.float32)


def norm_parts(values):
    centre = values - jnp.mean(values, axis=-1, keepdims=True)
    spread = jnp.mean(centre * centre, axis=-1, keepdims=True)
    root = lax.rsqrt(spread + norm_eps)
    return centre * root, root


def norm_forward(values, ln_ref):
    return norm_parts(values)[0] * ln_ref[0:1, :] + ln_ref[1:2, :]


def norm_backward(grad, values, ln_ref, ln_grad_ref):
    normed, root = norm_parts(values)
    ln_grad_ref[0:1, :] = jnp.sum(grad * normed, axis=0, keepdims=True)
    ln_grad_ref[1:2, :] = jnp.sum(grad, axis=0, keepdims=True)
    inner = grad * ln_ref[0:1, :]
    return root * (
        inner
        - jnp.mean(inner, axis=-1, keepdims=True)
        - normed * jnp.mean(inner * normed, axis=-1, keepdims=True)
    )


def at_tile(index, size):
    return pl.ds(pl.multiple_of(index * size, size), size)


def tile_mask(segq_ref, segk_ref, qi, ki, tile_q, tile_k, causal):
    seg_k = segk_ref[at_tile(ki, tile_k), :]
    seg_k = jnp.concatenate([seg_k] * (tile_q // TILE), axis=1)
    allowed = seg_k == segq_ref[:, at_tile(qi, tile_q)]
    if causal:
        shape = (tile_k, tile_q)
        ahead = lax.broadcasted_iota(jnp.int32, shape, 0) - lax.broadcasted_iota(
            jnp.int32, shape, 1
        )
        allowed = allowed & (ahead <= qi * tile_q - ki * tile_k)
    return allowed


def for_tiles(length, tile_q, tile_k, edge_ref, causal, step):
    count_q, count_k = length // tile_q, length // tile_k
    per_q, per_k = tile_q // TILE, tile_k // TILE

    def one(pair, carry):
        qi, ki = pair // count_k, lax.rem(pair, count_k)
        live = (edge_ref[0, qi * per_q] <= edge_ref[3, (ki + 1) * per_k - 1]) & (
            edge_ref[2, ki * per_k] <= edge_ref[1, (qi + 1) * per_q - 1]
        )
        if causal:
            live = live & (ki * tile_k < (qi + 1) * tile_q)

        @pl.when(live)
        def _():
            step(qi, ki)

        return carry

    lax.fori_loop(0, count_q * count_k, one, 0)


def tile_edges(seg_q, seg_k):
    last = TILE - 1
    return jnp.stack([seg_q[::TILE], seg_q[last::TILE], seg_k[::TILE], seg_k[last::TILE]])


def share_selector(rows, owners, shares, share, count):
    size = rows // (owners * shares)
    index = jnp.arange(count // shares)
    picked = index // size * (rows // owners) + share * size + index % size
    return (picked[:, None] == jnp.arange(count)[None, :]).astype(jnp.bfloat16)


def lay_weights(w_ref, piece_refs, part, first):
    own = piece_refs[0]
    matrices, rows = w_ref.shape[0], w_ref.shape[1] // 4
    half = own.shape[0] // 2
    me, side = lax.axis_index("dp"), lax.rem(lax.axis_index("vocab"), 2)
    for m in range(matrices):
        span = slice(first + m * rows, first + (m + 1) * rows)
        w_ref[m, pl.ds(pl.multiple_of(me * rows, rows), rows), :] = own[
            part * half + span.start : part * half + span.stop, :
        ]
        for k in range(1, 4):
            place = pl.ds(pl.multiple_of((me ^ k) * rows, rows), rows)

            @pl.when(side == part)
            def _():
                w_ref[m, place, :] = piece_refs[k][span, :]

            @pl.when(side != part)
            def _():
                w_ref[m, place, :] = piece_refs[k + 3][span, :]


def flip_sites(part, axis, bit):
    return lax.ppermute(part, axis, [(s, s ^ bit) for s in range(lax.axis_size(axis))])


def late_weights(attn, ffn, after, later):
    owners = lax.axis_size("dp")
    width = attn.shape[-1]
    attn, ffn = attn.astype(jnp.bfloat16), ffn.astype(jnp.bfloat16)
    if owners != 4:
        attn, ffn = (lax.all_gather(part, "dp", axis=1, tiled=True) for part in (attn, ffn))
        return ((attn[:4],), 0, 0), ((attn[4:],), 0, 0), ((ffn,), 0, 0), ffn[0, 0, 0]
    halves = [
        jnp.concatenate([attn[4 * k : 4 * k + 4].reshape(-1, width), ffn[k]]) for k in range(2)
    ]
    own = jnp.concatenate(halves)
    side = lax.axis_index("vocab") % 2
    mine = jnp.where(side == 0, halves[0], halves[1])
    mine, _ = lax.optimization_barrier((mine, after))
    got = [flip_sites(mine, "dp", k) for k in range(1, 4)]
    *got, _ = lax.optimization_barrier((*got, later))
    swapped = [flip_sites(part, "vocab", 1) for part in got]
    pieces = (own, *got, *swapped)
    rows = 4 * attn.shape[1]
    return (pieces, 0, 0), (pieces, 1, 0), (pieces, None, rows), swapped[-1][0, 0]


def attn_forward_kernel(causal, cross, pieces, part, first, *refs):
    refs = list(refs)
    x_ref, ln_ref, segq_ref, segk_ref = refs[:4]
    refs = refs[4:]
    key_ref = refs.pop(0) if cross else None
    piece_refs, refs = refs[:pieces], refs[pieces:]
    edge_ref, out_ref, a_ref, qt_ref, kt_ref, vt_ref, ot_ref, lse_ref = refs[:8]
    refs = refs[8:]
    w_ref = piece_refs[0]
    if pieces > 1:
        w_ref = refs.pop(0)
        lay_weights(w_ref, piece_refs, part, first)
    top_ref, sum_ref, acc_ref = refs
    length, width = x_ref.shape
    head_size = width // HEADS
    a_ref[...] = norm_forward(x_ref[...], ln_ref).astype(jnp.bfloat16)
    key_in = key_ref if cross else a_ref
    qt_ref[...] = dot_dims(a_ref[...], w_ref[0], 1, 0).astype(jnp.bfloat16).T
    kt_ref[...] = dot_dims(key_in[...], w_ref[1], 1, 0).astype(jnp.bfloat16).T
    vt_ref[...] = dot_dims(key_in[...], w_ref[2], 1, 0).astype(jnp.bfloat16).T
    top_ref[...] = jnp.full(top_ref.shape, masked, jnp.float32)
    sum_ref[...] = jnp.zeros(sum_ref.shape, jnp.float32)
    acc_ref[...] = jnp.zeros(acc_ref.shape, jnp.float32)
    scale = log_two_e / math.sqrt(head_size)
    bands = [slice(h * head_size, (h + 1) * head_size) for h in range(HEADS)]

    def step(qi, ki):
        q_at, k_at = at_tile(qi, 256), at_tile(ki, 256)
        allowed = tile_mask(segq_ref, segk_ref, qi, ki, 256, 256, causal)
        scores = [dot_dims(kt_ref[band, k_at], qt_ref[band, q_at], 0, 0) * scale for band in bands]
        scores = [jnp.where(allowed, part, masked) for part in scores]
        top = top_ref[:, q_at]
        new_top = jnp.maximum(
            top,
            jnp.concatenate([jnp.max(part, axis=0, keepdims=True) for part in scores], axis=0),
        )
        fade = jnp.exp2(top - new_top)
        parts = [jnp.exp2(scores[h] - new_top[h : h + 1]) for h in range(HEADS)]
        top_ref[:, q_at] = new_top
        sum_ref[:, q_at] = sum_ref[:, q_at] * fade + jnp.concatenate(
            [jnp.sum(part, axis=0, keepdims=True) for part in parts], axis=0
        )
        mixed = [
            dot_dims(vt_ref[bands[h], k_at], parts[h].astype(jnp.bfloat16), 1, 0)
            for h in range(HEADS)
        ]
        acc = acc_ref[:, q_at]
        acc_ref[:, q_at] = jnp.concatenate(
            [acc[bands[h]] * fade[h : h + 1] + mixed[h] for h in range(HEADS)], axis=0
        )

    for_tiles(length, 256, 256, edge_ref, causal, step)
    lse_ref[...] = top_ref[...] + jnp.log2(sum_ref[...])
    for h in range(HEADS):
        ot_ref[bands[h], :] = (acc_ref[bands[h], :] / sum_ref[h : h + 1, :]).astype(jnp.bfloat16)
    out_ref[...] = x_ref[...] + dot_dims(ot_ref[...], w_ref[3], 0, 0)


def attn_forward(x, ln, weights, seg_q, seg_k, key_in, causal):
    length, width = x.shape
    weights, part, first = weights
    cross = key_in is not None
    segs = (seg_q[None, :], jnp.broadcast_to(seg_k[:, None], (length, TILE)))
    edges = tile_edges(seg_q, seg_k)
    args = (x, ln, *segs) + ((key_in,) if cross else ()) + (*weights, edges)
    outs = (full(length, width), low(length, width)) + (low(width, length),) * 4
    outs = outs + (full(HEADS, length),)
    if len(weights) > 1:
        outs = outs + (low(4, width, width),)
    out, normed, *stored = call(
        partial(attn_forward_kernel, causal, cross, len(weights), part, first),
        outs,
        *args,
        scratch=[
            pltpu.VMEM((HEADS, length), jnp.float32),
            pltpu.VMEM((HEADS, length), jnp.float32),
            pltpu.VMEM((width, length), jnp.float32),
        ],
        smem_args=1,
        microseconds=20,
    )
    whole = stored.pop() if len(weights) > 1 else weights[0]
    return out, (x, ln, whole, segs, edges, causal, key_in, normed, stored)


def attn_backward_kernel(causal, cross, row_scale, *refs):
    g_ref, x_ref, ln_ref, w_ref, pick_ref, segq_ref, segk_ref, a_ref = refs[:8]
    refs = list(refs[8:])
    key_ref = refs.pop(0) if cross else a_ref
    qt_ref, kt_ref, vt_ref, ot_ref, lse_ref, edge_ref, out_ref, ln_grad_ref, block_ref, extra_ref = refs[:10]
    low_ref, gq_ref, gk_ref, gv_ref, got_ref, delta_ref, gqt_ref, gkt_ref, gvt_ref = refs[10:]
    length, width = x_ref.shape
    head_size = width // HEADS
    low_ref[...] = g_ref[...].astype(jnp.bfloat16)
    got_ref[...] = dot_dims(low_ref[...], w_ref[3], 1, 1).astype(jnp.bfloat16).T
    bands = [slice(h * head_size, (h + 1) * head_size) for h in range(HEADS)]
    for h in range(HEADS):
        delta_ref[h : h + 1, :] = jnp.sum(
            got_ref[bands[h], :].astype(jnp.float32) * ot_ref[bands[h], :].astype(jnp.float32),
            axis=0,
            keepdims=True,
        )
    for ref in (gqt_ref, gkt_ref, gvt_ref):
        ref[...] = jnp.zeros(ref.shape, jnp.float32)
    scale = log_two_e / math.sqrt(head_size)
    back = 1.0 / math.sqrt(head_size)

    def step(qi, ki):
        q_at, k_at = at_tile(qi, 256), at_tile(ki, TILE)
        allowed = tile_mask(segq_ref, segk_ref, qi, ki, 256, TILE, causal)
        scores = [dot_dims(kt_ref[band, k_at], qt_ref[band, q_at], 0, 0) for band in bands]
        grads = [dot_dims(vt_ref[band, k_at], got_ref[band, q_at], 0, 0) for band in bands]
        parts = [
            jnp.where(allowed, jnp.exp2(scores[h] * scale - lse_ref[h : h + 1, q_at]), 0.0)
            for h in range(HEADS)
        ]
        grads = [parts[h] * (grads[h] - delta_ref[h : h + 1, q_at]) for h in range(HEADS)]
        parts_t = [part.T.astype(jnp.bfloat16) for part in parts]
        grads_t = [part.T.astype(jnp.bfloat16) for part in grads]
        grads = [part.astype(jnp.bfloat16) for part in grads]
        for ref, place, terms in (
            (gvt_ref, k_at, [dot_dims(got_ref[bands[h], q_at], parts_t[h], 1, 0) for h in range(HEADS)]),
            (gkt_ref, k_at, [dot_dims(qt_ref[bands[h], q_at], grads_t[h], 1, 0) for h in range(HEADS)]),
            (gqt_ref, q_at, [dot_dims(kt_ref[bands[h], k_at], grads[h], 1, 0) for h in range(HEADS)]),
        ):
            ref[:, place] += jnp.concatenate(terms, axis=0)

    for_tiles(length, 256, TILE, edge_ref, causal, step)
    gq_ref[...] = (gqt_ref[...] * back).astype(jnp.bfloat16).T
    gk_ref[...] = (gkt_ref[...] * back).astype(jnp.bfloat16).T
    gv_ref[...] = gvt_ref[...].astype(jnp.bfloat16).T
    from_query = dot_dims(gq_ref[...], w_ref[0], 1, 1)
    from_keys = dot_dims(gk_ref[...], w_ref[1], 1, 1) + dot_dims(gv_ref[...], w_ref[2], 1, 1)
    if cross:
        extra_ref[...] = from_keys
    else:
        from_query = from_query + from_keys
    total = g_ref[...] + norm_backward(from_query, x_ref[...], ln_ref, ln_grad_ref)
    out_ref[...] = total
    owners = block_ref.shape[0]
    if not cross:
        columns = width // owners
        for owner in range(owners):
            band = slice(owner * columns, (owner + 1) * columns)
            extra_ref[owner] = (total[:, band] * row_scale).astype(jnp.bfloat16)
    own_a = dot_dims(pick_ref[...], a_ref[...], 1, 1).astype(jnp.bfloat16)
    own_key = dot_dims(pick_ref[...], key_ref[...], 1, 1).astype(jnp.bfloat16) if cross else own_a
    own_o = dot_dims(pick_ref[...], ot_ref[...], 1, 0).astype(jnp.bfloat16)
    size = own_a.shape[0] // owners
    products = ((own_a, gq_ref), (own_key, gk_ref), (own_key, gv_ref), (own_o, low_ref))
    for m, (rows, right_ref) in enumerate(products):
        product = dot_dims(rows, right_ref[...], 1, 0).astype(jnp.bfloat16)
        for owner in range(owners):
            block_ref[owner, m * size : (m + 1) * size, :] = product[owner * size : (owner + 1) * size]


def attn_backward(grad, stored, picks, owners, row_scale, before=()):
    x, ln, weights, segs, edges, causal, key_in, normed, kept = stored
    length, width = x.shape
    cross = key_in is not None
    extra = full(length, width) if cross else low(owners, length, width // owners)
    outs = (full(length, width), full(2, width), low(owners, 4 * picks.shape[0] // owners, width), extra)
    keys = (key_in,) if cross else ()
    return call(
        partial(attn_backward_kernel, causal, cross, row_scale),
        outs,
        grad,
        x,
        ln,
        weights,
        picks,
        *segs,
        normed,
        *keys,
        *kept,
        edges,
        scratch=[pltpu.VMEM((length, width), jnp.bfloat16)] * 4
        + [pltpu.VMEM((width, length), jnp.bfloat16), pltpu.VMEM((HEADS, length), jnp.float32)]
        + [pltpu.VMEM((width, length), jnp.float32)] * 3,
        smem_args=1,
        microseconds=25,
        before=before,
    )


def gelu_parts(hidden):
    root = math.sqrt(2.0 / math.pi)
    square = hidden * hidden
    bend = jnp.tanh(root * hidden * (1.0 + 0.044715 * square))
    value = 0.5 * hidden * (1.0 + bend)
    slope = 0.5 * (1.0 + bend) + 0.5 * hidden * (1.0 - bend * bend) * root * (
        1.0 + 3.0 * 0.044715 * square
    )
    return value, slope


def ffn_forward_kernel(chunk, pieces, first, x_ref, ln_ref, next_ref, *refs):
    piece_refs, (out_ref, a_ref, after_ref, *refs) = refs[:pieces], refs[pieces:]
    w_ref = piece_refs[0]
    if pieces > 1:
        (w_ref,) = refs
        for part in range(2):
            lay_weights(w_ref.at[part : part + 1], piece_refs, part, first)
    w_in_ref, w_out_ref = w_ref.at[0], w_ref.at[1]
    a_ref[...] = norm_forward(x_ref[...], ln_ref).astype(jnp.bfloat16)
    total = x_ref[...]
    for start in range(0, w_in_ref.shape[0], chunk):
        part = slice(start, start + chunk)
        hidden = dot_dims(a_ref[...], w_in_ref[part, :], 1, 1)
        active = gelu_parts(hidden)[0].astype(jnp.bfloat16)
        total = total + dot_dims(active, w_out_ref[part, :], 1, 0)
    out_ref[...] = total
    after_ref[...] = norm_forward(total, next_ref).astype(after_ref.dtype)


def ffn_forward(x, ln, ln_next, weights):
    length, width = x.shape
    weights, _, first = weights
    outs = (full(length, width), low(length, width), low(length, width))
    if len(weights) > 1:
        outs = outs + (low(2, 4 * (weights[0].shape[0] // 2 - first), width),)
    out, normed, after, *whole = call(
        partial(ffn_forward_kernel, 512, len(weights), first),
        outs,
        x,
        ln,
        ln_next,
        *weights,
        microseconds=12,
    )
    return out, after, (x, ln, whole[0] if whole else weights[0], normed, out, ln_next)


def ffn_backward_kernel(
    chunk, picked, after_ref, *refs
):
    if picked:
        place_ref, *refs = refs
        shape = (refs[0].shape[0], place_ref.shape[1])
        chosen = lax.broadcasted_iota(jnp.int32, shape, 0) == place_ref[...]
        after = dot_dims(chosen.astype(jnp.bfloat16), after_ref[...], 1, 0)
    else:
        after = after_ref[...]
    ffn_backward_rest(chunk, after, *refs)


def ffn_backward_rest(
    chunk, after, y_ref, next_ref, x_ref, ln_ref, a_ref, w_ref, pick_ref,
    out_ref, next_grad_ref, ln_grad_ref, in_ref, back_ref, low_ref, g_ref,
):
    w_in_ref, w_out_ref = w_ref.at[0], w_ref.at[1]
    g_ref[...] = norm_backward(after, y_ref[...], next_ref, next_grad_ref)
    low_ref[...] = g_ref[...].astype(jnp.bfloat16)
    total = jnp.zeros(g_ref.shape, jnp.float32)
    owners, size = in_ref.shape[:2]
    blocks = pick_ref.shape[0] // size
    for index in range(w_in_ref.shape[0] // chunk):
        part = slice(index * chunk, (index + 1) * chunk)
        hidden = dot_dims(a_ref[...], w_in_ref[part, :], 1, 1)
        value, slope = gelu_parts(hidden)
        grad = (dot_dims(low_ref[...], w_out_ref[part, :], 1, 1) * slope).astype(jnp.bfloat16)
        total = total + dot_dims(grad, w_in_ref[part, :], 1, 0)
        pairs = ((in_ref, grad, a_ref), (back_ref, value.astype(jnp.bfloat16), low_ref))
        for ref, left, right_ref in pairs:
            rows = dot_dims(pick_ref[...], left, 1, 1).astype(jnp.bfloat16)
            product = dot_dims(rows, right_ref[...], 1, 0).astype(jnp.bfloat16)
            for block in range(blocks):
                ref[index * blocks + block] = product[block * size : (block + 1) * size]
    out_ref[...] = g_ref[...] + norm_backward(total, x_ref[...], ln_ref, ln_grad_ref)


def ffn_backward(grad_after, stored, picks, owners, before=(), places=None):
    x, ln, weights, normed, out, ln_next = stored
    length, width = x.shape
    chunk = picks.shape[1]
    size = picks.shape[0] * weights.shape[1] // chunk // owners
    block = low(owners, size, width)
    return call(
        partial(ffn_backward_kernel, chunk, places is not None),
        (full(length, width), full(2, width), full(2, width), block, block),
        grad_after,
        *(() if places is None else (places[None, :],)),
        out,
        ln_next,
        x,
        ln,
        normed,
        weights,
        picks,
        scratch=[
            pltpu.VMEM((length, width), jnp.bfloat16),
            pltpu.VMEM((length, width), jnp.float32),
        ],
        microseconds=17,
        before=before,
    )


def loss_forward_kernel(chunks, final_ref, pick_ref, label_ref, table_ref, picked_ref, stat_ref, logit_ref):
    count, length = pick_ref.shape[0], final_ref.shape[0]
    places = lax.broadcasted_iota(jnp.int32, (count, length), 1)
    chosen = (places == pick_ref[...]).astype(jnp.bfloat16)
    picked_ref[...] = dot_dims(chosen, final_ref[...], 1, 0).astype(jnp.bfloat16)
    rows = table_ref.shape[0] // chunks
    top = jnp.full((1, count), masked, jnp.float32)
    label = jnp.zeros((1, count), jnp.float32)
    for index in range(chunks):
        span = slice(index * rows, (index + 1) * rows)
        logits = dot_dims(table_ref[span, :], picked_ref[...], 1, 1)
        logit_ref[span, :] = logits
        top = jnp.maximum(top, jnp.max(logits, axis=0, keepdims=True))
        hit = lax.broadcasted_iota(jnp.int32, logits.shape, 0) + index * rows == label_ref[...]
        label = label + jnp.sum(jnp.where(hit, logits, 0.0), axis=0, keepdims=True)
    total = jnp.zeros((1, count), jnp.float32)
    for index in range(chunks):
        span = slice(index * rows, (index + 1) * rows)
        total = total + jnp.sum(jnp.exp(logit_ref[span, :] - top), axis=0, keepdims=True)
    stat_ref[...] = jnp.concatenate([top, total, label, jnp.zeros((5, count), jnp.float32)], axis=0)


def loss_forward(final, pick_rows, labels, table):
    count, width = pick_rows.shape[0], final.shape[1]
    return call(
        partial(loss_forward_kernel, 8),
        (low(count, width), full(8, count)),
        final,
        pick_rows[:, None],
        labels[None, :],
        table,
        scratch=[pltpu.VMEM((table.shape[0], count), jnp.float32)],
        microseconds=6,
    )


def loss_backward_kernel(
    chunks, picked_ref, seen_ref, weight_ref, label_ref, table_ref, grad_ref, parts_ref, loss_ref
):
    tops, totals, labels = (
        jnp.concatenate([seen_ref[k, m : m + 1, :] for k in range(seen_ref.shape[0])], axis=0)
        for m in range(3)
    )
    top = jnp.max(tops, axis=0, keepdims=True)
    total = top + jnp.log(jnp.sum(totals * jnp.exp(tops - top), axis=0, keepdims=True))
    loss_ref[...] = (total - jnp.sum(labels, axis=0, keepdims=True)) * weight_ref[...]
    rows = table_ref.shape[0] // chunks
    columns = parts_ref.shape[2]
    grad = jnp.zeros(grad_ref.shape, jnp.float32)
    for index in range(chunks):
        span = slice(index * rows, (index + 1) * rows)
        logits = dot_dims(table_ref[span, :], picked_ref[...], 1, 1)
        hit = lax.broadcasted_iota(jnp.int32, logits.shape, 0) + index * rows == label_ref[...]
        slopes = weight_ref[...] * (jnp.exp(logits - total) - jnp.where(hit, 1.0, 0.0))
        slopes = slopes.astype(jnp.bfloat16)
        product = dot_dims(slopes, picked_ref[...], 1, 0).astype(jnp.bfloat16)
        for owner in range(parts_ref.shape[0]):
            parts_ref[owner, span, :] = product[:, owner * columns : (owner + 1) * columns]
        grad = grad + dot_dims(slopes, table_ref[span, :], 0, 0)
    grad_ref[...] = grad.astype(jnp.bfloat16)


def loss_backward(picked, seen, weight, labels, table, owners):
    count, width = picked.shape
    return call(
        partial(loss_backward_kernel, 8),
        (low(count, width), low(owners, table.shape[0], width // owners), full(1, count)),
        picked,
        seen,
        weight[None, :],
        labels[None, :],
        table,
        microseconds=8,
    )


def adam_parts(weight, grad, moment, second):
    moment = beta_one * moment + (1.0 - beta_one) * grad
    second = beta_two * second + (1.0 - beta_two) * grad * grad
    step = adam_direction(moment, second) + decay_rate * weight
    return weight - rate_matrix * step, moment, second


def update_kernel(*refs):
    factor_ref, basis_ref, *ins = refs[:14]
    outs = refs[14:]
    factor = factor_ref[0]
    for k in (0, 1):
        grad_ref, weight_ref, moment_ref, second_ref = ins[4 * k : 4 * k + 4]
        grad = grad_ref[...].astype(jnp.float32) * factor
        results = adam_parts(weight_ref[...], grad, moment_ref[...], second_ref[...])
        for ref, result in zip(outs[3 * k : 3 * k + 3], results):
            ref[...] = result
    g_ref, w_ref, m_ref, v_ref = ins[8:]
    new_w_ref, new_m_ref, new_v_ref = outs[6:]
    high = basis_ref[0].astype(jnp.bfloat16)
    rest = (basis_ref[0] - high.astype(jnp.float32)).astype(jnp.bfloat16)
    grad = g_ref[0]
    rotated = (dot_dims(grad, high, 1, 0) + dot_dims(grad, rest, 1, 0)) * factor
    moment = beta_one * m_ref[0] + (1.0 - beta_one) * rotated
    second = beta_two * v_ref[0] + (1.0 - beta_two) * rotated * rotated
    new_m_ref[0] = moment
    new_v_ref[0] = second
    step = adam_direction(moment, second)
    step_high = step.astype(jnp.bfloat16)
    step_rest = (step - step_high.astype(jnp.float32)).astype(jnp.bfloat16)
    back = (
        dot_dims(step_high, high, 1, 1)
        + dot_dims(step_high, rest, 1, 1)
        + dot_dims(step_rest, high, 1, 1)
    )
    new_w_ref[0] = w_ref[0] - rate_matrix * (back + decay_rate * w_ref[0])


def update_matrices(factor, bases, attn, table, ffn):
    def blocks(array):
        shape = (array.shape[0] // 4, *array.shape[1:])
        return pl.BlockSpec(shape, lambda k: (k,) + (0,) * (len(shape) - 1))

    arrays = (*attn, *table, *ffn)
    results = [part for group in (attn, table, ffn) for part in group[1:]]
    return pl.pallas_call(
        update_kernel,
        grid=(4,),
        out_shape=tuple(full(*part.shape) for part in results),
        in_specs=[smem, blocks(bases)] + [blocks(part) for part in arrays],
        out_specs=tuple(blocks(part) for part in results),
        compiler_params=pltpu.CompilerParams(vmem_limit_bytes=56 * 2**20),
        cost_estimate=cost_of(20),
    )(factor.reshape(1), bases, *arrays)


def small_factor(block):
    size = block.shape[0]
    eye = (
        lax.broadcasted_iota(jnp.int32, (size, size), 0)
        == lax.broadcasted_iota(jnp.int32, (size, size), 1)
    ).astype(jnp.float32)
    whole = jnp.concatenate([block, eye], axis=1)
    rows = [whole[8 * u : 8 * u + 8] for u in range(size // 8)]
    shape = rows[0].shape
    sub = lax.broadcasted_iota(jnp.int32, shape, 0)

    def lane_splat(value, lane):
        return jnp.broadcast_to(value[:, lane : lane + 1], shape)

    def row_splat(value, row):
        return jnp.broadcast_to(value[row : row + 1, :], shape)

    for g in range(len(rows)):
        first = 8 * g
        lanes = {
            u: [lane_splat(rows[u], first + s) for s in range(8)] for u in range(g, len(rows))
        }
        scale = jnp.zeros(shape, jnp.float32)
        for t in range(8):
            pivot = row_splat(lanes[g][t], t)
            root = lax.rsqrt(pivot)
            inverse = root * root
            scale = jnp.where(sub == t, root, scale)
            row_t = row_splat(rows[g], t) * inverse
            splats = {s: row_splat(lanes[g][s], t) * inverse for s in range(t + 1, 8)}
            for u in range(g, len(rows)):
                factor = lanes[u][t]
                if u == g:
                    factor = jnp.where(sub > t, factor, 0.0)
                rows[u] = rows[u] - factor * row_t
                for s in range(t + 1, 8):
                    lanes[u][s] = lanes[u][s] - factor * splats[s]
        rows[g] = rows[g] * scale
    return jnp.concatenate(rows, axis=0)[:, size:]


def renew_kernel(stat_ref, basis_ref, out_ref, gram_ref, rest_ref):
    size = stat_ref.shape[0]
    product = dot_exact(stat_ref[...], basis_ref[...], 1, 0)
    rest_ref[...] = product
    gram_ref[...] = dot_exact(product, product, 0, 0)
    for low in range(0, size, 128):
        high = low + 128
        block = gram_ref[low:high, low:high]
        corner = small_factor(block[:64, :64])
        across = dot_exact(corner, block[:64, 64:], 1, 0)
        second = small_factor(block[64:, 64:] - dot_exact(across, across, 0, 0))
        below = dot_exact(second, dot_exact(across, corner, 0, 0), 1, 0)
        inverse = jnp.concatenate(
            [
                jnp.concatenate([corner, jnp.zeros_like(corner)], axis=1),
                jnp.concatenate([-below, second], axis=1),
            ],
            axis=0,
        )
        columns = dot_exact(rest_ref[:, low:high], inverse, 1, 1)
        out_ref[:, low:high] = columns
        if high < size:
            panel = dot_exact(inverse, gram_ref[low:high, high:], 1, 0)
            gram_ref[high:, high:] -= dot_exact(panel, panel, 0, 0)
            rest_ref[:, high:] -= dot_exact(columns, panel, 1, 0)


def renew_basis(statistic, basis):
    shape = statistic.shape
    return call(
        renew_kernel,
        full(*shape),
        statistic,
        basis,
        scratch=[pltpu.VMEM(shape, jnp.float32), pltpu.VMEM(shape, jnp.float32)],
        microseconds=29,
    )


def peers_of(axis):
    size, me = lax.axis_size(axis), lax.axis_index(axis)
    return [
        (step, lax.rem(me + step, size), lax.rem(me + size - step, size)) for step in range(1, size)
    ]


def greet(*places):
    barrier = pltpu.get_barrier_semaphore()
    for axis, index in places:
        pl.semaphore_signal(barrier, inc=1, device_id={axis: index}, device_id_type=mesh_ids)
    pl.semaphore_wait(barrier, len(places))


def push(source, target, sems, slot, axis, index):
    copy = pltpu.make_async_remote_copy(
        src_ref=source,
        dst_ref=target,
        send_sem=sems[0].at[slot],
        recv_sem=sems[1].at[slot],
        device_id={axis: index},
        device_id_type=mesh_ids,
    )
    copy.start()
    return copy


def sem_pair(count):
    return [pltpu.SemaphoreType.DMA((count,)), pltpu.SemaphoreType.DMA((count,))]


def talk(kernel, outs, collective_id, *args, scratch=(), microseconds=15, before=()):
    def body(*refs):
        kernel(*refs[: len(args)], *refs[len(args) + len(before) :])

    return pl.pallas_call(
        body,
        out_shape=outs,
        in_specs=[vmem] * len(args) + [pl.BlockSpec(memory_space=pl.ANY)] * len(before),
        out_specs=jax.tree.map(lambda _: vmem, outs),
        scratch_shapes=list(scratch),
        compiler_params=pltpu.CompilerParams(
            collective_id=collective_id, has_side_effects=True, vmem_limit_bytes=56 * 2**20
        ),
        cost_estimate=cost_of(microseconds),
    )(*args, *before)


def gather_kernel(axis, *refs):
    count = (len(refs) - 2) // 2
    others = peers_of(axis)
    greet(*[(axis, to) for _, to, _ in others])
    me = lax.axis_index(axis)
    copies = [
        push(refs[k], refs[count + k].at[me], refs[-2:], k * len(others) + step - 1, axis, to)
        for k in range(count)
        for step, to, _ in others
    ]
    for k in range(count):
        refs[count + k][me] = refs[k][...]
    for copy in copies:
        copy.wait()


def gather_small(axis, collective_id, *arrays):
    size = lax.axis_size(axis)
    outs = tuple(jax.ShapeDtypeStruct((size, *x.shape), x.dtype) for x in arrays)
    sems = sem_pair((size - 1) * len(arrays))
    return talk(partial(gather_kernel, axis), outs, collective_id, *arrays, scratch=sems)


def sum_kernel(x_ref, out_ref, parts_ref, mine_ref, s0, r0, s1, r1):
    others = peers_of("vocab")
    greet(*[("vocab", to) for _, to, _ in others])
    size, me = lax.axis_size("vocab"), lax.axis_index("vocab")
    rows = mine_ref.shape[0]

    def rows_of(index):
        return pl.ds(pl.multiple_of(index * rows, rows), rows)

    copies = [
        push(x_ref.at[rows_of(to)], parts_ref.at[me], (s0, r0), step - 1, "vocab", to)
        for step, to, _ in others
    ]
    parts_ref[me] = x_ref[rows_of(me), :]
    for copy in copies:
        copy.wait()
    total = parts_ref[0].astype(jnp.float32)
    for index in range(1, size):
        total = total + parts_ref[index].astype(jnp.float32)
    mine_ref[...] = total.astype(mine_ref.dtype)
    copies = [
        push(mine_ref, out_ref.at[rows_of(me)], (s1, r1), step - 1, "vocab", to)
        for step, to, _ in others
    ]
    out_ref[rows_of(me), :] = mine_ref[...]
    for copy in copies:
        copy.wait()


def sum_vocab(x, collective_id):
    replicas = lax.axis_size("vocab")
    rows, columns = x.shape
    share = rows // replicas
    return talk(
        sum_kernel,
        jax.ShapeDtypeStruct(x.shape, x.dtype),
        collective_id,
        x,
        scratch=[
            pltpu.VMEM((replicas, share, columns), x.dtype),
            pltpu.VMEM((share, columns), x.dtype),
        ]
        + sem_pair(replicas - 1)
        + sem_pair(replicas - 1),
    )


def flip(index, bit):
    return index + bit - 2 * bit * lax.rem(index // bit, 2)


def tail_kernel(
    x_ref, few_ref, out_ref, sum_ref, parts_ref, seen_ref, line_ref, lines_ref,
    s0, r0, s1, r1, s2, r2, s3, r3, s4, r4,
):
    owners, replicas = peers_of("dp"), peers_of("vocab")
    greet(*[("dp", to) for _, to, _ in owners], *[("vocab", to) for _, to, _ in replicas])
    size, me, here = lax.axis_size("dp"), lax.axis_index("dp"), lax.axis_index("vocab")
    near, side = flip(here, 1), lax.rem(here, 2)
    rows = parts_ref.shape[1]

    def rows_of(index):
        return pl.ds(pl.multiple_of((side * size + index) * rows, rows), rows)

    few = [
        push(few_ref, seen_ref.at[here], (s2, r2), step - 1, "vocab", to) for step, to, _ in replicas
    ]
    wide = [
        push(x_ref.at[rows_of(to)], parts_ref.at[me], (s0, r0), step - 1, "dp", to)
        for step, to, _ in owners
    ]
    seen_ref[here] = few_ref[...]
    parts_ref[me] = x_ref[rows_of(me), :]
    for copy in few:
        copy.wait()
    line_ref[...] = jnp.sum(seen_ref[...], axis=0)
    few = [
        push(line_ref, lines_ref.at[me], (s3, r3), step - 1, "dp", to) for step, to, _ in owners
    ]
    lines_ref[me] = line_ref[...]
    for copy in wide:
        copy.wait()
    out_ref[rows_of(me), :] = jnp.sum(parts_ref[...], axis=0)
    mine = out_ref.at[rows_of(me)]
    wide = [push(mine, mine, (s1, r1), step - 1, "dp", to) for step, to, _ in owners]
    close = [push(mine, mine, (s4, r4), 0, "vocab", near)]
    for copy in few:
        copy.wait()
    sum_ref[...] = jnp.sum(lines_ref[...], axis=0)
    for copy, (step, _, origin) in zip(wide, owners):
        copy.wait()
        theirs = out_ref.at[rows_of(origin)]
        close.append(push(theirs, theirs, (s4, r4), step, "vocab", near))
    for copy in close:
        copy.wait()


def sum_tail(x, few, collective_id):
    owners, replicas = lax.axis_size("dp"), lax.axis_size("vocab")
    rows, columns = x.shape
    share = rows // (2 * owners)
    return talk(
        tail_kernel,
        (full(*x.shape), full(*few.shape)),
        collective_id,
        x,
        few,
        scratch=[
            pltpu.VMEM((owners, share, columns), jnp.float32),
            pltpu.VMEM((replicas, *few.shape), jnp.float32),
            pltpu.VMEM(few.shape, jnp.float32),
            pltpu.VMEM((owners, *few.shape), jnp.float32),
        ]
        + sem_pair(owners - 1)
        + sem_pair(owners - 1)
        + sem_pair(replicas - 1)
        + sem_pair(owners - 1)
        + sem_pair(owners),
    )


def far_replicas():
    here, size = lax.axis_index("vocab"), lax.axis_size("vocab")
    return [
        (step // 2 - 1, lax.rem(here + step, size), lax.rem(here + size - step, size))
        for step in range(2, size, 2)
    ]


def sum_tokens(rows_refs, place_ref, left_ref, table_ref, wide_ref, embed_ref, square_ref):
    owners, length, columns = rows_refs[0].shape
    for owner in range(owners):
        for k, rows_ref in enumerate(rows_refs):
            start = (owner * len(rows_refs) + k) * length
            span = slice(start, start + length)
            left = rows_ref[owner] * left_ref[span, :]
            wide_ref[span, :columns] = left
            wide_ref[span, columns:] = rows_ref[owner] - left
    tokens, half = wide_ref.shape[0], embed_ref.shape[0] // 2
    tile, step = half // 4, 1024
    square_ref[...] = jnp.zeros(square_ref.shape, jnp.float32)

    def one(index, carry):
        start = index * tile
        places = lax.broadcasted_iota(jnp.int32, (tile, step), 0) + start
        total = jnp.zeros((tile, 2 * columns), jnp.float32)
        for first in range(0, tokens, step):
            chosen = (places == place_ref[:, first : first + step]).astype(jnp.bfloat16)
            total = total + dot_dims(chosen, wide_ref[first : first + step, :], 1, 0)
        for side in range(2):
            span = pl.ds(pl.multiple_of(side * half + start, 16), tile)
            part = total[:, side * columns : (side + 1) * columns]
            part = part + table_ref[span, :].astype(jnp.float32)
            embed_ref[span, :] = part
            square_ref[...] += jnp.sum(part * part, axis=0, keepdims=True)
        return carry

    lax.fori_loop(0, 4, one, 0)


def gradient_kernel(chunks, count, inside, *refs):
    x_refs, refs = refs[:chunks], refs[chunks:]
    rows_refs, refs = refs[:count], refs[count:]
    if inside:
        (place_ref, left_ref, table_ref), refs = refs[:3], refs[3:]
    (out_ref, square_ref, *refs) = refs
    swapped_refs, refs = refs[:count], refs[count:]
    if inside:
        (embed_ref, embed_square_ref), refs = refs[:2], refs[2:]
        *refs, wide_ref = refs
    parts_ref, s0, r0, s1, r1, s2, r2, s3, r3, s4, r4 = refs
    owners = peers_of("dp")
    here, me = lax.axis_index("vocab"), lax.axis_index("dp")
    near = flip(here, 1)
    size = lax.axis_size("vocab")
    steps = range(2, size, 2)
    greet(
        *[("dp", to) for _, to, _ in owners],
        *[("vocab", lax.rem(here + step, size)) for step in steps],
        ("vocab", near),
    )

    def spread(c, origin, sems, slot, to):
        place = out_ref.at[c, origin]
        return push(place, place, sems, slot, "vocab", to)

    arriving = [
        [
            push(x_refs[c].at[to], parts_ref.at[c, me], (s0, r0), (step - 1) * chunks + c, "dp", to)
            for step, to, _ in owners
        ]
        for c in range(chunks)
    ]

    def half_of(ref):
        rows = ref.shape[1] // 2
        return pl.ds(pl.multiple_of(lax.rem(here, 2) * rows, rows), rows)

    swaps = [
        [
            push(
                rows_ref.at[to, half_of(rows_ref)],
                swapped_ref.at[me, half_of(rows_ref)],
                (s3, r3),
                k * len(owners) + step - 1,
                "dp",
                to,
            )
            for step, to, _ in owners
        ]
        for k, (rows_ref, swapped_ref) in enumerate(zip(rows_refs, swapped_refs))
    ]
    for rows_ref, swapped_ref in zip(rows_refs, swapped_refs):
        swapped_ref[me] = rows_ref[me]
    far, close = [], []
    square = jnp.zeros(square_ref.shape, jnp.float32)
    for c in range(chunks):
        parts_ref[c, me] = x_refs[c][me]
        for copy in arriving[c]:
            copy.wait()
        total = jnp.sum(parts_ref[c].astype(jnp.float32), axis=0)
        out_ref[c, here] = total.astype(out_ref.dtype)
        square = square + jnp.sum(total * total, axis=0, keepdims=True)
        far.append(
            [
                spread(c, here, (s1, r1), k * chunks + c, lax.rem(here + step, size))
                for k, step in enumerate(steps)
            ]
        )
        close.append(spread(c, here, (s2, r2), c, near))
    square_ref[...] = square
    moved = []
    for k, swapped_ref in enumerate(swapped_refs):
        for copy, (step, _, origin) in zip(swaps[k], owners):
            copy.wait()
            place = swapped_ref.at[origin, half_of(swapped_ref)]
            moved.append(push(place, place, (s4, r4), k * len(owners) + step - 1, "vocab", near))
    for copy in moved:
        copy.wait()
    if inside:
        sum_tokens(
            swapped_refs[:2], place_ref, left_ref, table_ref, wide_ref, embed_ref, embed_square_ref
        )
    for c in range(chunks):
        for k, step in enumerate(steps):
            far[c][k].wait()
            origin = lax.rem(here + size - step, size)
            close.append(spread(c, origin, (s2, r2), (k + 1) * chunks + c, near))
    for copy in close:
        copy.wait()


def share_gradients(blocks, rows, collective_id, before, tokens):
    owners, replicas = lax.axis_size("dp"), lax.axis_size("vocab")
    chunks = len(blocks)
    others = (replicas // 2 - 1) * chunks
    shape, kind = blocks[0].shape, blocks[0].dtype
    return talk(
        partial(gradient_kernel, chunks, len(rows), bool(tokens)),
        (
            jax.ShapeDtypeStruct((chunks, replicas, *shape[1:]), kind),
            full(1, shape[2]),
            *[jax.ShapeDtypeStruct(part.shape, part.dtype) for part in rows],
            *[full(*size) for part in tokens[2:] for size in (part.shape, (1, part.shape[1]))],
        ),
        collective_id,
        *blocks,
        *rows,
        *tokens,
        scratch=[pltpu.VMEM((chunks, *shape), kind)]
        + sem_pair((owners - 1) * chunks)
        + sem_pair(others)
        + sem_pair(others + chunks)
        + sem_pair(len(rows) * (owners - 1))
        + sem_pair(len(rows) * (owners - 1))
        + [pltpu.VMEM((part.shape[1], 2 * tokens[2].shape[1]), jnp.bfloat16) for part in tokens[:1]],
        microseconds=40,
        before=before,
    )


def swap_kernel(x_ref, out_ref, s0, r0, s1, r1):
    others = peers_of("dp")
    me, here = lax.axis_index("dp"), lax.axis_index("vocab")
    near, side = flip(here, 1), lax.rem(here, 2)
    greet(*[("dp", to) for _, to, _ in others], ("vocab", near))
    rows = x_ref.shape[1] // 2
    half = pl.ds(pl.multiple_of(side * rows, rows), rows)
    copies = [
        push(x_ref.at[to, half], out_ref.at[me, half], (s0, r0), step - 1, "dp", to)
        for step, to, _ in others
    ]
    out_ref[me] = x_ref[me]
    close = []
    for copy, (step, _, origin) in zip(copies, others):
        copy.wait()
        place = out_ref.at[origin, half]
        close.append(push(place, place, (s1, r1), step - 1, "vocab", near))
    for copy in close:
        copy.wait()


def swap_owners(x, collective_id, before):
    owners = lax.axis_size("dp")
    return talk(
        swap_kernel,
        jax.ShapeDtypeStruct(x.shape, x.dtype),
        collective_id,
        x,
        scratch=sem_pair(owners - 1) + sem_pair(owners - 1),
        before=before,
    )


def look_up_tokens(code_ref, paired_ref, found_ref):
    step = 256
    columns = found_ref.shape[1]

    def one(index, carry):
        span = pl.ds(pl.multiple_of(index * step, step), step)
        code = code_ref[span, :]
        places = lax.broadcasted_iota(jnp.int32, (step, paired_ref.shape[0]), 1)
        chosen = (places == lax.shift_right_arithmetic(code, 1)).astype(jnp.bfloat16)
        wide = dot_dims(chosen, paired_ref[...], 1, 0)
        left = jnp.bitwise_and(code, 1) == 1
        found_ref[span, :] = jnp.where(left, wide[:, :columns], wide[:, columns:]).astype(jnp.bfloat16)
        return carry

    lax.fori_loop(0, code_ref.shape[0] // step, one, 0)


def token_kernel(
    scale, inside, x_ref, place_ref, attn_ref, ffn_ref, code_ref, paired_ref, out_ref, attn_out_ref, ffn_out_ref,
    found_ref, near_ref, parts_ref, blocks_ref, row_ref,
    s0, r0, s1, r1, s2, r2, s3, r3, s4, r4, s5, r5, s6, r6,
):
    owners, others = peers_of("dp"), far_replicas()
    me, here = lax.axis_index("dp"), lax.axis_index("vocab")
    near, side = flip(here, 1), lax.rem(here, 2)
    greet(
        *[("dp", to) for _, to, _ in owners], *[("vocab", to) for _, to, _ in others], ("vocab", near)
    )
    count, length, columns = x_ref.shape
    half, pairs = length // 2, lax.axis_size("vocab") // 2
    share = half // pairs

    def half_of(which):
        return pl.ds(pl.multiple_of(which * half, half), half)

    def share_of(index):
        return pl.ds(pl.multiple_of(index // 2 * share, share), share)

    def place_of(index):
        return pl.ds(pl.multiple_of(side * half + index // 2 * share, share), share)

    def send_weights(ref, own_ref, slot, span):
        count, rows = own_ref.shape[0] // 2, own_ref.shape[1]
        mine = pl.ds(side * count, count)

        def place(origin):
            return ref.at[mine, pl.ds(pl.multiple_of(origin * rows + span[0], span[1]), span[1])]

        copies = [
            push(own_ref.at[mine, pl.ds(*span)], place(me), (s5, r5), slot + step - 1, "dp", to)
            for step, to, _ in owners
        ]
        return [(copy, place(origin), slot + step - 1) for copy, (step, _, origin) in zip(copies, owners)]

    def relay_weights(sent):
        relays = []
        for copy, place, slot in sent:
            copy.wait()
            relays.append(push(place, place, (s6, r6), slot, "vocab", near))
        return relays

    first = push(x_ref.at[:, half_of(1 - side)], near_ref, (s0, r0), 0, "vocab", near)
    some = ffn_ref.shape[1] // 2
    early = send_weights(attn_out_ref, attn_ref, 0, (0, attn_ref.shape[1]))
    early += send_weights(ffn_out_ref, ffn_ref, len(owners), (0, some))
    for ref, own_ref in ((attn_out_ref, attn_ref), (ffn_out_ref, ffn_ref)):
        rows = own_ref.shape[1]
        ref[:, pl.ds(pl.multiple_of(me * rows, rows), rows), :] = own_ref[...]
    first.wait()
    near_ref[...] += x_ref[:, half_of(side)]
    copies = [
        push(near_ref.at[:, share_of(to)], parts_ref.at[slot], (s1, r1), slot, "vocab", to)
        for slot, to, _ in others
    ]
    if inside:
        look_up_tokens(code_ref, paired_ref, found_ref)
    else:
        found_ref[...] = jnp.zeros(found_ref.shape, found_ref.dtype)
    for copy in copies:
        copy.wait()
    total = near_ref[:, share_of(here)]
    for slot, _, _ in others:
        total = total + parts_ref[slot]
    blocks_ref[...] = total
    copies = [
        push(
            blocks_ref.at[to],
            row_ref.at[me, place_of(here)],
            (s2, r2),
            step - 1,
            "dp",
            to,
        )
        for step, to, _ in owners
    ]
    row_ref[me, place_of(here)] = blocks_ref[me]
    for copy in copies:
        copy.wait()
    late = send_weights(ffn_out_ref, ffn_ref, 2 * len(owners), (some, some))
    mine = row_ref.at[:, place_of(here)]
    copies = [push(mine, mine, (s3, r3), slot, "vocab", to) for slot, to, _ in others]
    close = [push(mine, mine, (s4, r4), 0, "vocab", near)]
    for copy, (slot, _, origin) in zip(copies, others):
        copy.wait()
        theirs = row_ref.at[:, place_of(origin)]
        close.append(push(theirs, theirs, (s4, r4), slot + 1, "vocab", near))
    close += relay_weights(early)
    for copy in close[: pairs]:
        copy.wait()
    for owner in range(count):
        band = slice(owner * columns, (owner + 1) * columns)
        out_ref[:, band] = row_ref[owner].astype(jnp.float32) * scale + place_ref[:, band]
    close += relay_weights(late)
    for copy in close[pairs:]:
        copy.wait()


def gather_tokens(x, places, attn, ffn, codes, paired, scale, collective_id):
    owners, pairs = lax.axis_size("dp"), lax.axis_size("vocab") // 2
    _, length, columns = x.shape
    half = length // 2
    width = owners * columns
    whole = [low(w.shape[0], owners * w.shape[1], width) for w in (attn, ffn)]
    return talk(
        partial(token_kernel, scale, paired is not None),
        (full(length, width), *whole, low(codes.shape[0], columns)),
        collective_id,
        x,
        places,
        attn,
        ffn,
        codes,
        attn[0] if paired is None else paired,
        scratch=[
            pltpu.VMEM((owners, half, columns), x.dtype),
            pltpu.VMEM((pairs - 1, owners, half // pairs, columns), x.dtype),
            pltpu.VMEM((owners, half // pairs, columns), x.dtype),
            pltpu.VMEM((owners, length, columns), x.dtype),
        ]
        + sem_pair(1)
        + sem_pair(pairs - 1)
        + sem_pair(owners - 1)
        + sem_pair(pairs - 1)
        + sem_pair(pairs)
        + sem_pair(3 * owners - 3)
        + sem_pair(3 * owners - 3),
        microseconds=50,
    )


def sinusoid(length, model_width):
    places = np.arange(length, dtype=np.float32)[:, None]
    halves = np.arange(model_width // 2, dtype=np.float32)[None, :]
    angles = places * np.exp(halves * np.float32(-2.0 * math.log(10000.0) / model_width))
    angles = angles.astype(np.float64)
    return (
        np.stack([np.sin(angles), np.cos(angles)], axis=-1)
        .reshape(length, model_width)
        .astype(np.float32)
    )


def one_hot(ids, columns):
    return (ids[:, None] == columns[None, :]).astype(jnp.bfloat16)


def pick_weights(target_seg, pick_rows):
    sentence = jnp.take(target_seg, pick_rows, axis=0)
    return jnp.sum((sentence[:, None] == sentence[None, :]).astype(jnp.float32), axis=1)


def adam_direction(moment, second):
    return moment / (1.0 - beta_one**STEP) / (jnp.sqrt(second / (1.0 - beta_two**STEP)) + adam_eps)


def adam_update(weight, grad_item, moment, second, step_rate, decay_weight):
    moment = beta_one * moment + (1.0 - beta_one) * grad_item
    second = beta_two * second + (1.0 - beta_two) * grad_item * grad_item
    return (
        weight - step_rate * (adam_direction(moment, second) + decay_weight * weight),
        moment,
        second,
    )


def after(array, number):
    return array + jnp.where(jnp.isnan(number), 1, 0).astype(array.dtype)


def body(
    src_ids,
    src_seg,
    tgt_ids,
    tgt_seg,
    pick_pos,
    pick_label,
    attn_w,
    attn_m,
    attn_v,
    ffn_w,
    ffn_m,
    ffn_v,
    soap_basis,
    soap_stats,
    norm_p,
    norm_m,
    norm_v,
    embedding,
    embed_m,
    embed_v,
):
    owners, replicas = lax.axis_size("dp"), lax.axis_size("vocab")
    replica = lax.axis_index("vocab")
    own_table = embedding.astype(jnp.bfloat16)
    own_norms = jnp.pad(norm_p.astype(jnp.bfloat16).astype(jnp.float32), ((0, 2), (0, 0)))
    all_ids, norm_rows = gather_small("dp", 1, jnp.concatenate([src_ids, tgt_ids]), own_norms)
    norm_rows = jnp.swapaxes(norm_rows, 0, 1).reshape(16, -1)
    norms = [jnp.stack([norm_rows[k], norm_rows[7 + k]]) for k in range(7)]
    vocab_count, width = embedding.shape[0], attn_w.shape[2]
    source, source_seg, target, target_seg = (src_ids[0], src_seg[0], tgt_ids[0], tgt_seg[0])
    pick_rows, labels = (pick_pos[0], pick_label[0])
    length = source.shape[0]
    embed_scale = math.sqrt(width)
    half = vocab_count // 2
    halves = jnp.arange(half)
    paired = jnp.concatenate([own_table[:half], own_table[half:]], axis=1)

    def paired_places(ids):
        place = ids - replica * vocab_count
        inside = (place >= 0) & (place < vocab_count)
        return jnp.where(inside, place % half, -1), place < half

    def look_up(ids):
        place, left = paired_places(ids)
        wide = lax.dot_general(one_hot(place, halves), paired, (((1,), (0,)), ((), ())))
        return jnp.where(left[:, None], wide[:, :paired.shape[1] // 2], wide[:, paired.shape[1] // 2 :])

    source_part = look_up(all_ids[:, 0].reshape(-1))
    if owners == 4:
        place, left = paired_places(all_ids[:, 1].reshape(-1))
        codes = jnp.where(place < 0, -1, 2 * place + left.astype(jnp.int32))[:, None]
        whole_paired = jnp.pad(paired, ((0, -half % 128), (0, 0)))
    else:
        codes, whole_paired = jnp.zeros((16, 1), jnp.int32), None
    positional = sinusoid(length, width)
    enc_in, enc_attn_w, enc_ffn_w, target_part = gather_tokens(
        source_part.reshape(owners, length, -1),
        positional,
        attn_w[0:4].astype(jnp.bfloat16),
        ffn_w[0:2].astype(jnp.bfloat16),
        codes,
        whole_paired,
        embed_scale,
        2,
    )
    if owners != 4:
        target_part = look_up(all_ids[:, 1].reshape(-1))
    target_sum = lax.psum(target_part, "vocab")
    enc_mid, enc_attn = attn_forward(
        enc_in, norms[0], ((enc_attn_w,), 0, 0), source_seg, source_seg, None, False
    )
    self_w, cross_w, dec_ffn_w, ready = late_weights(attn_w[4:], ffn_w[2:], enc_in, enc_mid)
    enc_out, encoded, enc_ffn = ffn_forward(enc_mid, norms[1], norms[2], ((enc_ffn_w,), 0, 0))
    target_rows = swap_owners(target_sum.reshape(owners, length, -1), 3, (enc_out,))
    table_low = after(own_table, ready)
    table_low = lax.all_gather(after(table_low, target_rows[0, 0, 0]), "dp", axis=1, tiled=True)
    target_rows = jnp.swapaxes(target_rows, 0, 1).reshape(length, -1).astype(jnp.float32)
    dec_in = target_rows * embed_scale + positional
    dec_mid, dec_self = attn_forward(
        dec_in, norms[3], self_w, target_seg, target_seg, None, True
    )
    dec_late, dec_cross = attn_forward(
        dec_mid, norms[4], cross_w, target_seg, source_seg, encoded, False
    )
    dec_out, final_low, dec_ffn = ffn_forward(dec_late, norms[5], norms[6], dec_ffn_w)

    own_labels = labels - replica * vocab_count
    picked, own_stats = loss_forward(final_low, pick_rows, own_labels, table_low)
    (seen,) = gather_small("vocab", 4, own_stats)
    weight = 1.0 / pick_weights(target_seg, pick_rows)
    grad_picked, table_parts, losses = loss_backward(
        picked, seen, weight, own_labels, table_low, owners
    )
    grad_table = lax.psum_scatter(table_parts, "dp", scatter_dimension=0, tiled=False)
    grad_picked = sum_vocab(grad_picked, 5)
    loss_part = jnp.sum(losses)
    count_part = (target_seg[-1] + 1).astype(jnp.float32)

    picks = share_selector(width, owners, replicas, replica, width)
    hidden = ffn_w.shape[1] * owners
    hidden_picks = share_selector(hidden, owners, replicas, replica, 512)
    norm_grads = [None] * 7
    grad, norm_grads[6], norm_grads[5], *ffn_blocks = ffn_backward(
        grad_picked, dec_ffn, hidden_picks, owners, places=pick_rows
    )
    grad, norm_grads[4], block, grad_encoded = attn_backward(grad, dec_cross, picks, owners, None)
    early = lax.psum_scatter(
        jnp.concatenate([block, *ffn_blocks], axis=1), "dp", scatter_dimension=0, tiled=False
    )
    grad, norm_grads[3], self_block, target_rows = attn_backward(
        grad, dec_self, picks, owners, embed_scale
    )
    grad, norm_grads[2], norm_grads[1], *ffn_blocks = ffn_backward(
        grad_encoded, enc_ffn, hidden_picks, owners, before=(grad_table, grad)
    )
    early_sum = after(early, grad[0, 0])
    early = lax.all_gather(early_sum, "vocab")
    grad, norm_grads[0], block, source_rows = attn_backward(
        grad, enc_attn, picks, owners, embed_scale, before=(early_sum,)
    )
    norm_grad = jnp.stack([after(part, early[0, 0, 0]) for part in norm_grads])
    norm_grad = jnp.concatenate([norm_grad[:, 0], norm_grad[:, 1], jnp.zeros((2, width))], axis=0)
    norm_grad = jnp.swapaxes(norm_grad.reshape(16, owners, -1), 0, 1)
    place, left = paired_places(all_ids.reshape(-1))
    tokens = ()
    if owners == 4:
        ones = jnp.broadcast_to(left[:, None], (left.shape[0], width // owners))
        tokens = (place[None, :], ones.astype(jnp.bfloat16), grad_table)
    late, layer_squares, source_rows, target_rows, norm_grad, *found = share_gradients(
        [block, self_block, *ffn_blocks], [source_rows, target_rows, norm_grad], 7, (early,), tokens
    )
    g_norm = jnp.sum(norm_grad, axis=0)[:14]
    if owners == 4:
        g_embed, embed_squares = found
    else:
        token_grads = jnp.concatenate([source_rows, target_rows], axis=1).reshape(
            owners * 2 * length, -1
        )
        left = left[:, None]
        token_grads = jnp.concatenate(
            [jnp.where(left, token_grads, 0), jnp.where(left, 0, token_grads)], axis=1
        )
        g_paired = dot_dims(one_hot(place, halves), token_grads, 0, 0)
        g_embed = grad_table.astype(jnp.float32) + jnp.concatenate(
            jnp.split(g_paired, 2, axis=1), axis=0
        )
        embed_squares = g_embed * g_embed

    def by_matrix(shared, count):
        blocks = jnp.swapaxes(shared.reshape(replicas, count, -1, width), 0, 1)
        return blocks.reshape(count, -1, width)

    early = by_matrix(early, 3)
    g_attn = [by_matrix(part, 4) for part in (late[0], late[1], early[0])]
    g_attn = jnp.concatenate(g_attn)
    g_ffn = jnp.concatenate([late[2:].reshape(2, -1, width), early[1:]])

    matrix = replica // 2
    own_grad = lax.dynamic_index_in_dim(g_ffn, matrix, 0, keepdims=False)
    own_products = dot_dims(own_grad, own_grad, 0, 0)
    first_copy = (replica == 0).astype(jnp.float32)
    raw_squares = (
        jnp.sum(layer_squares)
        + jnp.sum(jnp.square(early_sum.astype(jnp.float32)))
        + jnp.sum(embed_squares)
        + first_copy * jnp.sum(g_norm * g_norm)
    )
    few = jnp.stack([first_copy * loss_part, first_copy * count_part, raw_squares])
    few = jnp.broadcast_to(jnp.pad(few, (0, 5))[:, None], (8, 128))
    own_products, few = sum_tail(own_products, few, 8)
    loss_sum, sentences, squares = few[0, 0], few[1, 0], few[2, 0]
    grad_norm = jnp.sqrt(squares) / sentences
    factor = jnp.minimum(1.0, clip_limit / (grad_norm + norm_eps)) / sentences
    g_norm = g_norm * factor

    def all_matrices(own):
        rows = own.shape[0] // 2
        half = lax.dynamic_slice_in_dim(own.astype(jnp.bfloat16), replica % 2 * rows, rows, 0)
        return lax.all_gather(half, "vocab").reshape(4, 2 * rows, -1)

    all_products = all_matrices(own_products)
    new_stats = stat_decay * soap_stats + (1.0 - stat_decay) * (factor * factor) * (
        all_products.astype(jnp.float32)
    )
    own_stat = stat_decay * lax.dynamic_index_in_dim(soap_stats, matrix, 0, keepdims=False) + (
        1.0 - stat_decay
    ) * (factor * factor) * own_products
    own_basis = renew_basis(own_stat, lax.dynamic_index_in_dim(soap_basis, matrix, 0, keepdims=False))
    new_basis = all_matrices(after(own_basis, new_stats[0, 0, 0])).astype(jnp.float32)

    new_norm, m_norm, v_norm = adam_update(norm_p, g_norm, norm_m, norm_v, rate_vector, 0.0)
    updated = update_matrices(
        factor,
        soap_basis,
        (g_attn, attn_w, attn_m, attn_v),
        (g_embed, embedding, embed_m, embed_v),
        (g_ffn, ffn_w, ffn_m, ffn_v),
    )
    new_attn, m_attn, v_attn, new_embed, m_embed, v_embed, new_ffn, m_ffn, v_ffn = updated
    return (
        loss_sum,
        sentences,
        grad_norm,
        new_attn,
        m_attn,
        v_attn,
        new_ffn,
        m_ffn,
        v_ffn,
        new_basis,
        new_stats,
        new_norm,
        m_norm,
        v_norm,
        new_embed,
        m_embed,
        v_embed,
    )


def solution(mesh):
    placed = (
        P("dp", None),
        P("dp", None),
        P("dp", None),
        P("dp", None),
        P("dp", None),
        P("dp", None),
        P(None, "dp", None),
        P(None, "dp", None),
        P(None, "dp", None),
        P(None, "dp", None),
        P(None, "dp", None),
        P(None, "dp", None),
        P(),
        P(),
        P(None, "dp"),
        P(None, "dp"),
        P(None, "dp"),
        P("vocab", "dp"),
        P("vocab", "dp"),
        P("vocab", "dp"),
    )
    return jax.shard_map(
        body,
        mesh=mesh,
        in_specs=placed,
        out_specs=(
            P(),
            P(),
            P(),
            P(None, "dp", None),
            P(None, "dp", None),
            P(None, "dp", None),
            P(None, "dp", None),
            P(None, "dp", None),
            P(None, "dp", None),
            P(),
            P(),
            P(None, "dp"),
            P(None, "dp"),
            P(None, "dp"),
            P("vocab", "dp"),
            P("vocab", "dp"),
            P("vocab", "dp"),
        ),
        check_vma=False,
    )
```

```python
from functools import partial
import math

import jax
import jax.numpy as jnp
import numpy as np
from jax import lax
from jax.experimental import pallas as pl
from jax.experimental.pallas import tpu as pltpu
from jax.sharding import PartitionSpec as P

HEADS = 8
STEP = 10
TILE = 128

highest = lax.Precision.HIGHEST
beta_one = 0.9
beta_two = 0.999
adam_eps = 1e-08
decay_rate = 0.01
rate_matrix = 0.03
rate_vector = 0.3
clip_limit = 1.0
stat_decay = 0.95
norm_eps = 1e-06
masked = -1e30
log_two_e = math.log2(math.e)
vmem = pl.BlockSpec(memory_space=pltpu.VMEM)
smem = pl.BlockSpec(memory_space=pltpu.SMEM)
mesh_ids = pl.DeviceIdType.MESH


def dot_dims(left, right, left_dim, right_dim):
    return lax.dot_general(
        left, right, (((left_dim,), (right_dim,)), ((), ())), preferred_element_type=jnp.float32
    )


def dot_exact(left, right, left_dim, right_dim):
    return lax.dot_general(
        left,
        right,
        (((left_dim,), (right_dim,)), ((), ())),
        precision=highest,
        preferred_element_type=jnp.float32,
    )


def cost_of(microseconds):
    return pl.CostEstimate(flops=microseconds * 10**9, bytes_accessed=0, transcendentals=0)


def call(kernel, outs, *args, scratch=(), smem_args=0, microseconds=5, before=(), far=()):
    any_spec = pl.BlockSpec(memory_space=pl.ANY)
    specs = [vmem] * (len(args) - smem_args) + [smem] * smem_args + [any_spec] * len(before)
    for k in far:
        specs[k] = any_spec

    def body(*refs):
        kernel(*refs[: len(args)], *refs[len(args) + len(before) :])

    return pl.pallas_call(
        body,
        out_shape=outs,
        in_specs=specs,
        out_specs=jax.tree.map(lambda _: vmem, outs),
        scratch_shapes=list(scratch),
        compiler_params=pltpu.CompilerParams(vmem_limit_bytes=56 * 2**20),
        cost_estimate=cost_of(microseconds),
    )(*args, *before)


def low(*shape):
    return jax.ShapeDtypeStruct(shape, jnp.bfloat16)


def full(*shape):
    return jax.ShapeDtypeStruct(shape, jnp.float32)


def norm_parts(values):
    centre = values - jnp.mean(values, axis=-1, keepdims=True)
    spread = jnp.mean(centre * centre, axis=-1, keepdims=True)
    root = lax.rsqrt(spread + norm_eps)
    return centre * root, root


def norm_forward(values, ln_ref):
    return norm_parts(values)[0] * ln_ref[0:1, :] + ln_ref[1:2, :]


def norm_backward(grad, values, ln_ref, ln_grad_ref):
    normed, root = norm_parts(values)
    ln_grad_ref[0:1, :] = jnp.sum(grad * normed, axis=0, keepdims=True)
    ln_grad_ref[1:2, :] = jnp.sum(grad, axis=0, keepdims=True)
    inner = grad * ln_ref[0:1, :]
    return root * (
        inner
        - jnp.mean(inner, axis=-1, keepdims=True)
        - normed * jnp.mean(inner * normed, axis=-1, keepdims=True)
    )


def at_tile(index, size):
    return pl.ds(pl.multiple_of(index * size, size), size)


def tile_mask(segq_ref, segk_ref, qi, ki, tile_q, tile_k, causal):
    seg_k = segk_ref[at_tile(ki, tile_k), :]
    seg_k = jnp.concatenate([seg_k] * (tile_q // TILE), axis=1)
    allowed = seg_k == segq_ref[:, at_tile(qi, tile_q)]
    if causal:
        shape = (tile_k, tile_q)
        ahead = lax.broadcasted_iota(jnp.int32, shape, 0) - lax.broadcasted_iota(
            jnp.int32, shape, 1
        )
        allowed = allowed & (ahead <= qi * tile_q - ki * tile_k)
    return allowed


def for_tiles(length, tile_q, tile_k, edge_ref, causal, step):
    count_q, count_k = length // tile_q, length // tile_k
    per_q, per_k = tile_q // TILE, tile_k // TILE

    def one(pair, carry):
        qi, ki = pair // count_k, lax.rem(pair, count_k)
        live = (edge_ref[0, qi * per_q] <= edge_ref[3, (ki + 1) * per_k - 1]) & (
            edge_ref[2, ki * per_k] <= edge_ref[1, (qi + 1) * per_q - 1]
        )
        if causal:
            live = live & (ki * tile_k < (qi + 1) * tile_q)

        @pl.when(live)
        def _():
            step(qi, ki)

        return carry

    lax.fori_loop(0, count_q * count_k, one, 0)


def tile_edges(seg_q, seg_k):
    last = TILE - 1
    return jnp.stack([seg_q[::TILE], seg_q[last::TILE], seg_k[::TILE], seg_k[last::TILE]])


def share_selector(rows, owners, shares, share, count):
    size = rows // (owners * shares)
    index = jnp.arange(count // shares)
    picked = index // size * (rows // owners) + share * size + index % size
    return (picked[:, None] == jnp.arange(count)[None, :]).astype(jnp.bfloat16)


def load_weights(w_ref, piece_refs, part, first, sems):
    if len(piece_refs) == 1:
        copies = [pltpu.make_async_copy(piece_refs[0], w_ref, sems.at[0])]
        copies[0].start()
        return copies
    own = piece_refs[0]
    matrices, rows = w_ref.shape[0], w_ref.shape[1] // 4
    half = own.shape[0] // 2
    me, side = lax.axis_index("dp"), lax.rem(lax.axis_index("vocab"), 2)
    copies = []
    for m in range(matrices):
        which = m if part is None else part
        start = first if part is None else first + m * rows

        def copy_from(ref, offset, owner, slot):
            place = pl.ds(pl.multiple_of(owner * rows, rows), rows)
            return pltpu.make_async_copy(
                ref.at[pl.ds(offset + start, rows)], w_ref.at[m, place], sems.at[slot]
            )

        copies.append(copy_from(own, which * half, me, 4 * m))
        copies[-1].start()
        for k in range(1, 4):
            mine, theirs = (copy_from(piece_refs[n], 0, me ^ k, 4 * m + k) for n in (k, k + 3))

            @pl.when(side == which)
            def _():
                mine.start()

            @pl.when(side != which)
            def _():
                theirs.start()

            copies.append(mine)
    return copies


def flip_sites(part, axis, bit):
    return lax.ppermute(part, axis, [(s, s ^ bit) for s in range(lax.axis_size(axis))])


def late_weights(attn, ffn, after, later):
    owners = lax.axis_size("dp")
    width = attn.shape[-1]
    attn, ffn = attn.astype(jnp.bfloat16), ffn.astype(jnp.bfloat16)
    if owners != 4:
        attn, ffn = (lax.all_gather(part, "dp", axis=1, tiled=True) for part in (attn, ffn))
        return ((attn[:4],), 0, 0), ((attn[4:],), 0, 0), ((ffn,), 0, 0), ffn[0, 0, 0]
    halves = [
        jnp.concatenate([attn[4 * k : 4 * k + 4].reshape(-1, width), ffn[k]]) for k in range(2)
    ]
    own = jnp.concatenate(halves)
    side = lax.axis_index("vocab") % 2
    mine = jnp.where(side == 0, halves[0], halves[1])
    mine, _ = lax.optimization_barrier((mine, after))
    got = [flip_sites(mine, "dp", k) for k in range(1, 4)]
    *got, _ = lax.optimization_barrier((*got, later))
    swapped = [flip_sites(part, "vocab", 1) for part in got]
    pieces = (own, *got, *swapped)
    rows = 4 * attn.shape[1]
    return (pieces, 0, 0), (pieces, 1, 0), (pieces, None, rows), swapped[-1][0, 0]


def attn_forward_kernel(causal, cross, pieces, part, first, *refs):
    refs = list(refs)
    x_ref, ln_ref, segq_ref, segk_ref = refs[:4]
    refs = refs[4:]
    key_ref = refs.pop(0) if cross else None
    piece_refs, refs = refs[:pieces], refs[pieces:]
    edge_ref, out_ref, a_ref, qt_ref, kt_ref, vt_ref, ot_ref, lse_ref = refs[:8]
    refs = refs[8:]
    w_ref, top_ref, sum_ref, acc_ref, sems = refs
    weights = load_weights(w_ref, piece_refs, part, first, sems)
    length, width = x_ref.shape
    head_size = width // HEADS
    a_ref[...] = norm_forward(x_ref[...], ln_ref).astype(jnp.bfloat16)
    key_in = key_ref if cross else a_ref
    for copy in weights:
        copy.wait()
    qt_ref[...] = dot_dims(a_ref[...], w_ref[0], 1, 0).astype(jnp.bfloat16).T
    kt_ref[...] = dot_dims(key_in[...], w_ref[1], 1, 0).astype(jnp.bfloat16).T
    vt_ref[...] = dot_dims(key_in[...], w_ref[2], 1, 0).astype(jnp.bfloat16).T
    top_ref[...] = jnp.full(top_ref.shape, masked, jnp.float32)
    sum_ref[...] = jnp.zeros(sum_ref.shape, jnp.float32)
    acc_ref[...] = jnp.zeros(acc_ref.shape, jnp.float32)
    scale = log_two_e / math.sqrt(head_size)
    bands = [slice(h * head_size, (h + 1) * head_size) for h in range(HEADS)]

    def step(qi, ki):
        q_at, k_at = at_tile(qi, 256), at_tile(ki, 256)
        allowed = tile_mask(segq_ref, segk_ref, qi, ki, 256, 256, causal)
        scores = [dot_dims(kt_ref[band, k_at], qt_ref[band, q_at], 0, 0) * scale for band in bands]
        scores = [jnp.where(allowed, part, masked) for part in scores]
        top = top_ref[:, q_at]
        new_top = jnp.maximum(
            top,
            jnp.concatenate([jnp.max(part, axis=0, keepdims=True) for part in scores], axis=0),
        )
        fade = jnp.exp2(top - new_top)
        parts = [jnp.exp2(scores[h] - new_top[h : h + 1]) for h in range(HEADS)]
        top_ref[:, q_at] = new_top
        sum_ref[:, q_at] = sum_ref[:, q_at] * fade + jnp.concatenate(
            [jnp.sum(part, axis=0, keepdims=True) for part in parts], axis=0
        )
        mixed = [
            dot_dims(vt_ref[bands[h], k_at], parts[h].astype(jnp.bfloat16), 1, 0)
            for h in range(HEADS)
        ]
        acc = acc_ref[:, q_at]
        acc_ref[:, q_at] = jnp.concatenate(
            [acc[bands[h]] * fade[h : h + 1] + mixed[h] for h in range(HEADS)], axis=0
        )

    for_tiles(length, 256, 256, edge_ref, causal, step)
    lse_ref[...] = top_ref[...] + jnp.log2(sum_ref[...])
    for h in range(HEADS):
        ot_ref[bands[h], :] = (acc_ref[bands[h], :] / sum_ref[h : h + 1, :]).astype(jnp.bfloat16)
    out_ref[...] = x_ref[...] + dot_dims(ot_ref[...], w_ref[3], 0, 0)


def attn_forward(x, ln, weights, seg_q, seg_k, key_in, causal):
    length, width = x.shape
    weights, part, first = weights
    cross = key_in is not None
    segs = (seg_q[None, :], jnp.broadcast_to(seg_k[:, None], (length, TILE)))
    edges = tile_edges(seg_q, seg_k)
    args = (x, ln, *segs) + ((key_in,) if cross else ()) + (*weights, edges)
    outs = (full(length, width), low(length, width)) + (low(width, length),) * 4
    outs = outs + (full(HEADS, length),)
    if len(weights) > 1:
        outs = outs + (low(4, width, width),)
    out, normed, *stored = call(
        partial(attn_forward_kernel, causal, cross, len(weights), part, first),
        outs,
        *args,
        scratch=[pltpu.VMEM((4, width, width), jnp.bfloat16)][: len(weights) == 1]
        + [
            pltpu.VMEM((HEADS, length), jnp.float32),
            pltpu.VMEM((HEADS, length), jnp.float32),
            pltpu.VMEM((width, length), jnp.float32),
            pltpu.SemaphoreType.DMA((16,)),
        ],
        smem_args=1,
        microseconds=20,
        far=range(len(args) - 1 - len(weights), len(args) - 1),
    )
    whole = stored.pop() if len(weights) > 1 else weights[0]
    return out, (x, ln, whole, segs, edges, causal, key_in, normed, stored)


def attn_backward_kernel(causal, cross, row_scale, *refs):
    g_ref, x_ref, ln_ref, w_ref, pick_ref, segq_ref, segk_ref, a_ref = refs[:8]
    refs = list(refs[8:])
    key_ref = refs.pop(0) if cross else a_ref
    qt_ref, kt_ref, vt_ref, ot_ref, lse_ref, edge_ref, out_ref, ln_grad_ref, block_ref, extra_ref = refs[:10]
    low_ref, gq_ref, gk_ref, gv_ref, got_ref, delta_ref, gqt_ref, gkt_ref, gvt_ref = refs[10:]
    length, width = x_ref.shape
    head_size = width // HEADS
    low_ref[...] = g_ref[...].astype(jnp.bfloat16)
    got_ref[...] = dot_dims(low_ref[...], w_ref[3], 1, 1).astype(jnp.bfloat16).T
    bands = [slice(h * head_size, (h + 1) * head_size) for h in range(HEADS)]
    for h in range(HEADS):
        delta_ref[h : h + 1, :] = jnp.sum(
            got_ref[bands[h], :].astype(jnp.float32) * ot_ref[bands[h], :].astype(jnp.float32),
            axis=0,
            keepdims=True,
        )
    for ref in (gqt_ref, gkt_ref, gvt_ref):
        ref[...] = jnp.zeros(ref.shape, jnp.float32)
    scale = log_two_e / math.sqrt(head_size)
    back = 1.0 / math.sqrt(head_size)

    def step(qi, ki):
        q_at, k_at = at_tile(qi, 256), at_tile(ki, TILE)
        allowed = tile_mask(segq_ref, segk_ref, qi, ki, 256, TILE, causal)
        scores = [dot_dims(kt_ref[band, k_at], qt_ref[band, q_at], 0, 0) for band in bands]
        grads = [dot_dims(vt_ref[band, k_at], got_ref[band, q_at], 0, 0) for band in bands]
        parts = [
            jnp.where(allowed, jnp.exp2(scores[h] * scale - lse_ref[h : h + 1, q_at]), 0.0)
            for h in range(HEADS)
        ]
        grads = [parts[h] * (grads[h] - delta_ref[h : h + 1, q_at]) for h in range(HEADS)]
        parts_t = [part.T.astype(jnp.bfloat16) for part in parts]
        grads_t = [part.T.astype(jnp.bfloat16) for part in grads]
        grads = [part.astype(jnp.bfloat16) for part in grads]
        for ref, place, terms in (
            (gvt_ref, k_at, [dot_dims(got_ref[bands[h], q_at], parts_t[h], 1, 0) for h in range(HEADS)]),
            (gkt_ref, k_at, [dot_dims(qt_ref[bands[h], q_at], grads_t[h], 1, 0) for h in range(HEADS)]),
            (gqt_ref, q_at, [dot_dims(kt_ref[bands[h], k_at], grads[h], 1, 0) for h in range(HEADS)]),
        ):
            ref[:, place] += jnp.concatenate(terms, axis=0)

    for_tiles(length, 256, TILE, edge_ref, causal, step)
    gq_ref[...] = (gqt_ref[...] * back).astype(jnp.bfloat16).T
    gk_ref[...] = (gkt_ref[...] * back).astype(jnp.bfloat16).T
    gv_ref[...] = gvt_ref[...].astype(jnp.bfloat16).T
    from_query = dot_dims(gq_ref[...], w_ref[0], 1, 1)
    from_keys = dot_dims(gk_ref[...], w_ref[1], 1, 1) + dot_dims(gv_ref[...], w_ref[2], 1, 1)
    if cross:
        extra_ref[...] = from_keys
    else:
        from_query = from_query + from_keys
    total = g_ref[...] + norm_backward(from_query, x_ref[...], ln_ref, ln_grad_ref)
    out_ref[...] = total
    owners = block_ref.shape[0]
    if not cross:
        columns = width // owners
        for owner in range(owners):
            band = slice(owner * columns, (owner + 1) * columns)
            extra_ref[owner] = (total[:, band] * row_scale).astype(jnp.bfloat16)
    own_a = dot_dims(pick_ref[...], a_ref[...], 1, 1).astype(jnp.bfloat16)
    own_key = dot_dims(pick_ref[...], key_ref[...], 1, 1).astype(jnp.bfloat16) if cross else own_a
    own_o = dot_dims(pick_ref[...], ot_ref[...], 1, 0).astype(jnp.bfloat16)
    size = own_a.shape[0] // owners
    products = ((own_a, gq_ref), (own_key, gk_ref), (own_key, gv_ref), (own_o, low_ref))
    for m, (rows, right_ref) in enumerate(products):
        product = dot_dims(rows, right_ref[...], 1, 0).astype(jnp.bfloat16)
        for owner in range(owners):
            block_ref[owner, m * size : (m + 1) * size, :] = product[owner * size : (owner + 1) * size]


def attn_backward(grad, stored, picks, owners, row_scale, before=()):
    x, ln, weights, segs, edges, causal, key_in, normed, kept = stored
    length, width = x.shape
    cross = key_in is not None
    extra = full(length, width) if cross else low(owners, length, width // owners)
    outs = (full(length, width), full(2, width), low(owners, 4 * picks.shape[0] // owners, width), extra)
    keys = (key_in,) if cross else ()
    return call(
        partial(attn_backward_kernel, causal, cross, row_scale),
        outs,
        grad,
        x,
        ln,
        weights,
        picks,
        *segs,
        normed,
        *keys,
        *kept,
        edges,
        scratch=[pltpu.VMEM((length, width), jnp.bfloat16)] * 4
        + [pltpu.VMEM((width, length), jnp.bfloat16), pltpu.VMEM((HEADS, length), jnp.float32)]
        + [pltpu.VMEM((width, length), jnp.float32)] * 3,
        smem_args=1,
        microseconds=25,
        before=before,
    )


def gelu_parts(hidden):
    root = math.sqrt(2.0 / math.pi)
    square = hidden * hidden
    bend = jnp.tanh(root * hidden * (1.0 + 0.044715 * square))
    value = 0.5 * hidden * (1.0 + bend)
    slope = 0.5 * (1.0 + bend) + 0.5 * hidden * (1.0 - bend * bend) * root * (
        1.0 + 3.0 * 0.044715 * square
    )
    return value, slope


def ffn_forward_kernel(chunk, pieces, first, x_ref, ln_ref, next_ref, *refs):
    piece_refs, (out_ref, a_ref, after_ref, w_ref, sems) = refs[:pieces], refs[pieces:]
    weights = load_weights(w_ref, piece_refs, None, first, sems)
    w_in_ref, w_out_ref = w_ref.at[0], w_ref.at[1]
    a_ref[...] = norm_forward(x_ref[...], ln_ref).astype(jnp.bfloat16)
    total = x_ref[...]
    for copy in weights:
        copy.wait()
    for start in range(0, w_in_ref.shape[0], chunk):
        part = slice(start, start + chunk)
        hidden = dot_dims(a_ref[...], w_in_ref[part, :], 1, 1)
        active = gelu_parts(hidden)[0].astype(jnp.bfloat16)
        total = total + dot_dims(active, w_out_ref[part, :], 1, 0)
    out_ref[...] = total
    after_ref[...] = norm_forward(total, next_ref).astype(after_ref.dtype)


def ffn_forward(x, ln, ln_next, weights):
    length, width = x.shape
    weights, _, first = weights
    outs = (full(length, width), low(length, width), low(length, width))
    if len(weights) > 1:
        outs = outs + (low(2, 4 * (weights[0].shape[0] // 2 - first), width),)
    out, normed, after, *whole = call(
        partial(ffn_forward_kernel, 512, len(weights), first),
        outs,
        x,
        ln,
        ln_next,
        *weights,
        scratch=[pltpu.VMEM(w.shape, w.dtype) for w in weights if len(weights) == 1]
        + [pltpu.SemaphoreType.DMA((8,))],
        microseconds=12,
        far=range(3, 3 + len(weights)),
    )
    return out, after, (x, ln, whole[0] if whole else weights[0], normed, out, ln_next)


def ffn_backward_kernel(
    chunk, picked, after_ref, *refs
):
    if picked:
        place_ref, *refs = refs
        shape = (refs[0].shape[0], place_ref.shape[1])
        chosen = lax.broadcasted_iota(jnp.int32, shape, 0) == place_ref[...]
        after = dot_dims(chosen.astype(jnp.bfloat16), after_ref[...], 1, 0)
    else:
        after = after_ref[...]
    ffn_backward_rest(chunk, after, *refs)


def ffn_backward_rest(
    chunk, after, y_ref, next_ref, x_ref, ln_ref, a_ref, w_ref, pick_ref,
    out_ref, next_grad_ref, ln_grad_ref, in_ref, back_ref, low_ref, g_ref,
):
    w_in_ref, w_out_ref = w_ref.at[0], w_ref.at[1]
    g_ref[...] = norm_backward(after, y_ref[...], next_ref, next_grad_ref)
    low_ref[...] = g_ref[...].astype(jnp.bfloat16)
    total = jnp.zeros(g_ref.shape, jnp.float32)
    owners, size = in_ref.shape[:2]
    blocks = pick_ref.shape[0] // size
    for index in range(w_in_ref.shape[0] // chunk):
        part = slice(index * chunk, (index + 1) * chunk)
        hidden = dot_dims(a_ref[...], w_in_ref[part, :], 1, 1)
        value, slope = gelu_parts(hidden)
        grad = (dot_dims(low_ref[...], w_out_ref[part, :], 1, 1) * slope).astype(jnp.bfloat16)
        total = total + dot_dims(grad, w_in_ref[part, :], 1, 0)
        pairs = ((in_ref, grad, a_ref), (back_ref, value.astype(jnp.bfloat16), low_ref))
        for ref, left, right_ref in pairs:
            rows = dot_dims(pick_ref[...], left, 1, 1).astype(jnp.bfloat16)
            product = dot_dims(rows, right_ref[...], 1, 0).astype(jnp.bfloat16)
            for block in range(blocks):
                ref[index * blocks + block] = product[block * size : (block + 1) * size]
    out_ref[...] = g_ref[...] + norm_backward(total, x_ref[...], ln_ref, ln_grad_ref)


def ffn_backward(grad_after, stored, picks, owners, before=(), places=None):
    x, ln, weights, normed, out, ln_next = stored
    length, width = x.shape
    chunk = picks.shape[1]
    size = picks.shape[0] * weights.shape[1] // chunk // owners
    block = low(owners, size, width)
    return call(
        partial(ffn_backward_kernel, chunk, places is not None),
        (full(length, width), full(2, width), full(2, width), block, block),
        grad_after,
        *(() if places is None else (places[None, :],)),
        out,
        ln_next,
        x,
        ln,
        normed,
        weights,
        picks,
        scratch=[
            pltpu.VMEM((length, width), jnp.bfloat16),
            pltpu.VMEM((length, width), jnp.float32),
        ],
        microseconds=17,
        before=before,
    )


def look_up_tokens(code_ref, paired_ref, found_ref):
    step = 256
    columns = found_ref.shape[1]

    def one(index, carry):
        span = pl.ds(pl.multiple_of(index * step, step), step)
        code = code_ref[span, :]
        places = lax.broadcasted_iota(jnp.int32, (step, paired_ref.shape[0]), 1)
        chosen = (places == lax.shift_right_arithmetic(code, 1)).astype(jnp.bfloat16)
        wide = dot_dims(chosen, paired_ref[...], 1, 0)
        left = jnp.bitwise_and(code, 1) == 1
        found_ref[span, :] = jnp.where(left, wide[:, :columns], wide[:, columns:]).astype(jnp.bfloat16)
        return carry

    lax.fori_loop(0, code_ref.shape[0] // step, one, 0)


def loss_forward_kernel(chunks, final_ref, pick_ref, label_ref, table_ref, picked_ref, stat_ref, logit_ref):
    count, length = pick_ref.shape[0], final_ref.shape[0]
    places = lax.broadcasted_iota(jnp.int32, (count, length), 1)
    chosen = (places == pick_ref[...]).astype(jnp.bfloat16)
    picked_ref[...] = dot_dims(chosen, final_ref[...], 1, 0).astype(jnp.bfloat16)
    rows = table_ref.shape[0] // chunks
    top = jnp.full((1, count), masked, jnp.float32)
    label = jnp.zeros((1, count), jnp.float32)
    for index in range(chunks):
        span = slice(index * rows, (index + 1) * rows)
        logits = dot_dims(table_ref[span, :], picked_ref[...], 1, 1)
        logit_ref[span, :] = logits
        top = jnp.maximum(top, jnp.max(logits, axis=0, keepdims=True))
        hit = lax.broadcasted_iota(jnp.int32, logits.shape, 0) + index * rows == label_ref[...]
        label = label + jnp.sum(jnp.where(hit, logits, 0.0), axis=0, keepdims=True)
    total = jnp.zeros((1, count), jnp.float32)
    for index in range(chunks):
        span = slice(index * rows, (index + 1) * rows)
        total = total + jnp.sum(jnp.exp(logit_ref[span, :] - top), axis=0, keepdims=True)
    stat_ref[...] = jnp.concatenate([top, total, label, jnp.zeros((5, count), jnp.float32)], axis=0)


def loss_forward(final, pick_rows, labels, table):
    count, width = pick_rows.shape[0], final.shape[1]
    return call(
        partial(loss_forward_kernel, 8),
        (low(count, width), full(8, count)),
        final,
        pick_rows[:, None],
        labels[None, :],
        table,
        scratch=[pltpu.VMEM((table.shape[0], count), jnp.float32)],
        microseconds=6,
    )


def loss_backward_kernel(
    chunks, picked_ref, seen_ref, weight_ref, label_ref, table_ref, grad_ref, parts_ref, loss_ref
):
    tops, totals, labels = (
        jnp.concatenate([seen_ref[k, m : m + 1, :] for k in range(seen_ref.shape[0])], axis=0)
        for m in range(3)
    )
    top = jnp.max(tops, axis=0, keepdims=True)
    total = top + jnp.log(jnp.sum(totals * jnp.exp(tops - top), axis=0, keepdims=True))
    loss_ref[...] = (total - jnp.sum(labels, axis=0, keepdims=True)) * weight_ref[...]
    rows = table_ref.shape[0] // chunks
    columns = parts_ref.shape[2]
    grad = jnp.zeros(grad_ref.shape, jnp.float32)
    for index in range(chunks):
        span = slice(index * rows, (index + 1) * rows)
        logits = dot_dims(table_ref[span, :], picked_ref[...], 1, 1)
        hit = lax.broadcasted_iota(jnp.int32, logits.shape, 0) + index * rows == label_ref[...]
        slopes = weight_ref[...] * (jnp.exp(logits - total) - jnp.where(hit, 1.0, 0.0))
        slopes = slopes.astype(jnp.bfloat16)
        product = dot_dims(slopes, picked_ref[...], 1, 0).astype(jnp.bfloat16)
        for owner in range(parts_ref.shape[0]):
            parts_ref[owner, span, :] = product[:, owner * columns : (owner + 1) * columns]
        grad = grad + dot_dims(slopes, table_ref[span, :], 0, 0)
    grad_ref[...] = grad.astype(jnp.bfloat16)


def loss_backward(picked, seen, weight, labels, table, owners):
    count, width = picked.shape
    return call(
        partial(loss_backward_kernel, 8),
        (low(count, width), low(owners, table.shape[0], width // owners), full(1, count)),
        picked,
        seen,
        weight[None, :],
        labels[None, :],
        table,
        microseconds=8,
    )


def adam_parts(weight, grad, moment, second):
    moment = beta_one * moment + (1.0 - beta_one) * grad
    second = beta_two * second + (1.0 - beta_two) * grad * grad
    step = adam_direction(moment, second) + decay_rate * weight
    return weight - rate_matrix * step, moment, second


def update_kernel(*refs):
    factor_ref, basis_ref, *ins = refs[:14]
    outs = refs[14:]
    factor = factor_ref[0]
    for k in (0, 1):
        grad_ref, weight_ref, moment_ref, second_ref = ins[4 * k : 4 * k + 4]
        grad = grad_ref[...].astype(jnp.float32) * factor
        results = adam_parts(weight_ref[...], grad, moment_ref[...], second_ref[...])
        for ref, result in zip(outs[3 * k : 3 * k + 3], results):
            ref[...] = result
    g_ref, w_ref, m_ref, v_ref = ins[8:]
    new_w_ref, new_m_ref, new_v_ref = outs[6:]
    high = basis_ref[0].astype(jnp.bfloat16)
    rest = (basis_ref[0] - high.astype(jnp.float32)).astype(jnp.bfloat16)
    grad = g_ref[0]
    rotated = (dot_dims(grad, high, 1, 0) + dot_dims(grad, rest, 1, 0)) * factor
    moment = beta_one * m_ref[0] + (1.0 - beta_one) * rotated
    second = beta_two * v_ref[0] + (1.0 - beta_two) * rotated * rotated
    new_m_ref[0] = moment
    new_v_ref[0] = second
    step = adam_direction(moment, second)
    step_high = step.astype(jnp.bfloat16)
    step_rest = (step - step_high.astype(jnp.float32)).astype(jnp.bfloat16)
    back = (
        dot_dims(step_high, high, 1, 1)
        + dot_dims(step_high, rest, 1, 1)
        + dot_dims(step_rest, high, 1, 1)
    )
    new_w_ref[0] = w_ref[0] - rate_matrix * (back + decay_rate * w_ref[0])


def update_matrices(factor, bases, attn, table, ffn):
    def blocks(array):
        shape = (array.shape[0] // 4, *array.shape[1:])
        return pl.BlockSpec(shape, lambda k: (k,) + (0,) * (len(shape) - 1))

    arrays = (*attn, *table, *ffn)
    results = [part for group in (attn, table, ffn) for part in group[1:]]
    return pl.pallas_call(
        update_kernel,
        grid=(4,),
        out_shape=tuple(full(*part.shape) for part in results),
        in_specs=[smem, blocks(bases)] + [blocks(part) for part in arrays],
        out_specs=tuple(blocks(part) for part in results),
        compiler_params=pltpu.CompilerParams(vmem_limit_bytes=56 * 2**20),
        cost_estimate=cost_of(20),
    )(factor.reshape(1), bases, *arrays)


def small_factor(block):
    size = block.shape[0]
    eye = (
        lax.broadcasted_iota(jnp.int32, (size, size), 0)
        == lax.broadcasted_iota(jnp.int32, (size, size), 1)
    ).astype(jnp.float32)
    whole = jnp.concatenate([block, eye], axis=1)
    rows = [whole[8 * u : 8 * u + 8] for u in range(size // 8)]
    shape = rows[0].shape
    sub = lax.broadcasted_iota(jnp.int32, shape, 0)

    def lane_splat(value, lane):
        return jnp.broadcast_to(value[:, lane : lane + 1], shape)

    def row_splat(value, row):
        return jnp.broadcast_to(value[row : row + 1, :], shape)

    for g in range(len(rows)):
        first = 8 * g
        lanes = {
            u: [lane_splat(rows[u], first + s) for s in range(8)] for u in range(g, len(rows))
        }
        scale = jnp.zeros(shape, jnp.float32)
        for t in range(8):
            pivot = row_splat(lanes[g][t], t)
            root = lax.rsqrt(pivot)
            inverse = root * root
            scale = jnp.where(sub == t, root, scale)
            row_t = row_splat(rows[g], t) * inverse
            splats = {s: row_splat(lanes[g][s], t) * inverse for s in range(t + 1, 8)}
            for u in range(g, len(rows)):
                factor = lanes[u][t]
                if u == g:
                    factor = jnp.where(sub > t, factor, 0.0)
                rows[u] = rows[u] - factor * row_t
                for s in range(t + 1, 8):
                    lanes[u][s] = lanes[u][s] - factor * splats[s]
        rows[g] = rows[g] * scale
    return jnp.concatenate(rows, axis=0)[:, size:]


def renew_kernel(
    product_ref, stats_ref, bases_ref, factor_ref, half_ref, stat_ref, basis_ref, out_ref, gram_ref, rest_ref, sems
):
    size = stat_ref.shape[0]
    here = lax.axis_index("vocab")
    copies = [
        pltpu.make_async_copy(ref.at[here // 2], place, sems.at[k])
        for k, (ref, place) in enumerate(((stats_ref, stat_ref), (bases_ref, basis_ref)))
    ]
    for copy in copies:
        copy.start()
    for copy in copies:
        copy.wait()
    statistic = stat_decay * stat_ref[...] + factor_ref[0] * product_ref[...]
    product = dot_exact(statistic, basis_ref[...], 1, 0)
    rest_ref[...] = product
    gram_ref[...] = dot_exact(product, product, 0, 0)
    for low in range(0, size, 128):
        high = low + 128
        block = gram_ref[low:high, low:high]
        corner = small_factor(block[:64, :64])
        across = dot_exact(corner, block[:64, 64:], 1, 0)
        second = small_factor(block[64:, 64:] - dot_exact(across, across, 0, 0))
        below = dot_exact(second, dot_exact(across, corner, 0, 0), 1, 0)
        inverse = jnp.concatenate(
            [
                jnp.concatenate([corner, jnp.zeros_like(corner)], axis=1),
                jnp.concatenate([-below, second], axis=1),
            ],
            axis=0,
        )
        columns = dot_exact(rest_ref[:, low:high], inverse, 1, 1)
        out_ref[:, low:high] = columns
        if high < size:
            panel = dot_exact(inverse, gram_ref[low:high, high:], 1, 0)
            gram_ref[high:, high:] -= dot_exact(panel, panel, 0, 0)
            rest_ref[:, high:] -= dot_exact(columns, panel, 1, 0)
    rows = size // 2
    half = pl.ds(pl.multiple_of(lax.rem(here, 2) * rows, rows), rows)
    half_ref[...] = out_ref[half, :].astype(jnp.bfloat16)


def renew_basis(products, stats, bases, factor):
    size = products.shape[0]
    return call(
        renew_kernel,
        low(size // 2, size),
        products,
        stats,
        bases,
        factor.reshape(1),
        scratch=[pltpu.VMEM((size, size), jnp.float32)] * 5 + [pltpu.SemaphoreType.DMA((2,))],
        smem_args=1,
        microseconds=29,
        far=(1, 2),
    )


def peers_of(axis):
    size, me = lax.axis_size(axis), lax.axis_index(axis)
    return [
        (step, lax.rem(me + step, size), lax.rem(me + size - step, size)) for step in range(1, size)
    ]


def greet(*places):
    barrier = pltpu.get_barrier_semaphore()
    for axis, index in places:
        pl.semaphore_signal(barrier, inc=1, device_id={axis: index}, device_id_type=mesh_ids)
    pl.semaphore_wait(barrier, len(places))


def push(source, target, sems, slot, axis, index):
    copy = pltpu.make_async_remote_copy(
        src_ref=source,
        dst_ref=target,
        send_sem=sems[0].at[slot],
        recv_sem=sems[1].at[slot],
        device_id={axis: index},
        device_id_type=mesh_ids,
    )
    copy.start()
    return copy


def sem_pair(count):
    return [pltpu.SemaphoreType.DMA((count,)), pltpu.SemaphoreType.DMA((count,))]


def talk(kernel, outs, collective_id, *args, scratch=(), microseconds=15, before=()):
    def body(*refs):
        kernel(*refs[: len(args)], *refs[len(args) + len(before) :])

    return pl.pallas_call(
        body,
        out_shape=outs,
        in_specs=[vmem] * len(args) + [pl.BlockSpec(memory_space=pl.ANY)] * len(before),
        out_specs=jax.tree.map(lambda _: vmem, outs),
        scratch_shapes=list(scratch),
        compiler_params=pltpu.CompilerParams(
            collective_id=collective_id, has_side_effects=True, vmem_limit_bytes=56 * 2**20
        ),
        cost_estimate=cost_of(microseconds),
    )(*args, *before)


def gather_kernel(axis, *refs):
    count = (len(refs) - 2) // 2
    others = peers_of(axis)
    greet(*[(axis, to) for _, to, _ in others])
    me = lax.axis_index(axis)
    copies = [
        push(refs[k], refs[count + k].at[me], refs[-2:], k * len(others) + step - 1, axis, to)
        for k in range(count)
        for step, to, _ in others
    ]
    for k in range(count):
        refs[count + k][me] = refs[k][...]
    for copy in copies:
        copy.wait()


def gather_small(axis, collective_id, *arrays):
    size = lax.axis_size(axis)
    outs = tuple(jax.ShapeDtypeStruct((size, *x.shape), x.dtype) for x in arrays)
    sems = sem_pair((size - 1) * len(arrays))
    return talk(partial(gather_kernel, axis), outs, collective_id, *arrays, scratch=sems)


def flip(index, bit):
    return index + bit - 2 * bit * lax.rem(index // bit, 2)


def far_replicas():
    here, size = lax.axis_index("vocab"), lax.axis_size("vocab")
    return [
        (step // 2 - 1, lax.rem(here + step, size), lax.rem(here + size - step, size))
        for step in range(2, size, 2)
    ]


def sum_kernel(x_ref, out_ref, near_ref, send_ref, parts_ref, s0, r0, s1, r1, s2, r2, s3, r3):
    here, others = lax.axis_index("vocab"), far_replicas()
    near, side = flip(here, 1), lax.rem(here, 2)
    greet(*[("vocab", to) for _, to, _ in others], ("vocab", near))
    half = near_ref.shape[0]
    share = parts_ref.shape[1]

    def half_of(which):
        return pl.ds(pl.multiple_of(which * half, half), half)

    def share_of(index, start):
        return pl.ds(pl.multiple_of(start + index // 2 * share, share), share)

    push(x_ref.at[half_of(1 - side)], near_ref, (s0, r0), 0, "vocab", near).wait()
    total = near_ref[...].astype(jnp.float32) + x_ref[half_of(side), :].astype(jnp.float32)
    send_ref[...] = total.astype(send_ref.dtype)
    copies = [
        push(send_ref.at[share_of(to, 0)], parts_ref.at[slot], (s1, r1), slot, "vocab", to)
        for slot, to, _ in others
    ]
    total = send_ref[share_of(here, 0), :].astype(jnp.float32)
    for copy, (slot, _, _) in zip(copies, others):
        copy.wait()
        total = total + parts_ref[slot].astype(jnp.float32)
    mine = share_of(here, side * half)
    out_ref[mine, :] = total.astype(out_ref.dtype)
    copies = [
        push(out_ref.at[mine], out_ref.at[mine], (s2, r2), slot, "vocab", to) for slot, to, _ in others
    ]
    close = [push(out_ref.at[mine], out_ref.at[mine], (s3, r3), 0, "vocab", near)]
    for copy, (slot, _, origin) in zip(copies, others):
        copy.wait()
        theirs = out_ref.at[share_of(origin, side * half)]
        close.append(push(theirs, theirs, (s3, r3), slot + 1, "vocab", near))
    for copy in close:
        copy.wait()


def sum_vocab(x, collective_id):
    pairs = lax.axis_size("vocab") // 2
    rows, columns = x.shape
    half = rows // 2
    return talk(
        sum_kernel,
        jax.ShapeDtypeStruct(x.shape, x.dtype),
        collective_id,
        x,
        scratch=[
            pltpu.VMEM((half, columns), x.dtype),
            pltpu.VMEM((half, columns), x.dtype),
            pltpu.VMEM((pairs - 1, half // pairs, columns), x.dtype),
        ]
        + sem_pair(1)
        + sem_pair(pairs - 1)
        + sem_pair(pairs - 1)
        + sem_pair(pairs),
    )


def tail_kernel(
    x_ref, few_ref, out_ref, sum_ref, parts_ref, seen_ref, line_ref, lines_ref,
    s0, r0, s1, r1, s2, r2, s3, r3, s4, r4,
):
    owners, replicas = peers_of("dp"), peers_of("vocab")
    greet(*[("dp", to) for _, to, _ in owners], *[("vocab", to) for _, to, _ in replicas])
    size, me, here = lax.axis_size("dp"), lax.axis_index("dp"), lax.axis_index("vocab")
    near, side = flip(here, 1), lax.rem(here, 2)
    rows = parts_ref.shape[1]

    def rows_of(index):
        return pl.ds(pl.multiple_of((side * size + index) * rows, rows), rows)

    few = [
        push(few_ref, seen_ref.at[here], (s2, r2), step - 1, "vocab", to) for step, to, _ in replicas
    ]
    wide = [
        push(x_ref.at[rows_of(to)], parts_ref.at[me], (s0, r0), step - 1, "dp", to)
        for step, to, _ in owners
    ]
    seen_ref[here] = few_ref[...]
    parts_ref[me] = x_ref[rows_of(me), :]
    for copy in few:
        copy.wait()
    line_ref[...] = jnp.sum(seen_ref[...], axis=0)
    few = [
        push(line_ref, lines_ref.at[me], (s3, r3), step - 1, "dp", to) for step, to, _ in owners
    ]
    lines_ref[me] = line_ref[...]
    for copy in wide:
        copy.wait()
    out_ref[rows_of(me), :] = jnp.sum(parts_ref[...], axis=0)
    mine = out_ref.at[rows_of(me)]
    wide = [push(mine, mine, (s1, r1), step - 1, "dp", to) for step, to, _ in owners]
    close = [push(mine, mine, (s4, r4), 0, "vocab", near)]
    for copy in few:
        copy.wait()
    sum_ref[...] = jnp.sum(lines_ref[...], axis=0)
    for copy, (step, _, origin) in zip(wide, owners):
        copy.wait()
        theirs = out_ref.at[rows_of(origin)]
        close.append(push(theirs, theirs, (s4, r4), step, "vocab", near))
    for copy in close:
        copy.wait()


def sum_tail(x, few, collective_id):
    owners, replicas = lax.axis_size("dp"), lax.axis_size("vocab")
    rows, columns = x.shape
    share = rows // (2 * owners)
    return talk(
        tail_kernel,
        (full(*x.shape), full(*few.shape)),
        collective_id,
        x,
        few,
        scratch=[
            pltpu.VMEM((owners, share, columns), jnp.float32),
            pltpu.VMEM((replicas, *few.shape), jnp.float32),
            pltpu.VMEM(few.shape, jnp.float32),
            pltpu.VMEM((owners, *few.shape), jnp.float32),
        ]
        + sem_pair(owners - 1)
        + sem_pair(owners - 1)
        + sem_pair(replicas - 1)
        + sem_pair(owners - 1)
        + sem_pair(owners),
    )


def sum_tokens(rows_refs, place_ref, left_ref, table_ref, wide_ref, embed_ref, square_ref):
    owners, length, columns = rows_refs[0].shape
    for owner in range(owners):
        for k, rows_ref in enumerate(rows_refs):
            start = (owner * len(rows_refs) + k) * length
            span = slice(start, start + length)
            left = rows_ref[owner] * left_ref[span, :]
            wide_ref[span, :columns] = left
            wide_ref[span, columns:] = rows_ref[owner] - left
    tokens, half = wide_ref.shape[0], embed_ref.shape[0] // 2
    tile, step = half // 4, 1024
    square_ref[...] = jnp.zeros(square_ref.shape, jnp.float32)

    def one(index, carry):
        start = index * tile
        places = lax.broadcasted_iota(jnp.int32, (tile, step), 0) + start
        total = jnp.zeros((tile, 2 * columns), jnp.float32)
        for first in range(0, tokens, step):
            chosen = (places == place_ref[:, first : first + step]).astype(jnp.bfloat16)
            total = total + dot_dims(chosen, wide_ref[first : first + step, :], 1, 0)
        for side in range(2):
            span = pl.ds(pl.multiple_of(side * half + start, 16), tile)
            part = total[:, side * columns : (side + 1) * columns]
            part = part + table_ref[span, :].astype(jnp.float32)
            embed_ref[span, :] = part
            square_ref[...] += jnp.sum(part * part, axis=0, keepdims=True)
        return carry

    lax.fori_loop(0, 4, one, 0)


def gradient_kernel(chunks, count, inside, *refs):
    x_refs, refs = refs[:chunks], refs[chunks:]
    rows_refs, refs = refs[:count], refs[count:]
    if inside:
        (place_ref, left_ref, table_ref), refs = refs[:3], refs[3:]
    (out_ref, square_ref, *refs) = refs
    swapped_refs, refs = refs[:count], refs[count:]
    if inside:
        (embed_ref, embed_square_ref), refs = refs[:2], refs[2:]
        *refs, wide_ref = refs
    parts_ref, s0, r0, s1, r1, s2, r2, s3, r3, s4, r4 = refs
    owners = peers_of("dp")
    here, me = lax.axis_index("vocab"), lax.axis_index("dp")
    near = flip(here, 1)
    size = lax.axis_size("vocab")
    steps = range(2, size, 2)
    greet(
        *[("dp", to) for _, to, _ in owners],
        *[("vocab", lax.rem(here + step, size)) for step in steps],
        ("vocab", near),
    )

    def spread(c, origin, sems, slot, to):
        place = out_ref.at[c, origin]
        return push(place, place, sems, slot, "vocab", to)

    arriving = [
        [
            push(x_refs[c].at[to], parts_ref.at[c, me], (s0, r0), (step - 1) * chunks + c, "dp", to)
            for step, to, _ in owners
        ]
        for c in range(chunks)
    ]

    def half_of(ref):
        rows = ref.shape[1] // 2
        return pl.ds(pl.multiple_of(lax.rem(here, 2) * rows, rows), rows)

    swaps = [
        [
            push(
                rows_ref.at[to, half_of(rows_ref)],
                swapped_ref.at[me, half_of(rows_ref)],
                (s3, r3),
                k * len(owners) + step - 1,
                "dp",
                to,
            )
            for step, to, _ in owners
        ]
        for k, (rows_ref, swapped_ref) in enumerate(zip(rows_refs, swapped_refs))
    ]
    for rows_ref, swapped_ref in zip(rows_refs, swapped_refs):
        swapped_ref[me] = rows_ref[me]
    far, close = [], []
    square = jnp.zeros(square_ref.shape, jnp.float32)
    for c in range(chunks):
        parts_ref[c, me] = x_refs[c][me]
        for copy in arriving[c]:
            copy.wait()
        total = jnp.sum(parts_ref[c].astype(jnp.float32), axis=0)
        out_ref[c, here] = total.astype(out_ref.dtype)
        square = square + jnp.sum(total * total, axis=0, keepdims=True)
        far.append(
            [
                spread(c, here, (s1, r1), k * chunks + c, lax.rem(here + step, size))
                for k, step in enumerate(steps)
            ]
        )
        close.append(spread(c, here, (s2, r2), c, near))
    square_ref[...] = square
    moved = []
    for k, swapped_ref in enumerate(swapped_refs):
        for copy, (step, _, origin) in zip(swaps[k], owners):
            copy.wait()
            place = swapped_ref.at[origin, half_of(swapped_ref)]
            moved.append(push(place, place, (s4, r4), k * len(owners) + step - 1, "vocab", near))
    for copy in moved:
        copy.wait()
    if inside:
        sum_tokens(
            swapped_refs[:2], place_ref, left_ref, table_ref, wide_ref, embed_ref, embed_square_ref
        )
    for c in range(chunks):
        for k, step in enumerate(steps):
            far[c][k].wait()
            origin = lax.rem(here + size - step, size)
            close.append(spread(c, origin, (s2, r2), (k + 1) * chunks + c, near))
    for copy in close:
        copy.wait()


def share_gradients(blocks, rows, collective_id, before, tokens):
    owners, replicas = lax.axis_size("dp"), lax.axis_size("vocab")
    chunks = len(blocks)
    others = (replicas // 2 - 1) * chunks
    shape, kind = blocks[0].shape, blocks[0].dtype
    return talk(
        partial(gradient_kernel, chunks, len(rows), bool(tokens)),
        (
            jax.ShapeDtypeStruct((chunks, replicas, *shape[1:]), kind),
            full(1, shape[2]),
            *[jax.ShapeDtypeStruct(part.shape, part.dtype) for part in rows],
            *[full(*size) for part in tokens[2:] for size in (part.shape, (1, part.shape[1]))],
        ),
        collective_id,
        *blocks,
        *rows,
        *tokens,
        scratch=[pltpu.VMEM((chunks, *shape), kind)]
        + sem_pair((owners - 1) * chunks)
        + sem_pair(others)
        + sem_pair(others + chunks)
        + sem_pair(len(rows) * (owners - 1))
        + sem_pair(len(rows) * (owners - 1))
        + [pltpu.VMEM((part.shape[1], 2 * tokens[2].shape[1]), jnp.bfloat16) for part in tokens[:1]],
        microseconds=40,
        before=before,
    )


def swap_kernel(scale, x_ref, place_ref, sum_ref, out_ref, s0, r0, s1, r1):
    others = peers_of("dp")
    me, here = lax.axis_index("dp"), lax.axis_index("vocab")
    near, side = flip(here, 1), lax.rem(here, 2)
    greet(*[("dp", to) for _, to, _ in others], ("vocab", near))
    rows = x_ref.shape[1] // 2
    half = pl.ds(pl.multiple_of(side * rows, rows), rows)
    copies = [
        push(x_ref.at[to, half], out_ref.at[me, half], (s0, r0), step - 1, "dp", to)
        for step, to, _ in others
    ]
    out_ref[me] = x_ref[me]
    close = []
    for copy, (step, _, origin) in zip(copies, others):
        copy.wait()
        place = out_ref.at[origin, half]
        close.append(push(place, place, (s1, r1), step - 1, "vocab", near))
    for copy in close:
        copy.wait()
    columns = out_ref.shape[2]
    for owner in range(out_ref.shape[0]):
        band = slice(owner * columns, (owner + 1) * columns)
        sum_ref[:, band] = out_ref[owner].astype(jnp.float32) * scale + place_ref[:, band]


def swap_owners(x, places, scale, collective_id, before):
    owners = lax.axis_size("dp")
    return talk(
        partial(swap_kernel, scale),
        full(*places.shape),
        collective_id,
        x,
        places,
        scratch=[pltpu.VMEM(x.shape, x.dtype)]
        + sem_pair(owners - 1) + sem_pair(owners - 1),
        before=before,
    )


def token_kernel(
    scale, inside, x_ref, place_ref, attn_ref, ffn_ref, code_ref, paired_ref, out_ref, attn_out_ref, ffn_out_ref,
    found_ref, near_ref, parts_ref, blocks_ref, row_ref,
    s0, r0, s1, r1, s2, r2, s3, r3, s4, r4, s5, r5, s6, r6,
):
    owners, others = peers_of("dp"), far_replicas()
    me, here = lax.axis_index("dp"), lax.axis_index("vocab")
    near, side = flip(here, 1), lax.rem(here, 2)
    greet(
        *[("dp", to) for _, to, _ in owners], *[("vocab", to) for _, to, _ in others], ("vocab", near)
    )
    count, length, columns = x_ref.shape
    half, pairs = length // 2, lax.axis_size("vocab") // 2
    share = half // pairs

    def half_of(which):
        return pl.ds(pl.multiple_of(which * half, half), half)

    def share_of(index):
        return pl.ds(pl.multiple_of(index // 2 * share, share), share)

    def place_of(index):
        return pl.ds(pl.multiple_of(side * half + index // 2 * share, share), share)

    def send_weights(ref, own_ref, slot, span):
        count, rows = own_ref.shape[0] // 2, own_ref.shape[1]
        mine = pl.ds(side * count, count)

        def place(origin):
            return ref.at[mine, pl.ds(pl.multiple_of(origin * rows + span[0], span[1]), span[1])]

        copies = [
            push(own_ref.at[mine, pl.ds(*span)], place(me), (s5, r5), slot + step - 1, "dp", to)
            for step, to, _ in owners
        ]
        return [(copy, place(origin), slot + step - 1) for copy, (step, _, origin) in zip(copies, owners)]

    def relay_weights(sent):
        relays = []
        for copy, place, slot in sent:
            copy.wait()
            relays.append(push(place, place, (s6, r6), slot, "vocab", near))
        return relays

    first = push(x_ref.at[:, half_of(1 - side)], near_ref, (s0, r0), 0, "vocab", near)
    some = ffn_ref.shape[1] // 2
    early = send_weights(attn_out_ref, attn_ref, 0, (0, attn_ref.shape[1]))
    early += send_weights(ffn_out_ref, ffn_ref, len(owners), (0, some))
    for ref, own_ref in ((attn_out_ref, attn_ref), (ffn_out_ref, ffn_ref)):
        rows = own_ref.shape[1]
        ref[:, pl.ds(pl.multiple_of(me * rows, rows), rows), :] = own_ref[...]
    first.wait()
    near_ref[...] += x_ref[:, half_of(side)]
    copies = [
        push(near_ref.at[:, share_of(to)], parts_ref.at[slot], (s1, r1), slot, "vocab", to)
        for slot, to, _ in others
    ]
    if inside:
        look_up_tokens(code_ref, paired_ref, found_ref)
    else:
        found_ref[...] = jnp.zeros(found_ref.shape, found_ref.dtype)
    for copy in copies:
        copy.wait()
    total = near_ref[:, share_of(here)]
    for slot, _, _ in others:
        total = total + parts_ref[slot]
    blocks_ref[...] = total
    copies = [
        push(
            blocks_ref.at[to],
            row_ref.at[me, place_of(here)],
            (s2, r2),
            step - 1,
            "dp",
            to,
        )
        for step, to, _ in owners
    ]
    row_ref[me, place_of(here)] = blocks_ref[me]
    for copy in copies:
        copy.wait()
    late = send_weights(ffn_out_ref, ffn_ref, 2 * len(owners), (some, some))
    mine = row_ref.at[:, place_of(here)]
    copies = [push(mine, mine, (s3, r3), slot, "vocab", to) for slot, to, _ in others]
    close = [push(mine, mine, (s4, r4), 0, "vocab", near)]
    for copy, (slot, _, origin) in zip(copies, others):
        copy.wait()
        theirs = row_ref.at[:, place_of(origin)]
        close.append(push(theirs, theirs, (s4, r4), slot + 1, "vocab", near))
    close += relay_weights(early)
    for copy in close[: pairs]:
        copy.wait()
    for owner in range(count):
        band = slice(owner * columns, (owner + 1) * columns)
        out_ref[:, band] = row_ref[owner].astype(jnp.float32) * scale + place_ref[:, band]
    close += relay_weights(late)
    for copy in close[pairs:]:
        copy.wait()


def gather_tokens(x, places, attn, ffn, codes, paired, scale, collective_id):
    owners, pairs = lax.axis_size("dp"), lax.axis_size("vocab") // 2
    _, length, columns = x.shape
    half = length // 2
    width = owners * columns
    whole = [low(w.shape[0], owners * w.shape[1], width) for w in (attn, ffn)]
    return talk(
        partial(token_kernel, scale, paired is not None),
        (full(length, width), *whole, low(codes.shape[0], columns)),
        collective_id,
        x,
        places,
        attn,
        ffn,
        codes,
        attn[0] if paired is None else paired,
        scratch=[
            pltpu.VMEM((owners, half, columns), x.dtype),
            pltpu.VMEM((pairs - 1, owners, half // pairs, columns), x.dtype),
            pltpu.VMEM((owners, half // pairs, columns), x.dtype),
            pltpu.VMEM((owners, length, columns), x.dtype),
        ]
        + sem_pair(1)
        + sem_pair(pairs - 1)
        + sem_pair(owners - 1)
        + sem_pair(pairs - 1)
        + sem_pair(pairs)
        + sem_pair(3 * owners - 3)
        + sem_pair(3 * owners - 3),
        microseconds=50,
    )


def sinusoid(length, model_width):
    places = np.arange(length, dtype=np.float32)[:, None]
    halves = np.arange(model_width // 2, dtype=np.float32)[None, :]
    angles = places * np.exp(halves * np.float32(-2.0 * math.log(10000.0) / model_width))
    angles = angles.astype(np.float64)
    return (
        np.stack([np.sin(angles), np.cos(angles)], axis=-1)
        .reshape(length, model_width)
        .astype(np.float32)
    )


def one_hot(ids, columns):
    return (ids[:, None] == columns[None, :]).astype(jnp.bfloat16)


def pick_weights(target_seg, pick_rows):
    sentence = jnp.take(target_seg, pick_rows, axis=0)
    return jnp.sum((sentence[:, None] == sentence[None, :]).astype(jnp.float32), axis=1)


def adam_direction(moment, second):
    return moment / (1.0 - beta_one**STEP) / (jnp.sqrt(second / (1.0 - beta_two**STEP)) + adam_eps)


def adam_update(weight, grad_item, moment, second, step_rate, decay_weight):
    moment = beta_one * moment + (1.0 - beta_one) * grad_item
    second = beta_two * second + (1.0 - beta_two) * grad_item * grad_item
    return (
        weight - step_rate * (adam_direction(moment, second) + decay_weight * weight),
        moment,
        second,
    )


def after(array, number):
    return array + jnp.where(jnp.isnan(number), 1, 0).astype(array.dtype)


def body(
    src_ids,
    src_seg,
    tgt_ids,
    tgt_seg,
    pick_pos,
    pick_label,
    attn_w,
    attn_m,
    attn_v,
    ffn_w,
    ffn_m,
    ffn_v,
    soap_basis,
    soap_stats,
    norm_p,
    norm_m,
    norm_v,
    embedding,
    embed_m,
    embed_v,
):
    owners, replicas = lax.axis_size("dp"), lax.axis_size("vocab")
    replica = lax.axis_index("vocab")
    own_table = embedding.astype(jnp.bfloat16)
    own_norms = jnp.pad(norm_p.astype(jnp.bfloat16).astype(jnp.float32), ((0, 2), (0, 0)))
    all_ids, norm_rows = gather_small("dp", 1, jnp.concatenate([src_ids, tgt_ids]), own_norms)
    norm_rows = jnp.swapaxes(norm_rows, 0, 1).reshape(16, -1)
    norms = [jnp.stack([norm_rows[k], norm_rows[7 + k]]) for k in range(7)]
    vocab_count, width = embedding.shape[0], attn_w.shape[2]
    source, source_seg, target, target_seg = (src_ids[0], src_seg[0], tgt_ids[0], tgt_seg[0])
    pick_rows, labels = (pick_pos[0], pick_label[0])
    length = source.shape[0]
    embed_scale = math.sqrt(width)
    half = vocab_count // 2
    halves = jnp.arange(half)
    paired = jnp.concatenate([own_table[:half], own_table[half:]], axis=1)

    def paired_places(ids):
        place = ids - replica * vocab_count
        inside = (place >= 0) & (place < vocab_count)
        return jnp.where(inside, place % half, -1), place < half

    def look_up(ids):
        place, left = paired_places(ids)
        wide = lax.dot_general(one_hot(place, halves), paired, (((1,), (0,)), ((), ())))
        return jnp.where(left[:, None], wide[:, :paired.shape[1] // 2], wide[:, paired.shape[1] // 2 :])

    if owners == 4:
        place, left = paired_places(jnp.swapaxes(all_ids, 0, 1).reshape(2, -1, 1))
        all_codes = jnp.where(place < 0, -1, 2 * place + left.astype(jnp.int32))
        codes = all_codes[1]
        whole_paired = jnp.pad(paired, ((0, -half % 128), (0, 0)))
        source_part = call(
            look_up_tokens, low(codes.shape[0], width // owners), all_codes[0], whole_paired
        )
    else:
        source_part = look_up(all_ids[:, 0].reshape(-1))
        codes, whole_paired = jnp.zeros((16, 1), jnp.int32), None
    positional = sinusoid(length, width)
    enc_in, enc_attn_w, enc_ffn_w, target_part = gather_tokens(
        source_part.reshape(owners, length, -1),
        positional,
        attn_w[0:4].astype(jnp.bfloat16),
        ffn_w[0:2].astype(jnp.bfloat16),
        codes,
        whole_paired,
        embed_scale,
        2,
    )
    if owners != 4:
        target_part = look_up(all_ids[:, 1].reshape(-1))
    target_sum = lax.psum(target_part, "vocab")
    enc_mid, enc_attn = attn_forward(
        enc_in, norms[0], ((enc_attn_w,), 0, 0), source_seg, source_seg, None, False
    )
    self_w, cross_w, dec_ffn_w, ready = late_weights(attn_w[4:], ffn_w[2:], enc_in, enc_mid)
    enc_out, encoded, enc_ffn = ffn_forward(enc_mid, norms[1], norms[2], ((enc_ffn_w,), 0, 0))
    dec_in = swap_owners(
        target_sum.reshape(owners, length, -1), positional, embed_scale, 3, (enc_out,)
    )
    late_table = after(own_table, ready.astype(jnp.float32) + dec_in[0, 0])
    table_low = lax.all_gather(late_table, "dp", axis=1, tiled=True)
    dec_mid, dec_self = attn_forward(
        dec_in, norms[3], self_w, target_seg, target_seg, None, True
    )
    dec_late, dec_cross = attn_forward(
        dec_mid, norms[4], cross_w, target_seg, source_seg, encoded, False
    )
    dec_out, final_low, dec_ffn = ffn_forward(dec_late, norms[5], norms[6], dec_ffn_w)

    own_labels = labels - replica * vocab_count
    picked, own_stats = loss_forward(final_low, pick_rows, own_labels, table_low)
    (seen,) = gather_small("vocab", 4, own_stats)
    weight = 1.0 / pick_weights(target_seg, pick_rows)
    grad_picked, table_parts, losses = loss_backward(
        picked, seen, weight, own_labels, table_low, owners
    )
    grad_table = lax.psum_scatter(table_parts, "dp", scatter_dimension=0, tiled=False)
    grad_picked = sum_vocab(grad_picked, 5)
    loss_part = jnp.sum(losses)
    count_part = (target_seg[-1] + 1).astype(jnp.float32)

    picks = share_selector(width, owners, replicas, replica, width)
    hidden = ffn_w.shape[1] * owners
    hidden_picks = share_selector(hidden, owners, replicas, replica, 512)
    norm_grads = [None] * 7
    grad, norm_grads[6], norm_grads[5], *ffn_blocks = ffn_backward(
        grad_picked, dec_ffn, hidden_picks, owners, places=pick_rows
    )
    grad, norm_grads[4], block, grad_encoded = attn_backward(grad, dec_cross, picks, owners, None)
    early = lax.psum_scatter(
        jnp.concatenate([block, *ffn_blocks], axis=1), "dp", scatter_dimension=0, tiled=False
    )
    grad, norm_grads[3], self_block, target_rows = attn_backward(
        grad, dec_self, picks, owners, embed_scale
    )
    grad, norm_grads[2], norm_grads[1], *ffn_blocks = ffn_backward(
        grad_encoded, enc_ffn, hidden_picks, owners, before=(grad_table, grad)
    )
    early_sum = after(early, grad[0, 0])
    early = lax.all_gather(early_sum, "vocab")
    grad, norm_grads[0], block, source_rows = attn_backward(
        grad, enc_attn, picks, owners, embed_scale, before=(early_sum,)
    )
    norm_grad = jnp.stack([after(part, early[0, 0, 0]) for part in norm_grads])
    norm_grad = jnp.concatenate([norm_grad[:, 0], norm_grad[:, 1], jnp.zeros((2, width))], axis=0)
    norm_grad = jnp.swapaxes(norm_grad.reshape(16, owners, -1), 0, 1)
    place, left = paired_places(all_ids.reshape(-1))
    tokens = ()
    if owners == 4:
        ones = jnp.broadcast_to(left[:, None], (left.shape[0], width // owners))
        tokens = (place[None, :], ones.astype(jnp.bfloat16), grad_table)
    late, layer_squares, source_rows, target_rows, norm_grad, *found = share_gradients(
        [block, self_block, *ffn_blocks], [source_rows, target_rows, norm_grad], 7, (early,), tokens
    )
    g_norm = jnp.sum(norm_grad, axis=0)[:14]
    if owners == 4:
        g_embed, embed_squares = found
    else:
        token_grads = jnp.concatenate([source_rows, target_rows], axis=1).reshape(
            owners * 2 * length, -1
        )
        left = left[:, None]
        token_grads = jnp.concatenate(
            [jnp.where(left, token_grads, 0), jnp.where(left, 0, token_grads)], axis=1
        )
        g_paired = dot_dims(one_hot(place, halves), token_grads, 0, 0)
        g_embed = grad_table.astype(jnp.float32) + jnp.concatenate(
            jnp.split(g_paired, 2, axis=1), axis=0
        )
        embed_squares = g_embed * g_embed

    def by_matrix(shared, count):
        blocks = jnp.swapaxes(shared.reshape(replicas, count, -1, width), 0, 1)
        return blocks.reshape(count, -1, width)

    early = by_matrix(early, 3)
    g_attn = [by_matrix(part, 4) for part in (late[0], late[1], early[0])]
    g_attn = jnp.concatenate(g_attn)
    g_ffn = jnp.concatenate([late[2:].reshape(2, -1, width), early[1:]])

    matrix = replica // 2
    own_grad = lax.dynamic_index_in_dim(g_ffn, matrix, 0, keepdims=False)
    own_products = dot_dims(own_grad, own_grad, 0, 0)
    first_copy = (replica == 0).astype(jnp.float32)
    raw_squares = (
        jnp.sum(layer_squares)
        + jnp.sum(jnp.square(early_sum.astype(jnp.float32)))
        + jnp.sum(embed_squares)
        + first_copy * jnp.sum(g_norm * g_norm)
    )
    few = jnp.stack([first_copy * loss_part, first_copy * count_part, raw_squares])
    few = jnp.broadcast_to(jnp.pad(few, (0, 5))[:, None], (8, 128))
    own_products, few = sum_tail(own_products, few, 8)
    loss_sum, sentences, squares = few[0, 0], few[1, 0], few[2, 0]
    grad_norm = jnp.sqrt(squares) / sentences
    factor = jnp.minimum(1.0, clip_limit / (grad_norm + norm_eps)) / sentences
    g_norm = g_norm * factor

    rows = width // 2
    own_half = lax.dynamic_slice_in_dim(own_products.astype(jnp.bfloat16), replica % 2 * rows, rows, 0)
    all_products = lax.all_gather(own_half, "vocab").reshape(4, width, width)
    weight_new = (1.0 - stat_decay) * (factor * factor)
    own_basis = renew_basis(own_products, soap_stats, soap_basis, weight_new)
    own_basis = after(own_basis, all_products[0, 0, 0])
    new_basis = lax.all_gather(own_basis, "vocab").reshape(4, width, width).astype(jnp.float32)
    new_stats = stat_decay * soap_stats + weight_new * all_products.astype(jnp.float32)

    new_norm, m_norm, v_norm = adam_update(norm_p, g_norm, norm_m, norm_v, rate_vector, 0.0)
    updated = update_matrices(
        factor,
        soap_basis,
        (g_attn, attn_w, attn_m, attn_v),
        (g_embed, embedding, embed_m, embed_v),
        (g_ffn, ffn_w, ffn_m, ffn_v),
    )
    new_attn, m_attn, v_attn, new_embed, m_embed, v_embed, new_ffn, m_ffn, v_ffn = updated
    return (
        loss_sum,
        sentences,
        grad_norm,
        new_attn,
        m_attn,
        v_attn,
        new_ffn,
        m_ffn,
        v_ffn,
        new_basis,
        new_stats,
        new_norm,
        m_norm,
        v_norm,
        new_embed,
        m_embed,
        v_embed,
    )


def solution(mesh):
    placed = (
        P("dp", None),
        P("dp", None),
        P("dp", None),
        P("dp", None),
        P("dp", None),
        P("dp", None),
        P(None, "dp", None),
        P(None, "dp", None),
        P(None, "dp", None),
        P(None, "dp", None),
        P(None, "dp", None),
        P(None, "dp", None),
        P(),
        P(),
        P(None, "dp"),
        P(None, "dp"),
        P(None, "dp"),
        P("vocab", "dp"),
        P("vocab", "dp"),
        P("vocab", "dp"),
    )
    return jax.shard_map(
        body,
        mesh=mesh,
        in_specs=placed,
        out_specs=(
            P(),
            P(),
            P(),
            P(None, "dp", None),
            P(None, "dp", None),
            P(None, "dp", None),
            P(None, "dp", None),
            P(None, "dp", None),
            P(None, "dp", None),
            P(),
            P(),
            P(None, "dp"),
            P(None, "dp"),
            P(None, "dp"),
            P("vocab", "dp"),
            P("vocab", "dp"),
            P("vocab", "dp"),
        ),
        check_vma=False,
    )
```

```python
from functools import partial
import math

import jax
import jax.numpy as jnp
import numpy as np
from jax import lax
from jax.experimental import pallas as pl
from jax.experimental.pallas import tpu as pltpu
from jax.sharding import PartitionSpec as P

HEADS = 8
STEP = 10
TILE = 128

highest = lax.Precision.HIGHEST
beta_one = 0.9
beta_two = 0.999
adam_eps = 1e-08
decay_rate = 0.01
rate_matrix = 0.03
rate_vector = 0.3
clip_limit = 1.0
stat_decay = 0.95
norm_eps = 1e-06
masked = -1e30
log_two_e = math.log2(math.e)
vmem = pl.BlockSpec(memory_space=pltpu.VMEM)
smem = pl.BlockSpec(memory_space=pltpu.SMEM)
mesh_ids = pl.DeviceIdType.MESH


def dot_dims(left, right, left_dim, right_dim):
    return lax.dot_general(
        left, right, (((left_dim,), (right_dim,)), ((), ())), preferred_element_type=jnp.float32
    )


def dot_exact(left, right, left_dim, right_dim):
    return lax.dot_general(
        left,
        right,
        (((left_dim,), (right_dim,)), ((), ())),
        precision=highest,
        preferred_element_type=jnp.float32,
    )


def cost_of(microseconds):
    return pl.CostEstimate(flops=microseconds * 10**9, bytes_accessed=0, transcendentals=0)


def call(kernel, outs, *args, scratch=(), smem_args=0, microseconds=5, before=(), far=()):
    any_spec = pl.BlockSpec(memory_space=pl.ANY)
    specs = [vmem] * (len(args) - smem_args) + [smem] * smem_args + [any_spec] * len(before)
    for k in far:
        specs[k] = any_spec

    def body(*refs):
        kernel(*refs[: len(args)], *refs[len(args) + len(before) :])

    return pl.pallas_call(
        body,
        out_shape=outs,
        in_specs=specs,
        out_specs=jax.tree.map(lambda _: vmem, outs),
        scratch_shapes=list(scratch),
        compiler_params=pltpu.CompilerParams(vmem_limit_bytes=56 * 2**20),
        cost_estimate=cost_of(microseconds),
    )(*args, *before)


def low(*shape):
    return jax.ShapeDtypeStruct(shape, jnp.bfloat16)


def full(*shape):
    return jax.ShapeDtypeStruct(shape, jnp.float32)


def norm_parts(values):
    centre = values - jnp.mean(values, axis=-1, keepdims=True)
    spread = jnp.mean(centre * centre, axis=-1, keepdims=True)
    root = lax.rsqrt(spread + norm_eps)
    return centre * root, root


def norm_forward(values, ln_ref):
    return norm_parts(values)[0] * ln_ref[0:1, :] + ln_ref[1:2, :]


def norm_backward(grad, values, ln_ref, ln_grad_ref):
    normed, root = norm_parts(values)
    ln_grad_ref[0:1, :] = jnp.sum(grad * normed, axis=0, keepdims=True)
    ln_grad_ref[1:2, :] = jnp.sum(grad, axis=0, keepdims=True)
    inner = grad * ln_ref[0:1, :]
    return root * (
        inner
        - jnp.mean(inner, axis=-1, keepdims=True)
        - normed * jnp.mean(inner * normed, axis=-1, keepdims=True)
    )


def at_tile(index, size):
    return pl.ds(pl.multiple_of(index * size, size), size)


def tile_mask(segq_ref, segk_ref, qi, ki, tile_q, tile_k, causal):
    seg_k = segk_ref[at_tile(ki, tile_k), :]
    seg_k = jnp.concatenate([seg_k] * (tile_q // TILE), axis=1)
    allowed = seg_k == segq_ref[:, at_tile(qi, tile_q)]
    if causal:
        shape = (tile_k, tile_q)
        ahead = lax.broadcasted_iota(jnp.int32, shape, 0) - lax.broadcasted_iota(
            jnp.int32, shape, 1
        )
        allowed = allowed & (ahead <= qi * tile_q - ki * tile_k)
    return allowed


def for_tiles(length, tile_q, tile_k, edge_ref, causal, step):
    count_q, count_k = length // tile_q, length // tile_k
    per_q, per_k = tile_q // TILE, tile_k // TILE

    def one(pair, carry):
        qi, ki = pair // count_k, lax.rem(pair, count_k)
        live = (edge_ref[0, qi * per_q] <= edge_ref[3, (ki + 1) * per_k - 1]) & (
            edge_ref[2, ki * per_k] <= edge_ref[1, (qi + 1) * per_q - 1]
        )
        if causal:
            live = live & (ki * tile_k < (qi + 1) * tile_q)

        @pl.when(live)
        def _():
            step(qi, ki)

        return carry

    lax.fori_loop(0, count_q * count_k, one, 0)


def tile_edges(seg_q, seg_k):
    last = TILE - 1
    return jnp.stack([seg_q[::TILE], seg_q[last::TILE], seg_k[::TILE], seg_k[last::TILE]])


def share_selector(rows, owners, shares, share, count):
    size = rows // (owners * shares)
    index = jnp.arange(count // shares)
    picked = index // size * (rows // owners) + share * size + index % size
    return (picked[:, None] == jnp.arange(count)[None, :]).astype(jnp.bfloat16)


def load_weights(w_ref, piece_refs, part, first, sems):
    if len(piece_refs) == 1:
        copies = [pltpu.make_async_copy(piece_refs[0], w_ref, sems.at[0])]
        copies[0].start()
        return copies
    own = piece_refs[0]
    matrices, rows = w_ref.shape[0], w_ref.shape[1] // 4
    half = own.shape[0] // 2
    me, side = lax.axis_index("dp"), lax.rem(lax.axis_index("vocab"), 2)
    copies = []
    for m in range(matrices):
        which = m if part is None else part
        start = first if part is None else first + m * rows

        def copy_from(ref, offset, owner, slot):
            place = pl.ds(pl.multiple_of(owner * rows, rows), rows)
            return pltpu.make_async_copy(
                ref.at[pl.ds(offset + start, rows)], w_ref.at[m, place], sems.at[slot]
            )

        copies.append(copy_from(own, which * half, me, 4 * m))
        copies[-1].start()
        for k in range(1, 4):
            mine, theirs = (copy_from(piece_refs[n], 0, me ^ k, 4 * m + k) for n in (k, k + 3))

            @pl.when(side == which)
            def _():
                mine.start()

            @pl.when(side != which)
            def _():
                theirs.start()

            copies.append(mine)
    return copies


def flip_sites(part, axis, bit):
    return lax.ppermute(part, axis, [(s, s ^ bit) for s in range(lax.axis_size(axis))])


def late_weights(attn, ffn, after, later):
    owners = lax.axis_size("dp")
    width = attn.shape[-1]
    attn, ffn = attn.astype(jnp.bfloat16), ffn.astype(jnp.bfloat16)
    if owners != 4:
        attn, ffn = (lax.all_gather(part, "dp", axis=1, tiled=True) for part in (attn, ffn))
        return ((attn[:4],), 0, 0), ((attn[4:],), 0, 0), ((ffn,), 0, 0), ffn
    halves = [
        jnp.concatenate([attn[4 * k : 4 * k + 4].reshape(-1, width), ffn[k]]) for k in range(2)
    ]
    own = jnp.concatenate(halves)
    side = lax.axis_index("vocab") % 2
    mine = jnp.where(side == 0, halves[0], halves[1])
    mine, _ = lax.optimization_barrier((mine, after))
    got = [flip_sites(mine, "dp", k) for k in range(1, 4)]
    *got, _ = lax.optimization_barrier((*got, later))
    swapped = [flip_sites(part, "vocab", 1) for part in got]
    pieces = (own, *got, *swapped)
    rows = 4 * attn.shape[1]
    return (pieces, 0, 0), (pieces, 1, 0), (pieces, None, rows), swapped[-1]


def attn_forward_kernel(causal, cross, pieces, part, first, *refs):
    refs = list(refs)
    x_ref, ln_ref, segq_ref, segk_ref = refs[:4]
    refs = refs[4:]
    key_ref = refs.pop(0) if cross else None
    piece_refs, refs = refs[:pieces], refs[pieces:]
    edge_ref, out_ref, a_ref, qt_ref, kt_ref, vt_ref, ot_ref, lse_ref = refs[:8]
    refs = refs[8:]
    w_ref, top_ref, sum_ref, acc_ref, sems = refs
    weights = load_weights(w_ref, piece_refs, part, first, sems)
    length, width = x_ref.shape
    head_size = width // HEADS
    a_ref[...] = norm_forward(x_ref[...], ln_ref).astype(jnp.bfloat16)
    key_in = key_ref if cross else a_ref
    for copy in weights:
        copy.wait()
    qt_ref[...] = dot_dims(a_ref[...], w_ref[0], 1, 0).astype(jnp.bfloat16).T
    kt_ref[...] = dot_dims(key_in[...], w_ref[1], 1, 0).astype(jnp.bfloat16).T
    vt_ref[...] = dot_dims(key_in[...], w_ref[2], 1, 0).astype(jnp.bfloat16).T
    top_ref[...] = jnp.full(top_ref.shape, masked, jnp.float32)
    sum_ref[...] = jnp.zeros(sum_ref.shape, jnp.float32)
    acc_ref[...] = jnp.zeros(acc_ref.shape, jnp.float32)
    scale = log_two_e / math.sqrt(head_size)
    bands = [slice(h * head_size, (h + 1) * head_size) for h in range(HEADS)]

    def step(qi, ki):
        q_at, k_at = at_tile(qi, 256), at_tile(ki, 256)
        allowed = tile_mask(segq_ref, segk_ref, qi, ki, 256, 256, causal)
        scores = [dot_dims(kt_ref[band, k_at], qt_ref[band, q_at], 0, 0) * scale for band in bands]
        scores = [jnp.where(allowed, part, masked) for part in scores]
        top = top_ref[:, q_at]
        new_top = jnp.maximum(
            top,
            jnp.concatenate([jnp.max(part, axis=0, keepdims=True) for part in scores], axis=0),
        )
        fade = jnp.exp2(top - new_top)
        parts = [jnp.exp2(scores[h] - new_top[h : h + 1]) for h in range(HEADS)]
        top_ref[:, q_at] = new_top
        sum_ref[:, q_at] = sum_ref[:, q_at] * fade + jnp.concatenate(
            [jnp.sum(part, axis=0, keepdims=True) for part in parts], axis=0
        )
        mixed = [
            dot_dims(vt_ref[bands[h], k_at], parts[h].astype(jnp.bfloat16), 1, 0)
            for h in range(HEADS)
        ]
        acc = acc_ref[:, q_at]
        acc_ref[:, q_at] = jnp.concatenate(
            [acc[bands[h]] * fade[h : h + 1] + mixed[h] for h in range(HEADS)], axis=0
        )

    for_tiles(length, 256, 256, edge_ref, causal, step)
    lse_ref[...] = top_ref[...] + jnp.log2(sum_ref[...])
    for h in range(HEADS):
        ot_ref[bands[h], :] = (acc_ref[bands[h], :] / sum_ref[h : h + 1, :]).astype(jnp.bfloat16)
    out_ref[...] = x_ref[...] + dot_dims(ot_ref[...], w_ref[3], 0, 0)


def attn_forward(x, ln, weights, seg_q, seg_k, key_in, causal):
    length, width = x.shape
    weights, part, first = weights
    cross = key_in is not None
    segs = (seg_q[None, :], jnp.broadcast_to(seg_k[:, None], (length, TILE)))
    edges = tile_edges(seg_q, seg_k)
    args = (x, ln, *segs) + ((key_in,) if cross else ()) + (*weights, edges)
    outs = (full(length, width), low(length, width)) + (low(width, length),) * 4
    outs = outs + (full(HEADS, length),)
    if len(weights) > 1:
        outs = outs + (low(4, width, width),)
    out, normed, *stored = call(
        partial(attn_forward_kernel, causal, cross, len(weights), part, first),
        outs,
        *args,
        scratch=[pltpu.VMEM((4, width, width), jnp.bfloat16)][: len(weights) == 1]
        + [
            pltpu.VMEM((HEADS, length), jnp.float32),
            pltpu.VMEM((HEADS, length), jnp.float32),
            pltpu.VMEM((width, length), jnp.float32),
            pltpu.SemaphoreType.DMA((16,)),
        ],
        smem_args=1,
        microseconds=20,
        far=range(len(args) - 1 - len(weights), len(args) - 1),
    )
    whole = stored.pop() if len(weights) > 1 else weights[0]
    return out, (x, ln, whole, segs, edges, causal, key_in, normed, stored)


def attn_backward_kernel(causal, cross, row_scale, *refs):
    g_ref, x_ref, ln_ref, w_ref, pick_ref, segq_ref, segk_ref, a_ref = refs[:8]
    refs = list(refs[8:])
    key_ref = refs.pop(0) if cross else a_ref
    qt_ref, kt_ref, vt_ref, ot_ref, lse_ref, edge_ref, out_ref, ln_grad_ref, block_ref, extra_ref = refs[:10]
    low_ref, gq_ref, gk_ref, gv_ref, got_ref, delta_ref, gqt_ref, gkt_ref, gvt_ref = refs[10:]
    length, width = x_ref.shape
    head_size = width // HEADS
    low_ref[...] = g_ref[...].astype(jnp.bfloat16)
    got_ref[...] = dot_dims(low_ref[...], w_ref[3], 1, 1).astype(jnp.bfloat16).T
    bands = [slice(h * head_size, (h + 1) * head_size) for h in range(HEADS)]
    for h in range(HEADS):
        delta_ref[h : h + 1, :] = jnp.sum(
            got_ref[bands[h], :].astype(jnp.float32) * ot_ref[bands[h], :].astype(jnp.float32),
            axis=0,
            keepdims=True,
        )
    for ref in (gqt_ref, gkt_ref, gvt_ref):
        ref[...] = jnp.zeros(ref.shape, jnp.float32)
    scale = log_two_e / math.sqrt(head_size)
    back = 1.0 / math.sqrt(head_size)

    def step(qi, ki):
        q_at, k_at = at_tile(qi, 256), at_tile(ki, TILE)
        allowed = tile_mask(segq_ref, segk_ref, qi, ki, 256, TILE, causal)
        scores = [dot_dims(kt_ref[band, k_at], qt_ref[band, q_at], 0, 0) for band in bands]
        grads = [dot_dims(vt_ref[band, k_at], got_ref[band, q_at], 0, 0) for band in bands]
        parts = [
            jnp.where(allowed, jnp.exp2(scores[h] * scale - lse_ref[h : h + 1, q_at]), 0.0)
            for h in range(HEADS)
        ]
        grads = [parts[h] * (grads[h] - delta_ref[h : h + 1, q_at]) for h in range(HEADS)]
        parts_t = [part.T.astype(jnp.bfloat16) for part in parts]
        grads_t = [part.T.astype(jnp.bfloat16) for part in grads]
        grads = [part.astype(jnp.bfloat16) for part in grads]
        for ref, place, terms in (
            (gvt_ref, k_at, [dot_dims(got_ref[bands[h], q_at], parts_t[h], 1, 0) for h in range(HEADS)]),
            (gkt_ref, k_at, [dot_dims(qt_ref[bands[h], q_at], grads_t[h], 1, 0) for h in range(HEADS)]),
            (gqt_ref, q_at, [dot_dims(kt_ref[bands[h], k_at], grads[h], 1, 0) for h in range(HEADS)]),
        ):
            ref[:, place] += jnp.concatenate(terms, axis=0)

    for_tiles(length, 256, TILE, edge_ref, causal, step)
    gq_ref[...] = (gqt_ref[...] * back).astype(jnp.bfloat16).T
    gk_ref[...] = (gkt_ref[...] * back).astype(jnp.bfloat16).T
    gv_ref[...] = gvt_ref[...].astype(jnp.bfloat16).T
    from_query = dot_dims(gq_ref[...], w_ref[0], 1, 1)
    from_keys = dot_dims(gk_ref[...], w_ref[1], 1, 1) + dot_dims(gv_ref[...], w_ref[2], 1, 1)
    if cross:
        extra_ref[...] = from_keys
    else:
        from_query = from_query + from_keys
    total = g_ref[...] + norm_backward(from_query, x_ref[...], ln_ref, ln_grad_ref)
    out_ref[...] = total
    owners = block_ref.shape[0]
    if not cross:
        columns = width // owners
        for owner in range(owners):
            band = slice(owner * columns, (owner + 1) * columns)
            extra_ref[owner] = (total[:, band] * row_scale).astype(jnp.bfloat16)
    own_a = dot_dims(pick_ref[...], a_ref[...], 1, 1).astype(jnp.bfloat16)
    own_key = dot_dims(pick_ref[...], key_ref[...], 1, 1).astype(jnp.bfloat16) if cross else own_a
    own_o = dot_dims(pick_ref[...], ot_ref[...], 1, 0).astype(jnp.bfloat16)
    size = own_a.shape[0] // owners
    products = ((own_a, gq_ref), (own_key, gk_ref), (own_key, gv_ref), (own_o, low_ref))
    for m, (rows, right_ref) in enumerate(products):
        product = dot_dims(rows, right_ref[...], 1, 0).astype(jnp.bfloat16)
        for owner in range(owners):
            block_ref[owner, m * size : (m + 1) * size, :] = product[owner * size : (owner + 1) * size]


def attn_backward(grad, stored, picks, owners, row_scale, before=()):
    x, ln, weights, segs, edges, causal, key_in, normed, kept = stored
    length, width = x.shape
    cross = key_in is not None
    extra = full(length, width) if cross else low(owners, length, width // owners)
    outs = (full(length, width), full(2, width), low(owners, 4 * picks.shape[0] // owners, width), extra)
    keys = (key_in,) if cross else ()
    return call(
        partial(attn_backward_kernel, causal, cross, row_scale),
        outs,
        grad,
        x,
        ln,
        weights,
        picks,
        *segs,
        normed,
        *keys,
        *kept,
        edges,
        scratch=[pltpu.VMEM((length, width), jnp.bfloat16)] * 4
        + [pltpu.VMEM((width, length), jnp.bfloat16), pltpu.VMEM((HEADS, length), jnp.float32)]
        + [pltpu.VMEM((width, length), jnp.float32)] * 3,
        smem_args=1,
        microseconds=25,
        before=before,
    )


def gelu_parts(hidden):
    root = math.sqrt(2.0 / math.pi)
    square = hidden * hidden
    bend = jnp.tanh(root * hidden * (1.0 + 0.044715 * square))
    value = 0.5 * hidden * (1.0 + bend)
    slope = 0.5 * (1.0 + bend) + 0.5 * hidden * (1.0 - bend * bend) * root * (
        1.0 + 3.0 * 0.044715 * square
    )
    return value, slope


def ffn_forward_kernel(chunk, pieces, first, x_ref, ln_ref, next_ref, *refs):
    piece_refs, (out_ref, a_ref, after_ref, w_ref, sems) = refs[:pieces], refs[pieces:]
    weights = load_weights(w_ref, piece_refs, None, first, sems)
    w_in_ref, w_out_ref = w_ref.at[0], w_ref.at[1]
    a_ref[...] = norm_forward(x_ref[...], ln_ref).astype(jnp.bfloat16)
    total = x_ref[...]
    for copy in weights:
        copy.wait()
    for start in range(0, w_in_ref.shape[0], chunk):
        part = slice(start, start + chunk)
        hidden = dot_dims(a_ref[...], w_in_ref[part, :], 1, 1)
        active = gelu_parts(hidden)[0].astype(jnp.bfloat16)
        total = total + dot_dims(active, w_out_ref[part, :], 1, 0)
    out_ref[...] = total
    after_ref[...] = norm_forward(total, next_ref).astype(after_ref.dtype)


def ffn_forward(x, ln, ln_next, weights):
    length, width = x.shape
    weights, _, first = weights
    outs = (full(length, width), low(length, width), low(length, width))
    if len(weights) > 1:
        outs = outs + (low(2, 4 * (weights[0].shape[0] // 2 - first), width),)
    out, normed, after, *whole = call(
        partial(ffn_forward_kernel, 512, len(weights), first),
        outs,
        x,
        ln,
        ln_next,
        *weights,
        scratch=[pltpu.VMEM(w.shape, w.dtype) for w in weights if len(weights) == 1]
        + [pltpu.SemaphoreType.DMA((8,))],
        microseconds=12,
        far=range(3, 3 + len(weights)),
    )
    return out, after, (x, ln, whole[0] if whole else weights[0], normed, out, ln_next)


def ffn_backward_kernel(
    chunk, picked, after_ref, *refs
):
    if picked:
        place_ref, *refs = refs
        shape = (refs[0].shape[0], place_ref.shape[1])
        chosen = lax.broadcasted_iota(jnp.int32, shape, 0) == place_ref[...]
        after = dot_dims(chosen.astype(jnp.bfloat16), after_ref[...], 1, 0)
    else:
        after = after_ref[...]
    ffn_backward_rest(chunk, after, *refs)


def ffn_backward_rest(
    chunk, after, y_ref, next_ref, x_ref, ln_ref, a_ref, w_ref, pick_ref,
    out_ref, next_grad_ref, ln_grad_ref, in_ref, back_ref, low_ref, g_ref,
):
    w_in_ref, w_out_ref = w_ref.at[0], w_ref.at[1]
    g_ref[...] = norm_backward(after, y_ref[...], next_ref, next_grad_ref)
    low_ref[...] = g_ref[...].astype(jnp.bfloat16)
    total = jnp.zeros(g_ref.shape, jnp.float32)
    owners, size = in_ref.shape[:2]
    blocks = pick_ref.shape[0] // size
    for index in range(w_in_ref.shape[0] // chunk):
        part = slice(index * chunk, (index + 1) * chunk)
        hidden = dot_dims(a_ref[...], w_in_ref[part, :], 1, 1)
        value, slope = gelu_parts(hidden)
        grad = (dot_dims(low_ref[...], w_out_ref[part, :], 1, 1) * slope).astype(jnp.bfloat16)
        total = total + dot_dims(grad, w_in_ref[part, :], 1, 0)
        pairs = ((in_ref, grad, a_ref), (back_ref, value.astype(jnp.bfloat16), low_ref))
        for ref, left, right_ref in pairs:
            rows = dot_dims(pick_ref[...], left, 1, 1).astype(jnp.bfloat16)
            product = dot_dims(rows, right_ref[...], 1, 0).astype(jnp.bfloat16)
            for block in range(blocks):
                ref[index * blocks + block] = product[block * size : (block + 1) * size]
    out_ref[...] = g_ref[...] + norm_backward(total, x_ref[...], ln_ref, ln_grad_ref)


def ffn_backward(grad_after, stored, picks, owners, before=(), places=None):
    x, ln, weights, normed, out, ln_next = stored
    length, width = x.shape
    chunk = picks.shape[1]
    size = picks.shape[0] * weights.shape[1] // chunk // owners
    block = low(owners, size, width)
    return call(
        partial(ffn_backward_kernel, chunk, places is not None),
        (full(length, width), full(2, width), full(2, width), block, block),
        grad_after,
        *(() if places is None else (places[None, :],)),
        out,
        ln_next,
        x,
        ln,
        normed,
        weights,
        picks,
        scratch=[
            pltpu.VMEM((length, width), jnp.bfloat16),
            pltpu.VMEM((length, width), jnp.float32),
        ],
        microseconds=17,
        before=before,
    )


def follow_kernel(x_ref, out_ref):
    out_ref[...] = x_ref[...]


def follow(x, *before):
    out = jax.ShapeDtypeStruct(x.shape, x.dtype)
    return call(follow_kernel, out, x, microseconds=1, before=before)


def square_kernel(x_ref, out_ref, square_ref):
    out_ref[...] = x_ref[...]
    values = x_ref[...].astype(jnp.float32)
    square_ref[...] = jnp.sum(values * values, axis=0, keepdims=True)


def follow_with_squares(x, *before):
    outs = (low(*x.shape), full(1, x.shape[1]))
    return call(square_kernel, outs, x, microseconds=1, before=before)


def norm_blocks_kernel(*refs):
    refs, out_ref = refs[:-1], refs[-1]
    owners, _, columns = out_ref.shape
    out_ref[...] = jnp.zeros(out_ref.shape, jnp.float32)
    for k, ref in enumerate(refs):
        for owner in range(owners):
            band = slice(owner * columns, (owner + 1) * columns)
            out_ref[owner, k : k + 1, :] = ref[0:1, band]
            out_ref[owner, len(refs) + k : len(refs) + k + 1, :] = ref[1:2, band]


def norm_blocks(grads, owners, *before):
    width = grads[0].shape[1]
    outs = full(owners, 16, width // owners)
    return call(norm_blocks_kernel, outs, *grads, microseconds=1, before=before)


def look_up_tokens(code_ref, paired_ref, found_ref):
    step = 256
    columns = found_ref.shape[1]

    def one(index, carry):
        span = pl.ds(pl.multiple_of(index * step, step), step)
        code = code_ref[span, :]
        places = lax.broadcasted_iota(jnp.int32, (step, paired_ref.shape[0]), 1)
        chosen = (places == lax.shift_right_arithmetic(code, 1)).astype(jnp.bfloat16)
        wide = dot_dims(chosen, paired_ref[...], 1, 0)
        left = jnp.bitwise_and(code, 1) == 1
        found_ref[span, :] = jnp.where(left, wide[:, :columns], wide[:, columns:]).astype(jnp.bfloat16)
        return carry

    lax.fori_loop(0, code_ref.shape[0] // step, one, 0)


def loss_forward_kernel(chunks, final_ref, pick_ref, label_ref, table_ref, picked_ref, stat_ref, logit_ref):
    count, length = pick_ref.shape[0], final_ref.shape[0]
    places = lax.broadcasted_iota(jnp.int32, (count, length), 1)
    chosen = (places == pick_ref[...]).astype(jnp.bfloat16)
    picked_ref[...] = dot_dims(chosen, final_ref[...], 1, 0).astype(jnp.bfloat16)
    rows = table_ref.shape[0] // chunks
    top = jnp.full((1, count), masked, jnp.float32)
    label = jnp.zeros((1, count), jnp.float32)
    for index in range(chunks):
        span = slice(index * rows, (index + 1) * rows)
        logits = dot_dims(table_ref[span, :], picked_ref[...], 1, 1)
        logit_ref[span, :] = logits
        top = jnp.maximum(top, jnp.max(logits, axis=0, keepdims=True))
        hit = lax.broadcasted_iota(jnp.int32, logits.shape, 0) + index * rows == label_ref[...]
        label = label + jnp.sum(jnp.where(hit, logits, 0.0), axis=0, keepdims=True)
    total = jnp.zeros((1, count), jnp.float32)
    for index in range(chunks):
        span = slice(index * rows, (index + 1) * rows)
        total = total + jnp.sum(jnp.exp(logit_ref[span, :] - top), axis=0, keepdims=True)
    stat_ref[...] = jnp.concatenate([top, total, label, jnp.zeros((5, count), jnp.float32)], axis=0)


def loss_forward(final, pick_rows, labels, table):
    count, width = pick_rows.shape[0], final.shape[1]
    return call(
        partial(loss_forward_kernel, 8),
        (low(count, width), full(8, count)),
        final,
        pick_rows[:, None],
        labels[None, :],
        table,
        scratch=[pltpu.VMEM((table.shape[0], count), jnp.float32)],
        microseconds=6,
    )


def loss_backward_kernel(
    chunks, picked_ref, seen_ref, weight_ref, label_ref, table_ref, grad_ref, parts_ref, loss_ref
):
    tops, totals, labels = (
        jnp.concatenate([seen_ref[k, m : m + 1, :] for k in range(seen_ref.shape[0])], axis=0)
        for m in range(3)
    )
    top = jnp.max(tops, axis=0, keepdims=True)
    total = top + jnp.log(jnp.sum(totals * jnp.exp(tops - top), axis=0, keepdims=True))
    loss_ref[...] = (total - jnp.sum(labels, axis=0, keepdims=True)) * weight_ref[...]
    rows = table_ref.shape[0] // chunks
    columns = parts_ref.shape[2]
    grad = jnp.zeros(grad_ref.shape, jnp.float32)
    for index in range(chunks):
        span = slice(index * rows, (index + 1) * rows)
        logits = dot_dims(table_ref[span, :], picked_ref[...], 1, 1)
        hit = lax.broadcasted_iota(jnp.int32, logits.shape, 0) + index * rows == label_ref[...]
        slopes = weight_ref[...] * (jnp.exp(logits - total) - jnp.where(hit, 1.0, 0.0))
        slopes = slopes.astype(jnp.bfloat16)
        product = dot_dims(slopes, picked_ref[...], 1, 0).astype(jnp.bfloat16)
        for owner in range(parts_ref.shape[0]):
            parts_ref[owner, span, :] = product[:, owner * columns : (owner + 1) * columns]
        grad = grad + dot_dims(slopes, table_ref[span, :], 0, 0)
    grad_ref[...] = grad.astype(jnp.bfloat16)


def loss_backward(picked, seen, weight, labels, table, owners):
    count, width = picked.shape
    return call(
        partial(loss_backward_kernel, 8),
        (low(count, width), low(owners, table.shape[0], width // owners), full(1, count)),
        picked,
        seen,
        weight[None, :],
        labels[None, :],
        table,
        microseconds=8,
    )


def adam_parts(weight, grad, moment, second):
    moment = beta_one * moment + (1.0 - beta_one) * grad
    second = beta_two * second + (1.0 - beta_two) * grad * grad
    step = adam_direction(moment, second) + decay_rate * weight
    return weight - rate_matrix * step, moment, second


def update_kernel(*refs):
    factor_ref, basis_ref, *ins = refs[:14]
    outs = refs[14:]
    factor = factor_ref[0]
    for k in (0, 1):
        grad_ref, weight_ref, moment_ref, second_ref = ins[4 * k : 4 * k + 4]
        grad = grad_ref[...].astype(jnp.float32) * factor
        results = adam_parts(weight_ref[...], grad, moment_ref[...], second_ref[...])
        for ref, result in zip(outs[3 * k : 3 * k + 3], results):
            ref[...] = result
    g_ref, w_ref, m_ref, v_ref = ins[8:]
    new_w_ref, new_m_ref, new_v_ref = outs[6:]
    high = basis_ref[0].astype(jnp.bfloat16)
    rest = (basis_ref[0] - high.astype(jnp.float32)).astype(jnp.bfloat16)
    grad = g_ref[0]
    rotated = (dot_dims(grad, high, 1, 0) + dot_dims(grad, rest, 1, 0)) * factor
    moment = beta_one * m_ref[0] + (1.0 - beta_one) * rotated
    second = beta_two * v_ref[0] + (1.0 - beta_two) * rotated * rotated
    new_m_ref[0] = moment
    new_v_ref[0] = second
    step = adam_direction(moment, second)
    step_high = step.astype(jnp.bfloat16)
    step_rest = (step - step_high.astype(jnp.float32)).astype(jnp.bfloat16)
    back = (
        dot_dims(step_high, high, 1, 1)
        + dot_dims(step_high, rest, 1, 1)
        + dot_dims(step_rest, high, 1, 1)
    )
    new_w_ref[0] = w_ref[0] - rate_matrix * (back + decay_rate * w_ref[0])


def update_matrices(factor, bases, attn, table, ffn):
    def blocks(array):
        shape = (array.shape[0] // 4, *array.shape[1:])
        return pl.BlockSpec(shape, lambda k: (k,) + (0,) * (len(shape) - 1))

    arrays = (*attn, *table, *ffn)
    results = [part for group in (attn, table, ffn) for part in group[1:]]
    return pl.pallas_call(
        update_kernel,
        grid=(4,),
        out_shape=tuple(full(*part.shape) for part in results),
        in_specs=[smem, blocks(bases)] + [blocks(part) for part in arrays],
        out_specs=tuple(blocks(part) for part in results),
        compiler_params=pltpu.CompilerParams(vmem_limit_bytes=56 * 2**20),
        cost_estimate=cost_of(20),
    )(factor.reshape(1), bases, *arrays)


def small_factor(block):
    size = block.shape[0]
    eye = (
        lax.broadcasted_iota(jnp.int32, (size, size), 0)
        == lax.broadcasted_iota(jnp.int32, (size, size), 1)
    ).astype(jnp.float32)
    whole = jnp.concatenate([block, eye], axis=1)
    rows = [whole[8 * u : 8 * u + 8] for u in range(size // 8)]
    shape = rows[0].shape
    sub = lax.broadcasted_iota(jnp.int32, shape, 0)

    def lane_splat(value, lane):
        return jnp.broadcast_to(value[:, lane : lane + 1], shape)

    def row_splat(value, row):
        return jnp.broadcast_to(value[row : row + 1, :], shape)

    for g in range(len(rows)):
        first = 8 * g
        lanes = {
            u: [lane_splat(rows[u], first + s) for s in range(8)] for u in range(g, len(rows))
        }
        scale = jnp.zeros(shape, jnp.float32)
        for t in range(8):
            pivot = row_splat(lanes[g][t], t)
            root = lax.rsqrt(pivot)
            inverse = root * root
            scale = jnp.where(sub == t, root, scale)
            row_t = row_splat(rows[g], t) * inverse
            splats = {s: row_splat(lanes[g][s], t) * inverse for s in range(t + 1, 8)}
            for u in range(g, len(rows)):
                factor = lanes[u][t]
                if u == g:
                    factor = jnp.where(sub > t, factor, 0.0)
                rows[u] = rows[u] - factor * row_t
                for s in range(t + 1, 8):
                    lanes[u][s] = lanes[u][s] - factor * splats[s]
        rows[g] = rows[g] * scale
    return jnp.concatenate(rows, axis=0)[:, size:]


def renew_kernel(
    product_ref, stats_ref, bases_ref, factor_ref, half_ref, stat_ref, basis_ref, out_ref, gram_ref, rest_ref, sems
):
    size = stat_ref.shape[0]
    here = lax.axis_index("vocab")
    copies = [
        pltpu.make_async_copy(ref.at[here // 2], place, sems.at[k])
        for k, (ref, place) in enumerate(((stats_ref, stat_ref), (bases_ref, basis_ref)))
    ]
    for copy in copies:
        copy.start()
    for copy in copies:
        copy.wait()
    statistic = stat_decay * stat_ref[...] + factor_ref[0] * product_ref[...]
    product = dot_exact(statistic, basis_ref[...], 1, 0)
    rest_ref[...] = product
    gram_ref[...] = dot_exact(product, product, 0, 0)
    for low in range(0, size, 128):
        high = low + 128
        block = gram_ref[low:high, low:high]
        corner = small_factor(block[:64, :64])
        across = dot_exact(corner, block[:64, 64:], 1, 0)
        second = small_factor(block[64:, 64:] - dot_exact(across, across, 0, 0))
        below = dot_exact(second, dot_exact(across, corner, 0, 0), 1, 0)
        inverse = jnp.concatenate(
            [
                jnp.concatenate([corner, jnp.zeros_like(corner)], axis=1),
                jnp.concatenate([-below, second], axis=1),
            ],
            axis=0,
        )
        columns = dot_exact(rest_ref[:, low:high], inverse, 1, 1)
        out_ref[:, low:high] = columns
        if high < size:
            panel = dot_exact(inverse, gram_ref[low:high, high:], 1, 0)
            gram_ref[high:, high:] -= dot_exact(panel, panel, 0, 0)
            rest_ref[:, high:] -= dot_exact(columns, panel, 1, 0)
    rows = size // 2
    half = pl.ds(pl.multiple_of(lax.rem(here, 2) * rows, rows), rows)
    half_ref[...] = out_ref[half, :].astype(jnp.bfloat16)


def renew_basis(products, stats, bases, factor):
    size = products.shape[0]
    return call(
        renew_kernel,
        low(size // 2, size),
        products,
        stats,
        bases,
        factor.reshape(1),
        scratch=[pltpu.VMEM((size, size), jnp.float32)] * 5 + [pltpu.SemaphoreType.DMA((2,))],
        smem_args=1,
        microseconds=29,
        far=(1, 2),
    )


def peers_of(axis):
    size, me = lax.axis_size(axis), lax.axis_index(axis)
    return [
        (step, lax.rem(me + step, size), lax.rem(me + size - step, size)) for step in range(1, size)
    ]


def greet(*places):
    barrier = pltpu.get_barrier_semaphore()
    for axis, index in places:
        pl.semaphore_signal(barrier, inc=1, device_id={axis: index}, device_id_type=mesh_ids)
    pl.semaphore_wait(barrier, len(places))


def push(source, target, sems, slot, axis, index):
    copy = pltpu.make_async_remote_copy(
        src_ref=source,
        dst_ref=target,
        send_sem=sems[0].at[slot],
        recv_sem=sems[1].at[slot],
        device_id={axis: index},
        device_id_type=mesh_ids,
    )
    copy.start()
    return copy


def sem_pair(count):
    return [pltpu.SemaphoreType.DMA((count,)), pltpu.SemaphoreType.DMA((count,))]


def talk(kernel, outs, collective_id, *args, scratch=(), microseconds=15, before=()):
    def body(*refs):
        kernel(*refs[: len(args)], *refs[len(args) + len(before) :])

    return pl.pallas_call(
        body,
        out_shape=outs,
        in_specs=[vmem] * len(args) + [pl.BlockSpec(memory_space=pl.ANY)] * len(before),
        out_specs=jax.tree.map(lambda _: vmem, outs),
        scratch_shapes=list(scratch),
        compiler_params=pltpu.CompilerParams(
            collective_id=collective_id, has_side_effects=True, vmem_limit_bytes=56 * 2**20
        ),
        cost_estimate=cost_of(microseconds),
    )(*args, *before)


def gather_kernel(axis, *refs):
    count = (len(refs) - 2) // 2
    others = peers_of(axis)
    greet(*[(axis, to) for _, to, _ in others])
    me = lax.axis_index(axis)
    copies = [
        push(refs[k], refs[count + k].at[me], refs[-2:], k * len(others) + step - 1, axis, to)
        for k in range(count)
        for step, to, _ in others
    ]
    for k in range(count):
        refs[count + k][me] = refs[k][...]
    for copy in copies:
        copy.wait()


def gather_small(axis, collective_id, *arrays):
    size = lax.axis_size(axis)
    outs = tuple(jax.ShapeDtypeStruct((size, *x.shape), x.dtype) for x in arrays)
    sems = sem_pair((size - 1) * len(arrays))
    return talk(partial(gather_kernel, axis), outs, collective_id, *arrays, scratch=sems)


def flip(index, bit):
    return index + bit - 2 * bit * lax.rem(index // bit, 2)


def far_replicas():
    here, size = lax.axis_index("vocab"), lax.axis_size("vocab")
    return [
        (step // 2 - 1, lax.rem(here + step, size), lax.rem(here + size - step, size))
        for step in range(2, size, 2)
    ]


def sum_kernel(x_ref, out_ref, near_ref, send_ref, parts_ref, s0, r0, s1, r1, s2, r2, s3, r3):
    here, others = lax.axis_index("vocab"), far_replicas()
    near, side = flip(here, 1), lax.rem(here, 2)
    greet(*[("vocab", to) for _, to, _ in others], ("vocab", near))
    half = near_ref.shape[0]
    share = parts_ref.shape[1]

    def half_of(which):
        return pl.ds(pl.multiple_of(which * half, half), half)

    def share_of(index, start):
        return pl.ds(pl.multiple_of(start + index // 2 * share, share), share)

    push(x_ref.at[half_of(1 - side)], near_ref, (s0, r0), 0, "vocab", near).wait()
    total = near_ref[...].astype(jnp.float32) + x_ref[half_of(side), :].astype(jnp.float32)
    send_ref[...] = total.astype(send_ref.dtype)
    copies = [
        push(send_ref.at[share_of(to, 0)], parts_ref.at[slot], (s1, r1), slot, "vocab", to)
        for slot, to, _ in others
    ]
    total = send_ref[share_of(here, 0), :].astype(jnp.float32)
    for copy, (slot, _, _) in zip(copies, others):
        copy.wait()
        total = total + parts_ref[slot].astype(jnp.float32)
    mine = share_of(here, side * half)
    out_ref[mine, :] = total.astype(out_ref.dtype)
    copies = [
        push(out_ref.at[mine], out_ref.at[mine], (s2, r2), slot, "vocab", to) for slot, to, _ in others
    ]
    close = [push(out_ref.at[mine], out_ref.at[mine], (s3, r3), 0, "vocab", near)]
    for copy, (slot, _, origin) in zip(copies, others):
        copy.wait()
        theirs = out_ref.at[share_of(origin, side * half)]
        close.append(push(theirs, theirs, (s3, r3), slot + 1, "vocab", near))
    for copy in close:
        copy.wait()


def sum_vocab(x, collective_id):
    pairs = lax.axis_size("vocab") // 2
    rows, columns = x.shape
    half = rows // 2
    return talk(
        sum_kernel,
        jax.ShapeDtypeStruct(x.shape, x.dtype),
        collective_id,
        x,
        scratch=[
            pltpu.VMEM((half, columns), x.dtype),
            pltpu.VMEM((half, columns), x.dtype),
            pltpu.VMEM((pairs - 1, half // pairs, columns), x.dtype),
        ]
        + sem_pair(1)
        + sem_pair(pairs - 1)
        + sem_pair(pairs - 1)
        + sem_pair(pairs),
    )


def tail_kernel(
    x_ref, few_ref, out_ref, sum_ref, parts_ref, seen_ref, line_ref, lines_ref,
    s0, r0, s1, r1, s2, r2, s3, r3, s4, r4,
):
    owners, replicas = peers_of("dp"), peers_of("vocab")
    greet(*[("dp", to) for _, to, _ in owners], *[("vocab", to) for _, to, _ in replicas])
    size, me, here = lax.axis_size("dp"), lax.axis_index("dp"), lax.axis_index("vocab")
    near, side = flip(here, 1), lax.rem(here, 2)
    rows = parts_ref.shape[1]

    def rows_of(index):
        return pl.ds(pl.multiple_of((side * size + index) * rows, rows), rows)

    few = [
        push(few_ref, seen_ref.at[here], (s2, r2), step - 1, "vocab", to) for step, to, _ in replicas
    ]
    wide = [
        push(x_ref.at[rows_of(to)], parts_ref.at[me], (s0, r0), step - 1, "dp", to)
        for step, to, _ in owners
    ]
    seen_ref[here] = few_ref[...]
    parts_ref[me] = x_ref[rows_of(me), :]
    for copy in few:
        copy.wait()
    line_ref[...] = jnp.sum(seen_ref[...], axis=0)
    few = [
        push(line_ref, lines_ref.at[me], (s3, r3), step - 1, "dp", to) for step, to, _ in owners
    ]
    lines_ref[me] = line_ref[...]
    for copy in wide:
        copy.wait()
    out_ref[rows_of(me), :] = jnp.sum(parts_ref[...], axis=0)
    mine = out_ref.at[rows_of(me)]
    wide = [push(mine, mine, (s1, r1), step - 1, "dp", to) for step, to, _ in owners]
    close = [push(mine, mine, (s4, r4), 0, "vocab", near)]
    for copy in few:
        copy.wait()
    sum_ref[...] = jnp.sum(lines_ref[...], axis=0)
    for copy, (step, _, origin) in zip(wide, owners):
        copy.wait()
        theirs = out_ref.at[rows_of(origin)]
        close.append(push(theirs, theirs, (s4, r4), step, "vocab", near))
    for copy in close:
        copy.wait()


def sum_tail(x, few, collective_id):
    owners, replicas = lax.axis_size("dp"), lax.axis_size("vocab")
    rows, columns = x.shape
    share = rows // (2 * owners)
    return talk(
        tail_kernel,
        (full(*x.shape), full(*few.shape)),
        collective_id,
        x,
        few,
        scratch=[
            pltpu.VMEM((owners, share, columns), jnp.float32),
            pltpu.VMEM((replicas, *few.shape), jnp.float32),
            pltpu.VMEM(few.shape, jnp.float32),
            pltpu.VMEM((owners, *few.shape), jnp.float32),
        ]
        + sem_pair(owners - 1)
        + sem_pair(owners - 1)
        + sem_pair(replicas - 1)
        + sem_pair(owners - 1)
        + sem_pair(owners),
    )


def sum_tokens(rows_refs, place_ref, left_ref, table_ref, wide_ref, embed_ref, square_ref):
    owners, length, columns = rows_refs[0].shape
    for owner in range(owners):
        for k, rows_ref in enumerate(rows_refs):
            start = (owner * len(rows_refs) + k) * length
            span = slice(start, start + length)
            left = rows_ref[owner] * left_ref[span, :]
            wide_ref[span, :columns] = left
            wide_ref[span, columns:] = rows_ref[owner] - left
    tokens, half = wide_ref.shape[0], embed_ref.shape[0] // 2
    tile, step = half // 4, 1024
    square_ref[...] = jnp.zeros(square_ref.shape, jnp.float32)

    def one(index, carry):
        start = index * tile
        places = lax.broadcasted_iota(jnp.int32, (tile, step), 0) + start
        total = jnp.zeros((tile, 2 * columns), jnp.float32)
        for first in range(0, tokens, step):
            chosen = (places == place_ref[:, first : first + step]).astype(jnp.bfloat16)
            total = total + dot_dims(chosen, wide_ref[first : first + step, :], 1, 0)
        for side in range(2):
            span = pl.ds(pl.multiple_of(side * half + start, 16), tile)
            part = total[:, side * columns : (side + 1) * columns]
            part = part + table_ref[span, :].astype(jnp.float32)
            embed_ref[span, :] = part
            square_ref[...] += jnp.sum(part * part, axis=0, keepdims=True)
        return carry

    lax.fori_loop(0, 4, one, 0)


def gradient_kernel(chunks, count, inside, *refs):
    x_refs, refs = refs[:chunks], refs[chunks:]
    rows_refs, refs = refs[:count], refs[count:]
    if inside:
        (place_ref, left_ref, table_ref), refs = refs[:3], refs[3:]
    (out_ref, square_ref, *refs) = refs
    swapped_refs, refs = refs[:count], refs[count:]
    if inside:
        (embed_ref, embed_square_ref), refs = refs[:2], refs[2:]
        *refs, wide_ref = refs
    parts_ref, s0, r0, s1, r1, s2, r2, s3, r3, s4, r4 = refs
    owners = peers_of("dp")
    here, me = lax.axis_index("vocab"), lax.axis_index("dp")
    near = flip(here, 1)
    size = lax.axis_size("vocab")
    steps = range(2, size, 2)
    greet(
        *[("dp", to) for _, to, _ in owners],
        *[("vocab", lax.rem(here + step, size)) for step in steps],
        ("vocab", near),
    )

    def spread(c, origin, sems, slot, to):
        place = out_ref.at[c, origin]
        return push(place, place, sems, slot, "vocab", to)

    arriving = [
        [
            push(x_refs[c].at[to], parts_ref.at[c, me], (s0, r0), (step - 1) * chunks + c, "dp", to)
            for step, to, _ in owners
        ]
        for c in range(chunks)
    ]

    def half_of(ref):
        rows = ref.shape[1] // 2
        return pl.ds(pl.multiple_of(lax.rem(here, 2) * rows, rows), rows)

    swaps = [
        [
            push(
                rows_ref.at[to, half_of(rows_ref)],
                swapped_ref.at[me, half_of(rows_ref)],
                (s3, r3),
                k * len(owners) + step - 1,
                "dp",
                to,
            )
            for step, to, _ in owners
        ]
        for k, (rows_ref, swapped_ref) in enumerate(zip(rows_refs, swapped_refs))
    ]
    for rows_ref, swapped_ref in zip(rows_refs, swapped_refs):
        swapped_ref[me] = rows_ref[me]
    far, close = [], []
    square = jnp.zeros(square_ref.shape, jnp.float32)
    for c in range(chunks):
        parts_ref[c, me] = x_refs[c][me]
        for copy in arriving[c]:
            copy.wait()
        total = jnp.sum(parts_ref[c].astype(jnp.float32), axis=0)
        out_ref[c, here] = total.astype(out_ref.dtype)
        square = square + jnp.sum(total * total, axis=0, keepdims=True)
        far.append(
            [
                spread(c, here, (s1, r1), k * chunks + c, lax.rem(here + step, size))
                for k, step in enumerate(steps)
            ]
        )
        close.append(spread(c, here, (s2, r2), c, near))
    square_ref[...] = square
    moved = []
    for k, swapped_ref in enumerate(swapped_refs):
        for copy, (step, _, origin) in zip(swaps[k], owners):
            copy.wait()
            place = swapped_ref.at[origin, half_of(swapped_ref)]
            moved.append(push(place, place, (s4, r4), k * len(owners) + step - 1, "vocab", near))
    for copy in moved:
        copy.wait()
    if inside:
        sum_tokens(
            swapped_refs[:2], place_ref, left_ref, table_ref, wide_ref, embed_ref, embed_square_ref
        )
    for c in range(chunks):
        for k, step in enumerate(steps):
            far[c][k].wait()
            origin = lax.rem(here + size - step, size)
            close.append(spread(c, origin, (s2, r2), (k + 1) * chunks + c, near))
    for copy in close:
        copy.wait()


def share_gradients(blocks, rows, collective_id, before, tokens):
    owners, replicas = lax.axis_size("dp"), lax.axis_size("vocab")
    chunks = len(blocks)
    others = (replicas // 2 - 1) * chunks
    shape, kind = blocks[0].shape, blocks[0].dtype
    return talk(
        partial(gradient_kernel, chunks, len(rows), bool(tokens)),
        (
            jax.ShapeDtypeStruct((chunks, replicas, *shape[1:]), kind),
            full(1, shape[2]),
            *[jax.ShapeDtypeStruct(part.shape, part.dtype) for part in rows],
            *[full(*size) for part in tokens[2:] for size in (part.shape, (1, part.shape[1]))],
        ),
        collective_id,
        *blocks,
        *rows,
        *tokens,
        scratch=[pltpu.VMEM((chunks, *shape), kind)]
        + sem_pair((owners - 1) * chunks)
        + sem_pair(others)
        + sem_pair(others + chunks)
        + sem_pair(len(rows) * (owners - 1))
        + sem_pair(len(rows) * (owners - 1))
        + [pltpu.VMEM((part.shape[1], 2 * tokens[2].shape[1]), jnp.bfloat16) for part in tokens[:1]],
        microseconds=40,
        before=before,
    )


def swap_kernel(scale, x_ref, place_ref, sum_ref, out_ref, s0, r0, s1, r1):
    others = peers_of("dp")
    me, here = lax.axis_index("dp"), lax.axis_index("vocab")
    near, side = flip(here, 1), lax.rem(here, 2)
    greet(*[("dp", to) for _, to, _ in others], ("vocab", near))
    rows = x_ref.shape[1] // 2
    half = pl.ds(pl.multiple_of(side * rows, rows), rows)
    copies = [
        push(x_ref.at[to, half], out_ref.at[me, half], (s0, r0), step - 1, "dp", to)
        for step, to, _ in others
    ]
    out_ref[me] = x_ref[me]
    close = []
    for copy, (step, _, origin) in zip(copies, others):
        copy.wait()
        place = out_ref.at[origin, half]
        close.append(push(place, place, (s1, r1), step - 1, "vocab", near))
    for copy in close:
        copy.wait()
    columns = out_ref.shape[2]
    for owner in range(out_ref.shape[0]):
        band = slice(owner * columns, (owner + 1) * columns)
        sum_ref[:, band] = out_ref[owner].astype(jnp.float32) * scale + place_ref[:, band]


def swap_owners(x, places, scale, collective_id, before):
    owners = lax.axis_size("dp")
    return talk(
        partial(swap_kernel, scale),
        full(*places.shape),
        collective_id,
        x,
        places,
        scratch=[pltpu.VMEM(x.shape, x.dtype)]
        + sem_pair(owners - 1) + sem_pair(owners - 1),
        before=before,
    )


def token_kernel(
    scale, inside, x_ref, place_ref, attn_ref, ffn_ref, code_ref, paired_ref, out_ref, attn_out_ref, ffn_out_ref,
    found_ref, near_ref, parts_ref, blocks_ref, row_ref,
    s0, r0, s1, r1, s2, r2, s3, r3, s4, r4, s5, r5, s6, r6,
):
    owners, others = peers_of("dp"), far_replicas()
    me, here = lax.axis_index("dp"), lax.axis_index("vocab")
    near, side = flip(here, 1), lax.rem(here, 2)
    greet(
        *[("dp", to) for _, to, _ in owners], *[("vocab", to) for _, to, _ in others], ("vocab", near)
    )
    count, length, columns = x_ref.shape
    half, pairs = length // 2, lax.axis_size("vocab") // 2
    share = half // pairs

    def half_of(which):
        return pl.ds(pl.multiple_of(which * half, half), half)

    def share_of(index):
        return pl.ds(pl.multiple_of(index // 2 * share, share), share)

    def place_of(index):
        return pl.ds(pl.multiple_of(side * half + index // 2 * share, share), share)

    def send_weights(ref, own_ref, slot, span):
        count, rows = own_ref.shape[0] // 2, own_ref.shape[1]
        mine = pl.ds(side * count, count)

        def place(origin):
            return ref.at[mine, pl.ds(pl.multiple_of(origin * rows + span[0], span[1]), span[1])]

        copies = [
            push(own_ref.at[mine, pl.ds(*span)], place(me), (s5, r5), slot + step - 1, "dp", to)
            for step, to, _ in owners
        ]
        return [(copy, place(origin), slot + step - 1) for copy, (step, _, origin) in zip(copies, owners)]

    def relay_weights(sent):
        relays = []
        for copy, place, slot in sent:
            copy.wait()
            relays.append(push(place, place, (s6, r6), slot, "vocab", near))
        return relays

    first = push(x_ref.at[:, half_of(1 - side)], near_ref, (s0, r0), 0, "vocab", near)
    some = ffn_ref.shape[1] // 2
    early = send_weights(attn_out_ref, attn_ref, 0, (0, attn_ref.shape[1]))
    early += send_weights(ffn_out_ref, ffn_ref, len(owners), (0, some))
    for ref, own_ref in ((attn_out_ref, attn_ref), (ffn_out_ref, ffn_ref)):
        rows = own_ref.shape[1]
        ref[:, pl.ds(pl.multiple_of(me * rows, rows), rows), :] = own_ref[...]
    first.wait()
    near_ref[...] += x_ref[:, half_of(side)]
    copies = [
        push(near_ref.at[:, share_of(to)], parts_ref.at[slot], (s1, r1), slot, "vocab", to)
        for slot, to, _ in others
    ]
    if inside:
        look_up_tokens(code_ref, paired_ref, found_ref)
    else:
        found_ref[...] = jnp.zeros(found_ref.shape, found_ref.dtype)
    for copy in copies:
        copy.wait()
    total = near_ref[:, share_of(here)]
    for slot, _, _ in others:
        total = total + parts_ref[slot]
    blocks_ref[...] = total
    copies = [
        push(
            blocks_ref.at[to],
            row_ref.at[me, place_of(here)],
            (s2, r2),
            step - 1,
            "dp",
            to,
        )
        for step, to, _ in owners
    ]
    row_ref[me, place_of(here)] = blocks_ref[me]
    for copy in copies:
        copy.wait()
    late = send_weights(ffn_out_ref, ffn_ref, 2 * len(owners), (some, some))
    mine = row_ref.at[:, place_of(here)]
    copies = [push(mine, mine, (s3, r3), slot, "vocab", to) for slot, to, _ in others]
    close = [push(mine, mine, (s4, r4), 0, "vocab", near)]
    for copy, (slot, _, origin) in zip(copies, others):
        copy.wait()
        theirs = row_ref.at[:, place_of(origin)]
        close.append(push(theirs, theirs, (s4, r4), slot + 1, "vocab", near))
    close += relay_weights(early)
    for copy in close[: pairs]:
        copy.wait()
    for owner in range(count):
        band = slice(owner * columns, (owner + 1) * columns)
        out_ref[:, band] = row_ref[owner].astype(jnp.float32) * scale + place_ref[:, band]
    close += relay_weights(late)
    for copy in close[pairs:]:
        copy.wait()


def gather_tokens(x, places, attn, ffn, codes, paired, scale, collective_id):
    owners, pairs = lax.axis_size("dp"), lax.axis_size("vocab") // 2
    _, length, columns = x.shape
    half = length // 2
    width = owners * columns
    whole = [low(w.shape[0], owners * w.shape[1], width) for w in (attn, ffn)]
    return talk(
        partial(token_kernel, scale, paired is not None),
        (full(length, width), *whole, low(codes.shape[0], columns)),
        collective_id,
        x,
        places,
        attn,
        ffn,
        codes,
        attn[0] if paired is None else paired,
        scratch=[
            pltpu.VMEM((owners, half, columns), x.dtype),
            pltpu.VMEM((pairs - 1, owners, half // pairs, columns), x.dtype),
            pltpu.VMEM((owners, half // pairs, columns), x.dtype),
            pltpu.VMEM((owners, length, columns), x.dtype),
        ]
        + sem_pair(1)
        + sem_pair(pairs - 1)
        + sem_pair(owners - 1)
        + sem_pair(pairs - 1)
        + sem_pair(pairs)
        + sem_pair(3 * owners - 3)
        + sem_pair(3 * owners - 3),
        microseconds=50,
    )


def sinusoid(length, model_width):
    places = np.arange(length, dtype=np.float32)[:, None]
    halves = np.arange(model_width // 2, dtype=np.float32)[None, :]
    angles = places * np.exp(halves * np.float32(-2.0 * math.log(10000.0) / model_width))
    angles = angles.astype(np.float64)
    return (
        np.stack([np.sin(angles), np.cos(angles)], axis=-1)
        .reshape(length, model_width)
        .astype(np.float32)
    )


def one_hot(ids, columns):
    return (ids[:, None] == columns[None, :]).astype(jnp.bfloat16)


def pick_weights(target_seg, pick_rows):
    sentence = jnp.take(target_seg, pick_rows, axis=0)
    return jnp.sum((sentence[:, None] == sentence[None, :]).astype(jnp.float32), axis=1)


def adam_direction(moment, second):
    return moment / (1.0 - beta_one**STEP) / (jnp.sqrt(second / (1.0 - beta_two**STEP)) + adam_eps)


def adam_update(weight, grad_item, moment, second, step_rate, decay_weight):
    moment = beta_one * moment + (1.0 - beta_one) * grad_item
    second = beta_two * second + (1.0 - beta_two) * grad_item * grad_item
    return (
        weight - step_rate * (adam_direction(moment, second) + decay_weight * weight),
        moment,
        second,
    )


def body(
    src_ids,
    src_seg,
    tgt_ids,
    tgt_seg,
    pick_pos,
    pick_label,
    attn_w,
    attn_m,
    attn_v,
    ffn_w,
    ffn_m,
    ffn_v,
    soap_basis,
    soap_stats,
    norm_p,
    norm_m,
    norm_v,
    embedding,
    embed_m,
    embed_v,
):
    owners, replicas = lax.axis_size("dp"), lax.axis_size("vocab")
    replica = lax.axis_index("vocab")
    own_table = embedding.astype(jnp.bfloat16)
    own_norms = jnp.pad(norm_p.astype(jnp.bfloat16).astype(jnp.float32), ((0, 2), (0, 0)))
    all_ids, norm_rows = gather_small("dp", 1, jnp.concatenate([src_ids, tgt_ids]), own_norms)
    norm_rows = jnp.swapaxes(norm_rows, 0, 1).reshape(16, -1)
    norms = [jnp.stack([norm_rows[k], norm_rows[7 + k]]) for k in range(7)]
    vocab_count, width = embedding.shape[0], attn_w.shape[2]
    source, source_seg, target, target_seg = (src_ids[0], src_seg[0], tgt_ids[0], tgt_seg[0])
    pick_rows, labels = (pick_pos[0], pick_label[0])
    length = source.shape[0]
    embed_scale = math.sqrt(width)
    half = vocab_count // 2
    halves = jnp.arange(half)
    paired = jnp.concatenate([own_table[:half], own_table[half:]], axis=1)

    def paired_places(ids):
        place = ids - replica * vocab_count
        inside = (place >= 0) & (place < vocab_count)
        return jnp.where(inside, place % half, -1), place < half

    def look_up(ids):
        place, left = paired_places(ids)
        wide = lax.dot_general(one_hot(place, halves), paired, (((1,), (0,)), ((), ())))
        return jnp.where(left[:, None], wide[:, :paired.shape[1] // 2], wide[:, paired.shape[1] // 2 :])

    if owners == 4:
        place, left = paired_places(jnp.swapaxes(all_ids, 0, 1).reshape(2, -1, 1))
        all_codes = jnp.where(place < 0, -1, 2 * place + left.astype(jnp.int32))
        codes = all_codes[1]
        whole_paired = jnp.pad(paired, ((0, -half % 128), (0, 0)))
        source_part = call(
            look_up_tokens, low(codes.shape[0], width // owners), all_codes[0], whole_paired
        )
    else:
        source_part = look_up(all_ids[:, 0].reshape(-1))
        codes, whole_paired = jnp.zeros((16, 1), jnp.int32), None
    positional = sinusoid(length, width)
    enc_in, enc_attn_w, enc_ffn_w, target_part = gather_tokens(
        source_part.reshape(owners, length, -1),
        positional,
        attn_w[0:4].astype(jnp.bfloat16),
        ffn_w[0:2].astype(jnp.bfloat16),
        codes,
        whole_paired,
        embed_scale,
        2,
    )
    if owners != 4:
        target_part = look_up(all_ids[:, 1].reshape(-1))
    target_sum = lax.psum(target_part, "vocab")
    enc_mid, enc_attn = attn_forward(
        enc_in, norms[0], ((enc_attn_w,), 0, 0), source_seg, source_seg, None, False
    )
    self_w, cross_w, dec_ffn_w, ready = late_weights(attn_w[4:], ffn_w[2:], enc_in, enc_mid)
    enc_out, encoded, enc_ffn = ffn_forward(enc_mid, norms[1], norms[2], ((enc_ffn_w,), 0, 0))
    weight = 1.0 / pick_weights(target_seg, pick_rows)
    picks = share_selector(width, owners, replicas, replica, width)
    hidden = ffn_w.shape[1] * owners
    hidden_picks = share_selector(hidden, owners, replicas, replica, 512)
    place, left = paired_places(all_ids.reshape(-1))
    tokens = ()
    if owners == 4:
        ones = jnp.broadcast_to(left[:, None], (left.shape[0], width // owners))
        tokens = (place[None, :], ones.astype(jnp.bfloat16))
    dec_in = swap_owners(
        target_sum.reshape(owners, length, -1),
        positional,
        embed_scale,
        3,
        (enc_out, weight, picks, hidden_picks, *tokens),
    )
    table_low = lax.all_gather(follow(own_table, ready, dec_in), "dp", axis=1, tiled=True)
    dec_mid, dec_self = attn_forward(
        dec_in, norms[3], self_w, target_seg, target_seg, None, True
    )
    dec_late, dec_cross = attn_forward(
        dec_mid, norms[4], cross_w, target_seg, source_seg, encoded, False
    )
    dec_out, final_low, dec_ffn = ffn_forward(dec_late, norms[5], norms[6], dec_ffn_w)

    own_labels = labels - replica * vocab_count
    picked, own_stats = loss_forward(final_low, pick_rows, own_labels, table_low)
    (seen,) = gather_small("vocab", 4, own_stats)
    grad_picked, table_parts, losses = loss_backward(
        picked, seen, weight, own_labels, table_low, owners
    )
    grad_table = lax.psum_scatter(table_parts, "dp", scatter_dimension=0, tiled=False)
    grad_picked = sum_vocab(grad_picked, 5)
    loss_part = jnp.sum(losses)
    count_part = (target_seg[-1] + 1).astype(jnp.float32)

    norm_grads = [None] * 7
    grad, norm_grads[6], norm_grads[5], *ffn_blocks = ffn_backward(
        grad_picked, dec_ffn, hidden_picks, owners, places=pick_rows
    )
    grad, norm_grads[4], block, grad_encoded = attn_backward(grad, dec_cross, picks, owners, None)
    early = lax.psum_scatter(
        jnp.concatenate([block, *ffn_blocks], axis=1), "dp", scatter_dimension=0, tiled=False
    )
    grad, norm_grads[3], self_block, target_rows = attn_backward(
        grad, dec_self, picks, owners, embed_scale
    )
    grad, norm_grads[2], norm_grads[1], *ffn_blocks = ffn_backward(
        grad_encoded, enc_ffn, hidden_picks, owners, before=(grad_table, grad)
    )
    early_sum, early_squares = follow_with_squares(early, grad)
    early = lax.all_gather(early_sum, "vocab")
    grad, norm_grads[0], block, source_rows = attn_backward(
        grad, enc_attn, picks, owners, embed_scale, before=(early_sum,)
    )
    norm_grad = norm_blocks(norm_grads, owners, early)
    late, layer_squares, source_rows, target_rows, norm_grad, *found = share_gradients(
        [block, self_block, *ffn_blocks], [source_rows, target_rows, norm_grad], 7, (early,), (*tokens, *[grad_table][: len(tokens)])
    )
    g_norm = jnp.sum(norm_grad, axis=0)[:14]
    if owners == 4:
        g_embed, embed_squares = found
    else:
        token_grads = jnp.concatenate([source_rows, target_rows], axis=1).reshape(
            owners * 2 * length, -1
        )
        left = left[:, None]
        token_grads = jnp.concatenate(
            [jnp.where(left, token_grads, 0), jnp.where(left, 0, token_grads)], axis=1
        )
        g_paired = dot_dims(one_hot(place, halves), token_grads, 0, 0)
        g_embed = grad_table.astype(jnp.float32) + jnp.concatenate(
            jnp.split(g_paired, 2, axis=1), axis=0
        )
        embed_squares = g_embed * g_embed

    def by_matrix(shared, count):
        blocks = jnp.swapaxes(shared.reshape(replicas, count, -1, width), 0, 1)
        return blocks.reshape(count, -1, width)

    early = by_matrix(early, 3)
    g_attn = [by_matrix(part, 4) for part in (late[0], late[1], early[0])]
    g_attn = jnp.concatenate(g_attn)
    g_ffn = jnp.concatenate([late[2:].reshape(2, -1, width), early[1:]])

    matrix = replica // 2
    own_grad = lax.dynamic_index_in_dim(g_ffn, matrix, 0, keepdims=False)
    own_products = dot_dims(own_grad, own_grad, 0, 0)
    first_copy = (replica == 0).astype(jnp.float32)
    raw_squares = (
        jnp.sum(layer_squares)
        + jnp.sum(early_squares)
        + jnp.sum(embed_squares)
        + first_copy * jnp.sum(g_norm * g_norm)
    )
    few = jnp.stack([first_copy * loss_part, first_copy * count_part, raw_squares])
    few = jnp.broadcast_to(jnp.pad(few, (0, 5))[:, None], (8, 128))
    own_products, few = sum_tail(own_products, few, 8)
    loss_sum, sentences, squares = few[0, 0], few[1, 0], few[2, 0]
    grad_norm = jnp.sqrt(squares) / sentences
    factor = jnp.minimum(1.0, clip_limit / (grad_norm + norm_eps)) / sentences
    g_norm = g_norm * factor

    rows = width // 2
    own_half = lax.dynamic_slice_in_dim(own_products.astype(jnp.bfloat16), replica % 2 * rows, rows, 0)
    all_products = lax.all_gather(own_half, "vocab").reshape(4, width, width)
    weight_new = (1.0 - stat_decay) * (factor * factor)
    own_basis = renew_basis(own_products, soap_stats, soap_basis, weight_new)
    own_basis = follow(own_basis, all_products)
    new_basis = lax.all_gather(own_basis, "vocab").reshape(4, width, width).astype(jnp.float32)
    new_stats = stat_decay * soap_stats + weight_new * all_products.astype(jnp.float32)

    new_norm, m_norm, v_norm = adam_update(norm_p, g_norm, norm_m, norm_v, rate_vector, 0.0)
    updated = update_matrices(
        factor,
        soap_basis,
        (g_attn, attn_w, attn_m, attn_v),
        (g_embed, embedding, embed_m, embed_v),
        (g_ffn, ffn_w, ffn_m, ffn_v),
    )
    new_attn, m_attn, v_attn, new_embed, m_embed, v_embed, new_ffn, m_ffn, v_ffn = updated
    return (
        loss_sum,
        sentences,
        grad_norm,
        new_attn,
        m_attn,
        v_attn,
        new_ffn,
        m_ffn,
        v_ffn,
        new_basis,
        new_stats,
        new_norm,
        m_norm,
        v_norm,
        new_embed,
        m_embed,
        v_embed,
    )


def solution(mesh):
    placed = (
        P("dp", None),
        P("dp", None),
        P("dp", None),
        P("dp", None),
        P("dp", None),
        P("dp", None),
        P(None, "dp", None),
        P(None, "dp", None),
        P(None, "dp", None),
        P(None, "dp", None),
        P(None, "dp", None),
        P(None, "dp", None),
        P(),
        P(),
        P(None, "dp"),
        P(None, "dp"),
        P(None, "dp"),
        P("vocab", "dp"),
        P("vocab", "dp"),
        P("vocab", "dp"),
    )
    return jax.shard_map(
        body,
        mesh=mesh,
        in_specs=placed,
        out_specs=(
            P(),
            P(),
            P(),
            P(None, "dp", None),
            P(None, "dp", None),
            P(None, "dp", None),
            P(None, "dp", None),
            P(None, "dp", None),
            P(None, "dp", None),
            P(),
            P(),
            P(None, "dp"),
            P(None, "dp"),
            P(None, "dp"),
            P("vocab", "dp"),
            P("vocab", "dp"),
            P("vocab", "dp"),
        ),
        check_vma=False,
    )
```

```python
from functools import partial
import math

import jax
import jax.numpy as jnp
import numpy as np
from jax import lax
from jax.experimental import pallas as pl
from jax.experimental.pallas import tpu as pltpu
from jax.sharding import PartitionSpec as P

HEADS = 8
STEP = 10
TILE = 128

highest = lax.Precision.HIGHEST
beta_one = 0.9
beta_two = 0.999
adam_eps = 1e-08
decay_rate = 0.01
rate_matrix = 0.03
rate_vector = 0.3
clip_limit = 1.0
stat_decay = 0.95
norm_eps = 1e-06
masked = -1e30
log_two_e = math.log2(math.e)
vmem = pl.BlockSpec(memory_space=pltpu.VMEM)
smem = pl.BlockSpec(memory_space=pltpu.SMEM)
mesh_ids = pl.DeviceIdType.MESH


def dot_dims(left, right, left_dim, right_dim):
    return lax.dot_general(
        left, right, (((left_dim,), (right_dim,)), ((), ())), preferred_element_type=jnp.float32
    )


def dot_exact(left, right, left_dim, right_dim):
    return lax.dot_general(
        left,
        right,
        (((left_dim,), (right_dim,)), ((), ())),
        precision=highest,
        preferred_element_type=jnp.float32,
    )


def cost_of(microseconds):
    return pl.CostEstimate(flops=microseconds * 10**9, bytes_accessed=0, transcendentals=0)


def call(kernel, outs, *args, scratch=(), smem_args=0, microseconds=5, before=(), far=()):
    any_spec = pl.BlockSpec(memory_space=pl.ANY)
    specs = [vmem] * (len(args) - smem_args) + [smem] * smem_args + [any_spec] * len(before)
    for k in far:
        specs[k] = any_spec

    def body(*refs):
        kernel(*refs[: len(args)], *refs[len(args) + len(before) :])

    return pl.pallas_call(
        body,
        out_shape=outs,
        in_specs=specs,
        out_specs=jax.tree.map(lambda _: vmem, outs),
        scratch_shapes=list(scratch),
        compiler_params=pltpu.CompilerParams(vmem_limit_bytes=56 * 2**20),
        cost_estimate=cost_of(microseconds),
    )(*args, *before)


def low(*shape):
    return jax.ShapeDtypeStruct(shape, jnp.bfloat16)


def full(*shape):
    return jax.ShapeDtypeStruct(shape, jnp.float32)


def norm_parts(values):
    centre = values - jnp.mean(values, axis=-1, keepdims=True)
    spread = jnp.mean(centre * centre, axis=-1, keepdims=True)
    root = lax.rsqrt(spread + norm_eps)
    return centre * root, root


def norm_forward(values, ln_ref):
    return norm_parts(values)[0] * ln_ref[0:1, :] + ln_ref[1:2, :]


def norm_backward(grad, values, ln_ref, ln_grad_ref):
    normed, root = norm_parts(values)
    ln_grad_ref[0:1, :] = jnp.sum(grad * normed, axis=0, keepdims=True)
    ln_grad_ref[1:2, :] = jnp.sum(grad, axis=0, keepdims=True)
    inner = grad * ln_ref[0:1, :]
    return root * (
        inner
        - jnp.mean(inner, axis=-1, keepdims=True)
        - normed * jnp.mean(inner * normed, axis=-1, keepdims=True)
    )


def at_tile(index, size):
    return pl.ds(pl.multiple_of(index * size, size), size)


def tile_mask(segq_ref, segk_ref, qi, ki, tile_q, tile_k, causal):
    seg_k = segk_ref[at_tile(ki, tile_k), :]
    seg_k = jnp.concatenate([seg_k] * (tile_q // TILE), axis=1)
    allowed = seg_k == segq_ref[:, at_tile(qi, tile_q)]
    if causal:
        shape = (tile_k, tile_q)
        ahead = lax.broadcasted_iota(jnp.int32, shape, 0) - lax.broadcasted_iota(
            jnp.int32, shape, 1
        )
        allowed = allowed & (ahead <= qi * tile_q - ki * tile_k)
    return allowed


def for_tiles(length, tile_q, tile_k, edge_ref, causal, step):
    count_q, count_k = length // tile_q, length // tile_k
    per_q, per_k = tile_q // TILE, tile_k // TILE

    def one(pair, carry):
        qi, ki = pair // count_k, lax.rem(pair, count_k)
        live = (edge_ref[0, qi * per_q] <= edge_ref[3, (ki + 1) * per_k - 1]) & (
            edge_ref[2, ki * per_k] <= edge_ref[1, (qi + 1) * per_q - 1]
        )
        if causal:
            live = live & (ki * tile_k < (qi + 1) * tile_q)

        @pl.when(live)
        def _():
            step(qi, ki)

        return carry

    lax.fori_loop(0, count_q * count_k, one, 0)


def tile_edges(seg_q, seg_k):
    last = TILE - 1
    return jnp.stack([seg_q[::TILE], seg_q[last::TILE], seg_k[::TILE], seg_k[last::TILE]])


def share_selector(rows, owners, shares, share, count):
    size = rows // (owners * shares)
    index = jnp.arange(count // shares)
    picked = index // size * (rows // owners) + share * size + index % size
    return (picked[:, None] == jnp.arange(count)[None, :]).astype(jnp.bfloat16)


def load_weights(w_ref, piece_refs, part, first, sems):
    if len(piece_refs) == 1:
        copies = [pltpu.make_async_copy(piece_refs[0], w_ref, sems.at[0])]
        copies[0].start()
        return copies
    own = piece_refs[0]
    matrices, rows = w_ref.shape[0], w_ref.shape[1] // 4
    half = own.shape[0] // 2
    me, side = lax.axis_index("dp"), lax.rem(lax.axis_index("vocab"), 2)
    copies = []
    for m in range(matrices):
        which = m if part is None else part
        start = first if part is None else first + m * rows

        def copy_from(ref, offset, owner, slot):
            place = pl.ds(pl.multiple_of(owner * rows, rows), rows)
            return pltpu.make_async_copy(
                ref.at[pl.ds(offset + start, rows)], w_ref.at[m, place], sems.at[slot]
            )

        copies.append(copy_from(own, which * half, me, 4 * m))
        copies[-1].start()
        for k in range(1, 4):
            mine, theirs = (copy_from(piece_refs[n], 0, me ^ k, 4 * m + k) for n in (k, k + 3))

            @pl.when(side == which)
            def _():
                mine.start()

            @pl.when(side != which)
            def _():
                theirs.start()

            copies.append(mine)
    return copies


def flip_sites(part, axis, bit):
    return lax.ppermute(part, axis, [(s, s ^ bit) for s in range(lax.axis_size(axis))])


def late_weights(attn, ffn, after, later):
    owners = lax.axis_size("dp")
    width = attn.shape[-1]
    attn, ffn = attn.astype(jnp.bfloat16), ffn.astype(jnp.bfloat16)
    if owners != 4:
        attn, ffn = (lax.all_gather(part, "dp", axis=1, tiled=True) for part in (attn, ffn))
        return ((attn[:4],), 0, 0), ((attn[4:],), 0, 0), ((ffn,), 0, 0), ffn
    halves = [
        jnp.concatenate([attn[4 * k : 4 * k + 4].reshape(-1, width), ffn[k]]) for k in range(2)
    ]
    own = jnp.concatenate(halves)
    side = lax.axis_index("vocab") % 2
    mine = jnp.where(side == 0, halves[0], halves[1])
    mine, _ = lax.optimization_barrier((mine, after))
    got = [flip_sites(mine, "dp", k) for k in range(1, 4)]
    *got, _ = lax.optimization_barrier((*got, later))
    swapped = [flip_sites(part, "vocab", 1) for part in got]
    pieces = (own, *got, *swapped)
    rows = 4 * attn.shape[1]
    return (pieces, 0, 0), (pieces, 1, 0), (pieces, None, rows), swapped[-1]


def attn_forward_kernel(causal, cross, pieces, part, first, *refs):
    refs = list(refs)
    x_ref, ln_ref, segq_ref, segk_ref = refs[:4]
    refs = refs[4:]
    key_ref = refs.pop(0) if cross else None
    piece_refs, refs = refs[:pieces], refs[pieces:]
    edge_ref, out_ref, a_ref, qt_ref, kt_ref, vt_ref, ot_ref, lse_ref = refs[:8]
    refs = refs[8:]
    w_ref, top_ref, sum_ref, acc_ref, sems = refs
    weights = load_weights(w_ref, piece_refs, part, first, sems)
    length, width = x_ref.shape
    head_size = width // HEADS
    a_ref[...] = norm_forward(x_ref[...], ln_ref).astype(jnp.bfloat16)
    key_in = key_ref if cross else a_ref
    for copy in weights:
        copy.wait()
    qt_ref[...] = dot_dims(a_ref[...], w_ref[0], 1, 0).astype(jnp.bfloat16).T
    kt_ref[...] = dot_dims(key_in[...], w_ref[1], 1, 0).astype(jnp.bfloat16).T
    vt_ref[...] = dot_dims(key_in[...], w_ref[2], 1, 0).astype(jnp.bfloat16).T
    top_ref[...] = jnp.full(top_ref.shape, masked, jnp.float32)
    sum_ref[...] = jnp.zeros(sum_ref.shape, jnp.float32)
    acc_ref[...] = jnp.zeros(acc_ref.shape, jnp.float32)
    scale = log_two_e / math.sqrt(head_size)
    bands = [slice(h * head_size, (h + 1) * head_size) for h in range(HEADS)]

    def step(qi, ki):
        q_at, k_at = at_tile(qi, 256), at_tile(ki, 256)
        allowed = tile_mask(segq_ref, segk_ref, qi, ki, 256, 256, causal)
        scores = [dot_dims(kt_ref[band, k_at], qt_ref[band, q_at], 0, 0) * scale for band in bands]
        scores = [jnp.where(allowed, part, masked) for part in scores]
        top = top_ref[:, q_at]
        new_top = jnp.maximum(
            top,
            jnp.concatenate([jnp.max(part, axis=0, keepdims=True) for part in scores], axis=0),
        )
        fade = jnp.exp2(top - new_top)
        parts = [jnp.exp2(scores[h] - new_top[h : h + 1]) for h in range(HEADS)]
        top_ref[:, q_at] = new_top
        sum_ref[:, q_at] = sum_ref[:, q_at] * fade + jnp.concatenate(
            [jnp.sum(part, axis=0, keepdims=True) for part in parts], axis=0
        )
        mixed = [
            dot_dims(vt_ref[bands[h], k_at], parts[h].astype(jnp.bfloat16), 1, 0)
            for h in range(HEADS)
        ]
        acc = acc_ref[:, q_at]
        acc_ref[:, q_at] = jnp.concatenate(
            [acc[bands[h]] * fade[h : h + 1] + mixed[h] for h in range(HEADS)], axis=0
        )

    for_tiles(length, 256, 256, edge_ref, causal, step)
    lse_ref[...] = top_ref[...] + jnp.log2(sum_ref[...])
    for h in range(HEADS):
        ot_ref[bands[h], :] = (acc_ref[bands[h], :] / sum_ref[h : h + 1, :]).astype(jnp.bfloat16)
    out_ref[...] = x_ref[...] + dot_dims(ot_ref[...], w_ref[3], 0, 0)


def attn_forward(x, ln, weights, seg_q, seg_k, key_in, causal):
    length, width = x.shape
    weights, part, first = weights
    cross = key_in is not None
    segs = (seg_q[None, :], jnp.broadcast_to(seg_k[:, None], (length, TILE)))
    edges = tile_edges(seg_q, seg_k)
    args = (x, ln, *segs) + ((key_in,) if cross else ()) + (*weights, edges)
    outs = (full(length, width), low(length, width)) + (low(width, length),) * 4
    outs = outs + (full(HEADS, length),)
    if len(weights) > 1:
        outs = outs + (low(4, width, width),)
    out, normed, *stored = call(
        partial(attn_forward_kernel, causal, cross, len(weights), part, first),
        outs,
        *args,
        scratch=[pltpu.VMEM((4, width, width), jnp.bfloat16)][: len(weights) == 1]
        + [
            pltpu.VMEM((HEADS, length), jnp.float32),
            pltpu.VMEM((HEADS, length), jnp.float32),
            pltpu.VMEM((width, length), jnp.float32),
            pltpu.SemaphoreType.DMA((16,)),
        ],
        smem_args=1,
        microseconds=20,
        far=range(len(args) - 1 - len(weights), len(args) - 1),
    )
    whole = stored.pop() if len(weights) > 1 else weights[0]
    return out, (x, ln, whole, segs, edges, causal, key_in, normed, stored)


def attn_backward_kernel(causal, cross, row_scale, *refs):
    g_ref, x_ref, ln_ref, w_ref, pick_ref, segq_ref, segk_ref, a_ref = refs[:8]
    refs = list(refs[8:])
    key_ref = refs.pop(0) if cross else a_ref
    qt_ref, kt_ref, vt_ref, ot_ref, lse_ref, edge_ref, out_ref, ln_grad_ref, block_ref, extra_ref = refs[:10]
    low_ref, gq_ref, gk_ref, gv_ref, got_ref, delta_ref, gqt_ref, gkt_ref, gvt_ref = refs[10:]
    length, width = x_ref.shape
    head_size = width // HEADS
    low_ref[...] = g_ref[...].astype(jnp.bfloat16)
    got_ref[...] = dot_dims(low_ref[...], w_ref[3], 1, 1).astype(jnp.bfloat16).T
    bands = [slice(h * head_size, (h + 1) * head_size) for h in range(HEADS)]
    for h in range(HEADS):
        delta_ref[h : h + 1, :] = jnp.sum(
            got_ref[bands[h], :].astype(jnp.float32) * ot_ref[bands[h], :].astype(jnp.float32),
            axis=0,
            keepdims=True,
        )
    for ref in (gqt_ref, gkt_ref, gvt_ref):
        ref[...] = jnp.zeros(ref.shape, jnp.float32)
    scale = log_two_e / math.sqrt(head_size)
    back = 1.0 / math.sqrt(head_size)

    def step(qi, ki):
        q_at, k_at = at_tile(qi, 256), at_tile(ki, TILE)
        allowed = tile_mask(segq_ref, segk_ref, qi, ki, 256, TILE, causal)
        scores = [dot_dims(kt_ref[band, k_at], qt_ref[band, q_at], 0, 0) for band in bands]
        grads = [dot_dims(vt_ref[band, k_at], got_ref[band, q_at], 0, 0) for band in bands]
        parts = [
            jnp.where(allowed, jnp.exp2(scores[h] * scale - lse_ref[h : h + 1, q_at]), 0.0)
            for h in range(HEADS)
        ]
        grads = [parts[h] * (grads[h] - delta_ref[h : h + 1, q_at]) for h in range(HEADS)]
        parts_t = [part.T.astype(jnp.bfloat16) for part in parts]
        grads_t = [part.T.astype(jnp.bfloat16) for part in grads]
        grads = [part.astype(jnp.bfloat16) for part in grads]
        for ref, place, terms in (
            (gvt_ref, k_at, [dot_dims(got_ref[bands[h], q_at], parts_t[h], 1, 0) for h in range(HEADS)]),
            (gkt_ref, k_at, [dot_dims(qt_ref[bands[h], q_at], grads_t[h], 1, 0) for h in range(HEADS)]),
            (gqt_ref, q_at, [dot_dims(kt_ref[bands[h], k_at], grads[h], 1, 0) for h in range(HEADS)]),
        ):
            ref[:, place] += jnp.concatenate(terms, axis=0)

    for_tiles(length, 256, TILE, edge_ref, causal, step)
    gq_ref[...] = (gqt_ref[...] * back).astype(jnp.bfloat16).T
    gk_ref[...] = (gkt_ref[...] * back).astype(jnp.bfloat16).T
    gv_ref[...] = gvt_ref[...].astype(jnp.bfloat16).T
    from_query = dot_dims(gq_ref[...], w_ref[0], 1, 1)
    from_keys = dot_dims(gk_ref[...], w_ref[1], 1, 1) + dot_dims(gv_ref[...], w_ref[2], 1, 1)
    if cross:
        extra_ref[...] = from_keys
    else:
        from_query = from_query + from_keys
    total = g_ref[...] + norm_backward(from_query, x_ref[...], ln_ref, ln_grad_ref)
    out_ref[...] = total
    owners = block_ref.shape[0]
    if not cross:
        columns = width // owners
        for owner in range(owners):
            band = slice(owner * columns, (owner + 1) * columns)
            extra_ref[owner] = (total[:, band] * row_scale).astype(jnp.bfloat16)
    own_a = dot_dims(pick_ref[...], a_ref[...], 1, 1).astype(jnp.bfloat16)
    own_key = dot_dims(pick_ref[...], key_ref[...], 1, 1).astype(jnp.bfloat16) if cross else own_a
    own_o = dot_dims(pick_ref[...], ot_ref[...], 1, 0).astype(jnp.bfloat16)
    size = own_a.shape[0] // owners
    products = ((own_a, gq_ref), (own_key, gk_ref), (own_key, gv_ref), (own_o, low_ref))
    for m, (rows, right_ref) in enumerate(products):
        product = dot_dims(rows, right_ref[...], 1, 0).astype(jnp.bfloat16)
        for owner in range(owners):
            block_ref[owner, m * size : (m + 1) * size, :] = product[owner * size : (owner + 1) * size]


def attn_backward(grad, stored, picks, owners, row_scale, before=()):
    x, ln, weights, segs, edges, causal, key_in, normed, kept = stored
    length, width = x.shape
    cross = key_in is not None
    extra = full(length, width) if cross else low(owners, length, width // owners)
    outs = (full(length, width), full(2, width), low(owners, 4 * picks.shape[0] // owners, width), extra)
    keys = (key_in,) if cross else ()
    return call(
        partial(attn_backward_kernel, causal, cross, row_scale),
        outs,
        grad,
        x,
        ln,
        weights,
        picks,
        *segs,
        normed,
        *keys,
        *kept,
        edges,
        scratch=[pltpu.VMEM((length, width), jnp.bfloat16)] * 4
        + [pltpu.VMEM((width, length), jnp.bfloat16), pltpu.VMEM((HEADS, length), jnp.float32)]
        + [pltpu.VMEM((width, length), jnp.float32)] * 3,
        smem_args=1,
        microseconds=25,
        before=before,
    )


def gelu_parts(hidden):
    root = math.sqrt(2.0 / math.pi)
    square = hidden * hidden
    bend = jnp.tanh(root * hidden * (1.0 + 0.044715 * square))
    value = 0.5 * hidden * (1.0 + bend)
    slope = 0.5 * (1.0 + bend) + 0.5 * hidden * (1.0 - bend * bend) * root * (
        1.0 + 3.0 * 0.044715 * square
    )
    return value, slope


def ffn_forward_kernel(chunk, pieces, first, x_ref, ln_ref, next_ref, *refs):
    piece_refs, (out_ref, a_ref, after_ref, w_ref, sems) = refs[:pieces], refs[pieces:]
    weights = load_weights(w_ref, piece_refs, None, first, sems)
    w_in_ref, w_out_ref = w_ref.at[0], w_ref.at[1]
    a_ref[...] = norm_forward(x_ref[...], ln_ref).astype(jnp.bfloat16)
    total = x_ref[...]
    for copy in weights:
        copy.wait()
    for start in range(0, w_in_ref.shape[0], chunk):
        part = slice(start, start + chunk)
        hidden = dot_dims(a_ref[...], w_in_ref[part, :], 1, 1)
        active = gelu_parts(hidden)[0].astype(jnp.bfloat16)
        total = total + dot_dims(active, w_out_ref[part, :], 1, 0)
    out_ref[...] = total
    after_ref[...] = norm_forward(total, next_ref).astype(after_ref.dtype)


def ffn_forward(x, ln, ln_next, weights):
    length, width = x.shape
    weights, _, first = weights
    outs = (full(length, width), low(length, width), low(length, width))
    if len(weights) > 1:
        outs = outs + (low(2, 4 * (weights[0].shape[0] // 2 - first), width),)
    out, normed, after, *whole = call(
        partial(ffn_forward_kernel, 512, len(weights), first),
        outs,
        x,
        ln,
        ln_next,
        *weights,
        scratch=[pltpu.VMEM(w.shape, w.dtype) for w in weights if len(weights) == 1]
        + [pltpu.SemaphoreType.DMA((8,))],
        microseconds=12,
        far=range(3, 3 + len(weights)),
    )
    return out, after, (x, ln, whole[0] if whole else weights[0], normed, out, ln_next)


def ffn_backward_kernel(
    chunk, picked, after_ref, *refs
):
    if picked:
        place_ref, *refs = refs
        shape = (refs[0].shape[0], place_ref.shape[1])
        chosen = lax.broadcasted_iota(jnp.int32, shape, 0) == place_ref[...]
        after = dot_dims(chosen.astype(jnp.bfloat16), after_ref[...], 1, 0)
    else:
        after = after_ref[...]
    ffn_backward_rest(chunk, after, *refs)


def ffn_backward_rest(
    chunk, after, y_ref, next_ref, x_ref, ln_ref, a_ref, w_ref, pick_ref,
    out_ref, next_grad_ref, ln_grad_ref, in_ref, back_ref, low_ref, g_ref,
):
    w_in_ref, w_out_ref = w_ref.at[0], w_ref.at[1]
    g_ref[...] = norm_backward(after, y_ref[...], next_ref, next_grad_ref)
    low_ref[...] = g_ref[...].astype(jnp.bfloat16)
    total = jnp.zeros(g_ref.shape, jnp.float32)
    owners, size = in_ref.shape[:2]
    blocks = pick_ref.shape[0] // size
    for index in range(w_in_ref.shape[0] // chunk):
        part = slice(index * chunk, (index + 1) * chunk)
        hidden = dot_dims(a_ref[...], w_in_ref[part, :], 1, 1)
        value, slope = gelu_parts(hidden)
        grad = (dot_dims(low_ref[...], w_out_ref[part, :], 1, 1) * slope).astype(jnp.bfloat16)
        total = total + dot_dims(grad, w_in_ref[part, :], 1, 0)
        pairs = ((in_ref, grad, a_ref), (back_ref, value.astype(jnp.bfloat16), low_ref))
        for ref, left, right_ref in pairs:
            rows = dot_dims(pick_ref[...], left, 1, 1).astype(jnp.bfloat16)
            product = dot_dims(rows, right_ref[...], 1, 0).astype(jnp.bfloat16)
            for block in range(blocks):
                ref[index * blocks + block] = product[block * size : (block + 1) * size]
    out_ref[...] = g_ref[...] + norm_backward(total, x_ref[...], ln_ref, ln_grad_ref)


def ffn_backward(grad_after, stored, picks, owners, before=(), places=None):
    x, ln, weights, normed, out, ln_next = stored
    length, width = x.shape
    chunk = picks.shape[1]
    size = picks.shape[0] * weights.shape[1] // chunk // owners
    block = low(owners, size, width)
    return call(
        partial(ffn_backward_kernel, chunk, places is not None),
        (full(length, width), full(2, width), full(2, width), block, block),
        grad_after,
        *(() if places is None else (places[None, :],)),
        out,
        ln_next,
        x,
        ln,
        normed,
        weights,
        picks,
        scratch=[
            pltpu.VMEM((length, width), jnp.bfloat16),
            pltpu.VMEM((length, width), jnp.float32),
        ],
        microseconds=17,
        before=before,
    )


def follow_kernel(x_ref, out_ref):
    out_ref[...] = x_ref[...]


def follow(x, *before):
    out = jax.ShapeDtypeStruct(x.shape, x.dtype)
    return call(follow_kernel, out, x, microseconds=1, before=before)


def square_kernel(x_ref, out_ref, square_ref):
    out_ref[...] = x_ref[...]
    values = x_ref[...].astype(jnp.float32)
    square_ref[...] = jnp.sum(values * values, axis=0, keepdims=True)


def follow_with_squares(x, *before):
    outs = (low(*x.shape), full(1, x.shape[1]))
    return call(square_kernel, outs, x, microseconds=1, before=before)


def norm_blocks_kernel(*refs):
    refs, out_ref = refs[:-1], refs[-1]
    owners, _, columns = out_ref.shape
    out_ref[...] = jnp.zeros(out_ref.shape, jnp.float32)
    for k, ref in enumerate(refs):
        for owner in range(owners):
            band = slice(owner * columns, (owner + 1) * columns)
            out_ref[owner, k : k + 1, :] = ref[0:1, band]
            out_ref[owner, len(refs) + k : len(refs) + k + 1, :] = ref[1:2, band]


def norm_blocks(grads, owners, *before):
    width = grads[0].shape[1]
    outs = full(owners, 16, width // owners)
    return call(norm_blocks_kernel, outs, *grads, microseconds=1, before=before)


def look_up_tokens(code_ref, paired_ref, found_ref):
    step = 256
    columns = found_ref.shape[1]

    def one(index, carry):
        span = pl.ds(pl.multiple_of(index * step, step), step)
        code = code_ref[span, :]
        places = lax.broadcasted_iota(jnp.int32, (step, paired_ref.shape[0]), 1)
        chosen = (places == lax.shift_right_arithmetic(code, 1)).astype(jnp.bfloat16)
        wide = dot_dims(chosen, paired_ref[...], 1, 0)
        left = jnp.bitwise_and(code, 1) == 1
        found_ref[span, :] = jnp.where(left, wide[:, :columns], wide[:, columns:]).astype(jnp.bfloat16)
        return carry

    lax.fori_loop(0, code_ref.shape[0] // step, one, 0)


def finish_kernel(weight_ref, stats_ref, products_ref, basis_ref, new_stats_ref, new_basis_ref):
    products = products_ref[...].astype(jnp.float32)
    new_stats_ref[...] = stat_decay * stats_ref[...] + weight_ref[0] * products
    new_basis_ref[...] = basis_ref[...].astype(jnp.float32)


def finish_matrices(weight, stats, products, bases):
    block = pl.BlockSpec((1, *stats.shape[1:]), lambda k: (k, 0, 0))
    return pl.pallas_call(
        finish_kernel,
        grid=stats.shape[:1],
        out_shape=(full(*stats.shape),) * 2,
        in_specs=[smem] + [block] * 3,
        out_specs=(block,) * 2,
        compiler_params=pltpu.CompilerParams(vmem_limit_bytes=56 * 2**20),
        cost_estimate=cost_of(5),
    )(weight.reshape(1), stats, products, bases)


def loss_forward_kernel(chunks, final_ref, pick_ref, label_ref, table_ref, picked_ref, stat_ref, logit_ref):
    count, length = pick_ref.shape[0], final_ref.shape[0]
    places = lax.broadcasted_iota(jnp.int32, (count, length), 1)
    chosen = (places == pick_ref[...]).astype(jnp.bfloat16)
    picked_ref[...] = dot_dims(chosen, final_ref[...], 1, 0).astype(jnp.bfloat16)
    rows = table_ref.shape[0] // chunks
    top = jnp.full((1, count), masked, jnp.float32)
    label = jnp.zeros((1, count), jnp.float32)
    for index in range(chunks):
        span = slice(index * rows, (index + 1) * rows)
        logits = dot_dims(table_ref[span, :], picked_ref[...], 1, 1)
        logit_ref[span, :] = logits
        top = jnp.maximum(top, jnp.max(logits, axis=0, keepdims=True))
        hit = lax.broadcasted_iota(jnp.int32, logits.shape, 0) + index * rows == label_ref[...]
        label = label + jnp.sum(jnp.where(hit, logits, 0.0), axis=0, keepdims=True)
    total = jnp.zeros((1, count), jnp.float32)
    for index in range(chunks):
        span = slice(index * rows, (index + 1) * rows)
        total = total + jnp.sum(jnp.exp(logit_ref[span, :] - top), axis=0, keepdims=True)
    stat_ref[...] = jnp.concatenate([top, total, label, jnp.zeros((5, count), jnp.float32)], axis=0)


def loss_forward(final, pick_rows, labels, table):
    count, width = pick_rows.shape[0], final.shape[1]
    return call(
        partial(loss_forward_kernel, 8),
        (low(count, width), full(8, count)),
        final,
        pick_rows[:, None],
        labels[None, :],
        table,
        scratch=[pltpu.VMEM((table.shape[0], count), jnp.float32)],
        microseconds=6,
    )


def loss_backward_kernel(
    chunks, picked_ref, seen_ref, weight_ref, label_ref, table_ref, grad_ref, parts_ref, loss_ref
):
    tops, totals, labels = (
        jnp.concatenate([seen_ref[k, m : m + 1, :] for k in range(seen_ref.shape[0])], axis=0)
        for m in range(3)
    )
    top = jnp.max(tops, axis=0, keepdims=True)
    total = top + jnp.log(jnp.sum(totals * jnp.exp(tops - top), axis=0, keepdims=True))
    loss_ref[...] = (total - jnp.sum(labels, axis=0, keepdims=True)) * weight_ref[...]
    rows = table_ref.shape[0] // chunks
    columns = parts_ref.shape[2]
    grad = jnp.zeros(grad_ref.shape, jnp.float32)
    for index in range(chunks):
        span = slice(index * rows, (index + 1) * rows)
        logits = dot_dims(table_ref[span, :], picked_ref[...], 1, 1)
        hit = lax.broadcasted_iota(jnp.int32, logits.shape, 0) + index * rows == label_ref[...]
        slopes = weight_ref[...] * (jnp.exp(logits - total) - jnp.where(hit, 1.0, 0.0))
        slopes = slopes.astype(jnp.bfloat16)
        product = dot_dims(slopes, picked_ref[...], 1, 0).astype(jnp.bfloat16)
        for owner in range(parts_ref.shape[0]):
            parts_ref[owner, span, :] = product[:, owner * columns : (owner + 1) * columns]
        grad = grad + dot_dims(slopes, table_ref[span, :], 0, 0)
    grad_ref[...] = grad.astype(jnp.bfloat16)


def loss_backward(picked, seen, weight, labels, table, owners):
    count, width = picked.shape
    return call(
        partial(loss_backward_kernel, 8),
        (low(count, width), low(owners, table.shape[0], width // owners), full(1, count)),
        picked,
        seen,
        weight[None, :],
        labels[None, :],
        table,
        microseconds=8,
    )


def adam_parts(weight, grad, moment, second):
    moment = beta_one * moment + (1.0 - beta_one) * grad
    second = beta_two * second + (1.0 - beta_two) * grad * grad
    step = adam_direction(moment, second) + decay_rate * weight
    return weight - rate_matrix * step, moment, second


def update_kernel(*refs):
    factor_ref, basis_ref, *ins = refs[:14]
    outs = refs[14:]
    factor = factor_ref[0]
    for k in (0, 1):
        grad_ref, weight_ref, moment_ref, second_ref = ins[4 * k : 4 * k + 4]
        grad = grad_ref[...].astype(jnp.float32) * factor
        results = adam_parts(weight_ref[...], grad, moment_ref[...], second_ref[...])
        for ref, result in zip(outs[3 * k : 3 * k + 3], results):
            ref[...] = result
    g_ref, w_ref, m_ref, v_ref = ins[8:]
    new_w_ref, new_m_ref, new_v_ref = outs[6:]
    high = basis_ref[0].astype(jnp.bfloat16)
    rest = (basis_ref[0] - high.astype(jnp.float32)).astype(jnp.bfloat16)
    grad = g_ref[0]
    rotated = (dot_dims(grad, high, 1, 0) + dot_dims(grad, rest, 1, 0)) * factor
    moment = beta_one * m_ref[0] + (1.0 - beta_one) * rotated
    second = beta_two * v_ref[0] + (1.0 - beta_two) * rotated * rotated
    new_m_ref[0] = moment
    new_v_ref[0] = second
    step = adam_direction(moment, second)
    step_high = step.astype(jnp.bfloat16)
    step_rest = (step - step_high.astype(jnp.float32)).astype(jnp.bfloat16)
    back = (
        dot_dims(step_high, high, 1, 1)
        + dot_dims(step_high, rest, 1, 1)
        + dot_dims(step_rest, high, 1, 1)
    )
    new_w_ref[0] = w_ref[0] - rate_matrix * (back + decay_rate * w_ref[0])


def update_matrices(factor, bases, attn, table, ffn):
    def blocks(array):
        shape = (array.shape[0] // 4, *array.shape[1:])
        return pl.BlockSpec(shape, lambda k: (k,) + (0,) * (len(shape) - 1))

    arrays = (*attn, *table, *ffn)
    results = [part for group in (attn, table, ffn) for part in group[1:]]
    return pl.pallas_call(
        update_kernel,
        grid=(4,),
        out_shape=tuple(full(*part.shape) for part in results),
        in_specs=[smem, blocks(bases)] + [blocks(part) for part in arrays],
        out_specs=tuple(blocks(part) for part in results),
        compiler_params=pltpu.CompilerParams(vmem_limit_bytes=56 * 2**20),
        cost_estimate=cost_of(20),
    )(factor.reshape(1), bases, *arrays)


def small_factor(block):
    size = block.shape[0]
    eye = (
        lax.broadcasted_iota(jnp.int32, (size, size), 0)
        == lax.broadcasted_iota(jnp.int32, (size, size), 1)
    ).astype(jnp.float32)
    whole = jnp.concatenate([block, eye], axis=1)
    rows = [whole[8 * u : 8 * u + 8] for u in range(size // 8)]
    shape = rows[0].shape
    sub = lax.broadcasted_iota(jnp.int32, shape, 0)

    def lane_splat(value, lane):
        return jnp.broadcast_to(value[:, lane : lane + 1], shape)

    def row_splat(value, row):
        return jnp.broadcast_to(value[row : row + 1, :], shape)

    for g in range(len(rows)):
        first = 8 * g
        lanes = {
            u: [lane_splat(rows[u], first + s) for s in range(8)] for u in range(g, len(rows))
        }
        scale = jnp.zeros(shape, jnp.float32)
        for t in range(8):
            pivot = row_splat(lanes[g][t], t)
            root = lax.rsqrt(pivot)
            inverse = root * root
            scale = jnp.where(sub == t, root, scale)
            row_t = row_splat(rows[g], t) * inverse
            splats = {s: row_splat(lanes[g][s], t) * inverse for s in range(t + 1, 8)}
            for u in range(g, len(rows)):
                factor = lanes[u][t]
                if u == g:
                    factor = jnp.where(sub > t, factor, 0.0)
                rows[u] = rows[u] - factor * row_t
                for s in range(t + 1, 8):
                    lanes[u][s] = lanes[u][s] - factor * splats[s]
        rows[g] = rows[g] * scale
    return jnp.concatenate(rows, axis=0)[:, size:]


def renew_kernel(
    product_ref, stats_ref, bases_ref, factor_ref, half_ref, stat_ref, basis_ref, out_ref, gram_ref, rest_ref, sems
):
    size = stat_ref.shape[0]
    here = lax.axis_index("vocab")
    copies = [
        pltpu.make_async_copy(ref.at[here // 2], place, sems.at[k])
        for k, (ref, place) in enumerate(((stats_ref, stat_ref), (bases_ref, basis_ref)))
    ]
    for copy in copies:
        copy.start()
    for copy in copies:
        copy.wait()
    statistic = stat_decay * stat_ref[...] + factor_ref[0] * product_ref[...]
    product = dot_exact(statistic, basis_ref[...], 1, 0)
    rest_ref[...] = product
    gram_ref[...] = dot_exact(product, product, 0, 0)
    for low in range(0, size, 128):
        high = low + 128
        block = gram_ref[low:high, low:high]
        corner = small_factor(block[:64, :64])
        across = dot_exact(corner, block[:64, 64:], 1, 0)
        second = small_factor(block[64:, 64:] - dot_exact(across, across, 0, 0))
        below = dot_exact(second, dot_exact(across, corner, 0, 0), 1, 0)
        inverse = jnp.concatenate(
            [
                jnp.concatenate([corner, jnp.zeros_like(corner)], axis=1),
                jnp.concatenate([-below, second], axis=1),
            ],
            axis=0,
        )
        columns = dot_exact(rest_ref[:, low:high], inverse, 1, 1)
        out_ref[:, low:high] = columns
        if high < size:
            panel = dot_exact(inverse, gram_ref[low:high, high:], 1, 0)
            gram_ref[high:, high:] -= dot_exact(panel, panel, 0, 0)
            rest_ref[:, high:] -= dot_exact(columns, panel, 1, 0)
    rows = size // 2
    half = pl.ds(pl.multiple_of(lax.rem(here, 2) * rows, rows), rows)
    half_ref[...] = out_ref[half, :].astype(jnp.bfloat16)


def renew_basis(products, stats, bases, factor):
    size = products.shape[0]
    return call(
        renew_kernel,
        low(size // 2, size),
        products,
        stats,
        bases,
        factor.reshape(1),
        scratch=[pltpu.VMEM((size, size), jnp.float32)] * 5 + [pltpu.SemaphoreType.DMA((2,))],
        smem_args=1,
        microseconds=29,
        far=(1, 2),
    )


def peers_of(axis):
    size, me = lax.axis_size(axis), lax.axis_index(axis)
    return [
        (step, lax.rem(me + step, size), lax.rem(me + size - step, size)) for step in range(1, size)
    ]


def greet(*places):
    barrier = pltpu.get_barrier_semaphore()
    for axis, index in places:
        pl.semaphore_signal(barrier, inc=1, device_id={axis: index}, device_id_type=mesh_ids)
    pl.semaphore_wait(barrier, len(places))


def push(source, target, sems, slot, axis, index):
    copy = pltpu.make_async_remote_copy(
        src_ref=source,
        dst_ref=target,
        send_sem=sems[0].at[slot],
        recv_sem=sems[1].at[slot],
        device_id={axis: index},
        device_id_type=mesh_ids,
    )
    copy.start()
    return copy


def sem_pair(count):
    return [pltpu.SemaphoreType.DMA((count,)), pltpu.SemaphoreType.DMA((count,))]


def talk(kernel, outs, collective_id, *args, scratch=(), microseconds=15, before=()):
    def body(*refs):
        kernel(*refs[: len(args)], *refs[len(args) + len(before) :])

    return pl.pallas_call(
        body,
        out_shape=outs,
        in_specs=[vmem] * len(args) + [pl.BlockSpec(memory_space=pl.ANY)] * len(before),
        out_specs=jax.tree.map(lambda _: vmem, outs),
        scratch_shapes=list(scratch),
        compiler_params=pltpu.CompilerParams(
            collective_id=collective_id, has_side_effects=True, vmem_limit_bytes=56 * 2**20
        ),
        cost_estimate=cost_of(microseconds),
    )(*args, *before)


def gather_kernel(axis, *refs):
    count = (len(refs) - 2) // 2
    others = peers_of(axis)
    greet(*[(axis, to) for _, to, _ in others])
    me = lax.axis_index(axis)
    copies = [
        push(refs[k], refs[count + k].at[me], refs[-2:], k * len(others) + step - 1, axis, to)
        for k in range(count)
        for step, to, _ in others
    ]
    for k in range(count):
        refs[count + k][me] = refs[k][...]
    for copy in copies:
        copy.wait()


def gather_small(axis, collective_id, *arrays):
    size = lax.axis_size(axis)
    outs = tuple(jax.ShapeDtypeStruct((size, *x.shape), x.dtype) for x in arrays)
    sems = sem_pair((size - 1) * len(arrays))
    return talk(partial(gather_kernel, axis), outs, collective_id, *arrays, scratch=sems)


def flip(index, bit):
    return index + bit - 2 * bit * lax.rem(index // bit, 2)


def far_replicas():
    here, size = lax.axis_index("vocab"), lax.axis_size("vocab")
    return [
        (step // 2 - 1, lax.rem(here + step, size), lax.rem(here + size - step, size))
        for step in range(2, size, 2)
    ]


def sum_kernel(x_ref, out_ref, near_ref, send_ref, parts_ref, s0, r0, s1, r1, s2, r2, s3, r3):
    here, others = lax.axis_index("vocab"), far_replicas()
    near, side = flip(here, 1), lax.rem(here, 2)
    greet(*[("vocab", to) for _, to, _ in others], ("vocab", near))
    half = near_ref.shape[0]
    share = parts_ref.shape[1]

    def half_of(which):
        return pl.ds(pl.multiple_of(which * half, half), half)

    def share_of(index, start):
        return pl.ds(pl.multiple_of(start + index // 2 * share, share), share)

    push(x_ref.at[half_of(1 - side)], near_ref, (s0, r0), 0, "vocab", near).wait()
    total = near_ref[...].astype(jnp.float32) + x_ref[half_of(side), :].astype(jnp.float32)
    send_ref[...] = total.astype(send_ref.dtype)
    copies = [
        push(send_ref.at[share_of(to, 0)], parts_ref.at[slot], (s1, r1), slot, "vocab", to)
        for slot, to, _ in others
    ]
    total = send_ref[share_of(here, 0), :].astype(jnp.float32)
    for copy, (slot, _, _) in zip(copies, others):
        copy.wait()
        total = total + parts_ref[slot].astype(jnp.float32)
    mine = share_of(here, side * half)
    out_ref[mine, :] = total.astype(out_ref.dtype)
    copies = [
        push(out_ref.at[mine], out_ref.at[mine], (s2, r2), slot, "vocab", to) for slot, to, _ in others
    ]
    close = [push(out_ref.at[mine], out_ref.at[mine], (s3, r3), 0, "vocab", near)]
    for copy, (slot, _, origin) in zip(copies, others):
        copy.wait()
        theirs = out_ref.at[share_of(origin, side * half)]
        close.append(push(theirs, theirs, (s3, r3), slot + 1, "vocab", near))
    for copy in close:
        copy.wait()


def sum_vocab(x, collective_id):
    pairs = lax.axis_size("vocab") // 2
    rows, columns = x.shape
    half = rows // 2
    return talk(
        sum_kernel,
        jax.ShapeDtypeStruct(x.shape, x.dtype),
        collective_id,
        x,
        scratch=[
            pltpu.VMEM((half, columns), x.dtype),
            pltpu.VMEM((half, columns), x.dtype),
            pltpu.VMEM((pairs - 1, half // pairs, columns), x.dtype),
        ]
        + sem_pair(1)
        + sem_pair(pairs - 1)
        + sem_pair(pairs - 1)
        + sem_pair(pairs),
    )


def tail_kernel(
    x_ref, few_ref, out_ref, sum_ref, parts_ref, seen_ref, line_ref, lines_ref,
    s0, r0, s1, r1, s2, r2, s3, r3, s4, r4,
):
    owners, replicas = peers_of("dp"), peers_of("vocab")
    greet(*[("dp", to) for _, to, _ in owners], *[("vocab", to) for _, to, _ in replicas])
    size, me, here = lax.axis_size("dp"), lax.axis_index("dp"), lax.axis_index("vocab")
    near, side = flip(here, 1), lax.rem(here, 2)
    rows = parts_ref.shape[1]

    def rows_of(index):
        return pl.ds(pl.multiple_of((side * size + index) * rows, rows), rows)

    few = [
        push(few_ref, seen_ref.at[here], (s2, r2), step - 1, "vocab", to) for step, to, _ in replicas
    ]
    wide = [
        push(x_ref.at[rows_of(to)], parts_ref.at[me], (s0, r0), step - 1, "dp", to)
        for step, to, _ in owners
    ]
    seen_ref[here] = few_ref[...]
    parts_ref[me] = x_ref[rows_of(me), :]
    for copy in few:
        copy.wait()
    line_ref[...] = jnp.sum(seen_ref[...], axis=0)
    few = [
        push(line_ref, lines_ref.at[me], (s3, r3), step - 1, "dp", to) for step, to, _ in owners
    ]
    lines_ref[me] = line_ref[...]
    for copy in wide:
        copy.wait()
    out_ref[rows_of(me), :] = jnp.sum(parts_ref[...], axis=0)
    mine = out_ref.at[rows_of(me)]
    wide = [push(mine, mine, (s1, r1), step - 1, "dp", to) for step, to, _ in owners]
    close = [push(mine, mine, (s4, r4), 0, "vocab", near)]
    for copy in few:
        copy.wait()
    sum_ref[...] = jnp.sum(lines_ref[...], axis=0)
    for copy, (step, _, origin) in zip(wide, owners):
        copy.wait()
        theirs = out_ref.at[rows_of(origin)]
        close.append(push(theirs, theirs, (s4, r4), step, "vocab", near))
    for copy in close:
        copy.wait()


def sum_tail(x, few, collective_id):
    owners, replicas = lax.axis_size("dp"), lax.axis_size("vocab")
    rows, columns = x.shape
    share = rows // (2 * owners)
    return talk(
        tail_kernel,
        (full(*x.shape), full(*few.shape)),
        collective_id,
        x,
        few,
        scratch=[
            pltpu.VMEM((owners, share, columns), jnp.float32),
            pltpu.VMEM((replicas, *few.shape), jnp.float32),
            pltpu.VMEM(few.shape, jnp.float32),
            pltpu.VMEM((owners, *few.shape), jnp.float32),
        ]
        + sem_pair(owners - 1)
        + sem_pair(owners - 1)
        + sem_pair(replicas - 1)
        + sem_pair(owners - 1)
        + sem_pair(owners),
    )


def sum_tokens(rows_refs, place_ref, left_ref, table_ref, wide_ref, embed_ref, square_ref):
    owners, length, columns = rows_refs[0].shape
    for owner in range(owners):
        for k, rows_ref in enumerate(rows_refs):
            start = (owner * len(rows_refs) + k) * length
            span = slice(start, start + length)
            left = rows_ref[owner] * left_ref[span, :]
            wide_ref[span, :columns] = left
            wide_ref[span, columns:] = rows_ref[owner] - left
    tokens, half = wide_ref.shape[0], embed_ref.shape[0] // 2
    tile, step = half // 4, 1024
    square_ref[...] = jnp.zeros(square_ref.shape, jnp.float32)

    def one(index, carry):
        start = index * tile
        places = lax.broadcasted_iota(jnp.int32, (tile, step), 0) + start
        total = jnp.zeros((tile, 2 * columns), jnp.float32)
        for first in range(0, tokens, step):
            chosen = (places == place_ref[:, first : first + step]).astype(jnp.bfloat16)
            total = total + dot_dims(chosen, wide_ref[first : first + step, :], 1, 0)
        for side in range(2):
            span = pl.ds(pl.multiple_of(side * half + start, 16), tile)
            part = total[:, side * columns : (side + 1) * columns]
            part = part + table_ref[span, :].astype(jnp.float32)
            embed_ref[span, :] = part
            square_ref[...] += jnp.sum(part * part, axis=0, keepdims=True)
        return carry

    lax.fori_loop(0, 4, one, 0)


def gradient_kernel(chunks, count, inside, *refs):
    x_refs, refs = refs[:chunks], refs[chunks:]
    rows_refs, refs = refs[:count], refs[count:]
    if inside:
        (place_ref, left_ref, table_ref), refs = refs[:3], refs[3:]
    (out_ref, square_ref, *refs) = refs
    swapped_refs, refs = refs[:count], refs[count:]
    if inside:
        (embed_ref, embed_square_ref), refs = refs[:2], refs[2:]
        *refs, wide_ref = refs
    parts_ref, s0, r0, s1, r1, s2, r2, s3, r3, s4, r4 = refs
    owners = peers_of("dp")
    here, me = lax.axis_index("vocab"), lax.axis_index("dp")
    near = flip(here, 1)
    size = lax.axis_size("vocab")
    steps = range(2, size, 2)
    greet(
        *[("dp", to) for _, to, _ in owners],
        *[("vocab", lax.rem(here + step, size)) for step in steps],
        ("vocab", near),
    )

    def spread(c, origin, sems, slot, to):
        place = out_ref.at[c, origin]
        return push(place, place, sems, slot, "vocab", to)

    arriving = [
        [
            push(x_refs[c].at[to], parts_ref.at[c, me], (s0, r0), (step - 1) * chunks + c, "dp", to)
            for step, to, _ in owners
        ]
        for c in range(chunks)
    ]

    def half_of(ref):
        rows = ref.shape[1] // 2
        return pl.ds(pl.multiple_of(lax.rem(here, 2) * rows, rows), rows)

    swaps = [
        [
            push(
                rows_ref.at[to, half_of(rows_ref)],
                swapped_ref.at[me, half_of(rows_ref)],
                (s3, r3),
                k * len(owners) + step - 1,
                "dp",
                to,
            )
            for step, to, _ in owners
        ]
        for k, (rows_ref, swapped_ref) in enumerate(zip(rows_refs, swapped_refs))
    ]
    for rows_ref, swapped_ref in zip(rows_refs, swapped_refs):
        swapped_ref[me] = rows_ref[me]
    far, close = [], []
    square = jnp.zeros(square_ref.shape, jnp.float32)
    for c in range(chunks):
        parts_ref[c, me] = x_refs[c][me]
        for copy in arriving[c]:
            copy.wait()
        total = jnp.sum(parts_ref[c].astype(jnp.float32), axis=0)
        out_ref[c, here] = total.astype(out_ref.dtype)
        square = square + jnp.sum(total * total, axis=0, keepdims=True)
        far.append(
            [
                spread(c, here, (s1, r1), k * chunks + c, lax.rem(here + step, size))
                for k, step in enumerate(steps)
            ]
        )
        close.append(spread(c, here, (s2, r2), c, near))
    square_ref[...] = square
    moved = []
    for k, swapped_ref in enumerate(swapped_refs):
        for copy, (step, _, origin) in zip(swaps[k], owners):
            copy.wait()
            place = swapped_ref.at[origin, half_of(swapped_ref)]
            moved.append(push(place, place, (s4, r4), k * len(owners) + step - 1, "vocab", near))
    for copy in moved:
        copy.wait()
    if inside:
        sum_tokens(
            swapped_refs[:2], place_ref, left_ref, table_ref, wide_ref, embed_ref, embed_square_ref
        )
    for c in range(chunks):
        for k, step in enumerate(steps):
            far[c][k].wait()
            origin = lax.rem(here + size - step, size)
            close.append(spread(c, origin, (s2, r2), (k + 1) * chunks + c, near))
    for copy in close:
        copy.wait()


def share_gradients(blocks, rows, collective_id, before, tokens):
    owners, replicas = lax.axis_size("dp"), lax.axis_size("vocab")
    chunks = len(blocks)
    others = (replicas // 2 - 1) * chunks
    shape, kind = blocks[0].shape, blocks[0].dtype
    return talk(
        partial(gradient_kernel, chunks, len(rows), bool(tokens)),
        (
            jax.ShapeDtypeStruct((chunks, replicas, *shape[1:]), kind),
            full(1, shape[2]),
            *[jax.ShapeDtypeStruct(part.shape, part.dtype) for part in rows],
            *[full(*size) for part in tokens[2:] for size in (part.shape, (1, part.shape[1]))],
        ),
        collective_id,
        *blocks,
        *rows,
        *tokens,
        scratch=[pltpu.VMEM((chunks, *shape), kind)]
        + sem_pair((owners - 1) * chunks)
        + sem_pair(others)
        + sem_pair(others + chunks)
        + sem_pair(len(rows) * (owners - 1))
        + sem_pair(len(rows) * (owners - 1))
        + [pltpu.VMEM((part.shape[1], 2 * tokens[2].shape[1]), jnp.bfloat16) for part in tokens[:1]],
        microseconds=40,
        before=before,
    )


def swap_kernel(scale, x_ref, place_ref, sum_ref, out_ref, s0, r0, s1, r1):
    others = peers_of("dp")
    me, here = lax.axis_index("dp"), lax.axis_index("vocab")
    near, side = flip(here, 1), lax.rem(here, 2)
    greet(*[("dp", to) for _, to, _ in others], ("vocab", near))
    rows = x_ref.shape[1] // 2
    half = pl.ds(pl.multiple_of(side * rows, rows), rows)
    copies = [
        push(x_ref.at[to, half], out_ref.at[me, half], (s0, r0), step - 1, "dp", to)
        for step, to, _ in others
    ]
    out_ref[me] = x_ref[me]
    close = []
    for copy, (step, _, origin) in zip(copies, others):
        copy.wait()
        place = out_ref.at[origin, half]
        close.append(push(place, place, (s1, r1), step - 1, "vocab", near))
    for copy in close:
        copy.wait()
    columns = out_ref.shape[2]
    for owner in range(out_ref.shape[0]):
        band = slice(owner * columns, (owner + 1) * columns)
        sum_ref[:, band] = out_ref[owner].astype(jnp.float32) * scale + place_ref[:, band]


def swap_owners(x, places, scale, collective_id, before):
    owners = lax.axis_size("dp")
    return talk(
        partial(swap_kernel, scale),
        full(*places.shape),
        collective_id,
        x,
        places,
        scratch=[pltpu.VMEM(x.shape, x.dtype)]
        + sem_pair(owners - 1) + sem_pair(owners - 1),
        before=before,
    )


def token_kernel(
    scale, inside, x_ref, place_ref, attn_ref, ffn_ref, code_ref, paired_ref, out_ref, attn_out_ref, ffn_out_ref,
    found_ref, near_ref, parts_ref, blocks_ref, row_ref,
    s0, r0, s1, r1, s2, r2, s3, r3, s4, r4, s5, r5, s6, r6,
):
    owners, others = peers_of("dp"), far_replicas()
    me, here = lax.axis_index("dp"), lax.axis_index("vocab")
    near, side = flip(here, 1), lax.rem(here, 2)
    greet(
        *[("dp", to) for _, to, _ in owners], *[("vocab", to) for _, to, _ in others], ("vocab", near)
    )
    count, length, columns = x_ref.shape
    half, pairs = length // 2, lax.axis_size("vocab") // 2
    share = half // pairs

    def half_of(which):
        return pl.ds(pl.multiple_of(which * half, half), half)

    def share_of(index):
        return pl.ds(pl.multiple_of(index // 2 * share, share), share)

    def place_of(index):
        return pl.ds(pl.multiple_of(side * half + index // 2 * share, share), share)

    def send_weights(ref, own_ref, slot, span):
        count, rows = own_ref.shape[0] // 2, own_ref.shape[1]
        mine = pl.ds(side * count, count)

        def place(origin):
            return ref.at[mine, pl.ds(pl.multiple_of(origin * rows + span[0], span[1]), span[1])]

        copies = [
            push(own_ref.at[mine, pl.ds(*span)], place(me), (s5, r5), slot + step - 1, "dp", to)
            for step, to, _ in owners
        ]
        return [(copy, place(origin), slot + step - 1) for copy, (step, _, origin) in zip(copies, owners)]

    def relay_weights(sent):
        relays = []
        for copy, place, slot in sent:
            copy.wait()
            relays.append(push(place, place, (s6, r6), slot, "vocab", near))
        return relays

    first = push(x_ref.at[:, half_of(1 - side)], near_ref, (s0, r0), 0, "vocab", near)
    some = ffn_ref.shape[1] // 2
    early = send_weights(attn_out_ref, attn_ref, 0, (0, attn_ref.shape[1]))
    early += send_weights(ffn_out_ref, ffn_ref, len(owners), (0, some))
    for ref, own_ref in ((attn_out_ref, attn_ref), (ffn_out_ref, ffn_ref)):
        rows = own_ref.shape[1]
        ref[:, pl.ds(pl.multiple_of(me * rows, rows), rows), :] = own_ref[...]
    first.wait()
    near_ref[...] += x_ref[:, half_of(side)]
    copies = [
        push(near_ref.at[:, share_of(to)], parts_ref.at[slot], (s1, r1), slot, "vocab", to)
        for slot, to, _ in others
    ]
    if inside:
        look_up_tokens(code_ref, paired_ref, found_ref)
    else:
        found_ref[...] = jnp.zeros(found_ref.shape, found_ref.dtype)
    for copy in copies:
        copy.wait()
    total = near_ref[:, share_of(here)]
    for slot, _, _ in others:
        total = total + parts_ref[slot]
    blocks_ref[...] = total
    copies = [
        push(
            blocks_ref.at[to],
            row_ref.at[me, place_of(here)],
            (s2, r2),
            step - 1,
            "dp",
            to,
        )
        for step, to, _ in owners
    ]
    row_ref[me, place_of(here)] = blocks_ref[me]
    for copy in copies:
        copy.wait()
    late = send_weights(ffn_out_ref, ffn_ref, 2 * len(owners), (some, some))
    mine = row_ref.at[:, place_of(here)]
    copies = [push(mine, mine, (s3, r3), slot, "vocab", to) for slot, to, _ in others]
    close = [push(mine, mine, (s4, r4), 0, "vocab", near)]
    for copy, (slot, _, origin) in zip(copies, others):
        copy.wait()
        theirs = row_ref.at[:, place_of(origin)]
        close.append(push(theirs, theirs, (s4, r4), slot + 1, "vocab", near))
    close += relay_weights(early)
    for copy in close[: pairs]:
        copy.wait()
    for owner in range(count):
        band = slice(owner * columns, (owner + 1) * columns)
        out_ref[:, band] = row_ref[owner].astype(jnp.float32) * scale + place_ref[:, band]
    close += relay_weights(late)
    for copy in close[pairs:]:
        copy.wait()


def gather_tokens(x, places, attn, ffn, codes, paired, scale, collective_id):
    owners, pairs = lax.axis_size("dp"), lax.axis_size("vocab") // 2
    _, length, columns = x.shape
    half = length // 2
    width = owners * columns
    whole = [low(w.shape[0], owners * w.shape[1], width) for w in (attn, ffn)]
    return talk(
        partial(token_kernel, scale, paired is not None),
        (full(length, width), *whole, low(codes.shape[0], columns)),
        collective_id,
        x,
        places,
        attn,
        ffn,
        codes,
        attn[0] if paired is None else paired,
        scratch=[
            pltpu.VMEM((owners, half, columns), x.dtype),
            pltpu.VMEM((pairs - 1, owners, half // pairs, columns), x.dtype),
            pltpu.VMEM((owners, half // pairs, columns), x.dtype),
            pltpu.VMEM((owners, length, columns), x.dtype),
        ]
        + sem_pair(1)
        + sem_pair(pairs - 1)
        + sem_pair(owners - 1)
        + sem_pair(pairs - 1)
        + sem_pair(pairs)
        + sem_pair(3 * owners - 3)
        + sem_pair(3 * owners - 3),
        microseconds=50,
    )


def sinusoid(length, model_width):
    places = np.arange(length, dtype=np.float32)[:, None]
    halves = np.arange(model_width // 2, dtype=np.float32)[None, :]
    angles = places * np.exp(halves * np.float32(-2.0 * math.log(10000.0) / model_width))
    angles = angles.astype(np.float64)
    return (
        np.stack([np.sin(angles), np.cos(angles)], axis=-1)
        .reshape(length, model_width)
        .astype(np.float32)
    )


def one_hot(ids, columns):
    return (ids[:, None] == columns[None, :]).astype(jnp.bfloat16)


def pick_weights(target_seg, pick_rows):
    sentence = jnp.take(target_seg, pick_rows, axis=0)
    return jnp.sum((sentence[:, None] == sentence[None, :]).astype(jnp.float32), axis=1)


def adam_direction(moment, second):
    first_scale, second_scale = 1.0 / (1.0 - beta_one**STEP), 1.0 / (1.0 - beta_two**STEP)
    return (moment * first_scale) / (jnp.sqrt(second * second_scale) + adam_eps)


def adam_update(weight, grad_item, moment, second, step_rate, decay_weight):
    moment = beta_one * moment + (1.0 - beta_one) * grad_item
    second = beta_two * second + (1.0 - beta_two) * grad_item * grad_item
    return (
        weight - step_rate * (adam_direction(moment, second) + decay_weight * weight),
        moment,
        second,
    )


def body(
    src_ids,
    src_seg,
    tgt_ids,
    tgt_seg,
    pick_pos,
    pick_label,
    attn_w,
    attn_m,
    attn_v,
    ffn_w,
    ffn_m,
    ffn_v,
    soap_basis,
    soap_stats,
    norm_p,
    norm_m,
    norm_v,
    embedding,
    embed_m,
    embed_v,
):
    owners, replicas = lax.axis_size("dp"), lax.axis_size("vocab")
    replica = lax.axis_index("vocab")
    own_table = embedding.astype(jnp.bfloat16)
    own_norms = jnp.pad(norm_p.astype(jnp.bfloat16).astype(jnp.float32), ((0, 2), (0, 0)))
    all_ids, norm_rows = gather_small("dp", 1, jnp.concatenate([src_ids, tgt_ids]), own_norms)
    norm_rows = jnp.swapaxes(norm_rows, 0, 1).reshape(16, -1)
    norms = [jnp.stack([norm_rows[k], norm_rows[7 + k]]) for k in range(7)]
    vocab_count, width = embedding.shape[0], attn_w.shape[2]
    source, source_seg, target, target_seg = (src_ids[0], src_seg[0], tgt_ids[0], tgt_seg[0])
    pick_rows, labels = (pick_pos[0], pick_label[0])
    length = source.shape[0]
    embed_scale = math.sqrt(width)
    half = vocab_count // 2
    halves = jnp.arange(half)
    paired = jnp.concatenate([own_table[:half], own_table[half:]], axis=1)

    def paired_places(ids):
        place = ids - replica * vocab_count
        inside = (place >= 0) & (place < vocab_count)
        return jnp.where(inside, place % half, -1), place < half

    def look_up(ids):
        place, left = paired_places(ids)
        wide = lax.dot_general(one_hot(place, halves), paired, (((1,), (0,)), ((), ())))
        return jnp.where(left[:, None], wide[:, :paired.shape[1] // 2], wide[:, paired.shape[1] // 2 :])

    if owners == 4:
        place, left = paired_places(jnp.swapaxes(all_ids, 0, 1).reshape(2, -1, 1))
        all_codes = jnp.where(place < 0, -1, 2 * place + left.astype(jnp.int32))
        codes = all_codes[1]
        whole_paired = jnp.pad(paired, ((0, -half % 128), (0, 0)))
        source_part = call(
            look_up_tokens, low(codes.shape[0], width // owners), all_codes[0], whole_paired
        )
    else:
        source_part = look_up(all_ids[:, 0].reshape(-1))
        codes, whole_paired = jnp.zeros((16, 1), jnp.int32), None
    positional = sinusoid(length, width)
    enc_in, enc_attn_w, enc_ffn_w, target_part = gather_tokens(
        source_part.reshape(owners, length, -1),
        positional,
        attn_w[0:4].astype(jnp.bfloat16),
        ffn_w[0:2].astype(jnp.bfloat16),
        codes,
        whole_paired,
        embed_scale,
        2,
    )
    if owners != 4:
        target_part = look_up(all_ids[:, 1].reshape(-1))
    target_sum = lax.psum(target_part, "vocab")
    enc_mid, enc_attn = attn_forward(
        enc_in, norms[0], ((enc_attn_w,), 0, 0), source_seg, source_seg, None, False
    )
    self_w, cross_w, dec_ffn_w, ready = late_weights(attn_w[4:], ffn_w[2:], enc_in, enc_mid)
    enc_out, encoded, enc_ffn = ffn_forward(enc_mid, norms[1], norms[2], ((enc_ffn_w,), 0, 0))
    weight = 1.0 / pick_weights(target_seg, pick_rows)
    picks = share_selector(width, owners, replicas, replica, width)
    hidden = ffn_w.shape[1] * owners
    hidden_picks = share_selector(hidden, owners, replicas, replica, 512)
    place, left = paired_places(all_ids.reshape(-1))
    tokens = ()
    if owners == 4:
        ones = jnp.broadcast_to(left[:, None], (left.shape[0], width // owners))
        tokens = (place[None, :], ones.astype(jnp.bfloat16))
    dec_in = swap_owners(
        target_sum.reshape(owners, length, -1),
        positional,
        embed_scale,
        3,
        (enc_out, weight, picks, hidden_picks, *tokens),
    )
    table_low = lax.all_gather(follow(own_table, ready, dec_in), "dp", axis=1, tiled=True)
    dec_mid, dec_self = attn_forward(
        dec_in, norms[3], self_w, target_seg, target_seg, None, True
    )
    dec_late, dec_cross = attn_forward(
        dec_mid, norms[4], cross_w, target_seg, source_seg, encoded, False
    )
    dec_out, final_low, dec_ffn = ffn_forward(dec_late, norms[5], norms[6], dec_ffn_w)

    own_labels = labels - replica * vocab_count
    picked, own_stats = loss_forward(final_low, pick_rows, own_labels, table_low)
    (seen,) = gather_small("vocab", 4, own_stats)
    grad_picked, table_parts, losses = loss_backward(
        picked, seen, weight, own_labels, table_low, owners
    )
    grad_table = lax.psum_scatter(table_parts, "dp", scatter_dimension=0, tiled=False)
    grad_picked = sum_vocab(grad_picked, 5)
    loss_part = jnp.sum(losses)
    count_part = (target_seg[-1] + 1).astype(jnp.float32)

    norm_grads = [None] * 7
    grad, norm_grads[6], norm_grads[5], *ffn_blocks = ffn_backward(
        grad_picked, dec_ffn, hidden_picks, owners, places=pick_rows
    )
    grad, norm_grads[4], block, grad_encoded = attn_backward(grad, dec_cross, picks, owners, None)
    early = lax.psum_scatter(
        jnp.concatenate([block, *ffn_blocks], axis=1), "dp", scatter_dimension=0, tiled=False
    )
    grad, norm_grads[3], self_block, target_rows = attn_backward(
        grad, dec_self, picks, owners, embed_scale
    )
    grad, norm_grads[2], norm_grads[1], *ffn_blocks = ffn_backward(
        grad_encoded, enc_ffn, hidden_picks, owners, before=(grad_table, grad)
    )
    early_sum, early_squares = follow_with_squares(early, grad)
    early = lax.all_gather(early_sum, "vocab")
    grad, norm_grads[0], block, source_rows = attn_backward(
        grad, enc_attn, picks, owners, embed_scale, before=(early_sum,)
    )
    norm_grad = norm_blocks(norm_grads, owners, early)
    late, layer_squares, source_rows, target_rows, norm_grad, *found = share_gradients(
        [block, self_block, *ffn_blocks], [source_rows, target_rows, norm_grad], 7, (early,), (*tokens, *[grad_table][: len(tokens)])
    )
    g_norm = jnp.sum(norm_grad, axis=0)[:14]
    if owners == 4:
        g_embed, embed_squares = found
    else:
        token_grads = jnp.concatenate([source_rows, target_rows], axis=1).reshape(
            owners * 2 * length, -1
        )
        left = left[:, None]
        token_grads = jnp.concatenate(
            [jnp.where(left, token_grads, 0), jnp.where(left, 0, token_grads)], axis=1
        )
        g_paired = dot_dims(one_hot(place, halves), token_grads, 0, 0)
        g_embed = grad_table.astype(jnp.float32) + jnp.concatenate(
            jnp.split(g_paired, 2, axis=1), axis=0
        )
        embed_squares = g_embed * g_embed

    def by_matrix(shared, count):
        blocks = jnp.swapaxes(shared.reshape(replicas, count, -1, width), 0, 1)
        return blocks.reshape(count, -1, width)

    early = by_matrix(early, 3)
    g_attn = [by_matrix(part, 4) for part in (late[0], late[1], early[0])]
    g_attn = jnp.concatenate(g_attn)
    g_ffn = jnp.concatenate([late[2:].reshape(2, -1, width), early[1:]])

    matrix = replica // 2
    own_grad = lax.dynamic_index_in_dim(g_ffn, matrix, 0, keepdims=False)
    own_products = dot_dims(own_grad, own_grad, 0, 0)
    first_copy = (replica == 0).astype(jnp.float32)
    raw_squares = (
        jnp.sum(layer_squares)
        + jnp.sum(early_squares)
        + jnp.sum(embed_squares)
        + first_copy * jnp.sum(g_norm * g_norm)
    )
    few = jnp.stack([first_copy * loss_part, first_copy * count_part, raw_squares])
    few = jnp.broadcast_to(jnp.pad(few, (0, 5))[:, None], (8, 128))
    own_products, few = sum_tail(own_products, few, 8)
    loss_sum, sentences, squares = few[0, 0], few[1, 0], few[2, 0]
    grad_norm = jnp.sqrt(squares) / sentences
    factor = jnp.minimum(1.0, clip_limit / (grad_norm + norm_eps)) / sentences
    g_norm = g_norm * factor

    rows = width // 2
    own_half = lax.dynamic_slice_in_dim(own_products.astype(jnp.bfloat16), replica % 2 * rows, rows, 0)
    all_products = lax.all_gather(own_half, "vocab").reshape(4, width, width)
    weight_new = (1.0 - stat_decay) * (factor * factor)
    own_basis = renew_basis(own_products, soap_stats, soap_basis, weight_new)
    own_basis = follow(own_basis, all_products)
    new_basis = lax.all_gather(own_basis, "vocab").reshape(4, width, width)
    new_stats, new_basis = finish_matrices(weight_new, soap_stats, all_products, new_basis)

    new_norm, m_norm, v_norm = adam_update(norm_p, g_norm, norm_m, norm_v, rate_vector, 0.0)
    updated = update_matrices(
        factor,
        soap_basis,
        (g_attn, attn_w, attn_m, attn_v),
        (g_embed, embedding, embed_m, embed_v),
        (g_ffn, ffn_w, ffn_m, ffn_v),
    )
    new_attn, m_attn, v_attn, new_embed, m_embed, v_embed, new_ffn, m_ffn, v_ffn = updated
    return (
        loss_sum,
        sentences,
        grad_norm,
        new_attn,
        m_attn,
        v_attn,
        new_ffn,
        m_ffn,
        v_ffn,
        new_basis,
        new_stats,
        new_norm,
        m_norm,
        v_norm,
        new_embed,
        m_embed,
        v_embed,
    )


def solution(mesh):
    placed = (
        P("dp", None),
        P("dp", None),
        P("dp", None),
        P("dp", None),
        P("dp", None),
        P("dp", None),
        P(None, "dp", None),
        P(None, "dp", None),
        P(None, "dp", None),
        P(None, "dp", None),
        P(None, "dp", None),
        P(None, "dp", None),
        P(),
        P(),
        P(None, "dp"),
        P(None, "dp"),
        P(None, "dp"),
        P("vocab", "dp"),
        P("vocab", "dp"),
        P("vocab", "dp"),
    )
    return jax.shard_map(
        body,
        mesh=mesh,
        in_specs=placed,
        out_specs=(
            P(),
            P(),
            P(),
            P(None, "dp", None),
            P(None, "dp", None),
            P(None, "dp", None),
            P(None, "dp", None),
            P(None, "dp", None),
            P(None, "dp", None),
            P(),
            P(),
            P(None, "dp"),
            P(None, "dp"),
            P(None, "dp"),
            P("vocab", "dp"),
            P("vocab", "dp"),
            P("vocab", "dp"),
        ),
        check_vma=False,
    )
```
